32 devices in a mesh: row: 8 (over y, x, core), col: 4 (over z).
Axes of the slice: x: 2, y: 2, z: 4, core: 2. Of those that a mesh axis runs over, the one named last changes fastest.
Arguments:
- tokens: bfloat16 [16384, 2048], P('row', 'col'), may hold values from -6 to 6
- segment_ids: int32 [16, 1024], P('row'), may hold values from 0 to 7, never falling along the last dimension, each value on 1 to 512 neighbouring positions
- norm_gain: float32 [2048], P('col'), may hold values from 0.5 to 1.5
- in_zx: bfloat16 [2048, 2, 4096], P('row', None, 'col'), may hold values from -0.125 to 0.125
- in_dt: bfloat16 [2048, 64], P('row', 'col'), may hold values from -0.125 to 0.125
- in_bc: bfloat16 [2048, 256], P('row', 'col'), may hold values from -0.125 to 0.125
- conv_x: float32 [4, 4096], P(None, 'col'), may hold values from -3 to 3
- conv_x_bias: float32 [4096], P('col'), may hold values from -3 to 3
- conv_bc: float32 [4, 256], P(None, 'col'), may hold values from -3 to 3
- conv_bc_bias: float32 [256], P('col'), may hold values from -3 to 3
- dt_bias: float32 [64], P('col'), may hold values from -5 to -1.5
- a_log: float32 [64], P('col'), may hold values from 0 to 2.77
- d_skip: float32 [64], P('col'), may hold values from 0.5 to 1.5
- inner_gain: float32 [4096], P('col'), may hold values from 0.5 to 1.5
- out_proj: bfloat16 [2048, 4096], P('row', 'col'), may hold values from -0.09375 to 0.09375
- cotangent: bfloat16 [16384, 2048], P('row', 'col'), may hold values from -6 to 6
Outputs:
- output: bfloat16 [16384, 2048], P('row', 'col')
- tokens_grad: bfloat16 [16384, 2048], P('row', 'col')
- norm_gain_grad: float32 [2048], P('col')
- in_zx_grad: float32 [2048, 2, 4096], P('row', None, 'col')
- in_dt_grad: float32 [2048, 64], P('row', 'col')
- in_bc_grad: float32 [2048, 256], P('row', 'col')
- conv_x_grad: float32 [4, 4096], P(None, 'col')
- conv_x_bias_grad: float32 [4096], P('col')
- conv_bc_grad: float32 [4, 256], P(None, 'col')
- conv_bc_bias_grad: float32 [256], P('col')
- dt_bias_grad: float32 [64], P('col')
- a_log_grad: float32 [64], P('col')
- d_skip_grad: float32 [64], P('col')
- inner_gain_grad: float32 [4096], P('col')
- out_proj_grad: float32 [2048, 4096], P('row', 'col')
The draws below stay inside these ranges and needn't reach their ends.
Inputs may be any that keep to these rules, and one draw needn't show every extreme that they name: `segment_ids`: within each row (one packed sequence) ids never fall; each document covers at most 512 tokens, and some document exactly that many.
All inputs are finite; a program needn't handle non-finite values.
Results may differ from the reference program's by a relative error of at most 0.012.
Values may be sent and summed in bfloat16 or wider, within the bound.
A program may use at most 320 MiB of HBM per device.

```python
import math
import jax
import jax.numpy as jnp
import numpy as np
from jax import lax

D = 2048
HEADS = 64
HEADDIM = 64
STATE = 128
KW = 4
SPAN = 256
SEQLEN = 1024
DOCS = 8
INNER = 4096
SEQS = 16
TOKENS = 16384


def block_scale(stream_key, extent, split, smallest, high):
    factor_of, own = 1.0, jax.random.fold_in(stream_key, 6)
    for axis_at, parts in split:
        heights = jnp.exp(jax.random.uniform(jax.random.fold_in(own, axis_at), (parts,), jnp.float32, smallest / len(split), high / len(split)))
        factor_of = factor_of * jnp.repeat(heights, extent[axis_at] // parts).reshape([-1 if axis == axis_at else 1 for axis in range(len(extent))])
    return factor_of


def split_up(number_of, total, reach, slope):
    loads = [(1 << 20) // math.isqrt(standing ** slope) + 1 for standing in range(2, number_of + 1)]
    spare, given = total - reach - (number_of - 1), [1] * (number_of - 1)
    while spare > 0:
        free = [i for i in range(number_of - 1) if given[i] < reach]
        mass, remaining = sum([loads[i] for i in free]), spare
        for i in free:
            addition = min(reach - given[i], max(1, remaining * loads[i] // mass), spare)
            given[i] = given[i] + addition
            spare = spare - addition
    return np.array([reach] + given)


def ragged(own_key, number_of, total, most, slope):
    if number_of == 2:
        one = jax.random.randint(own_key, (), max(1, total - most), min(most, total - 1) + 1)
        return jnp.stack([one, total - one])
    lengths = jnp.asarray(split_up(number_of, total, most, slope), jnp.int32)
    couples = (number_of - 1) // 2
    source_of, taker = lengths[1:1 + 2 * couples:2], lengths[2:2 + 2 * couples:2]
    room = jnp.minimum(source_of - 1, most - taker)
    passed = jax.random.randint(jax.random.fold_in(own_key, 1), (couples,), 0, 1 << 20) % (room + 1)
    lengths = lengths.at[1:1 + 2 * couples:2].set(source_of - passed).at[2:2 + 2 * couples:2].set(taker + passed)
    return lengths[jax.random.permutation(jax.random.fold_in(own_key, 2), number_of)]


def scatter_about(key, extent, width, limit, cuts=(), kind=jnp.bfloat16):
    values = jax.random.normal(key, extent, jnp.float32) * width
    if len(cuts) > 0:
        values = block_scale(key, extent, cuts, -0.22, 0.18) * values
    return jnp.clip(values, min=-limit, max=limit).astype(kind)


def setup_inputs(seed: int = 0) -> dict:
    keys = jax.random.split(jax.random.key(seed), 17)
    tokens = scatter_about(keys[0], (TOKENS, D), 1.0, 6.0, ((0, 8), (1, 4)))
    segment_ids = jax.vmap(lambda own: jnp.searchsorted(jnp.cumsum(ragged(own, DOCS, SEQLEN, SEQLEN // 2, 2)), jnp.arange(SEQLEN), side="right"))(jax.random.split(keys[1], SEQS)).reshape((SEQS, SEQLEN)).astype(jnp.int32)
    norm_gain = jnp.clip(1.0 + 0.1 * jax.random.normal(keys[2], (D,), jnp.float32), 0.5, 1.5)
    in_zx = scatter_about(keys[3], (D, 2, INNER), D ** -0.5, 0.125, ((0, 8), (2, 4)))
    in_dt = scatter_about(keys[4], (D, HEADS), D ** -0.5, 0.125, ((0, 8), (1, 4)))
    in_bc = scatter_about(keys[5], (D, 2 * STATE), D ** -0.5, 0.125, ((0, 8), (1, 4)))
    conv_x = scatter_about(keys[6], (KW, INNER), KW ** -0.5, 3.0, ((1, 4),), jnp.float32)
    conv_x_bias = scatter_about(keys[7], (INNER,), 0.5, 3.0, ((0, 4),), jnp.float32)
    conv_bc = scatter_about(keys[8], (KW, 2 * STATE), KW ** -0.5, 3.0, ((1, 4),), jnp.float32)
    conv_bc_bias = scatter_about(keys[9], (2 * STATE,), 0.5, 3.0, ((0, 4),), jnp.float32)
    dt_bias = jnp.clip(-5.0 + 3.5 * jax.random.uniform(keys[10], (HEADS,), jnp.float32) ** block_scale(keys[10], (HEADS,), ((0, 4),), -0.2, 0.2), -5.0, -1.5)
    a_log = jnp.clip(2.77 * jax.random.uniform(keys[11], (HEADS,), jnp.float32) ** block_scale(keys[11], (HEADS,), ((0, 4),), -0.2, 0.2), 0.0, 2.77)
    d_skip = jnp.clip(0.5 + 1.0 * jax.random.uniform(keys[12], (HEADS,), jnp.float32) ** block_scale(keys[12], (HEADS,), ((0, 4),), -0.2, 0.2), 0.5, 1.5)
    inner_gain = jnp.clip(1.0 + 0.1 * jax.random.normal(keys[13], (INNER,), jnp.float32), 0.5, 1.5)
    out_proj = scatter_about(keys[14], (D, INNER), INNER ** -0.5, 0.09375, ((0, 8), (1, 4)))
    cotangent = scatter_about(keys[15], (TOKENS, D), 1.0, 6.0, ((0, 8), (1, 4)))
    return dict(tokens=tokens, segment_ids=segment_ids, norm_gain=norm_gain, in_zx=in_zx, in_dt=in_dt, in_bc=in_bc, conv_x=conv_x, conv_x_bias=conv_x_bias, conv_bc=conv_bc, conv_bc_bias=conv_bc_bias, dt_bias=dt_bias, a_log=a_log, d_skip=d_skip, inner_gain=inner_gain, out_proj=out_proj, cotangent=cotangent)


EPS = 1e-05

@jax.custom_vjp
def low(v):
    return lax.optimization_barrier(v.astype(jnp.bfloat16)).astype(jnp.float32)

@jax.custom_vjp
def low_back(v):
    return v

def low_keep(v):
    return (low(v), None)

def low_pass(kept, grad):
    return (grad,)

def back_keep(v):
    return (v, None)

def back_low(kept, grad):
    return (low(grad),)
low.defvjp(low_keep, low_pass)
low_back.defvjp(back_keep, back_low)

def causal_conv(values, weight, shift_add, seg_rows):
    taps = weight.shape[0]
    length = values.shape[1]
    total = shift_add + weight[taps - 1] * values
    for lag_step in range(1, taps):
        earlier = jnp.pad(values, ((0, 0), (lag_step, 0), (0, 0)))[:, :length]
        earlier_seg = jnp.pad(seg_rows, ((0, 0), (lag_step, 0)), constant_values=-1)[:, :length]
        keeper = (earlier_seg == seg_rows).astype(values.dtype)
        total = total + weight[taps - 1 - lag_step] * earlier * keeper[..., None]
    return total

def span_scan(x_heads, b_rows, c_rows, dt_step, decay_rate, seg_line):
    highest = lax.Precision.HIGHEST
    length, heads, hdim = x_heads.shape
    nstate = b_rows.shape[1]
    blocks = length // SPAN
    x_blocks = x_heads.reshape(blocks, SPAN, heads, hdim)
    b_blocks = b_rows.reshape(blocks, SPAN, nstate)
    c_blocks = c_rows.reshape(blocks, SPAN, nstate)
    dt_blocks = dt_step.reshape(blocks, SPAN, heads)
    seg_blocks = seg_line.reshape(blocks, SPAN)
    log_decay = jnp.cumsum(-dt_blocks * decay_rate, axis=1)
    positions = jnp.arange(SPAN)
    causal = positions[:, None] >= positions[None, :]
    same_doc = (seg_blocks[:, :, None] == seg_blocks[:, None, :]) & causal[None]
    same_mask = same_doc[..., None]
    log_gap = log_decay[:, :, None, :] - log_decay[:, None, :, :]
    decays = jnp.where(same_mask, jnp.exp(jnp.where(same_mask, log_gap, 0.0)), 0.0)
    scores = jnp.einsum('ctn,csn->cts', c_blocks, b_blocks, precision=highest)
    weights = scores[..., None] * decays * dt_blocks[:, None, :, :]
    intra_out = jnp.einsum('ctsh,cshp->cthp', weights, x_blocks, precision=highest)
    last_seg = seg_blocks[:, -1]
    tail_mask = (seg_blocks == last_seg[:, None]).astype(x_heads.dtype)
    to_end = jnp.exp(log_decay[:, -1:, :] - log_decay) * dt_blocks * tail_mask[..., None]
    local_state = jnp.einsum('csh,cshp,csn->chpn', to_end, x_blocks, b_blocks, precision=highest)
    prev_last = jnp.concatenate([jnp.full((1,), -1, jnp.int32), last_seg[:-1].astype(jnp.int32)])
    carry_on = (last_seg == prev_last).astype(x_heads.dtype)
    span_decay = jnp.exp(log_decay[:, -1, :])

    def advance(state, items):
        block_state, keeping, factor = items
        return (keeping * factor[:, None, None] * state + block_state, state)
    zero_state = jnp.zeros((heads, hdim, nstate), x_heads.dtype)
    _, entering = lax.scan(advance, zero_state, (local_state, carry_on, span_decay))
    head_mask = (seg_blocks == prev_last[:, None]).astype(x_heads.dtype)
    from_prev = jnp.einsum('ctn,chpn->cthp', c_blocks, entering, precision=highest)
    from_prev = from_prev * (jnp.exp(log_decay) * head_mask[..., None])[..., None]
    return (intra_out + from_prev).reshape(length, heads, hdim)

def mixer(x_group, seg_group, params):
    norm_gain, in_zx, in_dt, in_bc, conv_x, conv_x_bias, conv_bc, conv_bc_bias, dt_bias, a_log, d_skip, inner_gain, out_proj = params
    highest = lax.Precision.HIGHEST
    seq_count = seg_group.shape[0]
    inv_root = lax.rsqrt(lax.optimization_barrier(jnp.mean(x_group * x_group, axis=1, keepdims=True)) + EPS)
    normed = low(x_group * inv_root * norm_gain)
    zx_raw = jnp.einsum('td,dki->tki', normed, in_zx, precision=highest)
    gate_raw = low_back(zx_raw[:, 0])
    x_raw = low_back(zx_raw[:, 1])
    dt_raw = low_back(jnp.dot(normed, in_dt, precision=highest))
    bc_raw = low_back(jnp.dot(normed, in_bc, precision=highest))
    x_conv = low(jax.nn.silu(causal_conv(x_raw.reshape(seq_count, SEQLEN, INNER), conv_x, conv_x_bias, seg_group)))
    bc_conv = low(jax.nn.silu(causal_conv(bc_raw.reshape(seq_count, SEQLEN, 2 * STATE), conv_bc, conv_bc_bias, seg_group)))
    dt_step = jax.nn.softplus(dt_raw + dt_bias).reshape(seq_count, SEQLEN, HEADS)
    decay_rate = jnp.exp(a_log)

    def one_sequence(items):
        x_seq, bc_seq, dt_seq, seg_seq = items
        return span_scan(x_seq.reshape(SEQLEN, HEADS, HEADDIM), bc_seq[:, :STATE], bc_seq[:, STATE:], dt_seq, decay_rate, seg_seq)
    scanned = lax.map(one_sequence, (x_conv, bc_conv, dt_step, seg_group))
    x_heads = x_conv.reshape(seq_count * SEQLEN, HEADS, HEADDIM)
    y_out = scanned.reshape(seq_count * SEQLEN, HEADS, HEADDIM) + d_skip[:, None] * x_heads
    gated = y_out.reshape(seq_count * SEQLEN, INNER) * jax.nn.silu(gate_raw)
    inner_root = lax.rsqrt(lax.optimization_barrier(jnp.mean(gated * gated, axis=1, keepdims=True)) + EPS)
    hidden = low(gated * inner_root * inner_gain)
    return x_group + jnp.dot(hidden, out_proj.T, precision=highest)

def reference(tokens, segment_ids, norm_gain, in_zx, in_dt, in_bc, conv_x, conv_x_bias, conv_bc, conv_bc_bias, dt_bias, a_log, d_skip, inner_gain, out_proj, cotangent):
    group = math.gcd(SEQS, max(1, 4096 // SEQLEN))
    x_input = tokens.astype(jnp.float32)
    params = (norm_gain.astype(jnp.float32), in_zx.astype(jnp.float32), in_dt.astype(jnp.float32), in_bc.astype(jnp.float32), conv_x.astype(jnp.float32), conv_x_bias.astype(jnp.float32), conv_bc.astype(jnp.float32), conv_bc_bias.astype(jnp.float32), dt_bias.astype(jnp.float32), a_log.astype(jnp.float32), d_skip.astype(jnp.float32), inner_gain.astype(jnp.float32), out_proj.astype(jnp.float32))

    def forward(x_all, *param_list):
        x_groups = x_all.reshape(SEQS // group, group * SEQLEN, D)
        seg_groups = segment_ids.reshape(SEQS // group, group, SEQLEN)

        def run_block(pair_items):
            return mixer(pair_items[0], pair_items[1], param_list)
        outs_all = lax.map(jax.checkpoint(run_block), (x_groups, seg_groups))
        return outs_all.reshape(TOKENS, D)
    output, pull_back = jax.vjp(forward, x_input, *params)
    grads = pull_back(cotangent.astype(jnp.float32))
    g_tokens, g_norm, g_zx, g_dt, g_bc, g_cx, g_cxb, g_cb, g_cbb, g_dtb, g_alog, g_dskip, g_igain, g_out = grads
    return (output.astype(jnp.bfloat16), g_tokens.astype(jnp.bfloat16), g_norm, g_zx, g_dt, g_bc, g_cx, g_cxb, g_cb, g_cbb, g_dtb, g_alog, g_dskip, g_igain, g_out)
```

```python
import functools

import jax
import jax.numpy as jnp
from jax import lax
from jax.experimental import pallas as pl
from jax.experimental.pallas import tpu as pltpu
from jax.sharding import Mesh, PartitionSpec as P

HEADDIM = 64
STATE = 128
KW = 4
EPS = 1e-05
SPAN = 256
GROUP = 256
PER = GROUP // HEADDIM
F32 = jnp.float32
BF16 = jnp.bfloat16
VMEM_LIMIT = 60 * 1024 * 1024


def dot_nn(a, b):
    return lax.dot_general(a, b, (((1,), (0,)), ((), ())), preferred_element_type=F32)


def dot_nt(a, b):
    return lax.dot_general(a, b, (((1,), (1,)), ((), ())), preferred_element_type=F32)


def dot_tn(a, b):
    return lax.dot_general(a, b, (((0,), (0,)), ((), ())), preferred_element_type=F32)


def dot_exact(a, b):
    return lax.dot_general(
        a, b, (((1,), (0,)), ((), ())), preferred_element_type=F32, precision=lax.Precision.HIGHEST
    )


def twice(v):
    return jnp.concatenate([v, v], axis=1)


def spread(cols):
    rows = cols.shape[0]
    lane = lax.broadcasted_iota(jnp.int32, (rows, 128), 1)
    low = lane < HEADDIM
    first = jnp.where(low, cols[:, 0:1], cols[:, 1:2])
    second = jnp.where(low, cols[:, 2:3], cols[:, 3:4])
    return jnp.concatenate([first, second], axis=1)


def head_mask(h):
    lane = lax.broadcasted_iota(jnp.int32, (1, GROUP), 1)
    return ((lane >= h * HEADDIM) & (lane < (h + 1) * HEADDIM)).astype(F32).astype(BF16)


def prep_kernel(
    small_ref, segc_ref, segr_ref, bcp_ref, hp_ref,
    bc_ref, bct_ref, g_ref, gt_ref, colp_ref, cumt_ref, kexp_ref, lag_ref,
):
    length = small_ref.shape[0]
    blocks = length // SPAN
    groups = colp_ref.shape[0]
    seg = segc_ref[...]
    pos = lax.broadcasted_iota(jnp.int32, (length, 128), 0)
    lag = jnp.zeros((length, 128), F32)
    for j in range(1, KW):
        lag = lag + ((pltpu.roll(seg, j, 0) == seg) & (pos >= j)).astype(F32)
    lag_ref[0:length, :] = lag
    lag_ref[length:, :] = jnp.zeros((8, 128), F32)
    lag2 = twice(lag)
    raw = small_ref[:, 0:256]
    v = bcp_ref[4:5, :] + bcp_ref[3:4, :] * raw
    for j in range(1, KW):
        v = v + bcp_ref[3 - j : 4 - j, :] * jnp.where(lag2 >= j, pltpu.roll(raw, j, 0), 0.0)
    act = v * jax.nn.sigmoid(v)
    bc_ref[...] = act.astype(BF16)
    bct_ref[...] = jnp.transpose(act).astype(BF16)
    z = small_ref[:, 256:384] + hp_ref[0:1, :]
    dt = jnp.maximum(z, 0.0) + jnp.log1p(jnp.exp(-jnp.abs(z)))
    a = -dt * jnp.exp(hp_ref[1:2, :])
    tri_r = lax.broadcasted_iota(jnp.int32, (SPAN, SPAN), 0)
    tri_c = lax.broadcasted_iota(jnp.int32, (SPAN, SPAN), 1)
    lower = (tri_r >= tri_c).astype(F32)
    seg_row = segr_ref[0:1, :]
    for c in range(blocks):
        r0 = c * SPAN
        rows = slice(r0, r0 + SPAN)
        cum = dot_exact(lower, a[rows])
        segb = seg[rows]
        last = seg[r0 + SPAN - 1 : r0 + SPAN]
        tail = (segb == last).astype(F32)
        end = cum[SPAN - 1 : SPAN]
        q = jnp.exp(end - cum) * tail
        if c > 0:
            prev = seg[r0 - 1 : r0]
            p = jnp.exp(cum) * (segb == prev).astype(F32)
            k = jnp.exp(end) * (last == prev).astype(F32)
        else:
            p = jnp.zeros_like(cum)
            k = jnp.zeros_like(end)
        kexp_ref[c : c + 1, :] = k
        cumt = jnp.transpose(cum)
        dtb = dt[rows]
        for g in range(groups):
            hs = slice(PER * g, PER * g + PER)
            colp_ref[g, rows, 0:4] = cum[:, hs]
            colp_ref[g, rows, 4:8] = dtb[:, hs]
            colp_ref[g, rows, 8:12] = p[:, hs]
            colp_ref[g, rows, 12:16] = q[:, hs]
            cumt_ref[g, 0:4, rows] = cumt[hs, :]
        bb = bc_ref[rows, 0:STATE]
        cc = bc_ref[rows, STATE : 2 * STATE]
        same = twice(segb) == seg_row[:, rows]
        g_ref[rows, :] = jnp.where(same & (tri_r >= tri_c), dot_nt(cc, bb), 0.0)
        gt_ref[rows, :] = jnp.where(same & (tri_r <= tri_c), dot_nt(bb, cc), 0.0)
    kexp_ref[blocks:, :] = jnp.zeros((kexp_ref.shape[0] - blocks, 128), F32)


def conv_rows(xr_ref, lag_ref, chan_ref, r0):
    cur = xr_ref[pl.ds(r0, SPAN), :]
    before = xr_ref[pl.ds(pl.multiple_of(jnp.maximum(r0 - 8, 0), 8), 8), :]
    both = jnp.concatenate([before, cur], axis=0)
    lag = twice(lag_ref[pl.ds(r0, SPAN), :])
    v = chan_ref[4:5, :] + chan_ref[3:4, :] * cur
    for j in range(1, KW):
        earlier = pltpu.roll(both, j, 0)[8:]
        v = v + chan_ref[3 - j : 4 - j, :] * jnp.where(lag >= j, earlier, 0.0)
    return cur, v


def scan_kernel(
    gate_ref, xr_ref, chan_ref, lag_ref, bc_ref, bct_ref, g_ref, colp_ref, cumt_ref, kexp_ref,
    y_ref, gated_ref, sq_ref, st_ref, state,
):
    length = gate_ref.shape[0]
    blocks = length // SPAN
    state[...] = jnp.zeros_like(state)

    @pl.when(pl.program_id(0) == 0)
    def _():
        sq_ref[...] = jnp.zeros_like(sq_ref)

    def body(c, carry):
        r0 = pl.multiple_of(c * SPAN, SPAN)
        rows = pl.ds(r0, SPAN)
        _, v = conv_rows(xr_ref, lag_ref, chan_ref, r0)
        xc = (v * jax.nn.sigmoid(v)).astype(BF16).astype(F32)
        cp = colp_ref[0, rows, :]
        xd = (spread(cp[:, 4:8]) * xc).astype(BF16)
        px = spread(cp[:, 8:12])
        qx = spread(cp[:, 12:16])
        gb = g_ref[rows, :]
        lefts, rights = [], []
        for h in range(PER):
            gap = cp[:, h : h + 1] - cumt_ref[0, h : h + 1, rows]
            lefts.append((gb * jnp.exp(jnp.minimum(gap, 0.0))).astype(BF16))
            rights.append(xd * head_mask(h))
        y = dot_nn(jnp.concatenate(lefts, axis=1), jnp.concatenate(rights, axis=0))
        st = state[...]
        stb = st.astype(BF16)
        st_ref[c] = stb
        y = y + px * dot_nn(bc_ref[rows, STATE : 2 * STATE], stb)
        kx = kexp_ref[pl.ds(c, 1), :]
        state[...] = kx * st + dot_nn(bct_ref[0:STATE, rows], (qx * xd.astype(F32)).astype(BF16))
        y = y + chan_ref[5:6, :] * xc
        y_ref[rows, :] = y
        gate = gate_ref[rows, :]
        gated = y * (gate * jax.nn.sigmoid(gate))
        gated_ref[rows, :] = gated.astype(BF16)
        sq = gated * gated
        sq_ref[rows, :] += sq[:, 0:128] + sq[:, 128:256]
        return carry

    lax.fori_loop(0, blocks, body, 0)


def scan_grad_kernel(
    gate_ref, xr_ref, y_ref, dh_ref, chan_ref, lag_ref, ir_ref, cf_ref, bc_ref, bct_ref, gt_ref,
    colp_ref, cumt_ref, kexp_ref, st_ref, segc_ref, segr_ref,
    dgate_ref, dxr_ref, hd_ref, end_ref, chg_ref, dbc_ref, nd_ref,
    dst, head, dgt,
):
    length = gate_ref.shape[0]
    blocks = length // SPAN
    step = pl.program_id(0)
    dst[...] = jnp.zeros_like(dst)
    head[...] = jnp.zeros_like(head)
    end_ref[...] = jnp.zeros_like(end_ref)
    chg_ref[...] = jnp.zeros_like(chg_ref)

    @pl.when(step == 0)
    def _():
        dgt[...] = jnp.zeros_like(dgt)
        dbc_ref[...] = jnp.zeros_like(dbc_ref)
        nd_ref[...] = jnp.zeros_like(nd_ref)

    def total(v):
        return jnp.sum(v, axis=0, keepdims=True)

    def body(back, carry):
        c = blocks - 1 - back
        r0 = pl.multiple_of(c * SPAN, SPAN)
        rows = pl.ds(r0, SPAN)
        cur, v = conv_rows(xr_ref, lag_ref, chan_ref, r0)
        sv = jax.nn.sigmoid(v)
        xc = (v * sv).astype(BF16).astype(F32)
        cp = colp_ref[0, rows, :]
        dtx = spread(cp[:, 4:8])
        px = spread(cp[:, 8:12])
        qx = spread(cp[:, 12:16])
        xd = (dtx * xc).astype(BF16)
        xdf = xd.astype(F32)
        gate = gate_ref[rows, :]
        y = y_ref[rows, :]
        dh = dh_ref[rows, :].astype(F32)
        ir = twice(ir_ref[rows, :])
        cf = twice(cf_ref[rows, :])
        sg = jax.nn.sigmoid(gate)
        sl = gate * sg
        gated = y * sl
        dgd = ir * (dh * chan_ref[6:7, :]) - gated * cf
        dy = dgd * sl
        dgate = dgd * y * (sg * (1.0 + gate * (1.0 - sg)))
        dgate_ref[rows, :] = dgate.astype(BF16)
        dyb = dy.astype(BF16)
        gt = gt_ref[rows, :]
        lefts, rights = [], []
        acc = dgt[rows, :]
        for h in range(PER):
            gap = cumt_ref[0, h : h + 1, rows] - cp[:, h : h + 1]
            et = jnp.exp(jnp.minimum(gap, 0.0))
            lefts.append((gt * et).astype(BF16))
            dym = dyb * head_mask(h)
            rights.append(dym)
            acc = acc + dot_nt(xd, dym) * et
        dgt[rows, :] = acc
        u = dot_nn(jnp.concatenate(lefts, axis=1), jnp.concatenate(rights, axis=0))
        ds = dst[...]
        dsb = ds.astype(BF16)
        bb = bc_ref[rows, 0:STATE]
        cc = bc_ref[rows, STATE : 2 * STATE]
        ui = qx * dot_nn(bb, dsb)
        u = u + ui
        dxc = chan_ref[5:6, :] * dy + dtx * u
        yscan = y - chan_ref[5:6, :] * xc
        terms = jnp.concatenate([dyb.astype(F32) * yscan - xdf * u, xc * u], axis=1)
        hi = terms.astype(BF16)
        lo = (terms - hi.astype(F32)).astype(BF16)
        pick_r = lax.broadcasted_iota(jnp.int32, (2 * GROUP, 128), 0)
        pick_c = lax.broadcasted_iota(jnp.int32, (2 * GROUP, 128), 1)
        pick = (pick_r // HEADDIM == pick_c).astype(F32).astype(BF16)
        sums = dot_nn(hi, pick) + dot_nn(lo, pick)
        hd_ref[0, rows, :] = sums[:, 0:8]
        stb = st_ref[c]
        kx = kexp_ref[pl.ds(c, 1), :]
        end_ref[pl.ds(c, 1), :] = total(xdf * ui) + kx * total(ds * stb.astype(F32))
        pdy = (px * dyb.astype(F32)).astype(BF16)
        dbc_ref[rows, 0:STATE] += dot_nt((qx * xdf).astype(BF16), dsb)
        dbc_ref[rows, STATE : 2 * STATE] += dot_nt(pdy, stb)
        dst[...] = kx * ds + dot_nn(bct_ref[STATE : 2 * STATE, rows], pdy)
        dv = dxc * (sv * (1.0 + v * (1.0 - sv)))
        after = pl.ds(pl.multiple_of(r0 + SPAN, 8), 8)
        wide = jnp.concatenate([dv, head[...]], axis=0)
        lagw = jnp.concatenate([twice(lag_ref[rows, :]), twice(lag_ref[after, :])], axis=0)
        head[...] = dv[0:8]
        dxr = chan_ref[3:4, :] * dv
        chg_ref[3:4, :] += total(cur * dv)
        chg_ref[4:5, :] += total(dv)
        chg_ref[5:6, :] += total(dy * xc)
        chg_ref[6:7, :] += total(dh * gated * ir)
        for j in range(1, KW):
            later = pltpu.roll(jnp.where(lagw >= j, wide, 0.0), SPAN + 8 - j, 0)[0:SPAN]
            dxr = dxr + chan_ref[3 - j : 4 - j, :] * later
            chg_ref[3 - j : 4 - j, :] += total(cur * later)
        dxr_ref[rows, :] = dxr.astype(BF16)
        nd = dgate * gate + dxr * cur
        nd_ref[rows, :] += nd[:, 0:128] + nd[:, 128:256]
        return carry

    lax.fori_loop(0, blocks, body, 0)

    @pl.when(step == pl.num_programs(0) - 1)
    def _():
        tri_r = lax.broadcasted_iota(jnp.int32, (SPAN, SPAN), 0)
        tri_c = lax.broadcasted_iota(jnp.int32, (SPAN, SPAN), 1)
        for c in range(blocks):
            rows = slice(c * SPAN, (c + 1) * SPAN)
            same = twice(segc_ref[rows, :]) == segr_ref[0:1, rows]
            full = jnp.where(same & (tri_r <= tri_c), dgt[rows, :], 0.0)
            dbc_ref[rows, 0:STATE] += dot_nn(full.astype(BF16), bc_ref[rows, STATE : 2 * STATE])
            dbc_ref[rows, STATE : 2 * STATE] += dot_nn(
                jnp.transpose(full).astype(BF16), bc_ref[rows, 0:STATE]
            )


def whole(shape):
    return pl.BlockSpec(shape, lambda g: (0,) * len(shape))


def tile(rows, first=0):
    return pl.BlockSpec((rows, GROUP), lambda g: (0, g + first))


def prep(small, segc, segr, bcp, hp, groups):
    length = small.shape[0]
    return pl.pallas_call(
        prep_kernel,
        out_shape=(
            jax.ShapeDtypeStruct((length, 2 * STATE), BF16),
            jax.ShapeDtypeStruct((2 * STATE, length), BF16),
            jax.ShapeDtypeStruct((length, SPAN), F32),
            jax.ShapeDtypeStruct((length, SPAN), F32),
            jax.ShapeDtypeStruct((groups, length, 16), F32),
            jax.ShapeDtypeStruct((groups, 8, length), F32),
            jax.ShapeDtypeStruct((8, 128), F32),
            jax.ShapeDtypeStruct((length + 8, 128), F32),
        ),
        compiler_params=pltpu.CompilerParams(vmem_limit_bytes=VMEM_LIMIT),
        name="prep",
    )(small, segc, segr, bcp, hp)


def scan(gate, xr, chan, lag, bc, bct, gmat, colp, cumt, kexp, first):
    length, width = gate.shape
    groups = width // GROUP
    blocks = length // SPAN
    return pl.pallas_call(
        scan_kernel,
        grid=(groups,),
        in_specs=[
            tile(length),
            tile(length),
            tile(8),
            whole((length + 8, 128)),
            whole((length, 2 * STATE)),
            whole((2 * STATE, length)),
            whole((length, SPAN)),
            pl.BlockSpec((1, length, 16), lambda g: (g + first, 0, 0)),
            pl.BlockSpec((1, 8, length), lambda g: (g + first, 0, 0)),
            tile(8, first),
        ],
        out_specs=[
            tile(length),
            tile(length),
            whole((length, 128)),
            pl.BlockSpec((blocks, STATE, GROUP), lambda g: (0, 0, g)),
        ],
        out_shape=(
            jax.ShapeDtypeStruct((length, width), F32),
            jax.ShapeDtypeStruct((length, width), BF16),
            jax.ShapeDtypeStruct((length, 128), F32),
            jax.ShapeDtypeStruct((blocks, STATE, width), BF16),
        ),
        scratch_shapes=[pltpu.VMEM((STATE, GROUP), F32)],
        compiler_params=pltpu.CompilerParams(vmem_limit_bytes=VMEM_LIMIT),
        name="scan",
    )(gate, xr, chan, lag, bc, bct, gmat, colp, cumt, kexp)


def scan_grad(
    gate, xr, y, dh, chan, lag, ir, cf, bc, bct, gtmat, colp, cumt, kexp, st, segc, segr, first
):
    length, width = gate.shape
    groups = width // GROUP
    blocks = length // SPAN
    return pl.pallas_call(
        scan_grad_kernel,
        grid=(groups,),
        in_specs=[
            tile(length),
            tile(length),
            tile(length),
            tile(length),
            tile(8),
            whole((length + 8, 128)),
            whole((length, 128)),
            whole((length, 128)),
            whole((length, 2 * STATE)),
            whole((2 * STATE, length)),
            whole((length, SPAN)),
            pl.BlockSpec((1, length, 16), lambda g: (g + first, 0, 0)),
            pl.BlockSpec((1, 8, length), lambda g: (g + first, 0, 0)),
            tile(8, first),
            pl.BlockSpec((blocks, STATE, GROUP), lambda g: (0, 0, g)),
            whole((length, 128)),
            whole((8, length)),
        ],
        out_specs=[
            tile(length),
            tile(length),
            pl.BlockSpec((1, length, 8), lambda g: (g, 0, 0)),
            tile(8),
            tile(8),
            whole((length, 2 * STATE)),
            whole((length, 128)),
        ],
        out_shape=(
            jax.ShapeDtypeStruct((length, width), BF16),
            jax.ShapeDtypeStruct((length, width), BF16),
            jax.ShapeDtypeStruct((groups, length, 8), F32),
            jax.ShapeDtypeStruct((8, width), F32),
            jax.ShapeDtypeStruct((8, width), F32),
            jax.ShapeDtypeStruct((length, 2 * STATE), F32),
            jax.ShapeDtypeStruct((length, 128), F32),
        ),
        scratch_shapes=[
            pltpu.VMEM((STATE, GROUP), F32),
            pltpu.VMEM((8, GROUP), F32),
            pltpu.VMEM((length, SPAN), F32),
        ],
        compiler_params=pltpu.CompilerParams(vmem_limit_bytes=VMEM_LIMIT),
        name="scan_grad",
    )(gate, xr, y, dh, chan, lag, ir, cf, bc, bct, gtmat, colp, cumt, kexp, st, segc, segr)


def shifted_silu(raw, taps, bias, lag):
    v = bias + taps[KW - 1] * raw
    for j in range(1, KW):
        earlier = jnp.pad(raw, ((j, 0), (0, 0)))[: raw.shape[0]]
        v = v + taps[KW - 1 - j] * jnp.where(lag[:, None] >= j, earlier, 0.0)
    return jax.nn.silu(v)


def build(nrow, nl):
    def swap(v):
        return lax.ppermute(v, "zh", [(0, 1), (1, 0)])

    def pair_sum(v):
        if nl == 2:
            return v + lax.ppermute(v, "zl", [(0, 1), (1, 0)])
        return lax.psum(v, "zl")

    def row_gather(v):
        return lax.all_gather(v, "row", axis=0, tiled=True)

    def row_scatter(v):
        return lax.psum_scatter(v, "row", scatter_dimension=0, tiled=True)

    def per_device(
        tokens, segment_ids, norm_gain, in_zx, in_dt, in_bc, conv_x, conv_x_bias, conv_bc,
        conv_bc_bias, dt_bias, a_log, d_skip, inner_gain, out_proj, cotangent,
    ):
        seq_count, length = segment_ids.shape
        assert seq_count == 2
        feat = tokens.shape[1]
        width = feat * 2 * nl
        cb = inner_gain.shape[0]
        hb = dt_bias.shape[0]
        inner = cb * 2 * nl
        blocks = length // SPAN
        gb = cb // GROUP
        mh = lax.axis_index("zh")
        ml = lax.axis_index("zl")
        first_h = mh == 0

        def mine(v, axis=0):
            return lax.dynamic_index_in_dim(v, mh, axis, keepdims=False)

        def other(v, axis=0):
            return lax.dynamic_index_in_dim(v, 1 - mh, axis, keepdims=False)

        def gather_features(v):
            halves = v.reshape(2, length, feat)
            own = mine(halves)
            got = swap(other(halves))
            both = jnp.where(first_h, jnp.stack([own, got]), jnp.stack([got, own]))
            if nl == 2:
                rest = lax.ppermute(both, "zl", [(0, 1), (1, 0)])
                every = jnp.where(ml == 0, jnp.stack([both, rest], 1), jnp.stack([rest, both], 1))
            else:
                every = jnp.moveaxis(lax.all_gather(both, "zl"), 0, 1)
            full = jnp.transpose(every, (2, 0, 1, 3)).reshape(length, width)
            return own, got, full

        def scatter_features(v):
            parts = v.reshape(length, 2, nl, feat)
            if nl == 2:
                keep = lax.dynamic_index_in_dim(parts, ml, 2, keepdims=False)
                send = lax.dynamic_index_in_dim(parts, 1 - ml, 2, keepdims=False)
                got = lax.ppermute(send, "zl", [(0, 1), (1, 0)])
                both = keep.astype(F32) + got.astype(F32)
            else:
                both = lax.psum_scatter(parts, "zl", scatter_dimension=2, tiled=False).astype(F32)
            return mine(both, 1), other(both, 1)

        def to_rows(own, got):
            back = swap(got)
            return jnp.where(
                first_h, jnp.concatenate([own, back], 0), jnp.concatenate([back, own], 0)
            )

        chan = jnp.concatenate(
            [
                conv_x,
                conv_x_bias[None],
                jnp.repeat(d_skip, HEADDIM)[None],
                inner_gain[None],
                jnp.pad(jnp.concatenate([dt_bias, a_log]), (0, cb - 2 * hb))[None],
            ],
            axis=0,
        )
        chans = (chan, swap(chan))
        bcn = conv_bc.shape[1]
        packed = jnp.concatenate([norm_gain, conv_bc.reshape(-1), conv_bc_bias])
        packs = lax.all_gather(packed, ("zh", "zl"))
        gain = packs[:, :feat].reshape(width)
        bc_taps = jnp.moveaxis(packs[:, feat : feat + KW * bcn].reshape(-1, KW, bcn), 0, 1)
        bc_taps = bc_taps.reshape(KW, 2 * STATE)
        bc_shift = packs[:, feat + KW * bcn :].reshape(2 * STATE)
        thin = lax.all_gather(jnp.concatenate([in_bc, in_dt], axis=1), ("row", "zh", "zl"))
        thin = thin.reshape(nrow, 2, nl, -1, bcn + hb)
        w_bc = jnp.transpose(thin[..., :bcn], (0, 3, 1, 2, 4)).reshape(width, 2 * STATE)
        w_dt = lax.dynamic_index_in_dim(thin[..., bcn:], ml, 2, keepdims=False)
        w_dt = [pick(w_dt, 1).reshape(width, hb) for pick in (mine, other)]
        w_small = jnp.concatenate([w_bc] + w_dt, axis=1)
        w_small = jnp.pad(w_small, ((0, 0), (0, 384 - w_small.shape[1])))

        x_own, x_got, x_full = gather_features(tokens)
        zx_pair = (in_zx, swap(in_zx))
        out_pair = (out_proj, swap(out_proj))
        w_gate = [row_gather(w[:, 0]) for w in zx_pair]
        w_x = [row_gather(w[:, 1]) for w in zx_pair]
        w_out = [row_gather(w) for w in out_pair]
        x32 = x_full.astype(F32)
        inv_root = lax.rsqrt(jnp.mean(x32 * x32, axis=1, keepdims=True) + EPS)
        normed = (x32 * inv_root * gain).astype(BF16)

        seg = mine(segment_ids)
        segc = jnp.broadcast_to(seg[:, None], (length, 128))
        segr = jnp.broadcast_to(seg[None, :], (8, length))
        small = dot_nn(normed, w_small)
        hp = jnp.concatenate([c[7, : 2 * hb].reshape(2, hb) for c in chans], axis=1)
        hp = jnp.pad(hp, ((0, 6), (0, 128 - 2 * hb)))
        bcp = jnp.concatenate([bc_taps, bc_shift[None], jnp.zeros((3, 2 * STATE), F32)], axis=0)
        bc, bct, gmat, gtmat, colp, cumt, kexp, lag = prep(small, segc, segr, bcp, hp, 2 * gb)
        kexp = jnp.repeat(kexp[:, : 2 * hb], HEADDIM, axis=1)

        gates, xrs, ys, gateds, sts = [], [], [], [], []
        gate_sq = 0.0
        for b in range(2):
            gates.append(dot_nn(normed, w_gate[b]))
            xrs.append(dot_nn(normed, w_x[b]))
            y, gated, sq, st = scan(
                gates[b], xrs[b], chans[b], lag, bc, bct, gmat, colp, cumt, kexp, b * gb
            )
            ys.append(y)
            gateds.append(gated)
            sts.append(st)
            gate_sq = gate_sq + jnp.sum(sq, axis=1)
        gate_sq = pair_sum(gate_sq)
        inner_root = lax.rsqrt(gate_sq / inner + EPS)[:, None]
        gains = [c[6] for c in chans]
        hidden = [(g.astype(F32) * inner_root * k).astype(BF16) for g, k in zip(gateds, gains)]
        partial_out = sum(dot_nt(h, w) for h, w in zip(hidden, w_out)).astype(BF16)
        o_own, o_got = scatter_features(partial_out)
        output = to_rows((o_own + x_own).astype(BF16), (o_got + x_got).astype(BF16))

        c_own, c_got, c_full = gather_features(cotangent)
        dh = [dot_nn(c_full, w).astype(BF16) for w in w_out]
        gate_dot = sum(
            jnp.sum(d.astype(F32) * g.astype(F32) * k, axis=1) for d, g, k in zip(dh, gateds, gains)
        )
        gate_dot = pair_sum(gate_dot)[:, None]
        coef = inner_root**3 / inner * gate_dot
        ir = jnp.broadcast_to(inner_root, (length, 128))
        cf = jnp.broadcast_to(coef, (length, 128))
        g_out = [row_scatter(dot_tn(c_full, h).astype(BF16)) for h in hidden]
        dgates, dxrs, hds, ends, chgs, dbc, nd = [], [], [], [], [], 0.0, 0.0
        for b in range(2):
            dgate, dxr, hd, end, chg, dbc_b, nd_b = scan_grad(
                gates[b], xrs[b], ys[b], dh[b], chans[b], lag, ir, cf, bc, bct, gtmat, colp, cumt,
                kexp, sts[b], segc, segr, b * gb,
            )
            dgates.append(dgate)
            dxrs.append(dxr)
            hds.append(jnp.moveaxis(hd, 0, 1))
            ends.append(end)
            chgs.append(chg)
            dbc = dbc + dbc_b
            nd = nd + nd_b

        hd = jnp.concatenate(hds, axis=1)
        d_cum = hd[..., :PER].reshape(blocks, SPAN, 2 * hb)
        d_dt = hd[..., PER:].reshape(length, 2 * hb)
        end = jnp.concatenate(ends, axis=1)[:blocks].reshape(blocks, 1, 2 * hb, HEADDIM).sum(-1)
        upper = jnp.triu(jnp.ones((SPAN, SPAN), F32))
        d_a = jnp.einsum("ts,csh->cth", upper, d_cum, precision=lax.Precision.HIGHEST) + end
        d_a = d_a.reshape(length, 2 * hb)
        z = small[:, 256 : 256 + 2 * hb] + hp[0, : 2 * hb]
        rate = jnp.exp(hp[1, : 2 * hb])
        dt = jax.nn.softplus(z)
        ddt_raw = (d_dt - rate * d_a) * jax.nn.sigmoid(z)
        g_dtb = jnp.sum(ddt_raw, axis=0)
        g_alog = -jnp.sum(d_a * dt, axis=0) * rate
        _, bc_pull = jax.vjp(
            lambda r, t, s: shifted_silu(r, t, s, lag[:length, 0]), small[:, :256], bc_taps, bc_shift
        )
        dbc_raw, g_cb, g_cbb = bc_pull(dbc)
        d_small = jnp.concatenate([dbc_raw, ddt_raw], axis=1).astype(BF16)
        d_small = jnp.pad(d_small, ((0, 0), (0, 384 - d_small.shape[1])))

        dn = dot_nt(d_small, w_small)
        for b in range(2):
            dn = dn + dot_nt(dgates[b], w_gate[b]) + dot_nt(dxrs[b], w_x[b])
        nd = jnp.sum(nd, axis=1) + jnp.sum(d_small.astype(F32) * small, axis=1)
        nd = pair_sum(nd)[:, None]
        d_own, d_got = scatter_features(dn.astype(BF16))
        gain4 = lax.dynamic_index_in_dim(gain.reshape(2, nl, feat), ml, 1, keepdims=False)
        k_own, k_got = mine(gain4), other(gain4)
        tail = inv_root * inv_root / width * nd
        t_own = c_own + inv_root * k_own * d_own - x_own * tail
        t_got = c_got + inv_root * k_got * d_got - x_got * tail
        tokens_grad = to_rows(t_own.astype(BF16), t_got.astype(BF16))
        g_gain = [jnp.sum(d * x * inv_root, axis=0) for d, x in ((d_own, x_own), (d_got, x_got))]

        g_gate = [row_scatter(dot_tn(normed, d).astype(BF16)) for d in dgates]
        g_x = [row_scatter(dot_tn(normed, d).astype(BF16)) for d in dxrs]
        g_small = row_scatter(dot_tn(normed, d_small))
        g_bc = g_small[:, : 2 * STATE].reshape(-1, 2, nl, bcn)
        g_bc = lax.psum_scatter(g_bc, "zl", scatter_dimension=2, tiled=False)
        g_dts = g_small[:, 2 * STATE : 2 * STATE + 2 * hb].reshape(-1, 2, hb)
        thin_own = jnp.concatenate([mine(g_bc, 1), g_dts[:, 0]], axis=1)
        thin_got = jnp.concatenate([other(g_bc, 1), g_dts[:, 1]], axis=1)
        thin = thin_own + swap(thin_got)

        def join(pair):
            return pair[0].astype(F32) + swap(pair[1]).astype(F32)

        g_zx = jnp.stack([join(g_gate), join(g_x)], axis=1)
        g_wout = join(g_out)

        def small_pack(b, pick):
            cbg = jnp.concatenate([g_cb, g_cbb[None]], axis=0).reshape(KW + 1, 2, nl, bcn)
            return (
                g_gain[b],
                chgs[b][0:7],
                g_dtb[b * hb : (b + 1) * hb],
                g_alog[b * hb : (b + 1) * hb],
                pick(cbg, 1),
            )

        own = small_pack(0, mine)
        got = small_pack(1, other)
        got = jax.tree.map(swap, got)
        both = jax.tree.map(jnp.add, own, got)
        both = lax.psum(both, "row")
        cbg = lax.psum_scatter(both[4], "zl", scatter_dimension=1, tiled=False)
        chg = both[1]
        return (
            output,
            tokens_grad,
            both[0],
            g_zx,
            thin[:, bcn:],
            thin[:, :bcn],
            chg[0:KW],
            chg[4],
            cbg[0:KW],
            cbg[KW],
            both[2],
            both[3],
            chg[5].reshape(hb, HEADDIM).sum(1),
            chg[6],
            g_wout,
        )

    return per_device


def solution(mesh):
    nrow, ncol = mesh.shape["row"], mesh.shape["col"]
    nl = ncol // 2
    split = Mesh(mesh.devices.reshape(nrow, 2, nl), ("row", "zh", "zl"))
    col = ("zh", "zl")
    in_specs = (
        P("row", col), P("row", None), P(col), P("row", None, col), P("row", col), P("row", col),
        P(None, col), P(col), P(None, col), P(col), P(col), P(col), P(col), P(col),
        P("row", col), P("row", col),
    )
    out_specs = (
        P("row", col), P("row", col), P(col), P("row", None, col), P("row", col), P("row", col),
        P(None, col), P(col), P(None, col), P(col), P(col), P(col), P(col), P(col), P("row", col),
    )
    return jax.shard_map(
        build(nrow, nl), mesh=split, in_specs=in_specs, out_specs=out_specs, check_vma=False
    )
```

```python
import functools

import jax
import jax.numpy as jnp
from jax import lax
from jax.experimental import pallas as pl
from jax.experimental.pallas import tpu as pltpu
from jax.sharding import Mesh, PartitionSpec as P

HEADDIM = 64
STATE = 128
KW = 4
EPS = 1e-05
SPAN = 256
GROUP = 256
PER = GROUP // HEADDIM
F32 = jnp.float32
BF16 = jnp.bfloat16
VMEM_LIMIT = 60 * 1024 * 1024


def dot_nn(a, b):
    return lax.dot_general(a, b, (((1,), (0,)), ((), ())), preferred_element_type=F32)


def dot_nt(a, b):
    return lax.dot_general(a, b, (((1,), (1,)), ((), ())), preferred_element_type=F32)


def dot_tn(a, b):
    return lax.dot_general(a, b, (((0,), (0,)), ((), ())), preferred_element_type=F32)


def dot_exact(a, b):
    return lax.dot_general(
        a, b, (((1,), (0,)), ((), ())), preferred_element_type=F32, precision=lax.Precision.HIGHEST
    )


def twice(v):
    return jnp.concatenate([v, v], axis=1)


def spread(cols):
    rows = cols.shape[0]
    lane = lax.broadcasted_iota(jnp.int32, (rows, 128), 1)
    low = lane < HEADDIM
    first = jnp.where(low, cols[:, 0:1], cols[:, 1:2])
    second = jnp.where(low, cols[:, 2:3], cols[:, 3:4])
    return jnp.concatenate([first, second], axis=1)


def head_mask(h):
    lane = lax.broadcasted_iota(jnp.int32, (1, GROUP), 1)
    return ((lane >= h * HEADDIM) & (lane < (h + 1) * HEADDIM)).astype(F32).astype(BF16)


def prep_kernel(
    small_ref, segc_ref, segr_ref, bcp_ref, hp_ref,
    bc_ref, bct_ref, g_ref, gt_ref, colp_ref, cumt_ref, kexp_ref, lag_ref,
):
    length = small_ref.shape[0]
    blocks = length // SPAN
    groups = colp_ref.shape[0]
    seg = segc_ref[...]
    pos = lax.broadcasted_iota(jnp.int32, (length, 128), 0)
    lag = jnp.zeros((length, 128), F32)
    for j in range(1, KW):
        lag = lag + ((pltpu.roll(seg, j, 0) == seg) & (pos >= j)).astype(F32)
    lag_ref[0:length, :] = lag
    lag_ref[length:, :] = jnp.zeros((8, 128), F32)
    lag2 = twice(lag)
    raw = small_ref[:, 0:256]
    v = bcp_ref[4:5, :] + bcp_ref[3:4, :] * raw
    for j in range(1, KW):
        v = v + bcp_ref[3 - j : 4 - j, :] * jnp.where(lag2 >= j, pltpu.roll(raw, j, 0), 0.0)
    act = v * jax.nn.sigmoid(v)
    bc_ref[...] = act.astype(BF16)
    bct_ref[...] = jnp.transpose(act).astype(BF16)
    z = small_ref[:, 256:384] + hp_ref[0:1, :]
    dt = jnp.maximum(z, 0.0) + jnp.log1p(jnp.exp(-jnp.abs(z)))
    a = -dt * jnp.exp(hp_ref[1:2, :])
    tri_r = lax.broadcasted_iota(jnp.int32, (SPAN, SPAN), 0)
    tri_c = lax.broadcasted_iota(jnp.int32, (SPAN, SPAN), 1)
    lower = (tri_r >= tri_c).astype(F32)
    seg_row = segr_ref[0:1, :]
    for c in range(blocks):
        r0 = c * SPAN
        rows = slice(r0, r0 + SPAN)
        cum = dot_exact(lower, a[rows])
        segb = seg[rows]
        last = seg[r0 + SPAN - 1 : r0 + SPAN]
        tail = (segb == last).astype(F32)
        end = cum[SPAN - 1 : SPAN]
        q = jnp.exp(end - cum) * tail
        if c > 0:
            prev = seg[r0 - 1 : r0]
            p = jnp.exp(cum) * (segb == prev).astype(F32)
            k = jnp.exp(end) * (last == prev).astype(F32)
        else:
            p = jnp.zeros_like(cum)
            k = jnp.zeros_like(end)
        kexp_ref[c : c + 1, :] = k
        cumt = jnp.transpose(cum)
        dtb = dt[rows]
        for g in range(groups):
            hs = slice(PER * g, PER * g + PER)
            colp_ref[g, rows, 0:4] = cum[:, hs]
            colp_ref[g, rows, 4:8] = dtb[:, hs]
            colp_ref[g, rows, 8:12] = p[:, hs]
            colp_ref[g, rows, 12:16] = q[:, hs]
            cumt_ref[g, 0:4, rows] = cumt[hs, :]
        bb = bc_ref[rows, 0:STATE]
        cc = bc_ref[rows, STATE : 2 * STATE]
        same = twice(segb) == seg_row[:, rows]
        g_ref[rows, :] = jnp.where(same & (tri_r >= tri_c), dot_nt(cc, bb), 0.0)
        gt_ref[rows, :] = jnp.where(same & (tri_r <= tri_c), dot_nt(bb, cc), 0.0)
    kexp_ref[blocks:, :] = jnp.zeros((kexp_ref.shape[0] - blocks, 128), F32)


def conv_rows(xr_ref, lag_ref, chan_ref, r0):
    cur = xr_ref[pl.ds(r0, SPAN), :]
    before = xr_ref[pl.ds(pl.multiple_of(jnp.maximum(r0 - 8, 0), 8), 8), :]
    both = jnp.concatenate([before, cur], axis=0)
    lag = twice(lag_ref[pl.ds(r0, SPAN), :])
    v = chan_ref[4:5, :] + chan_ref[3:4, :] * cur
    for j in range(1, KW):
        earlier = pltpu.roll(both, j, 0)[8:]
        v = v + chan_ref[3 - j : 4 - j, :] * jnp.where(lag >= j, earlier, 0.0)
    return cur, v


def scan_kernel(
    gate_ref, xr_ref, chan_ref, lag_ref, bc_ref, bct_ref, g_ref, colp_ref, cumt_ref, kexp_ref,
    y_ref, gated_ref, sq_ref, st_ref, state,
):
    length = gate_ref.shape[0]
    blocks = length // SPAN
    state[...] = jnp.zeros_like(state)

    @pl.when(pl.program_id(0) == 0)
    def _():
        sq_ref[...] = jnp.zeros_like(sq_ref)

    def body(c, carry):
        r0 = pl.multiple_of(c * SPAN, SPAN)
        rows = pl.ds(r0, SPAN)
        _, v = conv_rows(xr_ref, lag_ref, chan_ref, r0)
        xc = (v * jax.nn.sigmoid(v)).astype(BF16).astype(F32)
        cp = colp_ref[0, rows, :]
        xd = (spread(cp[:, 4:8]) * xc).astype(BF16)
        px = spread(cp[:, 8:12])
        qx = spread(cp[:, 12:16])
        gb = g_ref[rows, :]
        lefts, rights = [], []
        for h in range(PER):
            gap = cp[:, h : h + 1] - cumt_ref[0, h : h + 1, rows]
            lefts.append((gb * jnp.exp(jnp.minimum(gap, 0.0))).astype(BF16))
            rights.append(xd * head_mask(h))
        y = dot_nn(jnp.concatenate(lefts, axis=1), jnp.concatenate(rights, axis=0))
        st = state[...]
        stb = st.astype(BF16)
        st_ref[c] = stb
        y = y + px * dot_nn(bc_ref[rows, STATE : 2 * STATE], stb)
        kx = kexp_ref[pl.ds(c, 1), :]
        state[...] = kx * st + dot_nn(bct_ref[0:STATE, rows], (qx * xd.astype(F32)).astype(BF16))
        y = y + chan_ref[5:6, :] * xc
        y_ref[rows, :] = y
        gate = gate_ref[rows, :]
        gated = y * (gate * jax.nn.sigmoid(gate))
        gated_ref[rows, :] = gated.astype(BF16)
        sq = gated * gated
        sq_ref[rows, :] += sq[:, 0:128] + sq[:, 128:256]
        return carry

    lax.fori_loop(0, blocks, body, 0)


def scan_grad_kernel(
    gate_ref, xr_ref, y_ref, dh_ref, chan_ref, lag_ref, ir_ref, cf_ref, bc_ref, bct_ref, gt_ref,
    colp_ref, cumt_ref, kexp_ref, st_ref, segc_ref, segr_ref,
    dgate_ref, dxr_ref, hd_ref, end_ref, chg_ref, dbc_ref, nd_ref,
    dst, head, dgt,
):
    length = gate_ref.shape[0]
    blocks = length // SPAN
    step = pl.program_id(0)
    dst[...] = jnp.zeros_like(dst)
    head[...] = jnp.zeros_like(head)
    end_ref[...] = jnp.zeros_like(end_ref)
    chg_ref[...] = jnp.zeros_like(chg_ref)

    @pl.when(step == 0)
    def _():
        dgt[...] = jnp.zeros_like(dgt)
        dbc_ref[...] = jnp.zeros_like(dbc_ref)
        nd_ref[...] = jnp.zeros_like(nd_ref)

    def total(v):
        return jnp.sum(v, axis=0, keepdims=True)

    def body(back, carry):
        c = blocks - 1 - back
        r0 = pl.multiple_of(c * SPAN, SPAN)
        rows = pl.ds(r0, SPAN)
        cur, v = conv_rows(xr_ref, lag_ref, chan_ref, r0)
        sv = jax.nn.sigmoid(v)
        xc = (v * sv).astype(BF16).astype(F32)
        cp = colp_ref[0, rows, :]
        dtx = spread(cp[:, 4:8])
        px = spread(cp[:, 8:12])
        qx = spread(cp[:, 12:16])
        xd = (dtx * xc).astype(BF16)
        xdf = xd.astype(F32)
        gate = gate_ref[rows, :]
        y = y_ref[rows, :]
        dh = dh_ref[rows, :].astype(F32)
        ir = twice(ir_ref[rows, :])
        cf = twice(cf_ref[rows, :])
        sg = jax.nn.sigmoid(gate)
        sl = gate * sg
        gated = y * sl
        dgd = ir * (dh * chan_ref[6:7, :]) - gated * cf
        dy = dgd * sl
        dgate = dgd * y * (sg * (1.0 + gate * (1.0 - sg)))
        dgate_ref[rows, :] = dgate.astype(BF16)
        dyb = dy.astype(BF16)
        gt = gt_ref[rows, :]
        lefts, rights = [], []
        acc = dgt[rows, :]
        for h in range(PER):
            gap = cumt_ref[0, h : h + 1, rows] - cp[:, h : h + 1]
            et = jnp.exp(jnp.minimum(gap, 0.0))
            lefts.append((gt * et).astype(BF16))
            dym = dyb * head_mask(h)
            rights.append(dym)
            acc = acc + dot_nt(xd, dym) * et
        dgt[rows, :] = acc
        u = dot_nn(jnp.concatenate(lefts, axis=1), jnp.concatenate(rights, axis=0))
        ds = dst[...]
        dsb = ds.astype(BF16)
        bb = bc_ref[rows, 0:STATE]
        cc = bc_ref[rows, STATE : 2 * STATE]
        ui = qx * dot_nn(bb, dsb)
        u = u + ui
        dxc = chan_ref[5:6, :] * dy + dtx * u
        yscan = y - chan_ref[5:6, :] * xc
        terms = jnp.concatenate([dyb.astype(F32) * yscan - xdf * u, xc * u], axis=1)
        hi = terms.astype(BF16)
        lo = (terms - hi.astype(F32)).astype(BF16)
        pick_r = lax.broadcasted_iota(jnp.int32, (2 * GROUP, 128), 0)
        pick_c = lax.broadcasted_iota(jnp.int32, (2 * GROUP, 128), 1)
        pick = (pick_r // HEADDIM == pick_c).astype(F32).astype(BF16)
        sums = dot_nn(hi, pick) + dot_nn(lo, pick)
        hd_ref[0, rows, :] = sums[:, 0:8]
        stb = st_ref[c]
        kx = kexp_ref[pl.ds(c, 1), :]
        end_ref[pl.ds(c, 1), :] = total(xdf * ui) + kx * total(ds * stb.astype(F32))
        pdy = (px * dyb.astype(F32)).astype(BF16)
        dbc_ref[rows, 0:STATE] += dot_nt((qx * xdf).astype(BF16), dsb)
        dbc_ref[rows, STATE : 2 * STATE] += dot_nt(pdy, stb)
        dst[...] = kx * ds + dot_nn(bct_ref[STATE : 2 * STATE, rows], pdy)
        dv = dxc * (sv * (1.0 + v * (1.0 - sv)))
        after = pl.ds(pl.multiple_of(r0 + SPAN, 8), 8)
        wide = jnp.concatenate([dv, head[...]], axis=0)
        lagw = jnp.concatenate([twice(lag_ref[rows, :]), twice(lag_ref[after, :])], axis=0)
        head[...] = dv[0:8]
        dxr = chan_ref[3:4, :] * dv
        chg_ref[3:4, :] += total(cur * dv)
        chg_ref[4:5, :] += total(dv)
        chg_ref[5:6, :] += total(dy * xc)
        chg_ref[6:7, :] += total(dh * gated * ir)
        for j in range(1, KW):
            later = pltpu.roll(jnp.where(lagw >= j, wide, 0.0), SPAN + 8 - j, 0)[0:SPAN]
            dxr = dxr + chan_ref[3 - j : 4 - j, :] * later
            chg_ref[3 - j : 4 - j, :] += total(cur * later)
        dxr_ref[rows, :] = dxr.astype(BF16)
        nd = dgate * gate + dxr * cur
        nd_ref[rows, :] += nd[:, 0:128] + nd[:, 128:256]
        return carry

    lax.fori_loop(0, blocks, body, 0)

    @pl.when(step == pl.num_programs(0) - 1)
    def _():
        tri_r = lax.broadcasted_iota(jnp.int32, (SPAN, SPAN), 0)
        tri_c = lax.broadcasted_iota(jnp.int32, (SPAN, SPAN), 1)
        for c in range(blocks):
            rows = slice(c * SPAN, (c + 1) * SPAN)
            same = twice(segc_ref[rows, :]) == segr_ref[0:1, rows]
            full = jnp.where(same & (tri_r <= tri_c), dgt[rows, :], 0.0)
            dbc_ref[rows, 0:STATE] += dot_nn(full.astype(BF16), bc_ref[rows, STATE : 2 * STATE])
            dbc_ref[rows, STATE : 2 * STATE] += dot_nn(
                jnp.transpose(full).astype(BF16), bc_ref[rows, 0:STATE]
            )


def whole(shape):
    return pl.BlockSpec(shape, lambda g: (0,) * len(shape))


def tile(rows, first=0):
    return pl.BlockSpec((rows, GROUP), lambda g: (0, g + first))


def prep(small, segc, segr, bcp, hp, groups):
    length = small.shape[0]
    return pl.pallas_call(
        prep_kernel,
        out_shape=(
            jax.ShapeDtypeStruct((length, 2 * STATE), BF16),
            jax.ShapeDtypeStruct((2 * STATE, length), BF16),
            jax.ShapeDtypeStruct((length, SPAN), F32),
            jax.ShapeDtypeStruct((length, SPAN), F32),
            jax.ShapeDtypeStruct((groups, length, 16), F32),
            jax.ShapeDtypeStruct((groups, 8, length), F32),
            jax.ShapeDtypeStruct((8, 128), F32),
            jax.ShapeDtypeStruct((length + 8, 128), F32),
        ),
        compiler_params=pltpu.CompilerParams(vmem_limit_bytes=VMEM_LIMIT),
        name="prep",
    )(small, segc, segr, bcp, hp)


def scan(gate, xr, chan, lag, bc, bct, gmat, colp, cumt, kexp, first):
    length, width = gate.shape
    groups = width // GROUP
    blocks = length // SPAN
    return pl.pallas_call(
        scan_kernel,
        grid=(groups,),
        in_specs=[
            tile(length),
            tile(length),
            tile(8),
            whole((length + 8, 128)),
            whole((length, 2 * STATE)),
            whole((2 * STATE, length)),
            whole((length, SPAN)),
            pl.BlockSpec((1, length, 16), lambda g: (g + first, 0, 0)),
            pl.BlockSpec((1, 8, length), lambda g: (g + first, 0, 0)),
            tile(8, first),
        ],
        out_specs=[
            tile(length),
            tile(length),
            whole((length, 128)),
            pl.BlockSpec((blocks, STATE, GROUP), lambda g: (0, 0, g)),
        ],
        out_shape=(
            jax.ShapeDtypeStruct((length, width), F32),
            jax.ShapeDtypeStruct((length, width), BF16),
            jax.ShapeDtypeStruct((length, 128), F32),
            jax.ShapeDtypeStruct((blocks, STATE, width), BF16),
        ),
        scratch_shapes=[pltpu.VMEM((STATE, GROUP), F32)],
        compiler_params=pltpu.CompilerParams(vmem_limit_bytes=VMEM_LIMIT),
        name="scan",
    )(gate, xr, chan, lag, bc, bct, gmat, colp, cumt, kexp)


def scan_grad(
    gate, xr, y, dh, chan, lag, ir, cf, bc, bct, gtmat, colp, cumt, kexp, st, segc, segr, first
):
    length, width = gate.shape
    groups = width // GROUP
    blocks = length // SPAN
    return pl.pallas_call(
        scan_grad_kernel,
        grid=(groups,),
        in_specs=[
            tile(length),
            tile(length),
            tile(length),
            tile(length),
            tile(8),
            whole((length + 8, 128)),
            whole((length, 128)),
            whole((length, 128)),
            whole((length, 2 * STATE)),
            whole((2 * STATE, length)),
            whole((length, SPAN)),
            pl.BlockSpec((1, length, 16), lambda g: (g + first, 0, 0)),
            pl.BlockSpec((1, 8, length), lambda g: (g + first, 0, 0)),
            tile(8, first),
            pl.BlockSpec((blocks, STATE, GROUP), lambda g: (0, 0, g)),
            whole((length, 128)),
            whole((8, length)),
        ],
        out_specs=[
            tile(length),
            tile(length),
            pl.BlockSpec((1, length, 8), lambda g: (g, 0, 0)),
            tile(8),
            tile(8),
            whole((length, 2 * STATE)),
            whole((length, 128)),
        ],
        out_shape=(
            jax.ShapeDtypeStruct((length, width), BF16),
            jax.ShapeDtypeStruct((length, width), BF16),
            jax.ShapeDtypeStruct((groups, length, 8), F32),
            jax.ShapeDtypeStruct((8, width), F32),
            jax.ShapeDtypeStruct((8, width), F32),
            jax.ShapeDtypeStruct((length, 2 * STATE), F32),
            jax.ShapeDtypeStruct((length, 128), F32),
        ),
        scratch_shapes=[
            pltpu.VMEM((STATE, GROUP), F32),
            pltpu.VMEM((8, GROUP), F32),
            pltpu.VMEM((length, SPAN), F32),
        ],
        compiler_params=pltpu.CompilerParams(vmem_limit_bytes=VMEM_LIMIT),
        name="scan_grad",
    )(gate, xr, y, dh, chan, lag, ir, cf, bc, bct, gtmat, colp, cumt, kexp, st, segc, segr)


def back_kernel(a0, a1, a2, a3, a4, w0, w1, w2, w3, w4, nb_ref, dn_ref, gg_ref):
    total = dot_nt(a0[...], w0[...])
    for a, w in ((a1, w1), (a2, w2), (a3, w3), (a4, w4)):
        total = total + dot_nt(a[...], w[...])
    dn_ref[...] = total.astype(BF16)
    gg = jnp.sum(total * nb_ref[...].astype(F32), axis=0, keepdims=True)
    gg_ref[...] = jnp.broadcast_to(gg, gg_ref.shape)


def back(lefts, weights, nb):
    length, width = nb.shape
    return pl.pallas_call(
        back_kernel,
        grid=(width // 256,),
        in_specs=[whole(a.shape) for a in lefts]
        + [pl.BlockSpec((256, w.shape[1]), lambda n: (n, 0)) for w in weights]
        + [pl.BlockSpec((length, 256), lambda n: (0, n))],
        out_specs=[
            pl.BlockSpec((length, 256), lambda n: (0, n)),
            pl.BlockSpec((8, 256), lambda n: (0, n)),
        ],
        out_shape=(
            jax.ShapeDtypeStruct((length, width), BF16),
            jax.ShapeDtypeStruct((8, width), F32),
        ),
        compiler_params=pltpu.CompilerParams(vmem_limit_bytes=VMEM_LIMIT),
        name="back",
    )(*lefts, *weights, nb)


def shifted_silu(raw, taps, bias, lag):
    v = bias + taps[KW - 1] * raw
    for j in range(1, KW):
        earlier = jnp.pad(raw, ((j, 0), (0, 0)))[: raw.shape[0]]
        v = v + taps[KW - 1 - j] * jnp.where(lag[:, None] >= j, earlier, 0.0)
    return jax.nn.silu(v)


MESH_ID = pl.DeviceIdType.MESH


class Copies:
    def __init__(self, send, recv):
        self.send, self.recv, self.count, self.open = send, recv, 0, []

    def start(self, src, dst, to):
        copy = pltpu.make_async_remote_copy(
            src_ref=src, dst_ref=dst, send_sem=self.send.at[self.count],
            recv_sem=self.recv.at[self.count], device_id=to, device_id_type=MESH_ID,
        )
        self.count += 1
        copy.start()
        self.open.append(copy)
        return copy

    def finish(self):
        for copy in self.open:
            copy.wait_send()


def places():
    h, l, r = lax.axis_index("zh"), lax.axis_index("zl"), lax.axis_index("row")
    c, x, y = lax.rem(r, 2), lax.rem(r // 2, 2), r // 4
    rx, ry = r + 2 - 4 * x, r + 4 - 8 * y
    rc = r + 1 - 2 * c
    return h, l, r, c, x, y, rx, ry, rc


def meet(peers):
    barrier = pltpu.get_barrier_semaphore()
    for to in peers:
        pl.semaphore_signal(barrier, inc=1, device_id=to, device_id_type=MESH_ID)
    pl.semaphore_wait(barrier, len(peers))


GATHER_COPIES = 64
PIECES = 4


def gather_kernel(
    x_ref, wg_ref, wx_ref, thin_ref, par_ref,
    nb_ref, nt_ref, ir_ref, par_out, wg0_ref, wx0_ref, wg1_ref, wx1_ref, thin_out,
    xv, parv, send, recv, local,
):
    h, l, r, c, x, y, rx, ry, rc = places()
    rd = rx + ry - r
    me, zhp = h * 2 + l, (1 - h) * 2 + l
    zh, zl, zd = {"zh": 1 - h}, {"zl": 1 - l}, {"zh": 1 - h, "zl": 1 - l}
    to_x, to_y, to_c = {"row": rx}, {"row": ry}, {"row": rc}
    length, feat = x_ref.shape[1], x_ref.shape[2]
    step = length // PIECES
    shard = wg_ref.shape[0]
    meet((zh, zl, zd, to_x, to_y, to_c))
    copies = Copies(send, recv)
    start = copies.start

    def cols(block):
        return pl.ds(pl.multiple_of(block * feat, feat), feat)

    def toks(p):
        return pl.ds(p * step, step)

    def rows(row):
        return pl.ds(pl.multiple_of(row * shard, shard), shard)

    src = (wg_ref, wx_ref)
    first = (wg0_ref, wx0_ref)
    second = (wg1_ref, wx1_ref)
    keeps = [
        pltpu.make_async_copy(par_ref, parv.at[me], local.at[0]),
        pltpu.make_async_copy(thin_ref, thin_out.at[r, me], local.at[1]),
        pltpu.make_async_copy(x_ref.at[h], xv.at[:, cols(me)], local.at[2]),
        pltpu.make_async_copy(wg_ref, wg0_ref.at[rows(r)], local.at[3]),
        pltpu.make_async_copy(wx_ref, wx0_ref.at[rows(r)], local.at[4]),
    ]
    for keep in keeps:
        keep.start()
    pars = [start(par_ref, parv.at[me], to) for to in (zh, zl, zd)]
    thins = [start(thin_ref, thin_out.at[r, me], to) for to in (zh, zl, zd)]
    x1, x2, x3, wz = [], [], [], []
    for p in range(PIECES):
        x1.append(start(x_ref.at[1 - h, toks(p)], xv.at[toks(p), cols(me)], zh))
        if p % 2 == 1:
            k = p // 2
            wz.append(start(src[k], second[k].at[rows(r)], zh))
    own_x = [start(src[k], first[k].at[rows(r)], to_x) for k in range(2)]
    own_y = [start(src[k], first[k].at[rows(r)], to_y) for k in range(2)]
    sib = [start(src[k], first[k].at[rows(r)], to_c) for k in range(2)]
    for p in range(PIECES):
        x2.append(start(x_ref.at[h, toks(p)], xv.at[toks(p), cols(me)], zl))
    keeps[1].wait()
    for copy in thins:
        copy.wait_recv()
    thin_x = start(thin_out.at[r], thin_out.at[r], to_x)
    thin_y = start(thin_out.at[r], thin_out.at[r], to_y)
    sib.append(start(thin_out.at[r], thin_out.at[r], to_c))

    def onward(p):
        x1[p].wait_recv()
        x3.append(start(xv.at[toks(p), cols(zhp)], xv.at[toks(p), cols(zhp)], zl))

    diag = []

    def around(from_x, from_y, dst):
        for k in range(2):
            from_x[k].wait_recv()
            if k == 0:
                diag.append((start(dst[k].at[rows(rx)], dst[k].at[rows(rx)], to_y), dst[k]))
            sib.append(start(dst[k].at[rows(rx)], dst[k].at[rows(rx)], to_c))
            from_y[k].wait_recv()
            if k == 1:
                diag.append((start(dst[k].at[rows(ry)], dst[k].at[rows(ry)], to_x), dst[k]))
            sib.append(start(dst[k].at[rows(ry)], dst[k].at[rows(ry)], to_c))

    onward(0)
    thin_x.wait_recv()
    thin_d = start(thin_out.at[rx], thin_out.at[rx], to_y)
    sib.append(start(thin_out.at[rx], thin_out.at[rx], to_c))
    thin_y.wait_recv()
    sib.append(start(thin_out.at[ry], thin_out.at[ry], to_c))
    onward(1)
    around(own_x, own_y, first)
    got_x, got_y = [], []
    for k in range(2):
        wz[k].wait_recv()
        part = second[k].at[rows(r)]
        got_x.append(start(part, part, to_x))
        got_y.append(start(part, part, to_y))
        sib.append(start(part, part, to_c))
        onward(2 + k)
    thin_d.wait_recv()
    sib.append(start(thin_out.at[rd], thin_out.at[rd], to_c))
    for copy, dst in diag[0:2]:
        copy.wait_recv()
        sib.append(start(dst.at[rows(rd)], dst.at[rows(rd)], to_c))

    keeps[0].wait()
    keeps[2].wait()
    for copy in pars:
        copy.wait_recv()
    par_out[...] = parv[...]

    def norm(p):
        x2[p].wait_recv()
        x3[p].wait_recv()
        total = jnp.zeros((step, 1), F32)
        for b in range(4):
            part = xv[toks(p), b * feat : (b + 1) * feat].astype(F32)
            total = total + jnp.sum(part * part, axis=1, keepdims=True)
        root = lax.rsqrt(total / (4 * feat) + EPS)
        ir_ref[toks(p), :] = jnp.broadcast_to(root, (step, 128))
        for b in range(4):
            part = xv[toks(p), b * feat : (b + 1) * feat].astype(F32)
            part = (part * root * parv[b, 8:9, 0:feat]).astype(BF16)
            nb_ref[toks(p), b * feat : (b + 1) * feat] = part
            nt_ref[b * feat : (b + 1) * feat, toks(p)] = jnp.transpose(part.astype(F32)).astype(BF16)

    norm(0)
    norm(1)
    around(got_x, got_y, second)
    norm(2)
    norm(3)
    for copy, dst in diag[2:4]:
        copy.wait_recv()
        sib.append(start(dst.at[rows(rd)], dst.at[rows(rd)], to_c))
    for copy in sib:
        copy.wait_recv()
    keeps[3].wait()
    keeps[4].wait()
    copies.finish()


def gather_all(x, wg, wx, thin, par):
    _, length, feat = x.shape
    shard, cb = wg.shape
    anywhere = pl.BlockSpec(memory_space=pl.ANY)
    inside = pl.BlockSpec(memory_space=pltpu.VMEM)
    weight = jax.ShapeDtypeStruct((8 * shard, cb), BF16)
    return pl.pallas_call(
        gather_kernel,
        in_specs=[anywhere] * 5,
        out_specs=[inside] * 4 + [anywhere] * 5,
        out_shape=(
            jax.ShapeDtypeStruct((length, 4 * feat), BF16),
            jax.ShapeDtypeStruct((4 * feat, length), BF16),
            jax.ShapeDtypeStruct((length, 128), F32),
            jax.ShapeDtypeStruct((4,) + par.shape, F32),
            weight, weight, weight, weight,
            jax.ShapeDtypeStruct((8, 4) + thin.shape, BF16),
        ),
        scratch_shapes=[
            pltpu.VMEM((length, 4 * feat), BF16),
            pltpu.VMEM((4,) + par.shape, F32),
            pltpu.SemaphoreType.DMA((GATHER_COPIES,)),
            pltpu.SemaphoreType.DMA((GATHER_COPIES,)),
            pltpu.SemaphoreType.DMA((8,)),
        ],
        compiler_params=pltpu.CompilerParams(
            collective_id=0, has_side_effects=True, vmem_limit_bytes=VMEM_LIMIT
        ),
        name="gather_all",
    )(x, wg, wx, thin, par)


GRAD_COPIES = 96


def grad_kernel(
    nt_ref, dg0_ref, dx0_ref, dg1_ref, dx1_ref, ds_ref, small_ref,
    gz_ref, thin_out, small_out,
    cs, cr, ts, tr, fs, fr, kept, ss, sr, total, zs, zr, tfs, tfr, tkept, tss, tsr, tz, tzr,
    sbuf, srecv, szr, send, recv,
):
    h, l, r, c, x, y, rx, ry, rc = places()
    me = h * 2 + l
    zh, zl, zd = {"zh": 1 - h}, {"zl": 1 - l}, {"zh": 1 - h, "zl": 1 - l}
    to_x, to_y, to_c = {"row": rx}, {"row": ry}, {"row": rc}
    shard = gz_ref.shape[1]
    ncol = gz_ref.shape[2]
    meet((zh, zl, zd, to_x, to_y, to_c))
    copies = Copies(send, recv)
    start = copies.start

    def product(row, d_ref, at):
        left = nt_ref[pl.ds(pl.multiple_of(row * shard, shard), shard), :]
        return dot_nn(left, d_ref[:, at])

    def tiles(d_ref, body):
        width = d_ref.shape[1]
        wide = 256 if width % 256 == 0 else 128

        def one(n, carry):
            body(pl.ds(pl.multiple_of(n * wide, wide), wide))
            return carry

        lax.fori_loop(0, width // wide, one, 0)

    sbuf[0] = small_ref[...]
    small_hops = [to_c, to_x, to_y]
    small_copy = start(sbuf.at[0], srecv.at[0], to_c)

    quarters = [
        dict(d=dg0_ref, first=to_x, second=to_y, mine=x, along=y, b=0, k=0, swap=False),
        dict(d=dg1_ref, first=to_y, second=to_x, mine=y, along=x, b=1, k=0, swap=True),
        dict(d=dx0_ref, first=to_x, second=to_y, mine=x, along=y, b=0, k=1, swap=False),
        dict(d=dx1_ref, first=to_y, second=to_x, mine=y, along=x, b=1, k=1, swap=True),
    ]

    def spot(q, first, second):
        return 2 * first + second if q["swap"] else 2 * second + first

    def refs(i):
        if i == 4:
            return ts, tr, tfs, tfr, tkept, tss, tsr
        return (cs.at[i], cr.at[i], fs.at[i], fr.at[i], kept.at[i], ss.at[i], sr.at[i])

    thin_q = dict(d=ds_ref, first=to_x, second=to_y, mine=x, along=y, swap=False)

    def to_core(i, q):
        out, back = refs(i)[0:2]

        def each(j, carry):
            row = 2 * j + 1 - c

            def body(at):
                out[j, :, at] = product(row, q["d"], at).astype(BF16)

            tiles(q["d"], body)
            return carry

        lax.fori_loop(0, 4, each, 0)
        q["core"] = start(out, back, to_c)

    def to_first(i, q):
        _, back, fsend, frecv, keep, _, _ = refs(i)
        q["core"].wait_recv()

        def fill(dst, at_first):
            def each(s, carry):
                j = spot(q, at_first, s)
                row = 2 * j + c

                def body(at):
                    dst[s, :, at] = (product(row, q["d"], at) + back[j, :, at].astype(F32)).astype(BF16)

                tiles(q["d"], body)
                return carry

            lax.fori_loop(0, 2, each, 0)

        fill(fsend, 1 - q["mine"])
        q["f"] = start(fsend, frecv, q["first"])
        fill(keep, q["mine"])

    def to_second(i, q):
        _, _, _, frecv, keep, ssend, srcv = refs(i)
        q["f"].wait_recv()
        far = 1 - q["along"]
        ssend[...] = (keep[far].astype(F32) + frecv[far].astype(F32)).astype(BF16)
        q["s"] = start(ssend, srcv, q["second"])

    def settle(i, q):
        _, _, _, frecv, keep, _, srcv = refs(i)
        q["s"].wait_recv()
        near = q["along"]
        return keep[near].astype(F32) + frecv[near].astype(F32) + srcv[...].astype(F32)

    to_core(4, thin_q)
    to_core(0, quarters[0])
    to_core(1, quarters[1])
    to_first(4, thin_q)
    to_first(0, quarters[0])
    small_copy.wait_recv()
    sbuf[1] = sbuf[0] + srecv[0]
    small_copy = start(sbuf.at[1], srecv.at[1], to_x)
    to_core(2, quarters[2])
    to_first(1, quarters[1])
    to_core(3, quarters[3])
    to_first(2, quarters[2])
    to_second(4, thin_q)
    small_copy.wait_recv()
    sbuf[2] = sbuf[1] + srecv[1]
    small_copy = start(sbuf.at[2], srecv.at[2], to_y)
    to_first(3, quarters[3])
    tz[...] = settle(4, thin_q)
    thin_z = [start(tz, tzr.at[n], to) for n, to in enumerate((zh, zl, zd))]
    small_copy.wait_recv()
    sbuf[3] = sbuf[2] + srecv[2]
    small_z = [start(sbuf.at[3], szr.at[n], to) for n, to in enumerate((zh, zl, zd))]
    to_second(0, quarters[0])
    to_second(1, quarters[1])
    z_copy = [None, None]

    def send_z(i, k):
        zs[k] = settle(i, quarters[i]).astype(BF16)
        z_copy[k] = start(zs.at[k], zr.at[k], zh)

    total[0] = settle(0, quarters[0])
    send_z(1, 0)
    to_second(2, quarters[2])
    to_second(3, quarters[3])
    total[1] = settle(2, quarters[2])
    send_z(3, 1)
    for copy in thin_z:
        copy.wait_recv()
    for copy in small_z:
        copy.wait_recv()
    thin_out[0] = tz[...]
    small_out[0] = sbuf[3]
    for n in range(3):
        thin_out[n + 1] = tzr[n]
        small_out[n + 1] = szr[n]
    for k in range(2):
        z_copy[k].wait_recv()
        gz_ref[k] = total[k] + zr[k].astype(F32)
    copies.finish()


def grad_all(nt, dg0, dx0, dg1, dx1, d_small, small):
    width, length = nt.shape
    shard, cb = width // 8, dg0.shape[1]
    ns = d_small.shape[1]
    inside = pl.BlockSpec(memory_space=pltpu.VMEM)
    V = pltpu.VMEM
    return pl.pallas_call(
        grad_kernel,
        in_specs=[inside] * 7,
        out_specs=[inside] * 3,
        out_shape=(
            jax.ShapeDtypeStruct((2, shard, cb), F32),
            jax.ShapeDtypeStruct((4, shard, ns), F32),
            jax.ShapeDtypeStruct((4,) + small.shape, F32),
        ),
        scratch_shapes=[
            V((4, 4, shard, cb), BF16),
            V((4, 4, shard, cb), BF16),
            V((4, shard, ns), BF16),
            V((4, shard, ns), BF16),
            V((4, 2, shard, cb), BF16),
            V((4, 2, shard, cb), BF16),
            V((4, 2, shard, cb), BF16),
            V((4, shard, cb), BF16),
            V((4, shard, cb), BF16),
            V((2, shard, cb), F32),
            V((2, shard, cb), BF16),
            V((2, shard, cb), BF16),
            V((2, shard, ns), BF16),
            V((2, shard, ns), BF16),
            V((2, shard, ns), BF16),
            V((shard, ns), BF16),
            V((shard, ns), BF16),
            V((shard, ns), F32),
            V((3, shard, ns), F32),
            V((4,) + small.shape, F32),
            V((3,) + small.shape, F32),
            V((3,) + small.shape, F32),
            pltpu.SemaphoreType.DMA((GRAD_COPIES,)),
            pltpu.SemaphoreType.DMA((GRAD_COPIES,)),
        ],
        compiler_params=pltpu.CompilerParams(
            collective_id=1, has_side_effects=True, vmem_limit_bytes=VMEM_LIMIT
        ),
        name="grad_all",
    )(nt, dg0, dx0, dg1, dx1, d_small, small)


def build(nrow, nl):
    direct = nrow == 8 and nl == 2
    col = ("zh", "zl")

    def swap(v):
        return lax.ppermute(v, "zh", [(0, 1), (1, 0)])

    def swap_zl(v):
        return lax.ppermute(v, col, [(0, 1), (1, 0), (2, 3), (3, 2)])

    def swap_both(v):
        return lax.ppermute(v, col, [(0, 3), (3, 0), (1, 2), (2, 1)])

    def pair_sum(v):
        return v + swap_zl(v) if nl == 2 else lax.psum(v, "zl")

    def row_gather(v):
        return lax.all_gather(v, "row", axis=0, tiled=True)

    def row_scatter(v):
        return lax.psum_scatter(v, "row", scatter_dimension=0, tiled=True)

    def per_device(
        tokens, segment_ids, norm_gain, in_zx, in_dt, in_bc, conv_x, conv_x_bias, conv_bc,
        conv_bc_bias, dt_bias, a_log, d_skip, inner_gain, out_proj, cotangent,
    ):
        seq_count, length = segment_ids.shape
        assert seq_count == 2
        feat = tokens.shape[1]
        width = feat * 2 * nl
        cb = inner_gain.shape[0]
        hb = dt_bias.shape[0]
        inner = cb * 2 * nl
        blocks = length // SPAN
        gb = cb // GROUP
        mh = lax.axis_index("zh")
        ml = lax.axis_index("zl")
        first_h = mh == 0
        here = mh * nl + ml
        bcn = conv_bc.shape[1]

        def mine(v, axis=0):
            return lax.dynamic_index_in_dim(v, mh, axis, keepdims=False)

        def other(v, axis=0):
            return lax.dynamic_index_in_dim(v, 1 - mh, axis, keepdims=False)

        def seqs(v):
            return v.reshape(2, length, feat)

        def by_seq(own, away):
            return jnp.where(first_h, jnp.stack([own, away]), jnp.stack([away, own]))

        def gather_features(v):
            own, away = mine(seqs(v)), other(seqs(v))
            if direct:
                full = jnp.zeros((length, width), v.dtype)
                for part, at in (
                    (own, here),
                    (swap(away), (1 - mh) * nl + ml),
                    (swap_zl(own), mh * nl + 1 - ml),
                    (swap_both(away), (1 - mh) * nl + 1 - ml),
                ):
                    full = lax.dynamic_update_slice(full, part, (0, at * feat))
                return full
            both = by_seq(own, swap(away))
            every = jnp.moveaxis(lax.all_gather(both, "zl"), 0, 1)
            return jnp.transpose(every, (2, 0, 1, 3)).reshape(length, width)

        def scatter_features(v):
            def part(a, b):
                return lax.dynamic_slice(v, (0, (a * nl + b) * feat), (length, feat))

            if direct:
                own = part(mh, ml).astype(F32) + swap_zl(part(mh, 1 - ml)).astype(F32)
                away = swap(part(1 - mh, ml)).astype(F32)
                away = away + swap_both(part(1 - mh, 1 - ml)).astype(F32)
                return by_seq(own, away)
            parts = v.reshape(length, 2, nl, feat)
            both = lax.psum_scatter(parts, "zl", scatter_dimension=2, tiled=False)
            return by_seq(mine(both, 1), swap(other(both, 1))).astype(F32)

        chan = jnp.concatenate(
            [
                conv_x,
                conv_x_bias[None],
                jnp.repeat(d_skip, HEADDIM)[None],
                inner_gain[None],
                jnp.pad(jnp.concatenate([dt_bias, a_log]), (0, cb - 2 * hb))[None],
            ],
            axis=0,
        )
        packed = jnp.concatenate([norm_gain, conv_bc.reshape(-1), conv_bc_bias])
        thin = jnp.concatenate([in_bc, in_dt], axis=1)
        if direct:
            packed = jnp.pad(packed, (0, cb - packed.shape[0]))[None]
            par = jnp.concatenate([chan, packed, jnp.zeros((7, cb), F32)], axis=0)
            thin = jnp.pad(thin, ((0, 0), (0, 128 - thin.shape[1])))
            normed, normed_t, inv_root, par, wg0, wx0, wg1, wx1, thin = gather_all(
                seqs(tokens), in_zx[:, 0], in_zx[:, 1], thin, par
            )
            inv_root = inv_root[:, 0:1]
            w_gate, w_x = (wg0, wg1), (wx0, wx1)
            packs = par[:, 8]
            chans = (chan, lax.dynamic_index_in_dim(par, (1 - mh) * nl + ml, 0, keepdims=False)[0:8])
            thin = jnp.moveaxis(thin, 1, 0).reshape(2, nl, width, 128)
            thin = jnp.moveaxis(thin, 2, 0)
            late_out, late_cot, _ = lax.optimization_barrier((out_proj, cotangent, normed))
        else:
            chans = (chan, swap(chan))
            packs = lax.all_gather(packed, col)
            thin = lax.all_gather(thin, ("row", "zh", "zl")).reshape(nrow, 2, nl, -1, bcn + hb)
            thin = jnp.moveaxis(thin, 3, 1).reshape(width, 2, nl, bcn + hb)
            w_gate = [row_gather(w) for w in (in_zx[:, 0], swap(in_zx[:, 0]))]
            w_x = [row_gather(w) for w in (in_zx[:, 1], swap(in_zx[:, 1]))]
            late_out, late_cot = out_proj, cotangent
        gain = packs[:, :feat].reshape(width)
        bc_taps = jnp.moveaxis(packs[:, feat : feat + KW * bcn].reshape(-1, KW, bcn), 0, 1)
        bc_taps = bc_taps.reshape(KW, 2 * STATE)
        bc_shift = packs[:, feat + KW * bcn : feat + (KW + 1) * bcn].reshape(2 * STATE)
        w_bc = thin[..., :bcn].reshape(width, 2 * STATE)
        w_dt = lax.dynamic_index_in_dim(thin[..., bcn : bcn + hb], ml, 2, keepdims=False)
        w_small = jnp.concatenate([w_bc, mine(w_dt, 1), other(w_dt, 1)], axis=1)
        w_small = jnp.pad(w_small, ((0, 0), (0, 384 - w_small.shape[1])))
        if not direct:
            x32 = gather_features(tokens).astype(F32)
            inv_root = lax.rsqrt(jnp.mean(x32 * x32, axis=1, keepdims=True) + EPS)
            normed = (x32 * inv_root * gain).astype(BF16)
        w_out = [row_gather(w) for w in (late_out, swap(late_out))]
        c_full = gather_features(late_cot)

        seg = mine(segment_ids)
        segc = jnp.broadcast_to(seg[:, None], (length, 128))
        segr = jnp.broadcast_to(seg[None, :], (8, length))
        small = dot_nn(normed, w_small)
        hp = jnp.concatenate([c[7, : 2 * hb].reshape(2, hb) for c in chans], axis=1)
        hp = jnp.pad(hp, ((0, 6), (0, 128 - 2 * hb)))
        bcp = jnp.concatenate([bc_taps, bc_shift[None], jnp.zeros((3, 2 * STATE), F32)], axis=0)
        bc, bct, gmat, gtmat, colp, cumt, kexp, lag = prep(small, segc, segr, bcp, hp, 2 * gb)
        kexp = jnp.repeat(kexp[:, : 2 * hb], HEADDIM, axis=1)

        gates, xrs, ys, gateds, sts = [], [], [], [], []
        gate_sq = 0.0
        for b in range(2):
            gates.append(dot_nn(normed, w_gate[b]))
            xrs.append(dot_nn(normed, w_x[b]))
            y, gated, sq, st = scan(
                gates[b], xrs[b], chans[b], lag, bc, bct, gmat, colp, cumt, kexp, b * gb
            )
            ys.append(y)
            gateds.append(gated)
            sts.append(st)
            gate_sq = gate_sq + jnp.sum(sq, axis=1)
        gate_sq = pair_sum(gate_sq)
        inner_root = lax.rsqrt(gate_sq / inner + EPS)[:, None]
        gains = [c[6] for c in chans]
        hidden = [(g.astype(F32) * inner_root * k).astype(BF16) for g, k in zip(gateds, gains)]
        partial_out = sum(dot_nt(h, w) for h, w in zip(hidden, w_out)).astype(BF16)
        output = (scatter_features(partial_out) + seqs(tokens)).astype(BF16).reshape(tokens.shape)

        dh = [dot_nn(c_full, w).astype(BF16) for w in w_out]
        gate_dot = sum(
            jnp.sum(d.astype(F32) * g.astype(F32) * k, axis=1) for d, g, k in zip(dh, gateds, gains)
        )
        gate_dot = pair_sum(gate_dot)[:, None]
        coef = inner_root**3 / inner * gate_dot
        ir = jnp.broadcast_to(inner_root, (length, 128))
        cf = jnp.broadcast_to(coef, (length, 128))
        g_out = [row_scatter(dot_tn(c_full, h).astype(BF16)) for h in hidden]
        g_wout = g_out[0].astype(F32) + swap(g_out[1]).astype(F32)
        dgates, dxrs, hds, ends, chgs, dbc, nd = [], [], [], [], [], 0.0, 0.0
        for b in range(2):
            dgate, dxr, hd, end, chg, dbc_b, nd_b = scan_grad(
                gates[b], xrs[b], ys[b], dh[b], chans[b], lag, ir, cf, bc, bct, gtmat, colp, cumt,
                kexp, sts[b], segc, segr, b * gb,
            )
            dgates.append(dgate)
            dxrs.append(dxr)
            hds.append(jnp.moveaxis(hd, 0, 1))
            ends.append(end)
            chgs.append(chg)
            dbc = dbc + dbc_b
            nd = nd + nd_b

        hd = jnp.concatenate(hds, axis=1)
        d_cum = hd[..., :PER].reshape(blocks, SPAN, 2 * hb)
        d_dt = hd[..., PER:].reshape(length, 2 * hb)
        end = jnp.concatenate(ends, axis=1)[:blocks].reshape(blocks, 1, 2 * hb, HEADDIM).sum(-1)
        upper = jnp.triu(jnp.ones((SPAN, SPAN), F32))
        d_a = jnp.einsum("ts,csh->cth", upper, d_cum, precision=lax.Precision.HIGHEST) + end
        d_a = d_a.reshape(length, 2 * hb)
        z = small[:, 256 : 256 + 2 * hb] + hp[0, : 2 * hb]
        rate = jnp.exp(hp[1, : 2 * hb])
        dt = jax.nn.softplus(z)
        ddt_raw = (d_dt - rate * d_a) * jax.nn.sigmoid(z)
        g_dtb = jnp.sum(ddt_raw, axis=0)
        g_alog = -jnp.sum(d_a * dt, axis=0) * rate
        _, bc_pull = jax.vjp(
            lambda r, t, s: shifted_silu(r, t, s, lag[:length, 0]), small[:, :256], bc_taps, bc_shift
        )
        dbc_raw, g_cb, g_cbb = bc_pull(dbc)
        d_small = jnp.concatenate([dbc_raw, ddt_raw], axis=1).astype(BF16)
        d_small = jnp.pad(d_small, ((0, 0), (0, 384 - d_small.shape[1])))

        lefts = (dgates[0], dxrs[0], dgates[1], dxrs[1], d_small)
        dn, gg = back(lefts, (w_gate[0], w_x[0], w_gate[1], w_x[1], w_small), normed)
        nd = jnp.sum(nd, axis=1) + jnp.sum(d_small.astype(F32) * small, axis=1)
        nd = pair_sum(nd)[:, None]
        tail = jnp.concatenate([inv_root, inv_root * inv_root / width * nd], axis=1)
        tail = by_seq(tail, swap(tail))
        d_here = scatter_features(dn)
        x32 = seqs(tokens).astype(F32)
        tokens_grad = seqs(cotangent) + tail[..., 0:1] * norm_gain * d_here - x32 * tail[..., 1:2]
        tokens_grad = tokens_grad.astype(BF16).reshape(tokens.shape)
        g_gain = gg[0] / gain
        g_bcs = jnp.concatenate([g_cb, g_cbb[None]], axis=0)

        if direct:
            rows = []
            for b in range(2):
                hs = slice(b * hb, (b + 1) * hb)
                heads = jnp.concatenate([g_dtb[hs], g_alog[hs]])
                rows += [chgs[b][0:7], jnp.pad(heads, (0, cb - 2 * hb))[None]]
            last = jnp.concatenate([g_gain, g_bcs.reshape(-1)])
            last = jnp.pad(last, (0, 8 * cb - last.shape[0])).reshape(8, cb)
            gz, thins, smalls = grad_all(
                normed_t, dgates[0], dxrs[0], dgates[1], dxrs[1], d_small,
                jnp.concatenate(rows + [last], axis=0),
            )
            g_zx = jnp.transpose(gz, (1, 0, 2))
            g_bc = lax.dynamic_slice(thins.sum(0), (0, here * bcn), (thins.shape[1], bcn))
            g_dt = thins[0, :, 2 * STATE : 2 * STATE + hb]
            g_dt = g_dt + thins[1, :, 2 * STATE + hb : 2 * STATE + 2 * hb]
            chg = smalls[0, 0:8] + smalls[1, 8:16]
            last = smalls[:, 16:].sum(0).reshape(-1)
            g_gain = lax.dynamic_slice(last, (here * feat,), (feat,))
            g_bcs = last[width : width + (KW + 1) * 2 * STATE].reshape(KW + 1, 2 * nl, bcn)
            g_bcs = lax.dynamic_index_in_dim(g_bcs, here, 1, keepdims=False)
            g_dtb, g_alog = chg[7, :hb], chg[7, hb : 2 * hb]
        else:

            def join(own, away):
                return own.astype(F32) + swap(away).astype(F32)

            g_gate = [row_scatter(dot_tn(normed, d).astype(BF16)) for d in dgates]
            g_x = [row_scatter(dot_tn(normed, d).astype(BF16)) for d in dxrs]
            g_zx = jnp.stack([join(*g_gate), join(*g_x)], axis=1)
            thins = row_scatter(dot_tn(normed, d_small))
            g_bc = lax.psum(thins[:, : 2 * STATE], col).reshape(-1, 2 * nl, bcn)
            g_bc = lax.dynamic_index_in_dim(g_bc, here, 1, keepdims=False)
            g_dts = thins[:, 2 * STATE : 2 * STATE + 2 * hb].reshape(-1, 2, hb)
            g_dt = g_dts[:, 0] + swap(g_dts[:, 1])
            every = ("row", "zh", "zl")
            g_gain, g_bcs = lax.psum((g_gain, g_bcs), every)
            g_gain = lax.dynamic_slice(g_gain, (here * feat,), (feat,))
            g_bcs = g_bcs.reshape(KW + 1, 2 * nl, bcn)
            g_bcs = lax.dynamic_index_in_dim(g_bcs, here, 1, keepdims=False)
            chg = chgs[0] + swap(chgs[1])
            g_dtb = g_dtb[:hb] + swap(g_dtb[hb:])
            g_alog = g_alog[:hb] + swap(g_alog[hb:])
            chg, g_dtb, g_alog = lax.psum((chg, g_dtb, g_alog), "row")
        return (
            output,
            tokens_grad,
            g_gain,
            g_zx,
            g_dt,
            g_bc,
            chg[0:KW],
            chg[4],
            g_bcs[0:KW],
            g_bcs[KW],
            g_dtb,
            g_alog,
            chg[5].reshape(hb, HEADDIM).sum(1),
            chg[6],
            g_wout,
        )

    return per_device


def solution(mesh):
    nrow, ncol = mesh.shape["row"], mesh.shape["col"]
    nl = ncol // 2
    split = Mesh(mesh.devices.reshape(nrow, 2, nl), ("row", "zh", "zl"))
    col = ("zh", "zl")
    in_specs = (
        P("row", col), P("row", None), P(col), P("row", None, col), P("row", col), P("row", col),
        P(None, col), P(col), P(None, col), P(col), P(col), P(col), P(col), P(col),
        P("row", col), P("row", col),
    )
    out_specs = (
        P("row", col), P("row", col), P(col), P("row", None, col), P("row", col), P("row", col),
        P(None, col), P(col), P(None, col), P(col), P(col), P(col), P(col), P(col), P("row", col),
    )
    return jax.shard_map(
        build(nrow, nl), mesh=split, in_specs=in_specs, out_specs=out_specs, check_vma=False
    )
```

```python
import functools

import jax
import jax.numpy as jnp
from jax import lax
from jax.experimental import pallas as pl
from jax.experimental.pallas import tpu as pltpu
from jax.sharding import Mesh, PartitionSpec as P

HEADDIM = 64
STATE = 128
KW = 4
EPS = 1e-05
SPAN = 256
GROUP = 256
PER = GROUP // HEADDIM
F32 = jnp.float32
BF16 = jnp.bfloat16
VMEM_LIMIT = 60 * 1024 * 1024


def dot_nn(a, b):
    return lax.dot_general(a, b, (((1,), (0,)), ((), ())), preferred_element_type=F32)


def dot_nt(a, b):
    return lax.dot_general(a, b, (((1,), (1,)), ((), ())), preferred_element_type=F32)


def dot_tn(a, b):
    return lax.dot_general(a, b, (((0,), (0,)), ((), ())), preferred_element_type=F32)


def dot_exact(a, b):
    return lax.dot_general(
        a, b, (((1,), (0,)), ((), ())), preferred_element_type=F32, precision=lax.Precision.HIGHEST
    )


def twice(v):
    return jnp.concatenate([v, v], axis=1)


def across(v):
    return v if SPAN == 128 else twice(v)


def turned(v):
    n = v.shape[1]
    row = lax.broadcasted_iota(jnp.int32, (n, n), 0)
    col = lax.broadcasted_iota(jnp.int32, (n, n), 1)
    return dot_nt((row == col).astype(F32).astype(BF16), v).astype(BF16)


def spread(cols):
    rows = cols.shape[0]
    lane = lax.broadcasted_iota(jnp.int32, (rows, 128), 1)
    low = lane < HEADDIM
    first = jnp.where(low, cols[:, 0:1], cols[:, 1:2])
    second = jnp.where(low, cols[:, 2:3], cols[:, 3:4])
    return jnp.concatenate([first, second], axis=1)


def head_mask(h):
    lane = lax.broadcasted_iota(jnp.int32, (1, GROUP), 1)
    return ((lane >= h * HEADDIM) & (lane < (h + 1) * HEADDIM)).astype(F32).astype(BF16)


def prep_kernel(
    small_ref, segc_ref, segr_ref, bcp_ref, hp_ref,
    bc_ref, bct_ref, g_ref, gt_ref, colp_ref, cumt_ref, kexp_ref, lag_ref,
):
    length = small_ref.shape[0]
    blocks = length // SPAN
    groups = colp_ref.shape[0]
    seg = segc_ref[...]
    pos = lax.broadcasted_iota(jnp.int32, (length, 128), 0)
    lag = jnp.zeros((length, 128), F32)
    for j in range(1, KW):
        lag = lag + ((pltpu.roll(seg, j, 0) == seg) & (pos >= j)).astype(F32)
    lag_ref[0:length, :] = lag
    lag_ref[length:, :] = jnp.zeros((8, 128), F32)
    lag2 = twice(lag)
    raw = small_ref[:, 0:256]
    v = bcp_ref[4:5, :] + bcp_ref[3:4, :] * raw
    for j in range(1, KW):
        v = v + bcp_ref[3 - j : 4 - j, :] * jnp.where(lag2 >= j, pltpu.roll(raw, j, 0), 0.0)
    act = v * jax.nn.sigmoid(v)
    bc_ref[...] = act.astype(BF16)
    bct_ref[...] = turned(act.astype(BF16))
    z = small_ref[:, 256:384] + hp_ref[0:1, :]
    dt = jnp.maximum(z, 0.0) + jnp.log1p(jnp.exp(-jnp.abs(z)))
    a = -dt * jnp.exp(hp_ref[1:2, :])
    tri_r = lax.broadcasted_iota(jnp.int32, (SPAN, SPAN), 0)
    tri_c = lax.broadcasted_iota(jnp.int32, (SPAN, SPAN), 1)
    lower = (tri_r >= tri_c).astype(F32)
    seg_row = segr_ref[0:1, :]
    for c in range(blocks):
        r0 = c * SPAN
        rows = slice(r0, r0 + SPAN)
        cum = dot_exact(lower, a[rows])
        segb = seg[rows]
        last = seg[r0 + SPAN - 1 : r0 + SPAN]
        tail = (segb == last).astype(F32)
        end = cum[SPAN - 1 : SPAN]
        q = jnp.exp(end - cum) * tail
        if c > 0:
            prev = seg[r0 - 1 : r0]
            p = jnp.exp(cum) * (segb == prev).astype(F32)
            k = jnp.exp(end) * (last == prev).astype(F32)
        else:
            p = jnp.zeros_like(cum)
            k = jnp.zeros_like(end)
        kexp_ref[c : c + 1, :] = k
        cumt = jnp.transpose(cum)
        dtb = dt[rows]
        for g in range(groups):
            hs = slice(PER * g, PER * g + PER)
            colp_ref[g, rows, 0:4] = cum[:, hs]
            colp_ref[g, rows, 4:8] = dtb[:, hs]
            colp_ref[g, rows, 8:12] = p[:, hs]
            colp_ref[g, rows, 12:16] = q[:, hs]
            cumt_ref[g, 0:4, rows] = cumt[hs, :]
        bb = bc_ref[rows, 0:STATE]
        cc = bc_ref[rows, STATE : 2 * STATE]
        same = across(segb) == seg_row[:, rows]
        g_ref[rows, :] = jnp.where(same & (tri_r >= tri_c), dot_nt(cc, bb), 0.0)
        gt_ref[rows, :] = jnp.where(same & (tri_r <= tri_c), dot_nt(bb, cc), 0.0)
    if blocks < kexp_ref.shape[0]:
        kexp_ref[blocks:, :] = jnp.zeros((kexp_ref.shape[0] - blocks, 128), F32)


def conv_rows(xr_ref, lag_ref, chan_ref, r0):
    cur = xr_ref[pl.ds(r0, SPAN), :]
    before = xr_ref[pl.ds(pl.multiple_of(jnp.maximum(r0 - 8, 0), 8), 8), :]
    both = jnp.concatenate([before, cur], axis=0)
    lag = twice(lag_ref[pl.ds(r0, SPAN), :])
    v = chan_ref[4:5, :] + chan_ref[3:4, :] * cur
    for j in range(1, KW):
        earlier = pltpu.roll(both, j, 0)[8:]
        v = v + chan_ref[3 - j : 4 - j, :] * jnp.where(lag >= j, earlier, 0.0)
    return cur, v


def scan_kernel(
    nb_ref, wg_ref, wx_ref, chan_ref, lag_ref, bc_ref, bct_ref, g_ref, colp_ref, cumt_ref, kexp_ref,
    gate_ref, xr_ref, y_ref, gated_ref, sq_ref, st_ref, state,
):
    length = gate_ref.shape[0]
    blocks = length // SPAN
    state[...] = jnp.zeros_like(state)

    @pl.when(pl.program_id(0) == 0)
    def _():
        sq_ref[...] = jnp.zeros_like(sq_ref)

    def project(c, carry):
        rows = pl.ds(pl.multiple_of(c * 512, 512), 512)
        gate_ref[rows, :] = dot_nn(nb_ref[rows, :], wg_ref[...])
        xr_ref[rows, :] = dot_nn(nb_ref[rows, :], wx_ref[...])
        return carry

    lax.fori_loop(0, length // 512, project, 0)

    def body(c, carry):
        r0 = pl.multiple_of(c * SPAN, SPAN)
        rows = pl.ds(r0, SPAN)
        _, v = conv_rows(xr_ref, lag_ref, chan_ref, r0)
        xc = (v * jax.nn.sigmoid(v)).astype(BF16).astype(F32)
        cp = colp_ref[0, rows, :]
        xd = (spread(cp[:, 4:8]) * xc).astype(BF16)
        px = spread(cp[:, 8:12])
        qx = spread(cp[:, 12:16])
        gb = g_ref[rows, :]
        lefts, rights = [], []
        for h in range(PER):
            gap = cp[:, h : h + 1] - cumt_ref[0, h : h + 1, rows]
            lefts.append((gb * jnp.exp(jnp.minimum(gap, 0.0))).astype(BF16))
            rights.append(xd * head_mask(h))
        y = dot_nn(jnp.concatenate(lefts, axis=1), jnp.concatenate(rights, axis=0))
        st = state[...]
        stb = st.astype(BF16)
        st_ref[c] = stb
        y = y + px * dot_nn(bc_ref[rows, STATE : 2 * STATE], stb)
        kx = kexp_ref[pl.ds(c, 1), :]
        state[...] = kx * st + dot_nn(bct_ref[0:STATE, rows], (qx * xd.astype(F32)).astype(BF16))
        y = y + chan_ref[5:6, :] * xc
        y_ref[rows, :] = y
        gate = gate_ref[rows, :]
        gated = y * (gate * jax.nn.sigmoid(gate))
        gated_ref[rows, :] = gated.astype(BF16)
        sq = gated * gated
        sq_ref[rows, :] += sq[:, 0:128] + sq[:, 128:256]
        return carry

    lax.fori_loop(0, blocks, body, 0)


def scan_grad_kernel(
    place, gate_ref, xr_ref, y_ref, dh_ref, chan_ref, lag_ref, ir_ref, cf_ref, bc_ref, bct_ref, gt_ref,
    colp_ref, cumt_ref, kexp_ref, st_ref, segc_ref, segr_ref,
    small_ref, hp_ref, bcp_ref,
    dgate_ref, dxr_ref, chg_ref, nd_ref, ds_ref, pg_ref,
    dst, head, dgt, dbc_ref, end_ref, acc_a, acc_d, acc_e,
):
    length = gate_ref.shape[0]
    blocks = length // SPAN
    step = pl.program_id(0)
    dst[...] = jnp.zeros_like(dst)
    head[...] = jnp.zeros_like(head)
    end_ref[...] = jnp.zeros_like(end_ref)
    chg_ref[...] = jnp.zeros_like(chg_ref)

    @pl.when(step == 0)
    def _():
        dgt[...] = jnp.zeros_like(dgt)
        dbc_ref[...] = jnp.zeros_like(dbc_ref)
        nd_ref[...] = jnp.zeros_like(nd_ref)
        acc_a[...] = jnp.zeros_like(acc_a)
        acc_d[...] = jnp.zeros_like(acc_d)
        acc_e[...] = jnp.zeros_like(acc_e)

    pick_r = lax.broadcasted_iota(jnp.int32, (GROUP, 128), 0)
    pick_c = lax.broadcasted_iota(jnp.int32, (GROUP, 128), 1)
    pick32 = (pick_r // HEADDIM + PER * place == pick_c).astype(F32)
    pick = pick32.astype(BF16)

    def per_head(v):
        hi = v.astype(BF16)
        lo = (v - hi.astype(F32)).astype(BF16)
        return dot_nn(hi, pick) + dot_nn(lo, pick)

    def total(v):
        return jnp.sum(v, axis=0, keepdims=True)

    def body(back, carry):
        c = blocks - 1 - back
        r0 = pl.multiple_of(c * SPAN, SPAN)
        rows = pl.ds(r0, SPAN)
        cur, v = conv_rows(xr_ref, lag_ref, chan_ref, r0)
        sv = jax.nn.sigmoid(v)
        xc = (v * sv).astype(BF16).astype(F32)
        cp = colp_ref[0, rows, :]
        dtx = spread(cp[:, 4:8])
        px = spread(cp[:, 8:12])
        qx = spread(cp[:, 12:16])
        xd = (dtx * xc).astype(BF16)
        xdf = xd.astype(F32)
        gate = gate_ref[rows, :]
        y = y_ref[rows, :]
        dh = dh_ref[rows, :].astype(F32)
        ir = twice(ir_ref[rows, :])
        cf = twice(cf_ref[rows, :])
        sg = jax.nn.sigmoid(gate)
        sl = gate * sg
        gated = y * sl
        dgd = ir * (dh * chan_ref[6:7, :]) - gated * cf
        dy = dgd * sl
        dgate = dgd * y * (sg * (1.0 + gate * (1.0 - sg)))
        dgate_ref[rows, :] = dgate.astype(BF16)
        dyb = dy.astype(BF16)
        gt = gt_ref[rows, :]
        lefts, rights = [], []
        acc = dgt[rows, :]
        for h in range(PER):
            gap = cumt_ref[0, h : h + 1, rows] - cp[:, h : h + 1]
            et = jnp.exp(jnp.minimum(gap, 0.0))
            lefts.append((gt * et).astype(BF16))
            dym = dyb * head_mask(h)
            rights.append(dym)
            acc = acc + dot_nt(xd, dym) * et
        dgt[rows, :] = acc
        u = dot_nn(jnp.concatenate(lefts, axis=1), jnp.concatenate(rights, axis=0))
        ds = dst[...]
        dsb = ds.astype(BF16)
        bb = bc_ref[rows, 0:STATE]
        cc = bc_ref[rows, STATE : 2 * STATE]
        ui = qx * dot_nn(bb, dsb)
        u = u + ui
        dxc = chan_ref[5:6, :] * dy + dtx * u
        yscan = y - chan_ref[5:6, :] * xc
        acc_a[rows, :] += per_head(dyb.astype(F32) * yscan - xdf * u)
        acc_d[rows, :] += per_head(xc * u)
        stb = st_ref[c]
        kx = kexp_ref[pl.ds(c, 1), :]
        end_ref[pl.ds(c, 1), :] = total(xdf * ui) + kx * total(ds * stb.astype(F32))
        pdy = (px * dyb.astype(F32)).astype(BF16)
        dbc_ref[rows, 0:STATE] += dot_nt((qx * xdf).astype(BF16), dsb)
        dbc_ref[rows, STATE : 2 * STATE] += dot_nt(pdy, stb)
        dst[...] = kx * ds + dot_nn(bct_ref[STATE : 2 * STATE, rows], pdy)
        dv = dxc * (sv * (1.0 + v * (1.0 - sv)))
        after = pl.ds(pl.multiple_of(r0 + SPAN, 8), 8)
        wide = jnp.concatenate([dv, head[...]], axis=0)
        lagw = jnp.concatenate([twice(lag_ref[rows, :]), twice(lag_ref[after, :])], axis=0)
        head[...] = dv[0:8]
        dxr = chan_ref[3:4, :] * dv
        chg_ref[3:4, :] += total(cur * dv)
        chg_ref[4:5, :] += total(dv)
        chg_ref[5:6, :] += total(dy * xc)
        chg_ref[6:7, :] += total(dh * gated * ir)
        for j in range(1, KW):
            later = pltpu.roll(jnp.where(lagw >= j, wide, 0.0), SPAN + 8 - j, 0)[0:SPAN]
            dxr = dxr + chan_ref[3 - j : 4 - j, :] * later
            chg_ref[3 - j : 4 - j, :] += total(cur * later)
        dxr_ref[rows, :] = dxr.astype(BF16)
        nd = dgate * gate + dxr * cur
        nd_ref[rows, :] += nd[:, 0:128] + nd[:, 128:256]
        return carry

    lax.fori_loop(0, blocks, body, 0)

    acc_e[...] += dot_exact(end_ref[...], pick32)

    @pl.when(step == pl.num_programs(0) - 1)
    def _():
        tri_r = lax.broadcasted_iota(jnp.int32, (SPAN, SPAN), 0)
        tri_c = lax.broadcasted_iota(jnp.int32, (SPAN, SPAN), 1)
        upper = (tri_r <= tri_c).astype(F32)
        rate = jnp.exp(hp_ref[1:2, :])
        pg_ref[...] = jnp.zeros_like(pg_ref)
        for c in range(blocks):
            rows = slice(c * SPAN, (c + 1) * SPAN)
            same = across(segc_ref[rows, :]) == segr_ref[0:1, rows]
            full = jnp.where(same & (tri_r <= tri_c), dgt[rows, :], 0.0)
            dbc_ref[rows, 0:STATE] += dot_nn(full.astype(BF16), bc_ref[rows, STATE : 2 * STATE])
            dbc_ref[rows, STATE : 2 * STATE] += dot_nn(
                jnp.transpose(full).astype(BF16), bc_ref[rows, 0:STATE]
            )
            da = dot_exact(upper, acc_a[rows, :]) + acc_e[c : c + 1, :]
            raw = small_ref[rows, 2 * STATE :]
            z = raw + hp_ref[0:1, :]
            dt = jnp.maximum(z, 0.0) + jnp.log1p(jnp.exp(-jnp.abs(z)))
            ddt = (acc_d[rows, :] - rate * da) * jax.nn.sigmoid(z)
            pg_ref[5:6, 0:128] += total(ddt)
            pg_ref[6:7, 0:128] += -rate * total(da * dt)
            ds_ref[rows, 2 * STATE :] = ddt.astype(BF16)
            nd_ref[rows, :] += ddt * raw
        raw = small_ref[:, 0 : 2 * STATE]
        lag = twice(lag_ref[0:length, :])
        v = bcp_ref[4:5, :] + bcp_ref[3:4, :] * raw
        for j in range(1, KW):
            v = v + bcp_ref[3 - j : 4 - j, :] * jnp.where(lag >= j, pltpu.roll(raw, j, 0), 0.0)
        sv = jax.nn.sigmoid(v)
        dv = dbc_ref[...] * (sv * (1.0 + v * (1.0 - sv)))
        dr = bcp_ref[3:4, :] * dv
        pg_ref[3:4, :] = total(raw * dv)
        pg_ref[4:5, :] = total(dv)
        for j in range(1, KW):
            later = pltpu.roll(jnp.where(lag >= j, dv, 0.0), length - j, 0)
            dr = dr + bcp_ref[3 - j : 4 - j, :] * later
            pg_ref[3 - j : 4 - j, :] = total(raw * later)
        ds_ref[:, 0 : 2 * STATE] = dr.astype(BF16)
        nd = dr * raw
        nd_ref[...] += nd[:, 0:128] + nd[:, 128:256]


def whole(shape):
    return pl.BlockSpec(shape, lambda g: (0,) * len(shape))


def once(shape):
    return pl.BlockSpec(shape, lambda g: (0,) * len(shape), pipeline_mode=pl.Buffered(1))


def tile(rows):
    return pl.BlockSpec((rows, GROUP), lambda g: (0, g))


def prep_shapes(length, groups):
    return (
        jax.ShapeDtypeStruct((length, 2 * STATE), BF16),
        jax.ShapeDtypeStruct((2 * STATE, length), BF16),
        jax.ShapeDtypeStruct((length, SPAN), F32),
        jax.ShapeDtypeStruct((length, SPAN), F32),
        jax.ShapeDtypeStruct((groups, length, 16), F32),
        jax.ShapeDtypeStruct((groups, 8, length), F32),
        jax.ShapeDtypeStruct((8, 128), F32),
        jax.ShapeDtypeStruct((length + 8, 128), F32),
    )


def prep(small, segc, segr, bcp, hp, groups):
    return pl.pallas_call(
        prep_kernel,
        out_shape=prep_shapes(small.shape[0], groups),
        compiler_params=pltpu.CompilerParams(vmem_limit_bytes=VMEM_LIMIT),
        name="prep",
    )(small, segc, segr, bcp, hp)


def scan_specs(length, width, gb):
    last = 2 * gb - 1

    def at(g):
        return jnp.minimum(g, last)

    def strip(rows):
        return pl.BlockSpec((rows, GROUP), lambda g: (0, at(g)))

    weight = pl.BlockSpec((None, width, GROUP), lambda g: (at(g) // gb, 0, at(g) % gb))
    return [
        once((length, width)),
        weight,
        weight,
        strip(8),
        once((length + 8, 128)),
        once((length, 2 * STATE)),
        once((2 * STATE, length)),
        once((length, SPAN)),
        pl.BlockSpec((1, length, 16), lambda g: (at(g), 0, 0)),
        pl.BlockSpec((1, 8, length), lambda g: (at(g), 0, 0)),
        strip(8),
    ], [
        strip(length),
        strip(length),
        strip(length),
        strip(length),
        whole((length, 128)),
        pl.BlockSpec((length // SPAN, STATE, GROUP), lambda g: (0, 0, at(g))),
    ]


def scan_shapes(length, channels):
    return (
        jax.ShapeDtypeStruct((length, channels), F32),
        jax.ShapeDtypeStruct((length, channels), F32),
        jax.ShapeDtypeStruct((length, channels), F32),
        jax.ShapeDtypeStruct((length, channels), BF16),
        jax.ShapeDtypeStruct((length, 128), F32),
        jax.ShapeDtypeStruct((length // SPAN, STATE, channels), BF16),
    )


def scan(nb, wg, wx, chan, *rest):
    length, width = nb.shape
    channels = chan.shape[1]
    in_specs, out_specs = scan_specs(length, width, channels // GROUP // 2)
    return pl.pallas_call(
        scan_kernel,
        grid=(channels // GROUP,),
        in_specs=in_specs,
        out_specs=out_specs,
        out_shape=scan_shapes(length, channels),
        scratch_shapes=[pltpu.VMEM((STATE, GROUP), F32)],
        compiler_params=pltpu.CompilerParams(vmem_limit_bytes=VMEM_LIMIT),
        name="scan",
    )(nb, wg, wx, chan, *rest)


def scan_grad_specs(length, channels, shift=0):
    blocks = length // SPAN
    groups = channels // GROUP

    def at(g):
        return lax.rem(g + shift, groups)

    def tile(rows):
        return pl.BlockSpec((rows, GROUP), lambda g: (0, at(g)))

    ins = [
        tile(length),
        tile(length),
        tile(length),
        tile(length),
        tile(8),
        once((length + 8, 128)),
        once((length, 128)),
        once((length, 128)),
        once((length, 2 * STATE)),
        once((2 * STATE, length)),
        once((length, SPAN)),
        pl.BlockSpec((1, length, 16), lambda g: (at(g), 0, 0)),
        pl.BlockSpec((1, 8, length), lambda g: (at(g), 0, 0)),
        tile(8),
        pl.BlockSpec((blocks, STATE, GROUP), lambda g: (0, 0, at(g))),
        once((length, 128)),
        once((8, length)),
        once((length, 2 * STATE + 128)),
        once((8, 128)),
        once((8, 2 * STATE)),
    ]
    outs = [
        tile(length),
        tile(length),
        tile(8),
        once((length, 128)),
        once((length, 2 * STATE + 128)),
        once((8, 2 * STATE)),
    ]
    shapes = (
        jax.ShapeDtypeStruct((length, channels), BF16),
        jax.ShapeDtypeStruct((length, channels), BF16),
        jax.ShapeDtypeStruct((8, channels), F32),
        jax.ShapeDtypeStruct((length, 128), F32),
        jax.ShapeDtypeStruct((length, 2 * STATE + 128), BF16),
        jax.ShapeDtypeStruct((8, 2 * STATE), F32),
    )
    scratch = [
        pltpu.VMEM((STATE, GROUP), F32),
        pltpu.VMEM((8, GROUP), F32),
        pltpu.VMEM((length, SPAN), F32),
        pltpu.VMEM((length, 2 * STATE), F32),
        pltpu.VMEM((8, GROUP), F32),
        pltpu.VMEM((length, 128), F32),
        pltpu.VMEM((length, 128), F32),
        pltpu.VMEM((8, 128), F32),
    ]
    return ins, outs, shapes, scratch


def scan_grad(*args):
    length, channels = args[0].shape
    ins, outs, shapes, scratch = scan_grad_specs(length, channels)
    return pl.pallas_call(
        lambda *refs: scan_grad_kernel(pl.program_id(0), *refs),
        grid=(channels // GROUP,),
        in_specs=ins,
        out_specs=outs,
        out_shape=shapes,
        scratch_shapes=scratch,
        compiler_params=pltpu.CompilerParams(vmem_limit_bytes=VMEM_LIMIT),
        name="scan_grad",
    )(*args)


def back_kernel(a0, a1, a2, w0, w1, w2, nb_ref, dn_ref, gg_ref):
    cb = w0.shape[2]
    total = dot_nt(a2[...], w2[...])
    for a, w in ((a0, w0), (a1, w1)):
        for b in range(2):
            total = total + dot_nt(a[:, b * cb : (b + 1) * cb], w[b])
    dn_ref[0] = total.astype(BF16)
    gg = jnp.sum(total * nb_ref[...].astype(F32), axis=0, keepdims=True)
    gg_ref[...] = jnp.broadcast_to(gg, gg_ref.shape)


def back(dgate, dxr, d_small, wg, wx, w_small, nb):
    length, width = nb.shape
    cb = wg.shape[2]
    feat = max(width // 4, 256)
    per = feat // 256
    wide = pl.BlockSpec((2, 256, cb), lambda n: (0, n, 0))
    return pl.pallas_call(
        back_kernel,
        grid=(width // 256,),
        in_specs=[once(a.shape) for a in (dgate, dxr, d_small)]
        + [wide, wide]
        + [pl.BlockSpec((256, d_small.shape[1]), lambda n: (n, 0))]
        + [pl.BlockSpec((length, 256), lambda n: (0, n))],
        out_specs=[
            pl.BlockSpec((1, length, 256), lambda n: (n // per, 0, n % per)),
            pl.BlockSpec((8, 256), lambda n: (0, n)),
        ],
        out_shape=(
            jax.ShapeDtypeStruct((width // feat, length, feat), BF16),
            jax.ShapeDtypeStruct((8, width), F32),
        ),
        compiler_params=pltpu.CompilerParams(vmem_limit_bytes=VMEM_LIMIT),
        name="back",
    )(dgate, dxr, d_small, wg, wx, w_small, nb)


MESH_ID = pl.DeviceIdType.MESH


class Copies:
    def __init__(self, send, recv):
        self.send, self.recv, self.count, self.open = send, recv, 0, []

    def start(self, src, dst, to):
        copy = pltpu.make_async_remote_copy(
            src_ref=src, dst_ref=dst, send_sem=self.send.at[self.count],
            recv_sem=self.recv.at[self.count], device_id=to, device_id_type=MESH_ID,
        )
        self.count += 1
        copy.start()
        self.open.append(copy)
        return copy

    def finish(self):
        for copy in self.open:
            copy.wait_send()


def places():
    h, l, r = lax.axis_index("zh"), lax.axis_index("zl"), lax.axis_index("row")
    c, x, y = lax.rem(r, 2), lax.rem(r // 2, 2), r // 4
    rx, ry = r + 2 - 4 * x, r + 4 - 8 * y
    rc = r + 1 - 2 * c
    return h, l, r, c, x, y, rx, ry, rc


def meet(peers):
    barrier = pltpu.get_barrier_semaphore()
    for to in peers:
        pl.semaphore_signal(barrier, inc=1, device_id=to, device_id_type=MESH_ID)
    pl.semaphore_wait(barrier, len(peers))


GATHER_COPIES = 96
PIECES = 4
FINE = 8


def gather_kernel(
    x_ref, wg_ref, wx_ref, thin_ref, par_ref, segc_ref, segr_ref,
    nb_ref, nt_ref, ir_ref, par_out, ws_ref, small_ref, hp_ref, bcp_ref,
    bc_ref, bct_ref, g_ref, gt_ref, colp_ref, cumt_ref, kexp_ref, lag_ref, wg_out, wx_out,
    xv, parv, thin_v, stage, send, recv, local,
):
    h, l, r, c, x, y, rx, ry, rc = places()
    rd = rx + ry - r
    me, zhp = h * 2 + l, (1 - h) * 2 + l
    zh, zl, zd = {"zh": 1 - h}, {"zl": 1 - l}, {"zh": 1 - h, "zl": 1 - l}
    to_x, to_y, to_c = {"row": rx}, {"row": ry}, {"row": rc}
    length, feat = x_ref.shape[1], x_ref.shape[2]
    step = length // FINE
    shard = wg_ref.shape[0]
    meet((zh, zl, zd, to_x, to_y, to_c))
    copies = Copies(send, recv)
    start = copies.start

    def cols(block):
        return pl.ds(pl.multiple_of(block * feat, feat), feat)

    def toks(p):
        return pl.ds(p * step, step)

    def rows(row):
        return pl.ds(pl.multiple_of(row * shard, shard), shard)

    src = (wg_ref, wx_ref)
    dst = ((wg_out.at[0], wx_out.at[0]), (wg_out.at[1], wx_out.at[1]))
    keeps = [
        pltpu.make_async_copy(par_ref, parv.at[me], local.at[0]),
        pltpu.make_async_copy(thin_ref, thin_v.at[r, me], local.at[1]),
        pltpu.make_async_copy(x_ref.at[h], xv.at[:, cols(me)], local.at[2]),
        pltpu.make_async_copy(wg_ref, stage.at[0], local.at[3]),
        pltpu.make_async_copy(wx_ref, stage.at[1], local.at[4]),
    ]
    for keep in keeps:
        keep.start()
    laid = [pltpu.make_async_copy(stage.at[k], dst[0][k].at[rows(r)], local.at[5 + k]) for k in range(2)]
    pars = [start(par_ref, parv.at[me], to) for to in (zh, zl, zd)]
    thins = [start(thin_ref, thin_v.at[r, me], to) for to in (zh, zl, zd)]
    sib, sib_thin, x1, x3, wz, got, far = [], [], [], [], [], {}, {}
    bcn, hb = 2 * STATE // 4, colp_ref.shape[0] * PER // 2
    part = shard // 2

    def chunk(b, q, row):
        if b == 0:
            return dst[0][q].at[rows(row)]
        return dst[1][q // 2].at[pl.ds(pl.multiple_of(row * shard + q % 2 * part, part), part)]

    def send_w(q):
        wz.append(start(src[q // 2].at[pl.ds(q % 2 * part, part)], chunk(1, q, r), zh))

    def deal(b, q):
        if b == 0:
            got[b, q] = [start(src[q], chunk(b, q, r), to) for to in (to_x, to_y, to_c)]
        else:
            wz[q].wait_recv()
            got[b, q] = [start(chunk(b, q, r), chunk(b, q, r), to) for to in (to_x, to_y, to_c)]
        sib.append(got[b, q][2])

    def pass_on(b, q, n):
        piece = chunk(b, q, (rx, ry)[n])
        got[b, q][n].wait_recv()
        if n == q % 2:
            far[b, q] = start(piece, piece, (to_y, to_x)[n])
        sib.append(start(piece, piece, to_c))

    def corner(b, q):
        far[b, q].wait_recv()
        sib.append(start(chunk(b, q, rd), chunk(b, q, rd), to_c))

    def send_x():
        if len(x1) < FINE:
            p = len(x1)
            x1.append(start(x_ref.at[1 - h, toks(p)], xv.at[toks(p), cols(me)], zh))

    def pass_x(p):
        x1[p].wait_recv()
        x3.append(start(xv.at[toks(p), cols(zhp)], xv.at[toks(p), cols(zhp)], zl))
        send_x()

    for q in range(3):
        send_w(q)
    x2 = start(x_ref.at[h], xv.at[:, cols(me)], zl)
    for q in range(2):
        deal(0, q)
    for k in range(2):
        keeps[3 + k].wait()
        laid[k].start()
    keeps[1].wait()
    for copy in thins:
        copy.wait_recv()
    thin_go = [start(thin_v.at[r], thin_v.at[r], to) for to in (to_x, to_y, to_c)]
    sib_thin.append(thin_go[2])
    for q in range(2):
        for n in range(2):
            pass_on(0, q, n)
    thin_go[0].wait_recv()
    thin_d = start(thin_v.at[rx], thin_v.at[rx], to_y)
    sib_thin.append(start(thin_v.at[rx], thin_v.at[rx], to_c))
    thin_go[1].wait_recv()
    sib_thin.append(start(thin_v.at[ry], thin_v.at[ry], to_c))

    for copy in pars:
        copy.wait_recv()
    keeps[0].wait()
    keeps[2].wait()
    par_out[...] = parv[...]
    bcp_ref[...] = jnp.zeros_like(bcp_ref)
    bcp_ref[0:5, :] = sum(parv[b, 9:14, 0 : 2 * STATE] for b in range(4))
    hp_ref[...] = jnp.zeros_like(hp_ref)
    hp_ref[0:2, :] = parv[me, 14:16, 0:128] + pltpu.roll(parv[zhp, 14:16, 0:128], hb, 1)

    def norm(p):
        if p == 0:
            x2.wait_recv()
        x3[p].wait_recv()
        total = jnp.zeros((step, 1), F32)
        for b in range(4):
            value = xv[toks(p), b * feat : (b + 1) * feat].astype(F32)
            total = total + jnp.sum(value * value, axis=1, keepdims=True)
        root = lax.rsqrt(total / (4 * feat) + EPS)
        ir_ref[toks(p), :] = jnp.broadcast_to(root, (step, 128))
        for b in range(8):
            value = xv[toks(p), b * shard : (b + 1) * shard].astype(F32)
            gain = parv[b // 2, 8:9, b % 2 * shard : (b % 2 + 1) * shard]
            value = (value * root * gain).astype(BF16)
            nb_ref[toks(p), b * shard : (b + 1) * shard] = value
            nt_ref[b % 2, b // 2 * shard : (b // 2 + 1) * shard, toks(p)] = turned(value)

    def narrow(p):
        some = slice(p * (length // 2), (p + 1) * (length // 2))
        small_ref[some, :] = dot_nn(nb_ref[some, :], ws_ref[...])

    corner(0, 1)
    deal(1, 0)
    send_w(3)
    deal(1, 1)
    send_x()
    deal(1, 2)
    send_x()
    thin_d.wait_recv()
    sib_thin.append(start(thin_v.at[rd], thin_v.at[rd], to_c))
    for copy in sib_thin:
        copy.wait_recv()
    ws_ref[...] = jnp.zeros_like(ws_ref)
    for row in range(8):
        at = slice(row * shard, (row + 1) * shard)
        for b in range(4):
            ws_ref[at, b * bcn : (b + 1) * bcn] = thin_v[row, b, :, 0:bcn]
        ws_ref[at, 2 * STATE : 2 * STATE + hb] = thin_v[row, me, :, bcn : bcn + hb]
        ws_ref[at, 2 * STATE + hb : 2 * STATE + 2 * hb] = thin_v[row, zhp, :, bcn : bcn + hb]
    corner(0, 0)
    for q in range(3):
        pass_on(1, q, 0)
    pass_x(0)
    pass_x(1)
    for q in range(3):
        pass_on(1, q, 1)
    corner(1, 1)
    deal(1, 3)
    send_x()
    norm(0)
    norm(1)
    corner(1, 0)
    corner(1, 2)
    pass_x(2)
    pass_x(3)
    pass_on(1, 3, 0)
    pass_on(1, 3, 1)
    norm(2)
    pass_x(4)
    pass_x(5)
    norm(3)
    corner(1, 3)
    narrow(0)
    norm(4)
    pass_x(6)
    pass_x(7)
    norm(5)
    norm(6)
    norm(7)
    narrow(1)
    prep_kernel(
        small_ref, segc_ref, segr_ref, bcp_ref, hp_ref,
        bc_ref, bct_ref, g_ref, gt_ref, colp_ref, cumt_ref, kexp_ref, lag_ref,
    )
    for copy in sib:
        copy.wait_recv()
    for move in laid:
        move.wait()
    copies.finish()


def gather_all(x, wg, wx, thin, par, segc, segr, groups):
    _, length, feat = x.shape
    shard, cb = wg.shape
    anywhere = pl.BlockSpec(memory_space=pl.ANY)
    inside = pl.BlockSpec(memory_space=pltpu.VMEM)
    weight = jax.ShapeDtypeStruct((2, 8 * shard, cb), BF16)
    return pl.pallas_call(
        gather_kernel,
        in_specs=[anywhere] * 5 + [inside] * 2,
        out_specs=[inside] * 16 + [anywhere] * 2,
        out_shape=(
            jax.ShapeDtypeStruct((length, 4 * feat), BF16),
            jax.ShapeDtypeStruct((2, 4 * shard, length), BF16),
            jax.ShapeDtypeStruct((length, 128), F32),
            jax.ShapeDtypeStruct((4,) + par.shape, F32),
            jax.ShapeDtypeStruct((8 * shard, 2 * STATE + 128), BF16),
            jax.ShapeDtypeStruct((length, 2 * STATE + 128), F32),
            jax.ShapeDtypeStruct((8, 128), F32),
            jax.ShapeDtypeStruct((8, 2 * STATE), F32),
        )
        + prep_shapes(length, groups)
        + (weight, weight),
        scratch_shapes=[
            pltpu.VMEM((length, 4 * feat), BF16),
            pltpu.VMEM((4,) + par.shape, F32),
            pltpu.VMEM((8, 4) + thin.shape, BF16),
            pltpu.VMEM((2, shard, cb), BF16),
            pltpu.SemaphoreType.DMA((GATHER_COPIES,)),
            pltpu.SemaphoreType.DMA((GATHER_COPIES,)),
            pltpu.SemaphoreType.DMA((8,)),
        ],
        compiler_params=pltpu.CompilerParams(
            collective_id=0, has_side_effects=True, vmem_limit_bytes=VMEM_LIMIT
        ),
        name="gather_all",
    )(x, wg, wx, thin, par, segc, segr)


GRAD_COPIES = 96


def grad_kernel(
    dn_ref, raw_ref, nt_ref, dx_ref, ds_ref, small_ref, nd_ref, ir_ref, gate_ref,
    gz_ref, thin_out, small_out, own_out, away_out, row_out,
    raw_v, pa, pr, ps, rowv, rowr, local, cs, cr, ts, tr, fs, fr, ss, sr, zs, zr, tfs, tfr, tss, tsr, tz, tzr,
    sbuf, srecv, szr, send, recv,
):
    h, l, r, c, x, y, rx, ry, rc = places()
    me = h * 2 + l
    zh, zl, zd = {"zh": 1 - h}, {"zl": 1 - l}, {"zh": 1 - h, "zl": 1 - l}
    to_x, to_y, to_c = {"row": rx}, {"row": ry}, {"row": rc}
    shard = gz_ref.shape[1]
    ncol = gz_ref.shape[2]
    meet((zh, zl, zd, to_x, to_y, to_c))
    copies = Copies(send, recv)
    start = copies.start

    def product(side, d_ref, at):
        return dot_nn(nt_ref[side], d_ref[:, at])

    def tiles(d_ref, body):
        width = d_ref.shape[1]
        wide = 256 if width % 256 == 0 else 128

        def one(n, carry):
            body(pl.ds(pl.multiple_of(n * wide, wide), wide))
            return carry

        lax.fori_loop(0, width // wide, one, 0)

    length, feat = ps.shape
    piece = length // FINE

    def toks(p):
        return pl.ds(p * piece, piece)

    raw_copy = pltpu.make_async_copy(raw_ref.at[1], raw_v, local.at[2])
    raw_copy.start()
    near = [pltpu.make_async_copy(dn_ref.at[2 * k + l], pa.at[k], local.at[k]) for k in range(2)]
    for move in near:
        move.start()
    pair, far = [], []

    def give():
        p = len(pair)
        if p < FINE:
            pair.append(
                [start(dn_ref.at[2 * k + 1 - l, toks(p)], pr.at[k, toks(p)], zl) for k in range(2)]
            )

    def pair_done(p):
        if p == 0:
            for move in near:
                move.wait()
        for move in pair[p]:
            move.wait_recv()
        give()
        part = pa[1 - h, toks(p)].astype(F32) + pr[1 - h, toks(p)].astype(F32)
        ps[toks(p)] = part.astype(BF16)
        far.append(start(ps.at[toks(p)], away_out.at[toks(p)], zh))
        own_out[toks(p)] = pa[h, toks(p)].astype(F32) + pr[h, toks(p)].astype(F32)

    z_copy = [start(gate_ref, zr.at[0], zh), None]
    for _ in range(3):
        give()
    rowv[...] = jnp.zeros_like(rowv)
    rowv[0:1, :] = jnp.sum(jnp.transpose(nd_ref[...]), axis=0, keepdims=True)
    rowv[1:2, :] = jnp.transpose(ir_ref[...])[0:1, :]
    row_copies = [start(rowv, rowr.at[n], to) for n, to in enumerate((zh, zl, zd))]

    sbuf[0] = small_ref[...]
    small_hops = [to_c, to_x, to_y]
    small_copy = start(sbuf.at[0], srecv.at[0], to_c)

    dx0, dx1 = dx_ref.at[:, 0:ncol], dx_ref.at[:, ncol : 2 * ncol]
    quarters = [
        dict(d=dx1, first=to_x, second=to_y, mine=x, along=y, swap=False),
        dict(d=dx0, first=to_x, second=to_y, mine=x, along=y, swap=False),
        dict(first=to_y, second=to_x, mine=y, along=x, swap=True),
    ]

    def spot(q, first, second):
        return 2 * first + second if q["swap"] else 2 * second + first

    def refs(i):
        if i == 4:
            return ts, tr, tfs, tfr, tss, tsr
        return cs.at[i % 2], cr.at[i], fs.at[i], fr.at[i], ss.at[i], sr.at[i]

    thin_q = dict(d=ds_ref, first=to_y, second=to_x, mine=y, along=x, swap=True)

    def to_core(i, q):
        out, back = refs(i)[0:2]
        if i == 2:
            q["core"] = start(raw_ref.at[0], back, to_c)
            return

        def body(at):
            value = product(1 - c, q["d"], at).astype(BF16)
            for j in range(4):
                out[j, :, at] = value[j * shard : (j + 1) * shard]

        tiles(q["d"], body)
        q["core"] = start(out, back, to_c)

    def to_first(i, q, after=None):
        _, back, fsend, frecv, _, _ = refs(i)
        q["core"].wait_recv()
        if i == 2:
            raw_copy.wait()
            for j in range(4):
                back[j] = (raw_v[j].astype(F32) + back[j].astype(F32)).astype(BF16)
        else:

            def body(at):
                value = product(c, q["d"], at)
                for j in range(4):
                    part = value[j * shard : (j + 1) * shard] + back[j, :, at].astype(F32)
                    back[j, :, at] = part.astype(BF16)

            tiles(q["d"], body)
        for n in range(2):
            fsend[n] = back[spot(q, 1 - q["mine"], n)]
        if after is not None:
            after["f"].wait_recv()
        q["f"] = start(fsend, frecv, q["first"])

    def to_second(i, q):
        _, back, _, frecv, ssend, srcv = refs(i)
        if i != 0:
            q["f"].wait_recv()
        far = 1 - q["along"]
        kept = back[spot(q, q["mine"], far)].astype(F32)
        ssend[...] = (kept + frecv[far].astype(F32)).astype(BF16)
        q["s"] = start(ssend, srcv, q["second"])

    def settle(i, q):
        _, back, _, frecv, _, srcv = refs(i)
        q["s"].wait_recv()
        near = q["along"]
        kept = back[spot(q, q["mine"], near)].astype(F32)
        return kept + frecv[near].astype(F32) + srcv[...].astype(F32)

    to_core(2, quarters[2])
    to_core(0, quarters[0])
    to_first(2, quarters[2])
    to_first(0, quarters[0])
    pair_done(0)
    to_core(1, quarters[1])
    pair_done(1)
    to_core(4, thin_q)
    pair_done(2)
    small_copy.wait_recv()
    sbuf[1] = sbuf[0] + srecv[0]
    small_copy = start(sbuf.at[1], srecv.at[1], to_x)
    pair_done(3)
    to_second(2, quarters[2])
    to_first(1, quarters[1], quarters[0])
    to_second(0, quarters[0])
    to_first(4, thin_q)
    pair_done(4)
    small_copy.wait_recv()
    sbuf[2] = sbuf[1] + srecv[1]
    small_copy = start(sbuf.at[2], srecv.at[2], to_y)
    pair_done(5)
    gz_ref[0] = settle(2, quarters[2])
    zs[...] = settle(0, quarters[0]).astype(BF16)
    z_copy[1] = start(zs, zr.at[1], zh)
    pair_done(6)
    to_second(4, thin_q)
    small_copy.wait_recv()
    sbuf[3] = sbuf[2] + srecv[2]
    small_z = [
        start(sbuf.at[3, lo:], szr.at[n, lo:], to) for n, (to, lo) in enumerate(((zh, 8), (zl, 16), (zd, 16)))
    ]
    pair_done(7)
    to_second(1, quarters[1])
    tz[...] = settle(4, thin_q).astype(BF16)
    thin_z = []
    for n, (to, block) in enumerate(((zh, 2 * (1 - h) + l), (zl, 2 * h + 1 - l), (zd, 2 * (1 - h) + 1 - l))):
        lanes = pl.ds(pl.multiple_of(block // 2 * 128, 128), 128)
        thin_z.append(start(tz.at[:, lanes], tzr.at[n], to))
    thin_z.append(start(tz.at[:, 2 * STATE :], tzr.at[3], zh))
    gz_ref[1] = settle(1, quarters[1])
    row_out[0] = rowv[...]
    for n in range(3):
        row_copies[n].wait_recv()
        row_out[n + 1] = rowr[n]
    for copy in thin_z:
        copy.wait_recv()
    for copy in small_z:
        copy.wait_recv()
    total = tz[:, pl.ds(pl.multiple_of(h * 128, 128), 128)].astype(F32)
    for n in range(3):
        total = total + tzr[n].astype(F32)
    thin_out[:, 0:128] = total
    thin_out[:, 128:256] = tz[:, 2 * STATE :].astype(F32)
    thin_out[:, 256:384] = tzr[3].astype(F32)
    small_out[...] = jnp.zeros_like(small_out)
    small_out[0] = sbuf[3]
    for n, lo in enumerate((8, 16, 16)):
        small_out[n + 1, lo:] = szr[n, lo:]
    for move in far:
        move.wait_recv()
    for k in range(2):
        z_copy[k].wait_recv()
        gz_ref[k] += zr[k].astype(F32)
    copies.finish()


def grad_all(dn, raw, nt, dxr, d_small, small, nd, ir, gate_got):
    _, half, length = nt.shape
    feat = dn.shape[2]
    shard, cb = half // 4, dxr.shape[1] // 2
    ns = d_small.shape[1]
    inside = pl.BlockSpec(memory_space=pltpu.VMEM)
    anywhere = pl.BlockSpec(memory_space=pl.ANY)
    V = pltpu.VMEM
    return pl.pallas_call(
        grad_kernel,
        in_specs=[anywhere] * 2 + [inside] * 6 + [anywhere],
        out_specs=[inside] * 4 + [anywhere, inside],
        out_shape=(
            jax.ShapeDtypeStruct((2, shard, cb), F32),
            jax.ShapeDtypeStruct((shard, 384), F32),
            jax.ShapeDtypeStruct((4,) + small.shape, F32),
            jax.ShapeDtypeStruct((length, feat), F32),
            jax.ShapeDtypeStruct((length, feat), BF16),
            jax.ShapeDtypeStruct((4, 8, length), F32),
        ),
        scratch_shapes=[
            V((4, shard, cb), BF16),
            V((2, length, feat), BF16),
            V((2, length, feat), BF16),
            V((length, feat), BF16),
            V((8, length), F32),
            V((3, 8, length), F32),
            pltpu.SemaphoreType.DMA((3,)),
            V((2, 4, shard, cb), BF16),
            V((3, 4, shard, cb), BF16),
            V((4, shard, ns), BF16),
            V((4, shard, ns), BF16),
            V((3, 2, shard, cb), BF16),
            V((3, 2, shard, cb), BF16),
            V((3, shard, cb), BF16),
            V((3, shard, cb), BF16),
            V((shard, cb), BF16),
            V((2, shard, cb), BF16),
            V((2, shard, ns), BF16),
            V((2, shard, ns), BF16),
            V((shard, ns), BF16),
            V((shard, ns), BF16),
            V((shard, ns), BF16),
            V((4, shard, 128), BF16),
            V((4,) + small.shape, F32),
            V((3,) + small.shape, F32),
            V((3,) + small.shape, F32),
            pltpu.SemaphoreType.DMA((GRAD_COPIES,)),
            pltpu.SemaphoreType.DMA((GRAD_COPIES,)),
        ],
        compiler_params=pltpu.CompilerParams(
            collective_id=1, has_side_effects=True, vmem_limit_bytes=VMEM_LIMIT
        ),
        name="grad_all",
    )(dn, raw, nt, dxr, d_small, small, nd, ir, gate_got)


def table(send, recv):
    def copy(n, src, dst, to):
        return pltpu.make_async_remote_copy(
            src_ref=src, dst_ref=dst, send_sem=send.at[n], recv_sem=recv.at[n],
            device_id=to, device_id_type=MESH_ID,
        )

    return copy


SCAN_COPIES = 32


def scan_all_kernel(*refs):
    (cot_ref, out_ref, gains_ref), refs = refs[0:3], refs[3:]
    ins, refs = refs[0:11], refs[11:]
    gate_ref, xr_ref, y_ref, hid_ref, sq_ref, st_ref, po_ref, ir_ref, cf_ref, wo_ref = refs[0:10]
    state, cot_v, out_v, rows_v, sums, other, send, recv, local, row_sem = refs[10:]
    h, l, r, c, x, y, rx, ry, rc = places()
    rd = rx + ry - r
    me, zhp = h * 2 + l, (1 - h) * 2 + l
    zh, zl = {"zh": 1 - h}, {"zl": 1 - l}
    to_x, to_y, to_c = {"row": rx}, {"row": ry}, {"row": rc}
    length, feat = cot_ref.shape[1], cot_ref.shape[2]
    piece = length // PIECES
    shard = out_ref.shape[0]
    copy = table(send, recv)
    step = pl.program_id(0)
    channels = hid_ref.shape[1]
    groups = channels // GROUP

    def toks(p):
        return pl.ds(p * piece, piece)

    def cols(block):
        return pl.ds(pl.multiple_of(block * feat, feat), feat)

    def rows(row, half=None):
        if half is None:
            return pl.ds(pl.multiple_of(row * shard, shard), shard)
        return pl.ds(pl.multiple_of(row * shard + half * (shard // 2), shard // 2), shard // 2)

    def g1(p):
        return copy(p, cot_ref.at[1 - h, toks(p)], cf_ref.at[toks(p), cols(me)], zh)

    def g2(p):
        return copy(4 + p, cot_ref.at[h, toks(p)], cf_ref.at[toks(p), cols(me)], zl)

    def g3(p):
        part = cf_ref.at[toks(p), cols(zhp)]
        return copy(8 + p, part, part, zl)

    def wz():
        return copy(12, out_ref, wo_ref.at[1, rows(r)], zh)

    def own(n):
        return copy(13 + n, out_ref, wo_ref.at[0, rows(r)], (to_x, to_y, to_c)[n])

    def got(n):
        part = wo_ref.at[1, rows(r)]
        return copy(16 + n, part, part, (to_x, to_y, to_c)[n])

    def diag(b, n):
        part = wo_ref.at[b, rows((rx, ry)[n], n)]
        return copy(19 + 5 * b + n, part, part, (to_y, to_x)[n])

    def sib(b, n):
        part = wo_ref.at[b, rows((rx, ry, rd)[n])]
        return copy(21 + 5 * b + n, part, part, to_c)

    def load(n):
        return pltpu.make_async_copy((cot_ref.at[h], out_ref)[n], (cot_v, out_v)[n], local.at[n])

    def keep(n):
        to = (cf_ref.at[:, cols(me)], wo_ref.at[0, rows(r)])[n]
        return pltpu.make_async_copy((cot_v, out_v)[n], to, local.at[2 + n])

    def load_rows(n, slot):
        part = pl.ds(pl.multiple_of(n * 256, 256), 256)
        return pltpu.make_async_copy(wo_ref.at[:, part], rows_v.at[slot], row_sem.at[slot])

    def onward(p):
        g1(p).wait_recv()
        g3(p).start()

    def step0():
        meet((zh, zl, to_x, to_y, to_c))
        wz().start()
        for n in range(2):
            load(n).start()
        for n in range(3):
            own(n).start()
        for p in range(PIECES):
            g2(p).start()

    def step1():
        g1(0).start()
        for n in range(2):
            load(n).wait()
            keep(n).start()
        for n in range(2):
            own(n).wait_recv()
        for n in range(2):
            diag(0, n).start()
            sib(0, n).start()

    def step2():
        g1(1).start()
        for n in range(2):
            diag(0, n).wait_recv()
        sib(0, 2).start()

    def step3():
        g1(2).start()
        wz().wait_recv()
        for n in range(3):
            got(n).start()

    def step4():
        g1(3).start()

    def step5():
        for n in range(2):
            got(n).wait_recv()
        for n in range(2):
            diag(1, n).start()
            sib(1, n).start()

    def step6():
        for n in range(2):
            diag(1, n).wait_recv()
        sib(1, 2).start()
        onward(0)

    def step8():
        onward(1)

    def step10():
        onward(2)

    def step12():
        onward(3)

    acts = {
        0: step0, 1: step1, 2: step2, 3: step3, 4: step4, 5: step5, 6: step6, 8: step8, 10: step10, 12: step12,
    }
    for at, act in acts.items():
        pl.when(step == at)(act)

    @pl.when(step < groups)
    def _():
        part = hid_ref.at[:, pl.ds(pl.multiple_of(step * GROUP, GROUP), GROUP)]
        scan_kernel(*ins, gate_ref, xr_ref, y_ref, part, sq_ref, st_ref, state)

    def swap_sums():
        return copy(29, sums, other, zl)

    @pl.when(step == groups)
    def _():
        sums[...] = jnp.zeros_like(sums)
        sums[0:1, :] = jnp.sum(jnp.transpose(sq_ref[...]), axis=0, keepdims=True)
        swap_sums().start()
        keep(1).wait()
        for move in [own(2), got(2)] + [sib(b, n) for b in range(2) for n in range(3)]:
            move.wait_recv()
        load_rows(0, 0).start()
        swap_sums().wait()
        root = lax.rsqrt((sums[0:1, :] + other[0:1, :]) / (2 * channels) + EPS)
        ir_ref[...] = jnp.transpose(jnp.broadcast_to(root, (128, length)))
        for n in range(groups):
            part = slice(n * GROUP, (n + 1) * GROUP)
            value = hid_ref[:, part].astype(F32) * twice(ir_ref[...]) * gains_ref[6:7, part]
            hid_ref[:, part] = value.astype(BF16)

    @pl.when(step >= groups)
    def _():
        n = step - groups
        slot = lax.rem(n, 2)
        load_rows(n, slot).wait()

        @pl.when(step < 2 * groups - 1)
        def _():
            load_rows(n + 1, 1 - slot).start()

        half = channels // 2
        out = dot_nt(hid_ref[:, 0:half], rows_v[slot, 0]) + dot_nt(hid_ref[:, half:], rows_v[slot, 1])
        po_ref[0] = out.astype(BF16)

    @pl.when(step == 2 * groups - 1)
    def _():
        late = [g2(p) for p in range(PIECES)] + [g3(p) for p in range(PIECES)]
        for move in late:
            move.wait_recv()
        keep(0).wait()
        sent = [g1(p) for p in range(PIECES)] + late + [wz()]
        sent += [own(n) for n in range(3)] + [got(n) for n in range(3)]
        sent += [diag(b, n) for b in range(2) for n in range(2)]
        sent += [sib(b, n) for b in range(2) for n in range(3)]
        for move in sent:
            move.wait_send()


def scan_all(cot, out_proj, nb, wg, wx, chan, *rest):
    length, width = nb.shape
    channels = chan.shape[1]
    cb = channels // 2
    feat, shard = width // 4, out_proj.shape[0]
    groups = channels // GROUP
    per = feat // 256
    assert groups == 8 and width // 256 == groups
    in_specs, out_specs = scan_specs(length, width, cb // GROUP)
    out_specs[3] = once((length, channels))
    anywhere = pl.BlockSpec(memory_space=pl.ANY)
    shapes = scan_shapes(length, channels)

    def strip(g):
        n = jnp.maximum(g - groups, 0)
        return n // per, 0, n % per

    return pl.pallas_call(
        scan_all_kernel,
        grid=(2 * groups,),
        in_specs=[anywhere] * 2 + [once((8, channels))] + in_specs,
        out_specs=out_specs
        + [pl.BlockSpec((1, length, 256), strip), once((length, 128)), anywhere, anywhere],
        out_shape=shapes
        + (
            jax.ShapeDtypeStruct((4, length, feat), BF16),
            jax.ShapeDtypeStruct((length, 128), F32),
            jax.ShapeDtypeStruct((length, width), BF16),
            jax.ShapeDtypeStruct((2, width, cb), BF16),
        ),
        scratch_shapes=[
            pltpu.VMEM((STATE, GROUP), F32),
            pltpu.VMEM((length, feat), BF16),
            pltpu.VMEM((shard, cb), BF16),
            pltpu.VMEM((2, 2, 256, cb), BF16),
            pltpu.VMEM((8, length), F32),
            pltpu.VMEM((8, length), F32),
            pltpu.SemaphoreType.DMA((SCAN_COPIES,)),
            pltpu.SemaphoreType.DMA((SCAN_COPIES,)),
            pltpu.SemaphoreType.DMA((4,)),
            pltpu.SemaphoreType.DMA((2,)),
        ],
        compiler_params=pltpu.CompilerParams(
            collective_id=2, has_side_effects=True, vmem_limit_bytes=VMEM_LIMIT
        ),
        name="scan_all",
    )(cot, out_proj, chan, nb, wg, wx, chan, *rest)


EARLY = 640


def mid_kernel(
    cf_ref, wc_ref, hid_ref, ir_ref, po_ref,
    dh_ref, go_ref, coef_ref, sum_out,
    ct, dots, sums, other, send, recv,
):
    phase, g = pl.program_id(0), pl.program_id(1)
    last = pl.num_programs(1) - 1
    length, channels = hid_ref.shape
    shard = go_ref.shape[1]
    h, l = lax.axis_index("zh"), lax.axis_index("zl")
    to, zd = {"zl": 1 - l}, {"zh": 1 - h, "zl": 1 - l}
    copy = table(send, recv)
    at = pl.ds(pl.multiple_of(g * GROUP, GROUP), GROUP)

    def part():
        return copy(1, po_ref.at[2 * (1 - h) + 1 - l, pl.ds(0, EARLY)], sum_out, zd)

    @pl.when((phase == 0) & (g == 0))
    def _():
        meet((to, zd))
        part().start()
        dots[...] = jnp.zeros_like(dots)

    @pl.when(phase == 0)
    def _():
        dh = dot_nn(cf_ref[...], wc_ref[...])
        dh_ref[...] = dh.astype(BF16)
        term = dh * hid_ref[:, at].astype(F32)
        dots[...] += term[:, 0:128] + term[:, 128:256]
        ct[at, :] = turned(cf_ref[:, at])

    @pl.when((phase == 0) & (g == last))
    def _():
        sums[...] = jnp.zeros_like(sums)
        sums[0:1, :] = jnp.sum(jnp.transpose(dots[...]), axis=0, keepdims=True)
        move = copy(0, sums, other, to)
        move.start()
        move.wait()
        both = jnp.broadcast_to(sums[0:1, :] + other[0:1, :], (128, length))
        coef_ref[...] = jnp.transpose(both) * ir_ref[...] * ir_ref[...] / (2 * channels)

    @pl.when(phase == 1)
    def _():
        right = hid_ref[:, at]
        for n in range(go_ref.shape[0] // 4):
            value = dot_nn(ct[4 * n * shard : 4 * (n + 1) * shard, :], right).astype(BF16)
            for m in range(4):
                go_ref[4 * n + m] = value[m * shard : (m + 1) * shard]

    @pl.when((phase == 1) & (g == last))
    def _():
        part().wait()


def middle(cf, wo, hid, ir, po):
    length, width = cf.shape
    channels = hid.shape[1]
    gb = channels // 2 // GROUP
    n = channels // GROUP
    shard = width // 8
    assert n == width // 256

    def const(shape):
        return pl.BlockSpec(shape, lambda p, g: (0,) * len(shape), pipeline_mode=pl.Buffered(1))

    def first(p, g):
        return jnp.where(p == 0, g, n - 1)

    return pl.pallas_call(
        mid_kernel,
        grid=(2, n),
        in_specs=[
            const((length, width)),
            pl.BlockSpec((None, width, GROUP), lambda p, g: (first(p, g) // gb, 0, first(p, g) % gb)),
            const((length, channels)),
            const((length, 128)),
            pl.BlockSpec(memory_space=pl.ANY),
        ],
        out_specs=[
            pl.BlockSpec((length, GROUP), lambda p, g: (0, first(p, g))),
            pl.BlockSpec((8, shard, GROUP), lambda p, g: (0, 0, g * p)),
            const((length, 128)),
            pl.BlockSpec(memory_space=pl.ANY),
        ],
        out_shape=(
            jax.ShapeDtypeStruct((length, channels), BF16),
            jax.ShapeDtypeStruct((8, shard, channels), BF16),
            jax.ShapeDtypeStruct((length, 128), F32),
            jax.ShapeDtypeStruct((EARLY, po.shape[2]), BF16),
        ),
        scratch_shapes=[
            pltpu.VMEM((width, length), BF16),
            pltpu.VMEM((length, 128), F32),
            pltpu.VMEM((8, length), F32),
            pltpu.VMEM((8, length), F32),
            pltpu.SemaphoreType.DMA((2,)),
            pltpu.SemaphoreType.DMA((2,)),
        ],
        compiler_params=pltpu.CompilerParams(
            collective_id=3, has_side_effects=True, vmem_limit_bytes=VMEM_LIMIT
        ),
        name="middle",
    )(cf, wo, hid, ir, po)


SHIP_COPIES = 24


def scan_grad_all_kernel(*refs):
    (go_ref, po_ref, nt_ref), refs = refs[0:3], refs[3:]
    ins, refs = refs[0:20], refs[20:]
    outs, refs = refs[0:6], refs[6:]
    own_out, got_out, raw_out, gate_out, sum0, sum1, sum2 = refs[0:7]
    scratch, refs = refs[7:15], refs[15:]
    gm, gr, gf, gfr, gs, gsr, tm, ts, tr, tf, tfr, tg, tgr, send, recv, local = refs
    h, l, _, c, x, y, rx, ry, rc = places()
    zh, zl, zd = {"zh": 1 - h}, {"zl": 1 - l}, {"zh": 1 - h, "zl": 1 - l}
    to_x, to_y, to_c = {"row": rx}, {"row": ry}, {"row": rc}
    shard, cb = own_out.shape
    copy = table(send, recv)
    step = pl.program_id(0)
    groups = pl.num_programs(0)
    first, second = (to_x, to_y), (to_y, to_x)
    mine, along = (x, y), (y, x)
    dgate_ref = outs[0]

    def near(b, j):
        lanes = slice(b * cb, (b + 1) * cb)
        return pltpu.make_async_copy(go_ref.at[2 * j + c, :, lanes], gm.at[b, j], local.at[4 * b + j])

    def core(b, j):
        lanes = slice(b * cb, (b + 1) * cb)
        return copy(4 * b + j, go_ref.at[2 * j + 1 - c, :, lanes], gr.at[b, j], to_c)

    def hop1(b):
        return copy(8 + b, gf.at[b], gfr.at[b], first[b])

    def hop2(b):
        return copy(10 + b, gs.at[b], gsr.at[b], second[b])

    def out_sums():
        late = pl.ds(EARLY, po_ref.shape[1] - EARLY)
        return [
            copy(12, po_ref.at[2 * h + 1 - l], sum0, zl),
            copy(13, po_ref.at[2 * (1 - h) + l], sum1, zh),
            copy(14, po_ref.at[2 * (1 - h) + 1 - l, late], sum2, zd),
        ]

    def gate_core():
        return copy(15, ts, tr, to_c)

    def gate_hop1():
        return copy(16, tf, tfr, to_y)

    def gate_hop2():
        return copy(17, tg, tgr, to_x)

    def spot(b, at_first, at_second):
        return 2 * at_first + at_second if b else 2 * at_second + at_first

    def add(a, b):
        return a.astype(F32) + b.astype(F32)

    @pl.when(step == 0)
    def _():
        meet((zh, zl, zd, to_x, to_y, to_c))
        for b in range(2):
            for j in range(4):
                core(b, j).start()
                near(b, j).start()
        for move in out_sums():
            move.start()

    @pl.when(step == 2)
    def _():
        for b in range(2):
            for j in range(4):
                near(b, j).wait()
                core(b, j).wait_recv()
            for s in range(2):
                j = spot(b, 1 - mine[b], s)
                gf[b, s] = add(gm[b, j], gr[b, j]).astype(BF16)
            hop1(b).start()
            for s in range(2):
                j = spot(b, mine[b], s)
                gm[b, j] = add(gm[b, j], gr[b, j]).astype(BF16)

    @pl.when(step == 5)
    def _():
        for b in range(2):
            hop1(b).wait_recv()
            far = 1 - along[b]
            gs[b] = add(gm[b, spot(b, mine[b], far)], gfr[b, far]).astype(BF16)
            hop2(b).start()
        gate_core().wait_recv()
        for n in range(2):
            tf[n] = add(tm[spot(1, 1 - y, n)], tr[spot(1, 1 - y, n)]).astype(BF16)
        gate_hop1().start()
        for n in range(2):
            tm[spot(1, y, n)] = add(tm[spot(1, y, n)], tr[spot(1, y, n)]).astype(BF16)

    @pl.when(step == groups - 1)
    def _():
        gate_hop1().wait_recv()
        tg[...] = add(tm[spot(1, y, 1 - x)], tfr[1 - x]).astype(BF16)
        gate_hop2().start()

    scan_grad_kernel(lax.rem(step + groups // 2, groups), *ins, *outs, *scratch)

    def products(other, own):
        for side, ref in ((1 - c, other), (c, own)):
            value = dot_nn(nt_ref[side], dgate_ref[...]).astype(BF16)
            for j in range(4):
                ref[j] = value[j * shard : (j + 1) * shard]

    @pl.when(step < groups // 2)
    def _():
        lanes = pl.ds(pl.multiple_of(step * GROUP, GROUP), GROUP)
        products(ts.at[:, :, lanes], tm.at[:, :, lanes])

    @pl.when(step == groups // 2 - 1)
    def _():
        gate_core().start()

    @pl.when(step >= groups // 2)
    def _():
        products(raw_out.at[0], raw_out.at[1])

    @pl.when(step == groups - 1)
    def _():
        for b, out in enumerate((own_out, got_out)):
            hop2(b).wait_recv()
            own = along[b]
            total = add(gm[b, spot(b, mine[b], own)], gfr[b, own]) + gsr[b].astype(F32)
            out[...] = total.astype(out.dtype)
        gate_hop2().wait_recv()
        total = add(tm[spot(1, y, x)], tfr[x]) + tgr[...].astype(F32)
        gate_out[...] = total.astype(BF16)
        for b in range(2):
            for j in range(4):
                core(b, j).wait_send()
            hop1(b).wait_send()
            hop2(b).wait_send()
        for move in (gate_core(), gate_hop1(), gate_hop2()):
            move.wait_send()
        for move in out_sums():
            move.wait()


def scan_grad_all(go, po, nt, *args):
    length, channels = args[0].shape
    groups = channels // GROUP
    ins, outs, shapes, scratch = scan_grad_specs(length, channels, groups // 2)
    _, shard, _ = go.shape
    feat = po.shape[2]
    cb = channels // 2
    anywhere = pl.BlockSpec(memory_space=pl.ANY)
    V = pltpu.VMEM
    return pl.pallas_call(
        scan_grad_all_kernel,
        grid=(groups,),
        in_specs=[anywhere, anywhere, once(nt.shape)] + ins,
        out_specs=outs
        + [
            once((shard, cb)),
            once((shard, cb)),
            pl.BlockSpec((2, 4, shard, GROUP), lambda g: (0, 0, 0, jnp.maximum(g - groups // 2, 0))),
            once((shard, cb)),
            anywhere,
            anywhere,
            anywhere,
        ],
        out_shape=shapes
        + (
            jax.ShapeDtypeStruct((shard, cb), F32),
            jax.ShapeDtypeStruct((shard, cb), BF16),
            jax.ShapeDtypeStruct((2, 4, shard, cb), BF16),
            jax.ShapeDtypeStruct((shard, cb), BF16),
            jax.ShapeDtypeStruct((length, feat), BF16),
            jax.ShapeDtypeStruct((length, feat), BF16),
            jax.ShapeDtypeStruct((length - EARLY, feat), BF16),
        ),
        scratch_shapes=scratch
        + [
            V((2, 4, shard, cb), BF16),
            V((2, 4, shard, cb), BF16),
            V((2, 2, shard, cb), BF16),
            V((2, 2, shard, cb), BF16),
            V((2, shard, cb), BF16),
            V((2, shard, cb), BF16),
            V((4, shard, cb), BF16),
            V((4, shard, cb), BF16),
            V((4, shard, cb), BF16),
            V((2, shard, cb), BF16),
            V((2, shard, cb), BF16),
            V((shard, cb), BF16),
            V((shard, cb), BF16),
            pltpu.SemaphoreType.DMA((SHIP_COPIES,)),
            pltpu.SemaphoreType.DMA((SHIP_COPIES,)),
            pltpu.SemaphoreType.DMA((8,)),
        ],
        compiler_params=pltpu.CompilerParams(
            collective_id=4, has_side_effects=True, vmem_limit_bytes=VMEM_LIMIT
        ),
        name="scan_grad_all",
    )(go, po, nt, *args)


def build(nrow, nl):
    direct = nrow == 8 and nl == 2
    col = ("zh", "zl")

    def swap(v):
        return lax.ppermute(v, "zh", [(0, 1), (1, 0)])

    def pair_sum(v):
        return lax.psum(v, "zl")

    def row_gather(v):
        return lax.all_gather(v, "row", axis=0, tiled=True)

    def row_scatter(v):
        return lax.psum_scatter(v, "row", scatter_dimension=0, tiled=True)

    def per_device(
        tokens, segment_ids, norm_gain, in_zx, in_dt, in_bc, conv_x, conv_x_bias, conv_bc,
        conv_bc_bias, dt_bias, a_log, d_skip, inner_gain, out_proj, cotangent,
    ):
        seq_count, length = segment_ids.shape
        assert seq_count == 2
        feat = tokens.shape[1]
        width = feat * 2 * nl
        cb = inner_gain.shape[0]
        hb = dt_bias.shape[0]
        inner = cb * 2 * nl
        blocks = length // SPAN
        gb = cb // GROUP
        mh = lax.axis_index("zh")
        ml = lax.axis_index("zl")
        first_h = mh == 0
        here = mh * nl + ml
        bcn = conv_bc.shape[1]

        def mine(v, axis=0):
            return lax.dynamic_index_in_dim(v, mh, axis, keepdims=False)

        def other(v, axis=0):
            return lax.dynamic_index_in_dim(v, 1 - mh, axis, keepdims=False)

        def seqs(v):
            return v.reshape(2, length, feat)

        def by_seq(own, away):
            return jnp.where(first_h, jnp.stack([own, away]), jnp.stack([away, own]))

        def gather_features(v):
            own, away = mine(seqs(v)), other(seqs(v))
            both = by_seq(own, swap(away))
            every = jnp.moveaxis(lax.all_gather(both, "zl"), 0, 1)
            return jnp.transpose(every, (2, 0, 1, 3)).reshape(length, width)

        def scatter_features(v):
            parts = v.reshape(length, 2, nl, feat)
            both = lax.psum_scatter(parts, "zl", scatter_dimension=2, tiled=False)
            return by_seq(mine(both, 1), swap(other(both, 1))).astype(F32)

        chan = jnp.concatenate(
            [
                conv_x,
                conv_x_bias[None],
                jnp.repeat(d_skip, HEADDIM)[None],
                inner_gain[None],
                jnp.pad(jnp.concatenate([dt_bias, a_log]), (0, cb - 2 * hb))[None],
            ],
            axis=0,
        )
        thin = jnp.concatenate([in_bc, in_dt], axis=1)
        bc_rows = jnp.concatenate([conv_bc, conv_bc_bias[None]], axis=0)
        seg = mine(segment_ids)
        segc = jnp.broadcast_to(seg[:, None], (length, 128))
        segr = jnp.broadcast_to(seg[None, :], (8, length))
        if direct:
            extra = jnp.zeros((8, cb), F32)
            extra = lax.dynamic_update_slice(extra, norm_gain[None], (0, 0))
            extra = lax.dynamic_update_slice(extra, bc_rows, (1, here * bcn))
            extra = lax.dynamic_update_slice(extra, jnp.stack([dt_bias, a_log]), (6, 0))
            thin = jnp.pad(thin, ((0, 0), (0, 128 - thin.shape[1])))
            (
                normed, normed_t, inv_root, par, w_small, small, hp, bcp,
                bc, bct, gmat, gtmat, colp, cumt, kexp, lag, w_gate, w_x,
            ) = gather_all(
                seqs(tokens), in_zx[:, 0], in_zx[:, 1], thin, jnp.concatenate([chan, extra], axis=0),
                segc, segr, 2 * gb,
            )
            chan_got = lax.dynamic_index_in_dim(par, (1 - mh) * nl + ml, 0, keepdims=False)[0:8]
            gain = par[:, 8, :feat].reshape(width)
        else:
            chan_got = swap(chan)
            packed = jnp.concatenate([norm_gain, bc_rows.reshape(-1)])
            packs = lax.all_gather(packed, col)
            gain = packs[:, :feat].reshape(width)
            bc_all = jnp.moveaxis(packs[:, feat:].reshape(-1, KW + 1, bcn), 0, 1)
            bcp = jnp.pad(bc_all.reshape(KW + 1, 2 * STATE), ((0, 7 - KW), (0, 0)))
            hp = jnp.concatenate([c[7, : 2 * hb].reshape(2, hb) for c in (chan, chan_got)], axis=1)
            hp = jnp.pad(hp, ((0, 6), (0, 128 - 2 * hb)))
            thin = lax.all_gather(thin, ("row", "zh", "zl")).reshape(nrow, 2, nl, -1, bcn + hb)
            thin = jnp.moveaxis(thin, 3, 1).reshape(width, 2, nl, bcn + hb)
            w_gate = jnp.stack([row_gather(w) for w in (in_zx[:, 0], swap(in_zx[:, 0]))])
            w_x = jnp.stack([row_gather(w) for w in (in_zx[:, 1], swap(in_zx[:, 1]))])
            w_bc = thin[..., :bcn].reshape(width, 2 * STATE)
            w_dt = lax.dynamic_index_in_dim(thin[..., bcn:], ml, 2, keepdims=False)
            w_small = jnp.concatenate([w_bc, mine(w_dt, 1), other(w_dt, 1)], axis=1)
            w_small = jnp.pad(w_small, ((0, 0), (0, 384 - w_small.shape[1])))
            x32 = gather_features(tokens).astype(F32)
            inv_root = lax.rsqrt(jnp.mean(x32 * x32, axis=1, keepdims=True) + EPS)
            normed = (x32 * inv_root * gain).astype(BF16)
            small = dot_nn(normed, w_small)
            bc, bct, gmat, gtmat, colp, cumt, kexp, lag = prep(small, segc, segr, bcp, hp, 2 * gb)
        chans = jnp.concatenate([chan, chan_got], axis=1)
        kexp = jnp.repeat(kexp[:, : 2 * hb], HEADDIM, axis=1)

        seq_args = (lag, bc, bct, gmat, colp, cumt, kexp)
        gain_in = chans[6]
        if direct:
            gates, xrs, ys, hidden, _, sts, partial_out, ir, c_full, w_out = scan_all(
                seqs(cotangent), out_proj, normed, w_gate, w_x, chans, *seq_args
            )
            dh, g_out, cf, sum3 = middle(c_full, w_out, hidden, ir, partial_out)
        else:
            w_out = [row_gather(w) for w in (out_proj, swap(out_proj))]
            c_full = gather_features(cotangent)
            gates, xrs, ys, gateds, sq, sts = scan(normed, w_gate, w_x, chans, *seq_args)
            dh = jnp.concatenate([dot_nn(c_full, w).astype(BF16) for w in w_out], axis=1)
            gate_sq = pair_sum(jnp.sum(sq, axis=1))
            inner_root = lax.rsqrt(gate_sq / inner + EPS)[:, None]
            gate_dot = jnp.sum(dh.astype(F32) * gateds.astype(F32) * gain_in, axis=1)
            gate_dot = pair_sum(gate_dot)[:, None]
            hidden = (gateds.astype(F32) * inner_root * gain_in).astype(BF16)
            partial_out = dot_nt(hidden[:, :cb], w_out[0]) + dot_nt(hidden[:, cb:], w_out[1])
            partial_out = partial_out.astype(BF16)
            ir = jnp.broadcast_to(inner_root, (length, 128))
            cf = jnp.broadcast_to(inner_root**3 / inner * gate_dot, (length, 128))
            g_out = [dot_tn(c_full, hidden[:, :cb]), dot_tn(c_full, hidden[:, cb:])]
            g_out = [row_scatter(g.astype(BF16)) for g in g_out]
            g_wout = g_out[0].astype(F32) + swap(g_out[1]).astype(F32)
            out_here = scatter_features(partial_out)

        grad_args = (
            gates, xrs, ys, dh, chans, lag, ir, cf, bc, bct, gtmat, colp, cumt, kexp, sts, segc, segr,
            small, hp, bcp,
        )
        if direct:
            (
                dgates, dxrs, chg, nd, d_small, pg, g_own, g_got, gate_own, gate_got, sum0, sum1, sum2,
            ) = scan_grad_all(g_out, partial_out, normed_t, *grad_args)
            g_wout = g_own + swap(g_got).astype(F32)
            own = lax.dynamic_index_in_dim(partial_out, here, 0, keepdims=False)
            away = sum1.astype(F32) + jnp.concatenate([sum3, sum2], axis=0).astype(F32)
            out_here = by_seq(own.astype(F32) + sum0.astype(F32), away)
        else:
            dgates, dxrs, chg, nd, d_small, pg = scan_grad(*grad_args)
        output = (out_here + seqs(tokens)).astype(BF16).reshape(tokens.shape)
        g_dtb, g_alog = pg[5, : 2 * hb], pg[6, : 2 * hb]
        g_bcs = pg[: KW + 1]
        dn, gg = back(dgates, dxrs, d_small, w_gate, w_x, w_small, normed)
        g_gain = gg[0] / gain

        if direct:
            rows = []
            for b in range(2):
                hs = slice(b * hb, (b + 1) * hb)
                heads = jnp.concatenate([g_dtb[hs], g_alog[hs]])
                rows += [chg[0:7, b * cb : (b + 1) * cb], jnp.pad(heads, (0, cb - 2 * hb))[None]]
            last = jnp.concatenate([g_gain, g_bcs.reshape(-1)])
            last = jnp.pad(last, (0, 8 * cb - last.shape[0])).reshape(8, cb)
            gz, thins, smalls, d_own, d_away, rowv = grad_all(
                dn, gate_own, normed_t, dxrs, d_small, jnp.concatenate(rows + [last], axis=0), nd, inv_root,
                gate_got,
            )
            d_here = by_seq(d_own, d_away.astype(F32))
            roots = by_seq(rowv[0, 1], rowv[1, 1])
            dots = by_seq(rowv[0, 0] + rowv[2, 0], rowv[1, 0] + rowv[3, 0])
            g_zx = jnp.transpose(gz, (1, 0, 2))
            g_bc = lax.dynamic_slice(thins, (0, ml * bcn), (thins.shape[0], bcn))
            g_dt = thins[:, 128 : 128 + hb] + thins[:, 256 + hb : 256 + 2 * hb]
            chg = smalls[0, 0:8] + smalls[1, 8:16]
            last = smalls[:, 16:].sum(0).reshape(-1)
            g_gain = lax.dynamic_slice(last, (here * feat,), (feat,))
            g_bcs = last[width : width + (KW + 1) * 2 * STATE].reshape(KW + 1, 2 * nl, bcn)
            g_bcs = lax.dynamic_index_in_dim(g_bcs, here, 1, keepdims=False)
            g_dtb, g_alog = chg[7, :hb], chg[7, hb : 2 * hb]
        else:
            d_here = scatter_features(jnp.moveaxis(dn, 0, 1).reshape(length, width))
            dots = pair_sum(jnp.sum(nd, axis=1))
            dots = by_seq(dots, swap(dots))
            roots = by_seq(inv_root[:, 0], swap(inv_root[:, 0]))

            def join(own, away):
                return own.astype(F32) + swap(away).astype(F32)

            halves = (slice(0, cb), slice(cb, 2 * cb))
            g_gate = [row_scatter(dot_tn(normed, dgates[:, n]).astype(BF16)) for n in halves]
            g_x = [row_scatter(dot_tn(normed, dxrs[:, n]).astype(BF16)) for n in halves]
            g_zx = jnp.stack([join(*g_gate), join(*g_x)], axis=1)
            thins = row_scatter(dot_tn(normed, d_small))
            g_bc = lax.psum(thins[:, : 2 * STATE], col).reshape(-1, 2 * nl, bcn)
            g_bc = lax.dynamic_index_in_dim(g_bc, here, 1, keepdims=False)
            g_dts = thins[:, 2 * STATE : 2 * STATE + 2 * hb].reshape(-1, 2, hb)
            g_dt = g_dts[:, 0] + swap(g_dts[:, 1])
            every = ("row", "zh", "zl")
            g_gain, g_bcs = lax.psum((g_gain, g_bcs), every)
            g_gain = lax.dynamic_slice(g_gain, (here * feat,), (feat,))
            g_bcs = g_bcs.reshape(KW + 1, 2 * nl, bcn)
            g_bcs = lax.dynamic_index_in_dim(g_bcs, here, 1, keepdims=False)
            chg = chg[:, :cb] + swap(chg[:, cb:])
            g_dtb = g_dtb[:hb] + swap(g_dtb[hb:])
            g_alog = g_alog[:hb] + swap(g_alog[hb:])
            chg, g_dtb, g_alog = lax.psum((chg, g_dtb, g_alog), "row")
        roots, dots = roots[..., None], dots[..., None]
        x32 = seqs(tokens).astype(F32)
        tokens_grad = seqs(cotangent) + roots * norm_gain * d_here - x32 * (roots * roots / width * dots)
        tokens_grad = tokens_grad.astype(BF16).reshape(tokens.shape)
        return (
            output,
            tokens_grad,
            g_gain,
            g_zx,
            g_dt,
            g_bc,
            chg[0:KW],
            chg[4],
            g_bcs[0:KW],
            g_bcs[KW],
            g_dtb,
            g_alog,
            chg[5].reshape(hb, HEADDIM).sum(1),
            chg[6],
            g_wout,
        )

    return per_device


def solution(mesh):
    nrow, ncol = mesh.shape["row"], mesh.shape["col"]
    nl = ncol // 2
    split = Mesh(mesh.devices.reshape(nrow, 2, nl), ("row", "zh", "zl"))
    col = ("zh", "zl")
    in_specs = (
        P("row", col), P("row", None), P(col), P("row", None, col), P("row", col), P("row", col),
        P(None, col), P(col), P(None, col), P(col), P(col), P(col), P(col), P(col),
        P("row", col), P("row", col),
    )
    out_specs = (
        P("row", col), P("row", col), P(col), P("row", None, col), P("row", col), P("row", col),
        P(None, col), P(col), P(None, col), P(col), P(col), P(col), P(col), P(col), P("row", col),
    )
    return jax.shard_map(
        build(nrow, nl), mesh=split, in_specs=in_specs, out_specs=out_specs, check_vma=False
    )
```

```python
import functools

import jax
import jax.numpy as jnp
from jax import lax
from jax.experimental import pallas as pl
from jax.experimental.pallas import tpu as pltpu
from jax.sharding import Mesh, PartitionSpec as P

HEADDIM = 64
STATE = 128
KW = 4
EPS = 1e-05
SPAN = 256
GROUP = 256
PER = GROUP // HEADDIM
F32 = jnp.float32
BF16 = jnp.bfloat16
VMEM_LIMIT = 60 * 1024 * 1024


def dot_nn(a, b):
    return lax.dot_general(a, b, (((1,), (0,)), ((), ())), preferred_element_type=F32)


def dot_nt(a, b):
    return lax.dot_general(a, b, (((1,), (1,)), ((), ())), preferred_element_type=F32)


def dot_tn(a, b):
    return lax.dot_general(a, b, (((0,), (0,)), ((), ())), preferred_element_type=F32)


def dot_exact(a, b):
    return lax.dot_general(
        a, b, (((1,), (0,)), ((), ())), preferred_element_type=F32, precision=lax.Precision.HIGHEST
    )


def twice(v):
    return jnp.concatenate([v, v], axis=1)


def across(v):
    return v if SPAN == 128 else twice(v)


def turned(v):
    n = v.shape[1]
    row = lax.broadcasted_iota(jnp.int32, (n, n), 0)
    col = lax.broadcasted_iota(jnp.int32, (n, n), 1)
    return dot_nt((row == col).astype(F32).astype(BF16), v).astype(BF16)


def spread(cols):
    rows = cols.shape[0]
    lane = lax.broadcasted_iota(jnp.int32, (rows, 128), 1)
    low = lane < HEADDIM
    first = jnp.where(low, cols[:, 0:1], cols[:, 1:2])
    second = jnp.where(low, cols[:, 2:3], cols[:, 3:4])
    return jnp.concatenate([first, second], axis=1)


def head_mask(h):
    lane = lax.broadcasted_iota(jnp.int32, (1, GROUP), 1)
    return ((lane >= h * HEADDIM) & (lane < (h + 1) * HEADDIM)).astype(F32).astype(BF16)


def prep_lags(segc_ref, kexp_ref, lag_ref):
    seg = segc_ref[...]
    length = seg.shape[0]
    pos = lax.broadcasted_iota(jnp.int32, (length, 128), 0)
    lag = jnp.zeros((length, 128), F32)
    for j in range(1, KW):
        lag = lag + ((pltpu.roll(seg, j, 0) == seg) & (pos >= j)).astype(F32)
    lag_ref[0:length, :] = lag
    lag_ref[length:, :] = jnp.zeros((8, 128), F32)
    kexp_ref[...] = jnp.zeros_like(kexp_ref)


def prep_rows(
    lo, hi, small_ref, segc_ref, segr_ref, bcp_ref, hp_ref,
    bc_ref, bct_ref, g_ref, gt_ref, colp_ref, cumt_ref, kexp_ref, lag_ref,
):
    groups = colp_ref.shape[0]
    some = slice(lo, hi)
    lag2 = twice(lag_ref[some, :])
    raw = small_ref[some, 0:256]
    wide = raw if lo == 0 else small_ref[lo - 8 : hi, 0:256]
    v = bcp_ref[4:5, :] + bcp_ref[3:4, :] * raw
    for j in range(1, KW):
        earlier = pltpu.roll(wide, j, 0)[wide.shape[0] - (hi - lo) :]
        v = v + bcp_ref[3 - j : 4 - j, :] * jnp.where(lag2 >= j, earlier, 0.0)
    act = (v * jax.nn.sigmoid(v)).astype(BF16)
    bc_ref[some, :] = act
    bct_ref[:, some] = turned(act)
    z = small_ref[some, 256:384] + hp_ref[0:1, :]
    dt = jnp.maximum(z, 0.0) + jnp.log1p(jnp.exp(-jnp.abs(z)))
    a = -dt * jnp.exp(hp_ref[1:2, :])
    tri_r = lax.broadcasted_iota(jnp.int32, (SPAN, SPAN), 0)
    tri_c = lax.broadcasted_iota(jnp.int32, (SPAN, SPAN), 1)
    lower = (tri_r >= tri_c).astype(F32)
    seg_row = segr_ref[0:1, :]
    for c in range(lo // SPAN, hi // SPAN):
        r0 = c * SPAN
        rows = slice(r0, r0 + SPAN)
        here = slice(r0 - lo, r0 - lo + SPAN)
        cum = dot_exact(lower, a[here])
        segb = segc_ref[rows, :]
        last = segc_ref[r0 + SPAN - 1 : r0 + SPAN, :]
        tail = (segb == last).astype(F32)
        end = cum[SPAN - 1 : SPAN]
        q = jnp.exp(end - cum) * tail
        if c > 0:
            prev = segc_ref[r0 - 1 : r0, :]
            p = jnp.exp(cum) * (segb == prev).astype(F32)
            kexp_ref[c : c + 1, :] = jnp.exp(end) * (last == prev).astype(F32)
        else:
            p = jnp.zeros_like(cum)
        cumt = jnp.transpose(cum)
        dtb = dt[here]
        for g in range(groups):
            hs = slice(PER * g, PER * g + PER)
            colp_ref[g, rows, 0:4] = cum[:, hs]
            colp_ref[g, rows, 4:8] = dtb[:, hs]
            colp_ref[g, rows, 8:12] = p[:, hs]
            colp_ref[g, rows, 12:16] = q[:, hs]
            cumt_ref[g, 0:4, rows] = cumt[hs, :]
        bb = bc_ref[rows, 0:STATE]
        cc = bc_ref[rows, STATE : 2 * STATE]
        same = across(segb) == seg_row[:, rows]
        g_ref[rows, :] = jnp.where(same & (tri_r >= tri_c), dot_nt(cc, bb), 0.0)
        gt_ref[rows, :] = jnp.where(same & (tri_r <= tri_c), dot_nt(bb, cc), 0.0)


def prep_kernel(*refs):
    prep_lags(refs[1], refs[-2], refs[-1])
    prep_rows(0, refs[0].shape[0], *refs)


def conv_rows(xr_ref, lag_ref, chan_ref, r0):
    cur = xr_ref[pl.ds(r0, SPAN), :]
    before = xr_ref[pl.ds(pl.multiple_of(jnp.maximum(r0 - 8, 0), 8), 8), :]
    both = jnp.concatenate([before, cur], axis=0)
    lag = twice(lag_ref[pl.ds(r0, SPAN), :])
    v = chan_ref[4:5, :] + chan_ref[3:4, :] * cur
    for j in range(1, KW):
        earlier = pltpu.roll(both, j, 0)[8:]
        v = v + chan_ref[3 - j : 4 - j, :] * jnp.where(lag >= j, earlier, 0.0)
    return cur, v


def scan_kernel(
    nb_ref, wg_ref, wx_ref, chan_ref, lag_ref, bc_ref, bct_ref, g_ref, colp_ref, cumt_ref, kexp_ref,
    gate_ref, xr_ref, y_ref, gated_ref, sq_ref, st_ref, state,
):
    length = gate_ref.shape[0]
    blocks = length // SPAN
    state[...] = jnp.zeros_like(state)

    @pl.when(pl.program_id(0) == 0)
    def _():
        sq_ref[...] = jnp.zeros_like(sq_ref)

    def project(c, carry):
        rows = pl.ds(pl.multiple_of(c * 512, 512), 512)
        gate_ref[rows, :] = dot_nn(nb_ref[rows, :], wg_ref[...])
        xr_ref[rows, :] = dot_nn(nb_ref[rows, :], wx_ref[...])
        return carry

    lax.fori_loop(0, length // 512, project, 0)

    def body(c, carry):
        r0 = pl.multiple_of(c * SPAN, SPAN)
        rows = pl.ds(r0, SPAN)
        _, v = conv_rows(xr_ref, lag_ref, chan_ref, r0)
        xc = (v * jax.nn.sigmoid(v)).astype(BF16).astype(F32)
        cp = colp_ref[0, rows, :]
        xd = (spread(cp[:, 4:8]) * xc).astype(BF16)
        px = spread(cp[:, 8:12])
        qx = spread(cp[:, 12:16])
        gb = g_ref[rows, :]
        lefts, rights = [], []
        for h in range(PER):
            gap = cp[:, h : h + 1] - cumt_ref[0, h : h + 1, rows]
            lefts.append((gb * jnp.exp(jnp.minimum(gap, 0.0))).astype(BF16))
            rights.append(xd * head_mask(h))
        y = dot_nn(jnp.concatenate(lefts, axis=1), jnp.concatenate(rights, axis=0))
        st = state[...]
        stb = st.astype(BF16)
        st_ref[c] = stb
        y = y + px * dot_nn(bc_ref[rows, STATE : 2 * STATE], stb)
        kx = kexp_ref[pl.ds(c, 1), :]
        state[...] = kx * st + dot_nn(bct_ref[0:STATE, rows], (qx * xd.astype(F32)).astype(BF16))
        y = y + chan_ref[5:6, :] * xc
        y_ref[rows, :] = y
        gate = gate_ref[rows, :]
        gated = y * (gate * jax.nn.sigmoid(gate))
        gated_ref[rows, :] = gated.astype(BF16)
        sq = gated * gated
        sq_ref[rows, :] += sq[:, 0:128] + sq[:, 128:256]
        return carry

    lax.fori_loop(0, blocks, body, 0)


def scan_grad_kernel(
    place, gate_ref, xr_ref, y_ref, dh_ref, chan_ref, lag_ref, ir_ref, cf_ref, bc_ref, bct_ref, gt_ref,
    colp_ref, cumt_ref, kexp_ref, st_ref, segc_ref, segr_ref,
    small_ref, hp_ref, bcp_ref,
    dgate_ref, dxr_ref, chg_ref, nd_ref, ds_ref, pg_ref,
    dst, head, dgt, dbc_ref, end_ref, acc_a, acc_d, acc_e,
):
    length = gate_ref.shape[0]
    blocks = length // SPAN
    step = pl.program_id(0)
    dst[...] = jnp.zeros_like(dst)
    head[...] = jnp.zeros_like(head)
    end_ref[...] = jnp.zeros_like(end_ref)
    chg_ref[...] = jnp.zeros_like(chg_ref)

    @pl.when(step == 0)
    def _():
        dgt[...] = jnp.zeros_like(dgt)
        dbc_ref[...] = jnp.zeros_like(dbc_ref)
        nd_ref[...] = jnp.zeros_like(nd_ref)
        acc_a[...] = jnp.zeros_like(acc_a)
        acc_d[...] = jnp.zeros_like(acc_d)
        acc_e[...] = jnp.zeros_like(acc_e)

    pick_r = lax.broadcasted_iota(jnp.int32, (GROUP, 128), 0)
    pick_c = lax.broadcasted_iota(jnp.int32, (GROUP, 128), 1)
    pick32 = (pick_r // HEADDIM + PER * place == pick_c).astype(F32)
    pick = pick32.astype(BF16)

    def per_head(v):
        hi = v.astype(BF16)
        lo = (v - hi.astype(F32)).astype(BF16)
        return dot_nn(hi, pick) + dot_nn(lo, pick)

    def total(v):
        return jnp.sum(v, axis=0, keepdims=True)

    def body(back, carry):
        c = blocks - 1 - back
        r0 = pl.multiple_of(c * SPAN, SPAN)
        rows = pl.ds(r0, SPAN)
        cur, v = conv_rows(xr_ref, lag_ref, chan_ref, r0)
        sv = jax.nn.sigmoid(v)
        xc = (v * sv).astype(BF16).astype(F32)
        cp = colp_ref[0, rows, :]
        dtx = spread(cp[:, 4:8])
        px = spread(cp[:, 8:12])
        qx = spread(cp[:, 12:16])
        xd = (dtx * xc).astype(BF16)
        xdf = xd.astype(F32)
        gate = gate_ref[rows, :]
        y = y_ref[rows, :]
        dh = dh_ref[rows, :].astype(F32)
        ir = twice(ir_ref[rows, :])
        cf = twice(cf_ref[rows, :])
        sg = jax.nn.sigmoid(gate)
        sl = gate * sg
        gated = y * sl
        dgd = ir * (dh * chan_ref[6:7, :]) - gated * cf
        dy = dgd * sl
        dgate = dgd * y * (sg * (1.0 + gate * (1.0 - sg)))
        dgate_ref[rows, :] = dgate.astype(BF16)
        dyb = dy.astype(BF16)
        gt = gt_ref[rows, :]
        lefts, rights = [], []
        acc = dgt[rows, :]
        for h in range(PER):
            gap = cumt_ref[0, h : h + 1, rows] - cp[:, h : h + 1]
            et = jnp.exp(jnp.minimum(gap, 0.0))
            lefts.append((gt * et).astype(BF16))
            dym = dyb * head_mask(h)
            rights.append(dym)
            acc = acc + dot_nt(xd, dym) * et
        dgt[rows, :] = acc
        u = dot_nn(jnp.concatenate(lefts, axis=1), jnp.concatenate(rights, axis=0))
        ds = dst[...]
        dsb = ds.astype(BF16)
        bb = bc_ref[rows, 0:STATE]
        cc = bc_ref[rows, STATE : 2 * STATE]
        ui = qx * dot_nn(bb, dsb)
        u = u + ui
        dxc = chan_ref[5:6, :] * dy + dtx * u
        yscan = y - chan_ref[5:6, :] * xc
        acc_a[rows, :] += per_head(dyb.astype(F32) * yscan - xdf * u)
        acc_d[rows, :] += per_head(xc * u)
        stb = st_ref[c]
        kx = kexp_ref[pl.ds(c, 1), :]
        end_ref[pl.ds(c, 1), :] = total(xdf * ui) + kx * total(ds * stb.astype(F32))
        pdy = (px * dyb.astype(F32)).astype(BF16)
        dbc_ref[rows, 0:STATE] += dot_nt((qx * xdf).astype(BF16), dsb)
        dbc_ref[rows, STATE : 2 * STATE] += dot_nt(pdy, stb)
        dst[...] = kx * ds + dot_nn(bct_ref[STATE : 2 * STATE, rows], pdy)
        dv = dxc * (sv * (1.0 + v * (1.0 - sv)))
        after = pl.ds(pl.multiple_of(r0 + SPAN, 8), 8)
        wide = jnp.concatenate([dv, head[...]], axis=0)
        lagw = jnp.concatenate([twice(lag_ref[rows, :]), twice(lag_ref[after, :])], axis=0)
        head[...] = dv[0:8]
        dxr = chan_ref[3:4, :] * dv
        chg_ref[3:4, :] += total(cur * dv)
        chg_ref[4:5, :] += total(dv)
        chg_ref[5:6, :] += total(dy * xc)
        chg_ref[6:7, :] += total(dh * gated * ir)
        for j in range(1, KW):
            later = pltpu.roll(jnp.where(lagw >= j, wide, 0.0), SPAN + 8 - j, 0)[0:SPAN]
            dxr = dxr + chan_ref[3 - j : 4 - j, :] * later
            chg_ref[3 - j : 4 - j, :] += total(cur * later)
        dxr_ref[rows, :] = dxr.astype(BF16)
        nd = dgate * gate + dxr * cur
        nd_ref[rows, :] += nd[:, 0:128] + nd[:, 128:256]
        return carry

    lax.fori_loop(0, blocks, body, 0)

    acc_e[...] += dot_exact(end_ref[...], pick32)

    @pl.when(step == pl.num_programs(0) - 1)
    def _():
        tri_r = lax.broadcasted_iota(jnp.int32, (SPAN, SPAN), 0)
        tri_c = lax.broadcasted_iota(jnp.int32, (SPAN, SPAN), 1)
        upper = (tri_r <= tri_c).astype(F32)
        rate = jnp.exp(hp_ref[1:2, :])
        pg_ref[...] = jnp.zeros_like(pg_ref)
        for c in range(blocks):
            rows = slice(c * SPAN, (c + 1) * SPAN)
            same = across(segc_ref[rows, :]) == segr_ref[0:1, rows]
            full = jnp.where(same & (tri_r <= tri_c), dgt[rows, :], 0.0)
            dbc_ref[rows, 0:STATE] += dot_nn(full.astype(BF16), bc_ref[rows, STATE : 2 * STATE])
            dbc_ref[rows, STATE : 2 * STATE] += dot_nn(
                jnp.transpose(full).astype(BF16), bc_ref[rows, 0:STATE]
            )
            da = dot_exact(upper, acc_a[rows, :]) + acc_e[c : c + 1, :]
            raw = small_ref[rows, 2 * STATE :]
            z = raw + hp_ref[0:1, :]
            dt = jnp.maximum(z, 0.0) + jnp.log1p(jnp.exp(-jnp.abs(z)))
            ddt = (acc_d[rows, :] - rate * da) * jax.nn.sigmoid(z)
            pg_ref[5:6, 0:128] += total(ddt)
            pg_ref[6:7, 0:128] += -rate * total(da * dt)
            ds_ref[rows, 2 * STATE :] = ddt.astype(BF16)
            nd_ref[rows, :] += ddt * raw
        raw = small_ref[:, 0 : 2 * STATE]
        lag = twice(lag_ref[0:length, :])
        v = bcp_ref[4:5, :] + bcp_ref[3:4, :] * raw
        for j in range(1, KW):
            v = v + bcp_ref[3 - j : 4 - j, :] * jnp.where(lag >= j, pltpu.roll(raw, j, 0), 0.0)
        sv = jax.nn.sigmoid(v)
        dv = dbc_ref[...] * (sv * (1.0 + v * (1.0 - sv)))
        dr = bcp_ref[3:4, :] * dv
        pg_ref[3:4, :] = total(raw * dv)
        pg_ref[4:5, :] = total(dv)
        for j in range(1, KW):
            later = pltpu.roll(jnp.where(lag >= j, dv, 0.0), length - j, 0)
            dr = dr + bcp_ref[3 - j : 4 - j, :] * later
            pg_ref[3 - j : 4 - j, :] = total(raw * later)
        ds_ref[:, 0 : 2 * STATE] = dr.astype(BF16)
        nd = dr * raw
        nd_ref[...] += nd[:, 0:128] + nd[:, 128:256]


def whole(shape):
    return pl.BlockSpec(shape, lambda g: (0,) * len(shape))


def once(shape):
    return pl.BlockSpec(shape, lambda g: (0,) * len(shape), pipeline_mode=pl.Buffered(1))


def tile(rows):
    return pl.BlockSpec((rows, GROUP), lambda g: (0, g))


def prep_shapes(length, groups):
    return (
        jax.ShapeDtypeStruct((length, 2 * STATE), BF16),
        jax.ShapeDtypeStruct((2 * STATE, length), BF16),
        jax.ShapeDtypeStruct((length, SPAN), F32),
        jax.ShapeDtypeStruct((length, SPAN), F32),
        jax.ShapeDtypeStruct((groups, length, 16), F32),
        jax.ShapeDtypeStruct((groups, 8, length), F32),
        jax.ShapeDtypeStruct((8, 128), F32),
        jax.ShapeDtypeStruct((length + 8, 128), F32),
    )


def prep(small, segc, segr, bcp, hp, groups):
    return pl.pallas_call(
        prep_kernel,
        out_shape=prep_shapes(small.shape[0], groups),
        compiler_params=pltpu.CompilerParams(vmem_limit_bytes=VMEM_LIMIT),
        name="prep",
    )(small, segc, segr, bcp, hp)


def scan_specs(length, width, gb):
    last = 2 * gb - 1

    def at(g):
        return jnp.minimum(g, last)

    def strip(rows):
        return pl.BlockSpec((rows, GROUP), lambda g: (0, at(g)))

    weight = pl.BlockSpec((None, width, GROUP), lambda g: (at(g) // gb, 0, at(g) % gb))
    return [
        once((length, width)),
        weight,
        weight,
        strip(8),
        once((length + 8, 128)),
        once((length, 2 * STATE)),
        once((2 * STATE, length)),
        once((length, SPAN)),
        pl.BlockSpec((1, length, 16), lambda g: (at(g), 0, 0)),
        pl.BlockSpec((1, 8, length), lambda g: (at(g), 0, 0)),
        strip(8),
    ], [
        strip(length),
        strip(length),
        strip(length),
        strip(length),
        whole((length, 128)),
        pl.BlockSpec((length // SPAN, STATE, GROUP), lambda g: (0, 0, at(g))),
    ]


def scan_shapes(length, channels):
    return (
        jax.ShapeDtypeStruct((length, channels), F32),
        jax.ShapeDtypeStruct((length, channels), F32),
        jax.ShapeDtypeStruct((length, channels), F32),
        jax.ShapeDtypeStruct((length, channels), BF16),
        jax.ShapeDtypeStruct((length, 128), F32),
        jax.ShapeDtypeStruct((length // SPAN, STATE, channels), BF16),
    )


def scan(nb, wg, wx, chan, *rest):
    length, width = nb.shape
    channels = chan.shape[1]
    in_specs, out_specs = scan_specs(length, width, channels // GROUP // 2)
    return pl.pallas_call(
        scan_kernel,
        grid=(channels // GROUP,),
        in_specs=in_specs,
        out_specs=out_specs,
        out_shape=scan_shapes(length, channels),
        scratch_shapes=[pltpu.VMEM((STATE, GROUP), F32)],
        compiler_params=pltpu.CompilerParams(vmem_limit_bytes=VMEM_LIMIT),
        name="scan",
    )(nb, wg, wx, chan, *rest)


def scan_grad_specs(length, channels, shift=0):
    blocks = length // SPAN
    groups = channels // GROUP

    def at(g):
        return lax.rem(g + shift, groups)

    def tile(rows):
        return pl.BlockSpec((rows, GROUP), lambda g: (0, at(g)))

    ins = [
        tile(length),
        tile(length),
        tile(length),
        tile(length),
        tile(8),
        once((length + 8, 128)),
        once((length, 128)),
        once((length, 128)),
        once((length, 2 * STATE)),
        once((2 * STATE, length)),
        once((length, SPAN)),
        pl.BlockSpec((1, length, 16), lambda g: (at(g), 0, 0)),
        pl.BlockSpec((1, 8, length), lambda g: (at(g), 0, 0)),
        tile(8),
        pl.BlockSpec((blocks, STATE, GROUP), lambda g: (0, 0, at(g))),
        once((length, 128)),
        once((8, length)),
        once((length, 2 * STATE + 128)),
        once((8, 128)),
        once((8, 2 * STATE)),
    ]
    outs = [
        tile(length),
        tile(length),
        tile(8),
        once((length, 128)),
        once((length, 2 * STATE + 128)),
        once((8, 2 * STATE)),
    ]
    shapes = (
        jax.ShapeDtypeStruct((length, channels), BF16),
        jax.ShapeDtypeStruct((length, channels), BF16),
        jax.ShapeDtypeStruct((8, channels), F32),
        jax.ShapeDtypeStruct((length, 128), F32),
        jax.ShapeDtypeStruct((length, 2 * STATE + 128), BF16),
        jax.ShapeDtypeStruct((8, 2 * STATE), F32),
    )
    scratch = [
        pltpu.VMEM((STATE, GROUP), F32),
        pltpu.VMEM((8, GROUP), F32),
        pltpu.VMEM((length, SPAN), F32),
        pltpu.VMEM((length, 2 * STATE), F32),
        pltpu.VMEM((8, GROUP), F32),
        pltpu.VMEM((length, 128), F32),
        pltpu.VMEM((length, 128), F32),
        pltpu.VMEM((8, 128), F32),
    ]
    return ins, outs, shapes, scratch


def scan_grad(*args):
    length, channels = args[0].shape
    ins, outs, shapes, scratch = scan_grad_specs(length, channels)
    return pl.pallas_call(
        lambda *refs: scan_grad_kernel(pl.program_id(0), *refs),
        grid=(channels // GROUP,),
        in_specs=ins,
        out_specs=outs,
        out_shape=shapes,
        scratch_shapes=scratch,
        compiler_params=pltpu.CompilerParams(vmem_limit_bytes=VMEM_LIMIT),
        name="scan_grad",
    )(*args)


def back_kernel(a0, a1, a2, w0, w1, w2, nb_ref, dn_ref, gg_ref):
    cb = w0.shape[2]
    total = dot_nt(a2[...], w2[...])
    for a, w in ((a0, w0), (a1, w1)):
        for b in range(2):
            total = total + dot_nt(a[:, b * cb : (b + 1) * cb], w[b])
    dn_ref[0] = total.astype(BF16)
    gg = jnp.sum(total * nb_ref[...].astype(F32), axis=0, keepdims=True)
    gg_ref[...] = jnp.broadcast_to(gg, gg_ref.shape)


def back(dgate, dxr, d_small, wg, wx, w_small, nb):
    length, width = nb.shape
    cb = wg.shape[2]
    feat = max(width // 4, 256)
    per = feat // 256
    wide = pl.BlockSpec((2, 256, cb), lambda n: (0, n, 0))
    return pl.pallas_call(
        back_kernel,
        grid=(width // 256,),
        in_specs=[once(a.shape) for a in (dgate, dxr, d_small)]
        + [wide, wide]
        + [pl.BlockSpec((256, d_small.shape[1]), lambda n: (n, 0))]
        + [pl.BlockSpec((length, 256), lambda n: (0, n))],
        out_specs=[
            pl.BlockSpec((1, length, 256), lambda n: (n // per, 0, n % per)),
            pl.BlockSpec((8, 256), lambda n: (0, n)),
        ],
        out_shape=(
            jax.ShapeDtypeStruct((width // feat, length, feat), BF16),
            jax.ShapeDtypeStruct((8, width), F32),
        ),
        compiler_params=pltpu.CompilerParams(vmem_limit_bytes=VMEM_LIMIT),
        name="back",
    )(dgate, dxr, d_small, wg, wx, w_small, nb)


MESH_ID = pl.DeviceIdType.MESH


class Copies:
    def __init__(self, send, recv):
        self.send, self.recv, self.count, self.open = send, recv, 0, []

    def start(self, src, dst, to):
        copy = pltpu.make_async_remote_copy(
            src_ref=src, dst_ref=dst, send_sem=self.send.at[self.count],
            recv_sem=self.recv.at[self.count], device_id=to, device_id_type=MESH_ID,
        )
        self.count += 1
        copy.start()
        self.open.append(copy)
        return copy

    def finish(self):
        for copy in self.open:
            copy.wait_send()


def places():
    h, l, r = lax.axis_index("zh"), lax.axis_index("zl"), lax.axis_index("row")
    c, x, y = lax.rem(r, 2), lax.rem(r // 2, 2), r // 4
    rx, ry = r + 2 - 4 * x, r + 4 - 8 * y
    rc = r + 1 - 2 * c
    return h, l, r, c, x, y, rx, ry, rc


def meet(peers):
    barrier = pltpu.get_barrier_semaphore()
    for to in peers:
        pl.semaphore_signal(barrier, inc=1, device_id=to, device_id_type=MESH_ID)
    pl.semaphore_wait(barrier, len(peers))


GATHER_COPIES = 96
PIECES = 4
FINE = 8


def gather_kernel(
    x_ref, wg_ref, wx_ref, thin_ref, par_ref, segc_ref, segr_ref,
    nb_ref, nt_ref, ir_ref, par_out, ws_ref, small_ref, hp_ref, bcp_ref,
    bc_ref, bct_ref, g_ref, gt_ref, colp_ref, cumt_ref, kexp_ref, lag_ref, wg_out, wx_out,
    xv, parv, thin_v, stage, send, recv, local,
):
    h, l, r, c, x, y, rx, ry, rc = places()
    rd = rx + ry - r
    me, zhp = h * 2 + l, (1 - h) * 2 + l
    zh, zl, zd = {"zh": 1 - h}, {"zl": 1 - l}, {"zh": 1 - h, "zl": 1 - l}
    to_x, to_y, to_c = {"row": rx}, {"row": ry}, {"row": rc}
    length, feat = x_ref.shape[1], x_ref.shape[2]
    step = length // FINE
    shard = wg_ref.shape[0]
    meet((zh, zl, zd, to_x, to_y, to_c))
    copies = Copies(send, recv)
    start = copies.start

    def cols(block):
        return pl.ds(pl.multiple_of(block * feat, feat), feat)

    def toks(p):
        return pl.ds(p * step, step)

    def rows(row):
        return pl.ds(pl.multiple_of(row * shard, shard), shard)

    src = (wg_ref, wx_ref)
    dst = ((wg_out.at[0], wx_out.at[0]), (wg_out.at[1], wx_out.at[1]))
    keeps = [
        pltpu.make_async_copy(par_ref, parv.at[me], local.at[0]),
        pltpu.make_async_copy(thin_ref, thin_v.at[r, me], local.at[1]),
        pltpu.make_async_copy(x_ref.at[h], xv.at[:, cols(me)], local.at[2]),
        pltpu.make_async_copy(wg_ref, stage.at[0], local.at[3]),
        pltpu.make_async_copy(wx_ref, stage.at[1], local.at[4]),
    ]
    for keep in keeps:
        keep.start()
    laid = [pltpu.make_async_copy(stage.at[k], dst[0][k].at[rows(r)], local.at[5 + k]) for k in range(2)]
    pars = [start(par_ref, parv.at[me], to) for to in (zh, zl, zd)]
    thins = [start(thin_ref, thin_v.at[r, me], to) for to in (zh, zl, zd)]
    sib, sib_thin, x1, x3, wz, got, far = [], [], [], [], [], {}, {}
    bcn, hb = 2 * STATE // 4, colp_ref.shape[0] * PER // 2
    part = shard // 2

    def chunk(b, q, row):
        if b == 0:
            return dst[0][q].at[rows(row)]
        return dst[1][q // 2].at[pl.ds(pl.multiple_of(row * shard + q % 2 * part, part), part)]

    def send_w(q):
        wz.append(start(src[q // 2].at[pl.ds(q % 2 * part, part)], chunk(1, q, r), zh))

    def deal(b, q):
        if b == 0:
            got[b, q] = [start(src[q], chunk(b, q, r), to) for to in (to_x, to_y, to_c)]
        else:
            wz[q].wait_recv()
            got[b, q] = [start(chunk(b, q, r), chunk(b, q, r), to) for to in (to_x, to_y, to_c)]
        sib.append(got[b, q][2])

    def pass_on(b, q, n):
        piece = chunk(b, q, (rx, ry)[n])
        got[b, q][n].wait_recv()
        if n == q % 2:
            far[b, q] = start(piece, piece, (to_y, to_x)[n])
        sib.append(start(piece, piece, to_c))

    def corner(b, q):
        far[b, q].wait_recv()
        sib.append(start(chunk(b, q, rd), chunk(b, q, rd), to_c))

    def send_x():
        if len(x1) < FINE:
            p = len(x1)
            x1.append(start(x_ref.at[1 - h, toks(p)], xv.at[toks(p), cols(me)], zh))

    def pass_x(p):
        x1[p].wait_recv()
        x3.append(start(xv.at[toks(p), cols(zhp)], xv.at[toks(p), cols(zhp)], zl))

    x2 = {}

    def send_own(k):
        rows_k = pl.ds(k * 2 * step, 2 * step)
        x2[k] = start(x_ref.at[h, rows_k], xv.at[rows_k, cols(me)], zl)

    def thin_on(n):
        row = (rx, ry, rd)[n]
        thin_go[n].wait_recv()
        if n == 0:
            thin_go.append(start(thin_v.at[row], thin_v.at[row], to_y))
        sib_thin.append(start(thin_v.at[row], thin_v.at[row], to_c))

    def norm(p):
        if p % 2 == 0:
            x2[p // 2].wait_recv()
        x3[p].wait_recv()
        total = jnp.zeros((step, 1), F32)
        for b in range(4):
            value = xv[toks(p), b * feat : (b + 1) * feat].astype(F32)
            total = total + jnp.sum(value * value, axis=1, keepdims=True)
        root = lax.rsqrt(total / (4 * feat) + EPS)
        ir_ref[toks(p), :] = jnp.broadcast_to(root, (step, 128))
        for b in range(8):
            value = xv[toks(p), b * shard : (b + 1) * shard].astype(F32)
            gain = parv[b // 2, 8:9, b % 2 * shard : (b % 2 + 1) * shard]
            value = (value * root * gain).astype(BF16)
            nb_ref[toks(p), b * shard : (b + 1) * shard] = value
            nt_ref[b % 2, b // 2 * shard : (b // 2 + 1) * shard, toks(p)] = turned(value)

    prep_refs = (
        small_ref, segc_ref, segr_ref, bcp_ref, hp_ref,
        bc_ref, bct_ref, g_ref, gt_ref, colp_ref, cumt_ref, kexp_ref, lag_ref,
    )

    def narrow(p):
        lo, hi = p * (length // 2), (p + 1) * (length // 2)
        small_ref[lo:hi, :] = dot_nn(nb_ref[lo:hi, :], ws_ref[...])
        prep_rows(lo, hi, *prep_refs)

    def parameters():
        for copy in pars:
            copy.wait_recv()
        for n in range(3):
            if n != 1:
                keeps[n].wait()
        par_out[...] = parv[...]
        bcp_ref[...] = jnp.zeros_like(bcp_ref)
        bcp_ref[0:5, :] = sum(parv[b, 9:14, 0 : 2 * STATE] for b in range(4))
        hp_ref[...] = jnp.zeros_like(hp_ref)
        hp_ref[0:2, :] = parv[me, 14:16, 0:128] + pltpu.roll(parv[zhp, 14:16, 0:128], hb, 1)
        prep_lags(segc_ref, kexp_ref, lag_ref)

    def narrow_weights():
        for copy in sib_thin:
            copy.wait_recv()
        ws_ref[...] = jnp.zeros_like(ws_ref)
        for row in range(8):
            at = slice(row * shard, (row + 1) * shard)
            for b in range(4):
                ws_ref[at, b * bcn : (b + 1) * bcn] = thin_v[row, b, :, 0:bcn]
            ws_ref[at, 2 * STATE : 2 * STATE + hb] = thin_v[row, me, :, bcn : bcn + hb]
            ws_ref[at, 2 * STATE + hb : 2 * STATE + 2 * hb] = thin_v[row, zhp, :, bcn : bcn + hb]

    send_w(0)
    send_own(2)
    send_x()
    deal(0, 0)
    send_own(3)
    deal(0, 1)
    send_x()
    send_x()
    for k in range(2):
        keeps[3 + k].wait()
        laid[k].start()
    pass_on(0, 1, 1)
    keeps[1].wait()
    for copy in thins:
        copy.wait_recv()
    thin_go = [start(thin_v.at[r], thin_v.at[r], to) for to in (to_x, to_y, to_c)]
    sib_thin.append(thin_go.pop())
    parameters()
    send_w(1)
    send_own(1)
    thin_on(0)
    pass_on(0, 0, 0)
    pass_x(0)
    send_own(0)
    send_w(2)
    thin_on(1)
    send_x()
    thin_on(2)
    pass_x(1)
    pass_on(0, 0, 1)
    send_w(3)
    deal(1, 0)
    pass_on(1, 0, 0)
    corner(0, 1)
    pass_x(2)
    send_x()
    deal(1, 1)
    norm(0)
    pass_x(3)
    pass_on(1, 1, 1)
    deal(1, 2)
    pass_x(4)
    send_x()
    corner(0, 0)
    narrow_weights()
    deal(1, 3)
    corner(1, 0)
    norm(1)
    norm(2)
    send_x()
    norm(3)
    pass_x(5)
    pass_on(1, 3, 1)
    send_x()
    norm(4)
    corner(1, 1)
    narrow(0)
    pass_x(6)
    pass_on(1, 2, 1)
    pass_on(1, 3, 0)
    pass_on(1, 1, 0)
    pass_on(1, 2, 0)
    norm(5)
    pass_on(0, 1, 0)
    pass_on(1, 0, 1)
    pass_x(7)
    corner(1, 2)
    norm(6)
    corner(1, 3)
    norm(7)
    narrow(1)
    for copy in sib:
        copy.wait_recv()
    for move in laid:
        move.wait()
    copies.finish()


def gather_all(x, wg, wx, thin, par, segc, segr, groups):
    _, length, feat = x.shape
    shard, cb = wg.shape
    anywhere = pl.BlockSpec(memory_space=pl.ANY)
    inside = pl.BlockSpec(memory_space=pltpu.VMEM)
    weight = jax.ShapeDtypeStruct((2, 8 * shard, cb), BF16)
    return pl.pallas_call(
        gather_kernel,
        in_specs=[anywhere] * 5 + [inside] * 2,
        out_specs=[inside] * 16 + [anywhere] * 2,
        out_shape=(
            jax.ShapeDtypeStruct((length, 4 * feat), BF16),
            jax.ShapeDtypeStruct((2, 4 * shard, length), BF16),
            jax.ShapeDtypeStruct((length, 128), F32),
            jax.ShapeDtypeStruct((4,) + par.shape, F32),
            jax.ShapeDtypeStruct((8 * shard, 2 * STATE + 128), BF16),
            jax.ShapeDtypeStruct((length, 2 * STATE + 128), F32),
            jax.ShapeDtypeStruct((8, 128), F32),
            jax.ShapeDtypeStruct((8, 2 * STATE), F32),
        )
        + prep_shapes(length, groups)
        + (weight, weight),
        scratch_shapes=[
            pltpu.VMEM((length, 4 * feat), BF16),
            pltpu.VMEM((4,) + par.shape, F32),
            pltpu.VMEM((8, 4) + thin.shape, BF16),
            pltpu.VMEM((2, shard, cb), BF16),
            pltpu.SemaphoreType.DMA((GATHER_COPIES,)),
            pltpu.SemaphoreType.DMA((GATHER_COPIES,)),
            pltpu.SemaphoreType.DMA((8,)),
        ],
        compiler_params=pltpu.CompilerParams(
            collective_id=0, has_side_effects=True, vmem_limit_bytes=VMEM_LIMIT
        ),
        name="gather_all",
    )(x, wg, wx, thin, par, segc, segr)


GRAD_COPIES = 96
HALVES = 2


def grad_kernel(
    raw_ref, wg_ref, wx_ref, ws_ref, nb_ref, gate_ref, nt_ref, dg_ref, dx_ref, ds_ref, small_ref, nd_ref, ir_ref,
    gz_ref, thin_out, small_out, own_out, away_out, row_out,
    raw_v, dn_v, wt, wst, nbt, ggv, tile_sem, pr, rowv, rowr, local, cs, cr, ts, tr, fs, fr, ss, sr, zs, zr, tfs, tfr, tss, tsr, tz, tzr,
    sbuf, srecv, szr, send, recv,
):
    h, l, r, c, x, y, rx, ry, rc = places()
    me = h * 2 + l
    zh, zl, zd = {"zh": 1 - h}, {"zl": 1 - l}, {"zh": 1 - h, "zl": 1 - l}
    to_x, to_y, to_c = {"row": rx}, {"row": ry}, {"row": rc}
    shard = gz_ref.shape[1]
    ncol = gz_ref.shape[2]
    meet((zh, zl, zd, to_x, to_y, to_c))
    copies = Copies(send, recv)
    start = copies.start

    def product(side, d_ref, at):
        return dot_nn(nt_ref[side], d_ref[:, at])

    def tiles(d_ref, body):
        width = d_ref.shape[1]
        wide = 256 if width % 256 == 0 else 128

        def one(n, carry):
            body(pl.ds(pl.multiple_of(n * wide, wide), wide))
            return carry

        lax.fori_loop(0, width // wide, one, 0)

    _, length, feat = dn_v.shape
    piece = length // HALVES
    strips = 4 * feat // 256

    def toks(p):
        return pl.ds(p * piece, piece)

    raw_copy = pltpu.make_async_copy(raw_ref.at[1], raw_v, local.at[0])
    raw_copy.start()

    def loads(k, slot):
        strip = pl.ds(pl.multiple_of(lax.rem(k, strips) * 256, 256), 256)
        rows = pl.ds(pl.multiple_of(k // strips * piece, piece), piece)
        return [
            pltpu.make_async_copy(wg_ref.at[:, strip], wt.at[slot, 0], tile_sem.at[slot, 0]),
            pltpu.make_async_copy(wx_ref.at[:, strip], wt.at[slot, 1], tile_sem.at[slot, 1]),
            pltpu.make_async_copy(ws_ref.at[strip], wst.at[slot], tile_sem.at[slot, 2]),
            pltpu.make_async_copy(nb_ref.at[rows, strip], nbt.at[slot], tile_sem.at[slot, 3]),
        ]

    for move in loads(0, 0):
        move.start()
    ggv[...] = jnp.zeros_like(ggv)
    pair, far, kept = [], [], []

    def back(p):
        def strip(n, carry):
            k = p * strips + n
            slot = lax.rem(k, 2)
            for move in loads(k, slot):
                move.wait()

            @pl.when(k + 1 < HALVES * strips)
            def _():
                for move in loads(k + 1, 1 - slot):
                    move.start()

            value = dot_nt(ds_ref[toks(p), :], wst[slot])
            for m, d_ref in enumerate((dg_ref, dx_ref)):
                for b in range(2):
                    value = value + dot_nt(d_ref[toks(p), b * ncol : (b + 1) * ncol], wt[slot, m, b])
            lanes = pl.ds(pl.multiple_of(lax.rem(n, feat // 256) * 256, 256), 256)
            dn_v[n // (feat // 256), toks(p), lanes] = value.astype(BF16)
            ggv[pl.ds(n, 1), :] += jnp.sum(value * nbt[slot].astype(F32), axis=0, keepdims=True)
            return carry

        lax.fori_loop(0, strips, strip, 0)
        pair.append([start(dn_v.at[2 * k + 1 - l, toks(p)], pr.at[k, toks(p)], zl) for k in range(2)])

    def pair_done(p):
        for move in pair[p]:
            move.wait_recv()
        away, own = 2 * (1 - h) + l, 2 * h + l
        value = dn_v[away, toks(p)].astype(F32) + pr[1 - h, toks(p)].astype(F32)
        dn_v[away, toks(p)] = value.astype(BF16)
        far.append(start(dn_v.at[away, toks(p)], away_out.at[toks(p)], zh))
        value = dn_v[own, toks(p)].astype(F32) + pr[h, toks(p)].astype(F32)
        dn_v[own, toks(p)] = value.astype(BF16)
        kept.append(pltpu.make_async_copy(dn_v.at[own, toks(p)], own_out.at[toks(p)], local.at[1 + p]))
        kept[p].start()

    z_copy = [start(gate_ref, zr.at[0], zh), None]
    rowv[...] = jnp.zeros_like(rowv)
    rowv[0:1, :] = jnp.sum(jnp.transpose(nd_ref[...]), axis=0, keepdims=True)
    rowv[1:2, :] = jnp.transpose(ir_ref[...])[0:1, :]
    row_copies = [start(rowv, rowr.at[n], to) for n, to in enumerate((zh, zl, zd))]

    def begin_small():
        sbuf[0] = small_ref[...]
        for n in range(strips):
            row, lanes = n // 4, slice(n % 4 * 256, n % 4 * 256 + 256)
            sbuf[0, 16 + row : 17 + row, lanes] = ggv[n : n + 1, :] / small_ref[20 + row : 21 + row, lanes]
        return start(sbuf.at[0], srecv.at[0], to_c)

    dx0, dx1 = dx_ref.at[:, 0:ncol], dx_ref.at[:, ncol : 2 * ncol]
    quarters = [
        dict(d=dx1, first=to_x, second=to_y, mine=x, along=y, swap=False),
        dict(d=dx0, first=to_y, second=to_x, mine=y, along=x, swap=True),
        dict(first=to_y, second=to_x, mine=y, along=x, swap=True),
    ]

    def spot(q, first, second):
        return 2 * first + second if q["swap"] else 2 * second + first

    def refs(i):
        if i == 4:
            return ts, tr, tfs, tfr, tss, tsr
        return cs, cr.at[i], fs.at[i // 2], fr.at[i], ss.at[i], sr.at[i]

    thin_q = dict(d=ds_ref, first=to_y, second=to_x, mine=y, along=x, swap=True)

    def gone(i, name):
        if i == 1:
            earlier = quarters[0][name]
            earlier.wait_send()
            copies.open = [move for move in copies.open if move is not earlier]

    def first_done(q):
        if "seen" not in q:
            q["f"].wait_recv()
            q["seen"] = True

    def to_core(i, q):
        out, back = refs(i)[0:2]
        if i == 2:
            q["core"] = start(raw_ref.at[0], back, to_c)
            return
        gone(i, "core")

        def body(at):
            value = product(1 - c, q["d"], at).astype(BF16)
            for j in range(4):
                out[j, :, at] = value[j * shard : (j + 1) * shard]

        tiles(q["d"], body)
        q["core"] = start(out, back, to_c)

    def to_first(i, q, after=None):
        _, back, fsend, frecv, _, _ = refs(i)
        q["core"].wait_recv()
        if i == 2:
            raw_copy.wait()
            for j in range(4):
                back[j] = (raw_v[j].astype(F32) + back[j].astype(F32)).astype(BF16)
        else:

            def body(at):
                value = product(c, q["d"], at)
                for j in range(4):
                    part = value[j * shard : (j + 1) * shard] + back[j, :, at].astype(F32)
                    back[j, :, at] = part.astype(BF16)

            tiles(q["d"], body)
        gone(i, "f")
        for n in range(2):
            fsend[n] = back[spot(q, 1 - q["mine"], n)]
        if after is not None:
            first_done(after)
        q["f"] = start(fsend, frecv, q["first"])

    def to_second(i, q):
        _, back, _, frecv, ssend, srcv = refs(i)
        first_done(q)
        far = 1 - q["along"]
        kept = back[spot(q, q["mine"], far)].astype(F32)
        ssend[...] = (kept + frecv[far].astype(F32)).astype(BF16)
        q["s"] = start(ssend, srcv, q["second"])

    def settle(i, q):
        _, back, _, frecv, _, srcv = refs(i)
        q["s"].wait_recv()
        near = q["along"]
        kept = back[spot(q, q["mine"], near)].astype(F32)
        return kept + frecv[near].astype(F32) + srcv[...].astype(F32)

    def hop_small(n, to):
        small_copy[0].wait_recv()
        sbuf[n] = sbuf[n - 1] + srecv[n - 1]
        if to is not None:
            small_copy[0] = start(sbuf.at[n], srecv.at[n], to)

    to_core(2, quarters[2])
    back(0)
    to_core(0, quarters[0])
    to_first(2, quarters[2])
    to_first(0, quarters[0])
    back(1)
    pair_done(0)
    to_core(1, quarters[1])
    to_second(0, quarters[0])
    to_core(4, thin_q)
    small_copy = [begin_small()]
    zs[...] = settle(0, quarters[0]).astype(BF16)
    z_copy[1] = start(zs, zr.at[1], zh)
    to_first(4, thin_q)
    hop_small(1, to_x)
    to_second(2, quarters[2])
    to_first(1, quarters[1])
    to_second(4, thin_q)
    tz[...] = settle(4, thin_q).astype(BF16)
    thin_z = []
    for n, (to, block) in enumerate(((zh, 2 * (1 - h) + l), (zl, 2 * h + 1 - l), (zd, 2 * (1 - h) + 1 - l))):
        lanes = pl.ds(pl.multiple_of(block // 2 * 128, 128), 128)
        thin_z.append(start(tz.at[:, lanes], tzr.at[n], to))
    thin_z.append(start(tz.at[:, 2 * STATE :], tzr.at[3], zh))
    hop_small(2, to_y)
    pair_done(1)
    hop_small(3, None)
    small_z = [
        start(sbuf.at[3, lo:], szr.at[n, lo:], to) for n, (to, lo) in enumerate(((zh, 8), (zl, 16), (zd, 16)))
    ]
    to_second(1, quarters[1])
    gz_ref[0] = settle(2, quarters[2])
    gz_ref[1] = settle(1, quarters[1])
    row_out[0] = rowv[...]
    for n in range(3):
        row_copies[n].wait_recv()
        row_out[n + 1] = rowr[n]
    for copy in thin_z:
        copy.wait_recv()
    for copy in small_z:
        copy.wait_recv()
    total = tz[:, pl.ds(pl.multiple_of(h * 128, 128), 128)].astype(F32)
    for n in range(3):
        total = total + tzr[n].astype(F32)
    thin_out[:, 0:128] = total
    thin_out[:, 128:256] = tz[:, 2 * STATE :].astype(F32)
    thin_out[:, 256:384] = tzr[3].astype(F32)
    small_out[...] = jnp.zeros_like(small_out)
    small_out[0] = sbuf[3]
    for n, lo in enumerate((8, 16, 16)):
        small_out[n + 1, lo:] = szr[n, lo:]
    for move in far:
        move.wait_recv()
    for move in kept:
        move.wait()
    for k in range(2):
        z_copy[k].wait_recv()
        gz_ref[k] += zr[k].astype(F32)
    copies.finish()


def grad_all(raw, wg, wx, ws, nb, gate_got, nt, dgate, dxr, d_small, small, nd, ir):
    _, half, length = nt.shape
    feat = half // 2
    shard, cb = half // 4, dxr.shape[1] // 2
    ns = d_small.shape[1]
    inside = pl.BlockSpec(memory_space=pltpu.VMEM)
    anywhere = pl.BlockSpec(memory_space=pl.ANY)
    V = pltpu.VMEM
    return pl.pallas_call(
        grad_kernel,
        in_specs=[anywhere] * 6 + [inside] * 7,
        out_specs=[inside] * 3 + [anywhere, anywhere, inside],
        out_shape=(
            jax.ShapeDtypeStruct((2, shard, cb), F32),
            jax.ShapeDtypeStruct((shard, 384), F32),
            jax.ShapeDtypeStruct((4,) + small.shape, F32),
            jax.ShapeDtypeStruct((length, feat), BF16),
            jax.ShapeDtypeStruct((length, feat), BF16),
            jax.ShapeDtypeStruct((4, 8, length), F32),
        ),
        scratch_shapes=[
            V((4, shard, cb), BF16),
            V((4, length, feat), BF16),
            V((2, 2, 2, 256, cb), BF16),
            V((2, 256, ns), BF16),
            V((2, length // HALVES, 256), BF16),
            V((4 * feat // 256, 256), F32),
            pltpu.SemaphoreType.DMA((2, 4)),
            V((2, length, feat), BF16),
            V((8, length), F32),
            V((3, 8, length), F32),
            pltpu.SemaphoreType.DMA((1 + HALVES,)),
            V((4, shard, cb), BF16),
            V((3, 4, shard, cb), BF16),
            V((4, shard, ns), BF16),
            V((4, shard, ns), BF16),
            V((2, 2, shard, cb), BF16),
            V((3, 2, shard, cb), BF16),
            V((3, shard, cb), BF16),
            V((3, shard, cb), BF16),
            V((shard, cb), BF16),
            V((2, shard, cb), BF16),
            V((2, shard, ns), BF16),
            V((2, shard, ns), BF16),
            V((shard, ns), BF16),
            V((shard, ns), BF16),
            V((shard, ns), BF16),
            V((4, shard, 128), BF16),
            V((4,) + small.shape, F32),
            V((3,) + small.shape, F32),
            V((3,) + small.shape, F32),
            pltpu.SemaphoreType.DMA((GRAD_COPIES,)),
            pltpu.SemaphoreType.DMA((GRAD_COPIES,)),
        ],
        compiler_params=pltpu.CompilerParams(
            collective_id=1, has_side_effects=True, vmem_limit_bytes=VMEM_LIMIT
        ),
        name="grad_all",
    )(raw, wg, wx, ws, nb, gate_got, nt, dgate, dxr, d_small, small, nd, ir)


def table(send, recv):
    def copy(n, src, dst, to):
        return pltpu.make_async_remote_copy(
            src_ref=src, dst_ref=dst, send_sem=send.at[n], recv_sem=recv.at[n],
            device_id=to, device_id_type=MESH_ID,
        )

    return copy


SCAN_COPIES = 32


def scan_all_kernel(*refs):
    (cot_ref, out_ref, gains_ref), refs = refs[0:3], refs[3:]
    ins, refs = refs[0:11], refs[11:]
    gate_ref, xr_ref, y_ref, hid_ref, sq_ref, st_ref, po_ref, ir_ref, cf_ref, wo_ref = refs[0:10]
    state, cot_v, out_v, rows_v, sums, other, send, recv, local, row_sem = refs[10:]
    h, l, r, c, x, y, rx, ry, rc = places()
    rd = rx + ry - r
    me, zhp = h * 2 + l, (1 - h) * 2 + l
    zh, zl = {"zh": 1 - h}, {"zl": 1 - l}
    to_x, to_y, to_c = {"row": rx}, {"row": ry}, {"row": rc}
    length, feat = cot_ref.shape[1], cot_ref.shape[2]
    piece = length // PIECES
    shard = out_ref.shape[0]
    copy = table(send, recv)
    step = pl.program_id(0)
    channels = hid_ref.shape[1]
    groups = channels // GROUP

    def toks(p):
        return pl.ds(p * piece, piece)

    def cols(block):
        return pl.ds(pl.multiple_of(block * feat, feat), feat)

    def rows(row, half=None):
        if half is None:
            return pl.ds(pl.multiple_of(row * shard, shard), shard)
        return pl.ds(pl.multiple_of(row * shard + half * (shard // 2), shard // 2), shard // 2)

    def g1(p):
        return copy(p, cot_ref.at[1 - h, toks(p)], cf_ref.at[toks(p), cols(me)], zh)

    def g2():
        return copy(4, cot_ref.at[h], cf_ref.at[:, cols(me)], zl)

    def g3(p):
        part = cf_ref.at[toks(p), cols(zhp)]
        return copy(8 + p, part, part, zl)

    def wz():
        return copy(12, out_ref, wo_ref.at[1, rows(r)], zh)

    def own(n):
        return copy(13 + n, out_ref, wo_ref.at[0, rows(r)], (to_x, to_y, to_c)[n])

    def got(n):
        part = wo_ref.at[1, rows(r)]
        return copy(16 + n, part, part, (to_x, to_y, to_c)[n])

    def diag(b, n):
        part = wo_ref.at[b, rows((rx, ry)[n], n)]
        return copy(19 + 5 * b + n, part, part, (to_y, to_x)[n])

    def sib(b, n):
        part = wo_ref.at[b, rows((rx, ry, rd)[n])]
        return copy(21 + 5 * b + n, part, part, to_c)

    def load(n):
        return pltpu.make_async_copy((cot_ref.at[h], out_ref)[n], (cot_v, out_v)[n], local.at[n])

    def keep(n):
        to = (cf_ref.at[:, cols(me)], wo_ref.at[0, rows(r)])[n]
        return pltpu.make_async_copy((cot_v, out_v)[n], to, local.at[2 + n])

    def load_rows(n, slot):
        part = pl.ds(pl.multiple_of(n * 256, 256), 256)
        return pltpu.make_async_copy(wo_ref.at[:, part], rows_v.at[slot], row_sem.at[slot])

    def onward(p):
        g1(p).wait_recv()
        g3(p).start()

    def step0():
        meet((zh, zl, to_x, to_y, to_c))
        wz().start()
        for n in range(2):
            load(n).start()
        for n in range(3):
            own(n).start()
        g2().start()

    def step1():
        for n in range(2):
            load(n).wait()
            keep(n).start()

    def step2():
        g1(0).start()
        for n in range(2):
            own(n).wait_recv()
        for n in range(2):
            diag(0, n).start()
            sib(0, n).start()

    def step3():
        g1(1).start()
        wz().wait_recv()
        for n in range(3):
            got(n).start()

    def step4():
        g1(2).start()
        g1(3).start()
        for n in range(2):
            diag(0, n).wait_recv()
        sib(0, 2).start()

    def step5():
        for n in range(2):
            got(n).wait_recv()
        for n in range(2):
            diag(1, n).start()
            sib(1, n).start()

    def step6():
        for n in range(2):
            diag(1, n).wait_recv()
        sib(1, 2).start()
        onward(0)

    def step8():
        onward(1)

    def step9():
        onward(2)

    def step10():
        onward(3)

    acts = {
        0: step0, 1: step1, 2: step2, 3: step3, 4: step4, 5: step5, 6: step6, 8: step8, 9: step9, 10: step10,
    }
    for at, act in acts.items():
        pl.when(step == at)(act)

    @pl.when(step < groups)
    def _():
        part = hid_ref.at[:, pl.ds(pl.multiple_of(step * GROUP, GROUP), GROUP)]
        scan_kernel(*ins, gate_ref, xr_ref, y_ref, part, sq_ref, st_ref, state)

    def swap_sums():
        return copy(29, sums, other, zl)

    @pl.when(step == groups)
    def _():
        sums[...] = jnp.zeros_like(sums)
        sums[0:1, :] = jnp.sum(jnp.transpose(sq_ref[...]), axis=0, keepdims=True)
        swap_sums().start()
        keep(1).wait()
        for move in [own(2), got(2)] + [sib(b, n) for b in range(2) for n in range(3)]:
            move.wait_recv()
        load_rows(0, 0).start()
        swap_sums().wait()
        root = lax.rsqrt((sums[0:1, :] + other[0:1, :]) / (2 * channels) + EPS)
        ir_ref[...] = jnp.transpose(jnp.broadcast_to(root, (128, length)))
        for n in range(groups):
            part = slice(n * GROUP, (n + 1) * GROUP)
            value = hid_ref[:, part].astype(F32) * twice(ir_ref[...]) * gains_ref[6:7, part]
            hid_ref[:, part] = value.astype(BF16)

    @pl.when(step >= groups)
    def _():
        n = step - groups
        slot = lax.rem(n, 2)
        load_rows(n, slot).wait()

        @pl.when(step < 2 * groups - 1)
        def _():
            load_rows(n + 1, 1 - slot).start()

        half = channels // 2
        out = dot_nt(hid_ref[:, 0:half], rows_v[slot, 0]) + dot_nt(hid_ref[:, half:], rows_v[slot, 1])
        po_ref[0] = out.astype(BF16)

    @pl.when(step == 2 * groups - 1)
    def _():
        late = [g2()] + [g3(p) for p in range(PIECES)]
        for move in late:
            move.wait_recv()
        keep(0).wait()
        sent = [g1(p) for p in range(PIECES)] + late + [wz()]
        sent += [own(n) for n in range(3)] + [got(n) for n in range(3)]
        sent += [diag(b, n) for b in range(2) for n in range(2)]
        sent += [sib(b, n) for b in range(2) for n in range(3)]
        for move in sent:
            move.wait_send()


def scan_all(cot, out_proj, nb, wg, wx, chan, *rest):
    length, width = nb.shape
    channels = chan.shape[1]
    cb = channels // 2
    feat, shard = width // 4, out_proj.shape[0]
    groups = channels // GROUP
    per = feat // 256
    assert groups == 8 and width // 256 == groups
    in_specs, out_specs = scan_specs(length, width, cb // GROUP)
    out_specs[3] = once((length, channels))
    anywhere = pl.BlockSpec(memory_space=pl.ANY)
    shapes = scan_shapes(length, channels)

    def strip(g):
        n = jnp.maximum(g - groups, 0)
        return n // per, 0, n % per

    return pl.pallas_call(
        scan_all_kernel,
        grid=(2 * groups,),
        in_specs=[anywhere] * 2 + [once((8, channels))] + in_specs,
        out_specs=out_specs
        + [pl.BlockSpec((1, length, 256), strip), once((length, 128)), anywhere, anywhere],
        out_shape=shapes
        + (
            jax.ShapeDtypeStruct((4, length, feat), BF16),
            jax.ShapeDtypeStruct((length, 128), F32),
            jax.ShapeDtypeStruct((length, width), BF16),
            jax.ShapeDtypeStruct((2, width, cb), BF16),
        ),
        scratch_shapes=[
            pltpu.VMEM((STATE, GROUP), F32),
            pltpu.VMEM((length, feat), BF16),
            pltpu.VMEM((shard, cb), BF16),
            pltpu.VMEM((2, 2, 256, cb), BF16),
            pltpu.VMEM((8, length), F32),
            pltpu.VMEM((8, length), F32),
            pltpu.SemaphoreType.DMA((SCAN_COPIES,)),
            pltpu.SemaphoreType.DMA((SCAN_COPIES,)),
            pltpu.SemaphoreType.DMA((4,)),
            pltpu.SemaphoreType.DMA((2,)),
        ],
        compiler_params=pltpu.CompilerParams(
            collective_id=2, has_side_effects=True, vmem_limit_bytes=VMEM_LIMIT
        ),
        name="scan_all",
    )(cot, out_proj, chan, nb, wg, wx, chan, *rest)


EARLY = 640


def mid_kernel(
    cf_ref, wc_ref, hid_ref, ir_ref, po_ref,
    dh_ref, go_ref, coef_ref, sum_out,
    ct, dots, sums, other, send, recv,
):
    phase, g = pl.program_id(0), pl.program_id(1)
    last = pl.num_programs(1) - 1
    length, channels = hid_ref.shape
    shard = go_ref.shape[1]
    h, l = lax.axis_index("zh"), lax.axis_index("zl")
    to, zd = {"zl": 1 - l}, {"zh": 1 - h, "zl": 1 - l}
    copy = table(send, recv)
    at = pl.ds(pl.multiple_of(g * GROUP, GROUP), GROUP)

    def part():
        return copy(1, po_ref.at[2 * (1 - h) + 1 - l, pl.ds(0, EARLY)], sum_out, zd)

    @pl.when((phase == 0) & (g == 0))
    def _():
        meet((to, zd))
        part().start()
        dots[...] = jnp.zeros_like(dots)

    @pl.when(phase == 0)
    def _():
        dh = dot_nn(cf_ref[...], wc_ref[...])
        dh_ref[...] = dh.astype(BF16)
        term = dh * hid_ref[:, at].astype(F32)
        dots[...] += term[:, 0:128] + term[:, 128:256]
        ct[at, :] = turned(cf_ref[:, at])

    @pl.when((phase == 0) & (g == last))
    def _():
        sums[...] = jnp.zeros_like(sums)
        sums[0:1, :] = jnp.sum(jnp.transpose(dots[...]), axis=0, keepdims=True)
        move = copy(0, sums, other, to)
        move.start()
        move.wait()
        both = jnp.broadcast_to(sums[0:1, :] + other[0:1, :], (128, length))
        coef_ref[...] = jnp.transpose(both) * ir_ref[...] * ir_ref[...] / (2 * channels)

    @pl.when(phase == 1)
    def _():
        right = hid_ref[:, at]
        for n in range(go_ref.shape[0] // 4):
            value = dot_nn(ct[4 * n * shard : 4 * (n + 1) * shard, :], right).astype(BF16)
            for m in range(4):
                go_ref[4 * n + m] = value[m * shard : (m + 1) * shard]

    @pl.when((phase == 1) & (g == last))
    def _():
        part().wait()


def middle(cf, wo, hid, ir, po):
    length, width = cf.shape
    channels = hid.shape[1]
    gb = channels // 2 // GROUP
    n = channels // GROUP
    shard = width // 8
    assert n == width // 256

    def const(shape):
        return pl.BlockSpec(shape, lambda p, g: (0,) * len(shape), pipeline_mode=pl.Buffered(1))

    def first(p, g):
        return jnp.where(p == 0, g, n - 1)

    return pl.pallas_call(
        mid_kernel,
        grid=(2, n),
        in_specs=[
            const((length, width)),
            pl.BlockSpec((None, width, GROUP), lambda p, g: (first(p, g) // gb, 0, first(p, g) % gb)),
            const((length, channels)),
            const((length, 128)),
            pl.BlockSpec(memory_space=pl.ANY),
        ],
        out_specs=[
            pl.BlockSpec((length, GROUP), lambda p, g: (0, first(p, g))),
            pl.BlockSpec((8, shard, GROUP), lambda p, g: (0, 0, g * p)),
            const((length, 128)),
            pl.BlockSpec(memory_space=pl.ANY),
        ],
        out_shape=(
            jax.ShapeDtypeStruct((length, channels), BF16),
            jax.ShapeDtypeStruct((8, shard, channels), BF16),
            jax.ShapeDtypeStruct((length, 128), F32),
            jax.ShapeDtypeStruct((EARLY, po.shape[2]), BF16),
        ),
        scratch_shapes=[
            pltpu.VMEM((width, length), BF16),
            pltpu.VMEM((length, 128), F32),
            pltpu.VMEM((8, length), F32),
            pltpu.VMEM((8, length), F32),
            pltpu.SemaphoreType.DMA((2,)),
            pltpu.SemaphoreType.DMA((2,)),
        ],
        compiler_params=pltpu.CompilerParams(
            collective_id=3, has_side_effects=True, vmem_limit_bytes=VMEM_LIMIT
        ),
        name="middle",
    )(cf, wo, hid, ir, po)


SHIP_COPIES = 24


def scan_grad_all_kernel(*refs):
    (go_ref, po_ref, nt_ref), refs = refs[0:3], refs[3:]
    ins, refs = refs[0:20], refs[20:]
    outs, refs = refs[0:6], refs[6:]
    own_out, raw_out, gate_out, sum0, sum1, sum2 = refs[0:6]
    scratch, refs = refs[6:14], refs[14:]
    gm, gr, gf, gfr, gs, gsr, gz, gzr, tm, ts, tr, tf, tfr, tg, tgr, send, recv, local = refs
    h, l, _, c, x, y, rx, ry, rc = places()
    zh, zl, zd = {"zh": 1 - h}, {"zl": 1 - l}, {"zh": 1 - h, "zl": 1 - l}
    to_x, to_y, to_c = {"row": rx}, {"row": ry}, {"row": rc}
    shard, cb = own_out.shape
    copy = table(send, recv)
    step = pl.program_id(0)
    groups = pl.num_programs(0)
    first, second = (to_x, to_y), (to_y, to_x)
    mine, along = (x, y), (y, x)
    dgate_ref = outs[0]

    def near(b, j):
        lanes = slice(b * cb, (b + 1) * cb)
        return pltpu.make_async_copy(go_ref.at[2 * j + c, :, lanes], gm.at[b, j], local.at[4 * b + j])

    def core(b, j):
        lanes = slice(b * cb, (b + 1) * cb)
        return copy(4 * b + j, go_ref.at[2 * j + 1 - c, :, lanes], gr.at[b, j], to_c)

    def hop1(b):
        return copy(8 + b, gf.at[b], gfr.at[b], first[b])

    def hop2(b):
        return copy(10 + b, gs.at[b], gsr.at[b], second[b])

    def hop3():
        return copy(18, gz, gzr, zh)

    def settle(b):
        hop2(b).wait_recv()
        own = along[b]
        return add(gm[b, spot(b, mine[b], own)], gfr[b, own]) + gsr[b].astype(F32)

    def out_sums():
        late = pl.ds(EARLY, po_ref.shape[1] - EARLY)
        return [
            copy(12, po_ref.at[2 * h + 1 - l], sum0, zl),
            copy(13, po_ref.at[2 * (1 - h) + l], sum1, zh),
            copy(14, po_ref.at[2 * (1 - h) + 1 - l, late], sum2, zd),
        ]

    def gate_core():
        return copy(15, ts, tr, to_c)

    def gate_hop1():
        return copy(16, tf, tfr, to_y)

    def gate_hop2():
        return copy(17, tg, tgr, to_x)

    def spot(b, at_first, at_second):
        return 2 * at_first + at_second if b else 2 * at_second + at_first

    def add(a, b):
        return a.astype(F32) + b.astype(F32)

    @pl.when(step == 0)
    def _():
        meet((zh, zl, zd, to_x, to_y, to_c))
        for b in range(2):
            for j in range(4):
                core(b, j).start()
                near(b, j).start()
        for move in out_sums():
            move.start()

    @pl.when(step == 1)
    def _():
        for b in range(2):
            for j in range(4):
                near(b, j).wait()
                core(b, j).wait_recv()
            for s in range(2):
                j = spot(b, 1 - mine[b], s)
                gf[b, s] = add(gm[b, j], gr[b, j]).astype(BF16)
            hop1(b).start()
            for s in range(2):
                j = spot(b, mine[b], s)
                gm[b, j] = add(gm[b, j], gr[b, j]).astype(BF16)

    @pl.when(step == 4)
    def _():
        for b in range(2):
            hop1(b).wait_recv()
            far = 1 - along[b]
            gs[b] = add(gm[b, spot(b, mine[b], far)], gfr[b, far]).astype(BF16)
            hop2(b).start()

    @pl.when(step == 5)
    def _():
        gate_core().wait_recv()
        for n in range(2):
            tf[n] = add(tm[spot(1, 1 - y, n)], tr[spot(1, 1 - y, n)]).astype(BF16)
        gate_hop1().start()
        for n in range(2):
            tm[spot(1, y, n)] = add(tm[spot(1, y, n)], tr[spot(1, y, n)]).astype(BF16)

    @pl.when(step == 6)
    def _():
        gz[...] = settle(1).astype(BF16)
        hop3().start()

    @pl.when(step == groups - 1)
    def _():
        gate_hop1().wait_recv()
        tg[...] = add(tm[spot(1, y, 1 - x)], tfr[1 - x]).astype(BF16)
        gate_hop2().start()

    scan_grad_kernel(lax.rem(step + groups // 2, groups), *ins, *outs, *scratch)

    def products(other, own):
        for side, ref in ((1 - c, other), (c, own)):
            value = dot_nn(nt_ref[side], dgate_ref[...]).astype(BF16)
            for j in range(4):
                ref[j] = value[j * shard : (j + 1) * shard]

    @pl.when(step < groups // 2)
    def _():
        lanes = pl.ds(pl.multiple_of(step * GROUP, GROUP), GROUP)
        products(ts.at[:, :, lanes], tm.at[:, :, lanes])

    @pl.when(step == groups // 2 - 1)
    def _():
        gate_core().start()

    @pl.when(step >= groups // 2)
    def _():
        products(raw_out.at[0], raw_out.at[1])

    @pl.when(step == groups - 1)
    def _():
        own_out[...] = settle(0)
        hop3().wait_recv()
        own_out[...] += gzr[...].astype(F32)
        gate_hop2().wait_recv()
        total = add(tm[spot(1, y, x)], tfr[x]) + tgr[...].astype(F32)
        gate_out[...] = total.astype(BF16)
        for b in range(2):
            for j in range(4):
                core(b, j).wait_send()
            hop1(b).wait_send()
            hop2(b).wait_send()
        for move in (gate_core(), gate_hop1(), gate_hop2(), hop3()):
            move.wait_send()
        for move in out_sums():
            move.wait()


def scan_grad_all(go, po, nt, *args):
    length, channels = args[0].shape
    groups = channels // GROUP
    ins, outs, shapes, scratch = scan_grad_specs(length, channels, groups // 2)
    _, shard, _ = go.shape
    feat = po.shape[2]
    cb = channels // 2
    anywhere = pl.BlockSpec(memory_space=pl.ANY)
    V = pltpu.VMEM
    return pl.pallas_call(
        scan_grad_all_kernel,
        grid=(groups,),
        in_specs=[anywhere, anywhere, once(nt.shape)] + ins,
        out_specs=outs
        + [
            once((shard, cb)),
            pl.BlockSpec((2, 4, shard, GROUP), lambda g: (0, 0, 0, jnp.maximum(g - groups // 2, 0))),
            once((shard, cb)),
            anywhere,
            anywhere,
            anywhere,
        ],
        out_shape=shapes
        + (
            jax.ShapeDtypeStruct((shard, cb), F32),
            jax.ShapeDtypeStruct((2, 4, shard, cb), BF16),
            jax.ShapeDtypeStruct((shard, cb), BF16),
            jax.ShapeDtypeStruct((length, feat), BF16),
            jax.ShapeDtypeStruct((length, feat), BF16),
            jax.ShapeDtypeStruct((length - EARLY, feat), BF16),
        ),
        scratch_shapes=scratch
        + [
            V((2, 4, shard, cb), BF16),
            V((2, 4, shard, cb), BF16),
            V((2, 2, shard, cb), BF16),
            V((2, 2, shard, cb), BF16),
            V((2, shard, cb), BF16),
            V((2, shard, cb), BF16),
            V((shard, cb), BF16),
            V((shard, cb), BF16),
            V((4, shard, cb), BF16),
            V((4, shard, cb), BF16),
            V((4, shard, cb), BF16),
            V((2, shard, cb), BF16),
            V((2, shard, cb), BF16),
            V((shard, cb), BF16),
            V((shard, cb), BF16),
            pltpu.SemaphoreType.DMA((SHIP_COPIES,)),
            pltpu.SemaphoreType.DMA((SHIP_COPIES,)),
            pltpu.SemaphoreType.DMA((8,)),
        ],
        compiler_params=pltpu.CompilerParams(
            collective_id=4, has_side_effects=True, vmem_limit_bytes=VMEM_LIMIT
        ),
        name="scan_grad_all",
    )(go, po, nt, *args)


def build(nrow, nl):
    direct = nrow == 8 and nl == 2
    col = ("zh", "zl")

    def swap(v):
        return lax.ppermute(v, "zh", [(0, 1), (1, 0)])

    def pair_sum(v):
        return lax.psum(v, "zl")

    def row_gather(v):
        return lax.all_gather(v, "row", axis=0, tiled=True)

    def row_scatter(v):
        return lax.psum_scatter(v, "row", scatter_dimension=0, tiled=True)

    def per_device(
        tokens, segment_ids, norm_gain, in_zx, in_dt, in_bc, conv_x, conv_x_bias, conv_bc,
        conv_bc_bias, dt_bias, a_log, d_skip, inner_gain, out_proj, cotangent,
    ):
        seq_count, length = segment_ids.shape
        assert seq_count == 2
        feat = tokens.shape[1]
        width = feat * 2 * nl
        cb = inner_gain.shape[0]
        hb = dt_bias.shape[0]
        inner = cb * 2 * nl
        blocks = length // SPAN
        gb = cb // GROUP
        mh = lax.axis_index("zh")
        ml = lax.axis_index("zl")
        first_h = mh == 0
        here = mh * nl + ml
        bcn = conv_bc.shape[1]

        def mine(v, axis=0):
            return lax.dynamic_index_in_dim(v, mh, axis, keepdims=False)

        def other(v, axis=0):
            return lax.dynamic_index_in_dim(v, 1 - mh, axis, keepdims=False)

        def seqs(v):
            return v.reshape(2, length, feat)

        def by_seq(own, away):
            return jnp.where(first_h, jnp.stack([own, away]), jnp.stack([away, own]))

        def place(own, away):
            both = jnp.zeros((2,) + own.shape, own.dtype)
            both = lax.dynamic_update_slice(both, own[None], (mh, 0, 0))
            return lax.dynamic_update_slice(both, away[None], (1 - mh, 0, 0)).reshape(-1, own.shape[1])

        def gather_features(v):
            own, away = mine(seqs(v)), other(seqs(v))
            both = by_seq(own, swap(away))
            every = jnp.moveaxis(lax.all_gather(both, "zl"), 0, 1)
            return jnp.transpose(every, (2, 0, 1, 3)).reshape(length, width)

        def scatter_features(v):
            parts = v.reshape(length, 2, nl, feat)
            both = lax.psum_scatter(parts, "zl", scatter_dimension=2, tiled=False)
            return by_seq(mine(both, 1), swap(other(both, 1))).astype(F32)

        chan = jnp.concatenate(
            [
                conv_x,
                conv_x_bias[None],
                jnp.repeat(d_skip, HEADDIM)[None],
                inner_gain[None],
                jnp.pad(jnp.concatenate([dt_bias, a_log]), (0, cb - 2 * hb))[None],
            ],
            axis=0,
        )
        thin = jnp.concatenate([in_bc, in_dt], axis=1)
        bc_rows = jnp.concatenate([conv_bc, conv_bc_bias[None]], axis=0)
        seg = mine(segment_ids)
        segc = jnp.broadcast_to(seg[:, None], (length, 128))
        segr = jnp.broadcast_to(seg[None, :], (8, length))
        if direct:
            extra = jnp.zeros((8, cb), F32)
            extra = lax.dynamic_update_slice(extra, norm_gain[None], (0, 0))
            extra = lax.dynamic_update_slice(extra, bc_rows, (1, here * bcn))
            extra = lax.dynamic_update_slice(extra, jnp.stack([dt_bias, a_log]), (6, 0))
            thin = jnp.pad(thin, ((0, 0), (0, 128 - thin.shape[1])))
            (
                normed, normed_t, inv_root, par, w_small, small, hp, bcp,
                bc, bct, gmat, gtmat, colp, cumt, kexp, lag, w_gate, w_x,
            ) = gather_all(
                seqs(tokens), in_zx[:, 0], in_zx[:, 1], thin, jnp.concatenate([chan, extra], axis=0),
                segc, segr, 2 * gb,
            )
            chan_got = lax.dynamic_index_in_dim(par, (1 - mh) * nl + ml, 0, keepdims=False)[0:8]
            gain = par[:, 8, :feat].reshape(width)
        else:
            chan_got = swap(chan)
            packed = jnp.concatenate([norm_gain, bc_rows.reshape(-1)])
            packs = lax.all_gather(packed, col)
            gain = packs[:, :feat].reshape(width)
            bc_all = jnp.moveaxis(packs[:, feat:].reshape(-1, KW + 1, bcn), 0, 1)
            bcp = jnp.pad(bc_all.reshape(KW + 1, 2 * STATE), ((0, 7 - KW), (0, 0)))
            hp = jnp.concatenate([c[7, : 2 * hb].reshape(2, hb) for c in (chan, chan_got)], axis=1)
            hp = jnp.pad(hp, ((0, 6), (0, 128 - 2 * hb)))
            thin = lax.all_gather(thin, ("row", "zh", "zl")).reshape(nrow, 2, nl, -1, bcn + hb)
            thin = jnp.moveaxis(thin, 3, 1).reshape(width, 2, nl, bcn + hb)
            w_gate = jnp.stack([row_gather(w) for w in (in_zx[:, 0], swap(in_zx[:, 0]))])
            w_x = jnp.stack([row_gather(w) for w in (in_zx[:, 1], swap(in_zx[:, 1]))])
            w_bc = thin[..., :bcn].reshape(width, 2 * STATE)
            w_dt = lax.dynamic_index_in_dim(thin[..., bcn:], ml, 2, keepdims=False)
            w_small = jnp.concatenate([w_bc, mine(w_dt, 1), other(w_dt, 1)], axis=1)
            w_small = jnp.pad(w_small, ((0, 0), (0, 384 - w_small.shape[1])))
            x32 = gather_features(tokens).astype(F32)
            inv_root = lax.rsqrt(jnp.mean(x32 * x32, axis=1, keepdims=True) + EPS)
            normed = (x32 * inv_root * gain).astype(BF16)
            small = dot_nn(normed, w_small)
            bc, bct, gmat, gtmat, colp, cumt, kexp, lag = prep(small, segc, segr, bcp, hp, 2 * gb)
        chans = jnp.concatenate([chan, chan_got], axis=1)
        kexp = jnp.repeat(kexp[:, : 2 * hb], HEADDIM, axis=1)

        seq_args = (lag, bc, bct, gmat, colp, cumt, kexp)
        gain_in = chans[6]
        if direct:
            gates, xrs, ys, hidden, _, sts, partial_out, ir, c_full, w_out = scan_all(
                seqs(cotangent), out_proj, normed, w_gate, w_x, chans, *seq_args
            )
            dh, g_out, cf, sum3 = middle(c_full, w_out, hidden, ir, partial_out)
        else:
            w_out = [row_gather(w) for w in (out_proj, swap(out_proj))]
            c_full = gather_features(cotangent)
            gates, xrs, ys, gateds, sq, sts = scan(normed, w_gate, w_x, chans, *seq_args)
            dh = jnp.concatenate([dot_nn(c_full, w).astype(BF16) for w in w_out], axis=1)
            gate_sq = pair_sum(jnp.sum(sq, axis=1))
            inner_root = lax.rsqrt(gate_sq / inner + EPS)[:, None]
            gate_dot = jnp.sum(dh.astype(F32) * gateds.astype(F32) * gain_in, axis=1)
            gate_dot = pair_sum(gate_dot)[:, None]
            hidden = (gateds.astype(F32) * inner_root * gain_in).astype(BF16)
            partial_out = dot_nt(hidden[:, :cb], w_out[0]) + dot_nt(hidden[:, cb:], w_out[1])
            partial_out = partial_out.astype(BF16)
            ir = jnp.broadcast_to(inner_root, (length, 128))
            cf = jnp.broadcast_to(inner_root**3 / inner * gate_dot, (length, 128))
            g_out = [dot_tn(c_full, hidden[:, :cb]), dot_tn(c_full, hidden[:, cb:])]
            g_out = [row_scatter(g.astype(BF16)) for g in g_out]
            g_wout = g_out[0].astype(F32) + swap(g_out[1]).astype(F32)
            out_here = scatter_features(partial_out)

        grad_args = (
            gates, xrs, ys, dh, chans, lag, ir, cf, bc, bct, gtmat, colp, cumt, kexp, sts, segc, segr,
            small, hp, bcp,
        )
        if direct:
            (
                dgates, dxrs, chg, nd, d_small, pg, g_wout, gate_own, gate_got, sum0, sum1, sum2,
            ) = scan_grad_all(g_out, partial_out, normed_t, *grad_args)
            own = lax.dynamic_index_in_dim(partial_out, here, 0, keepdims=False).astype(F32)
            own = own + sum0.astype(F32) + mine(seqs(tokens)).astype(F32)
            away = sum1.astype(F32) + jnp.concatenate([sum3, sum2], axis=0).astype(F32)
            away = away + other(seqs(tokens)).astype(F32)
            output = place(own.astype(BF16), away.astype(BF16))
        else:
            dgates, dxrs, chg, nd, d_small, pg = scan_grad(*grad_args)
            output = (out_here + seqs(tokens)).astype(BF16).reshape(tokens.shape)
        g_dtb, g_alog = pg[5, : 2 * hb], pg[6, : 2 * hb]
        g_bcs = pg[: KW + 1]

        def finish(pick, d, root, dot):
            root, dot = root[:, None], dot[:, None]
            grad = pick(seqs(cotangent)).astype(F32) + root * norm_gain * d
            return (grad - pick(seqs(tokens)).astype(F32) * (root * root / width * dot)).astype(BF16)

        if direct:
            rows = []
            for b in range(2):
                hs = slice(b * hb, (b + 1) * hb)
                heads = jnp.concatenate([g_dtb[hs], g_alog[hs]])
                rows += [chg[0:7, b * cb : (b + 1) * cb], jnp.pad(heads, (0, cb - 2 * hb))[None]]
            last = jnp.pad(g_bcs.reshape(-1), (0, width - g_bcs.size))
            last = jnp.concatenate([jnp.zeros_like(gain), last, gain, jnp.zeros_like(gain)]).reshape(8, cb)
            gz, thins, smalls, d_own, d_away, rowv = grad_all(
                gate_own, w_gate, w_x, w_small, normed, gate_got, normed_t, dgates, dxrs, d_small,
                jnp.concatenate(rows + [last], axis=0), nd, inv_root,
            )
            own = finish(mine, d_own.astype(F32), rowv[0, 1], rowv[0, 0] + rowv[2, 0])
            away = finish(other, d_away.astype(F32), rowv[1, 1], rowv[1, 0] + rowv[3, 0])
            tokens_grad = place(own, away)
            g_zx = jnp.transpose(gz, (1, 0, 2))
            g_bc = lax.dynamic_slice(thins, (0, ml * bcn), (thins.shape[0], bcn))
            g_dt = thins[:, 128 : 128 + hb] + thins[:, 256 + hb : 256 + 2 * hb]
            chg = smalls[0, 0:8] + smalls[1, 8:16]
            last = smalls[:, 16:].sum(0).reshape(-1)
            g_gain = lax.dynamic_slice(last, (here * feat,), (feat,))
            g_bcs = last[width : width + (KW + 1) * 2 * STATE].reshape(KW + 1, 2 * nl, bcn)
            g_bcs = lax.dynamic_index_in_dim(g_bcs, here, 1, keepdims=False)
            g_dtb, g_alog = chg[7, :hb], chg[7, hb : 2 * hb]
        else:
            dn, gg = back(dgates, dxrs, d_small, w_gate, w_x, w_small, normed)
            g_gain = gg[0] / gain
            d_here = scatter_features(jnp.moveaxis(dn, 0, 1).reshape(length, width))
            dots = pair_sum(jnp.sum(nd, axis=1))
            own = finish(mine, mine(d_here), inv_root[:, 0], dots)
            away = finish(other, other(d_here), swap(inv_root[:, 0]), swap(dots))
            tokens_grad = place(own, away)

            def join(own, away):
                return own.astype(F32) + swap(away).astype(F32)

            halves = (slice(0, cb), slice(cb, 2 * cb))
            g_gate = [row_scatter(dot_tn(normed, dgates[:, n]).astype(BF16)) for n in halves]
            g_x = [row_scatter(dot_tn(normed, dxrs[:, n]).astype(BF16)) for n in halves]
            g_zx = jnp.stack([join(*g_gate), join(*g_x)], axis=1)
            thins = row_scatter(dot_tn(normed, d_small))
            g_bc = lax.psum(thins[:, : 2 * STATE], col).reshape(-1, 2 * nl, bcn)
            g_bc = lax.dynamic_index_in_dim(g_bc, here, 1, keepdims=False)
            g_dts = thins[:, 2 * STATE : 2 * STATE + 2 * hb].reshape(-1, 2, hb)
            g_dt = g_dts[:, 0] + swap(g_dts[:, 1])
            every = ("row", "zh", "zl")
            g_gain, g_bcs = lax.psum((g_gain, g_bcs), every)
            g_gain = lax.dynamic_slice(g_gain, (here * feat,), (feat,))
            g_bcs = g_bcs.reshape(KW + 1, 2 * nl, bcn)
            g_bcs = lax.dynamic_index_in_dim(g_bcs, here, 1, keepdims=False)
            chg = chg[:, :cb] + swap(chg[:, cb:])
            g_dtb = g_dtb[:hb] + swap(g_dtb[hb:])
            g_alog = g_alog[:hb] + swap(g_alog[hb:])
            chg, g_dtb, g_alog = lax.psum((chg, g_dtb, g_alog), "row")
        return (
            output,
            tokens_grad,
            g_gain,
            g_zx,
            g_dt,
            g_bc,
            chg[0:KW],
            chg[4],
            g_bcs[0:KW],
            g_bcs[KW],
            g_dtb,
            g_alog,
            chg[5].reshape(hb, HEADDIM).sum(1),
            chg[6],
            g_wout,
        )

    return per_device


def solution(mesh):
    nrow, ncol = mesh.shape["row"], mesh.shape["col"]
    nl = ncol // 2
    split = Mesh(mesh.devices.reshape(nrow, 2, nl), ("row", "zh", "zl"))
    col = ("zh", "zl")
    in_specs = (
        P("row", col), P("row", None), P(col), P("row", None, col), P("row", col), P("row", col),
        P(None, col), P(col), P(None, col), P(col), P(col), P(col), P(col), P(col),
        P("row", col), P("row", col),
    )
    out_specs = (
        P("row", col), P("row", col), P(col), P("row", None, col), P("row", col), P("row", col),
        P(None, col), P(col), P(None, col), P(col), P(col), P(col), P(col), P(col), P("row", col),
    )
    return jax.shard_map(
        build(nrow, nl), mesh=split, in_specs=in_specs, out_specs=out_specs, check_vma=False
    )
```

```python
import functools

import jax
import jax.numpy as jnp
from jax import lax
from jax.experimental import pallas as pl
from jax.experimental.pallas import tpu as pltpu
from jax.sharding import Mesh, PartitionSpec as P

HEADDIM = 64
STATE = 128
KW = 4
EPS = 1e-05
SPAN = 256
GROUP = 256
PER = GROUP // HEADDIM
F32 = jnp.float32
BF16 = jnp.bfloat16
VMEM_LIMIT = 60 * 1024 * 1024


def dot_nn(a, b):
    return lax.dot_general(a, b, (((1,), (0,)), ((), ())), preferred_element_type=F32)


def dot_nt(a, b):
    return lax.dot_general(a, b, (((1,), (1,)), ((), ())), preferred_element_type=F32)


def dot_tn(a, b):
    return lax.dot_general(a, b, (((0,), (0,)), ((), ())), preferred_element_type=F32)


def dot_exact(a, b):
    return lax.dot_general(
        a, b, (((1,), (0,)), ((), ())), preferred_element_type=F32, precision=lax.Precision.HIGHEST
    )


def twice(v):
    return jnp.concatenate([v, v], axis=1)


def across(v):
    return v if SPAN == 128 else twice(v)


def turned(v):
    n = v.shape[1]
    row = lax.broadcasted_iota(jnp.int32, (n, n), 0)
    col = lax.broadcasted_iota(jnp.int32, (n, n), 1)
    return dot_nt((row == col).astype(F32).astype(BF16), v).astype(BF16)


def spread(cols):
    rows = cols.shape[0]
    lane = lax.broadcasted_iota(jnp.int32, (rows, 128), 1)
    low = lane < HEADDIM
    first = jnp.where(low, cols[:, 0:1], cols[:, 1:2])
    second = jnp.where(low, cols[:, 2:3], cols[:, 3:4])
    return jnp.concatenate([first, second], axis=1)


def head_mask(h):
    lane = lax.broadcasted_iota(jnp.int32, (1, GROUP), 1)
    return ((lane >= h * HEADDIM) & (lane < (h + 1) * HEADDIM)).astype(F32).astype(BF16)


def prep_lags(segc_ref, kexp_ref, lag_ref):
    seg = segc_ref[...]
    length = seg.shape[0]
    pos = lax.broadcasted_iota(jnp.int32, (length, 128), 0)
    lag = jnp.zeros((length, 128), F32)
    for j in range(1, KW):
        lag = lag + ((pltpu.roll(seg, j, 0) == seg) & (pos >= j)).astype(F32)
    lag_ref[0:length, :] = lag
    lag_ref[length:, :] = jnp.zeros((8, 128), F32)
    kexp_ref[...] = jnp.zeros_like(kexp_ref)


def prep_rows(
    lo, hi, small_ref, segc_ref, segr_ref, bcp_ref, hp_ref,
    bc_ref, bct_ref, g_ref, gt_ref, colp_ref, cumt_ref, kexp_ref, lag_ref,
):
    groups = colp_ref.shape[0]
    some = slice(lo, hi)
    lag2 = twice(lag_ref[some, :])
    raw = small_ref[some, 0:256]
    wide = raw if lo == 0 else small_ref[lo - 8 : hi, 0:256]
    v = bcp_ref[4:5, :] + bcp_ref[3:4, :] * raw
    for j in range(1, KW):
        earlier = pltpu.roll(wide, j, 0)[wide.shape[0] - (hi - lo) :]
        v = v + bcp_ref[3 - j : 4 - j, :] * jnp.where(lag2 >= j, earlier, 0.0)
    act = (v * jax.nn.sigmoid(v)).astype(BF16)
    bc_ref[some, :] = act
    bct_ref[:, some] = turned(act)
    z = small_ref[some, 256:384] + hp_ref[0:1, :]
    dt = jnp.maximum(z, 0.0) + jnp.log1p(jnp.exp(-jnp.abs(z)))
    a = -dt * jnp.exp(hp_ref[1:2, :])
    tri_r = lax.broadcasted_iota(jnp.int32, (SPAN, SPAN), 0)
    tri_c = lax.broadcasted_iota(jnp.int32, (SPAN, SPAN), 1)
    lower = (tri_r >= tri_c).astype(F32)
    seg_row = segr_ref[0:1, :]
    for c in range(lo // SPAN, hi // SPAN):
        r0 = c * SPAN
        rows = slice(r0, r0 + SPAN)
        here = slice(r0 - lo, r0 - lo + SPAN)
        cum = dot_exact(lower, a[here])
        segb = segc_ref[rows, :]
        last = segc_ref[r0 + SPAN - 1 : r0 + SPAN, :]
        tail = (segb == last).astype(F32)
        end = cum[SPAN - 1 : SPAN]
        q = jnp.exp(end - cum) * tail
        if c > 0:
            prev = segc_ref[r0 - 1 : r0, :]
            p = jnp.exp(cum) * (segb == prev).astype(F32)
            kexp_ref[c : c + 1, :] = jnp.exp(end) * (last == prev).astype(F32)
        else:
            p = jnp.zeros_like(cum)
        cumt = jnp.transpose(cum)
        dtb = dt[here]
        for g in range(groups):
            hs = slice(PER * g, PER * g + PER)
            colp_ref[g, rows, 0:4] = cum[:, hs]
            colp_ref[g, rows, 4:8] = dtb[:, hs]
            colp_ref[g, rows, 8:12] = p[:, hs]
            colp_ref[g, rows, 12:16] = q[:, hs]
            cumt_ref[g, 0:4, rows] = cumt[hs, :]
        bb = bc_ref[rows, 0:STATE]
        cc = bc_ref[rows, STATE : 2 * STATE]
        same = across(segb) == seg_row[:, rows]
        g_ref[rows, :] = jnp.where(same & (tri_r >= tri_c), dot_nt(cc, bb), 0.0)
        gt_ref[rows, :] = jnp.where(same & (tri_r <= tri_c), dot_nt(bb, cc), 0.0)


def prep_kernel(*refs):
    prep_lags(refs[1], refs[-2], refs[-1])
    prep_rows(0, refs[0].shape[0], *refs)


def conv_rows(xr_ref, lag_ref, chan_ref, r0):
    cur = xr_ref[pl.ds(r0, SPAN), :]
    before = xr_ref[pl.ds(pl.multiple_of(jnp.maximum(r0 - 8, 0), 8), 8), :]
    both = jnp.concatenate([before, cur], axis=0)
    lag = twice(lag_ref[pl.ds(r0, SPAN), :])
    v = chan_ref[4:5, :] + chan_ref[3:4, :] * cur
    for j in range(1, KW):
        earlier = pltpu.roll(both, j, 0)[8:]
        v = v + chan_ref[3 - j : 4 - j, :] * jnp.where(lag >= j, earlier, 0.0)
    return cur, v


def scan_kernel(
    nb_ref, wg_ref, wx_ref, chan_ref, lag_ref, bc_ref, bct_ref, g_ref, colp_ref, cumt_ref, kexp_ref,
    gate_ref, xr_ref, v_ref, y_ref, gated_ref, sq_ref, st_ref, xs, state,
):
    length = gate_ref.shape[0]
    blocks = length // SPAN
    state[...] = jnp.zeros_like(state)

    @pl.when(pl.program_id(0) == 0)
    def _():
        sq_ref[...] = jnp.zeros_like(sq_ref)

    def project(c, carry):
        rows = pl.ds(pl.multiple_of(c * 512, 512), 512)
        gate_ref[rows, :] = dot_nn(nb_ref[rows, :], wg_ref[...])
        xs[rows, :] = dot_nn(nb_ref[rows, :], wx_ref[...])
        return carry

    lax.fori_loop(0, length // 512, project, 0)

    def body(c, carry):
        r0 = pl.multiple_of(c * SPAN, SPAN)
        rows = pl.ds(r0, SPAN)
        cur, v = conv_rows(xs, lag_ref, chan_ref, r0)
        xr_ref[rows, :] = cur.astype(BF16)
        v_ref[rows, :] = v
        xc = (v * jax.nn.sigmoid(v)).astype(BF16).astype(F32)
        cp = colp_ref[0, rows, :]
        xd = (spread(cp[:, 4:8]) * xc).astype(BF16)
        px = spread(cp[:, 8:12])
        qx = spread(cp[:, 12:16])
        gb = g_ref[rows, :]
        lefts, rights = [], []
        for h in range(PER):
            gap = cp[:, h : h + 1] - cumt_ref[0, h : h + 1, rows]
            lefts.append((gb * jnp.exp(jnp.minimum(gap, 0.0))).astype(BF16))
            rights.append(xd * head_mask(h))
        y = dot_nn(jnp.concatenate(lefts, axis=1), jnp.concatenate(rights, axis=0))
        st = state[...]
        stb = st.astype(BF16)
        st_ref[c] = stb
        y = y + px * dot_nn(bc_ref[rows, STATE : 2 * STATE], stb)
        kx = kexp_ref[pl.ds(c, 1), :]
        state[...] = kx * st + dot_nn(bct_ref[0:STATE, rows], (qx * xd.astype(F32)).astype(BF16))
        y = y + chan_ref[5:6, :] * xc
        y_ref[rows, :] = y
        gate = gate_ref[rows, :]
        gated = y * (gate * jax.nn.sigmoid(gate))
        gated_ref[rows, :] = gated.astype(BF16)
        sq = gated * gated
        sq_ref[rows, :] += sq[:, 0:128] + sq[:, 128:256]
        return carry

    lax.fori_loop(0, blocks, body, 0)


def scan_grad_kernel(
    place, gate_ref, xr_ref, v_ref, y_ref, dh_ref, chan_ref, lag_ref, ir_ref, cf_ref, bc_ref, bct_ref, gt_ref,
    colp_ref, cumt_ref, kexp_ref, st_ref, segc_ref, segr_ref,
    small_ref, hp_ref, bcp_ref,
    dgate_ref, dxr_ref, chg_ref, ds_ref, pg_ref,
    dst, head, dgt, dbc_ref, end_ref, acc_a, acc_d, acc_e,
):
    length = gate_ref.shape[0]
    blocks = length // SPAN
    step = pl.program_id(0)
    dst[...] = jnp.zeros_like(dst)
    head[...] = jnp.zeros_like(head)
    end_ref[...] = jnp.zeros_like(end_ref)
    chg_ref[...] = jnp.zeros_like(chg_ref)

    @pl.when(step == 0)
    def _():
        dgt[...] = jnp.zeros_like(dgt)
        dbc_ref[...] = jnp.zeros_like(dbc_ref)
        acc_a[...] = jnp.zeros_like(acc_a)
        acc_d[...] = jnp.zeros_like(acc_d)
        acc_e[...] = jnp.zeros_like(acc_e)

    pick_r = lax.broadcasted_iota(jnp.int32, (GROUP, 128), 0)
    pick_c = lax.broadcasted_iota(jnp.int32, (GROUP, 128), 1)
    pick32 = (pick_r // HEADDIM + PER * place == pick_c).astype(F32)
    pick = pick32.astype(BF16)

    def per_head(v):
        hi = v.astype(BF16)
        lo = (v - hi.astype(F32)).astype(BF16)
        return dot_nn(hi, pick) + dot_nn(lo, pick)

    def total(v):
        return jnp.sum(v, axis=0, keepdims=True)

    def body(back, carry):
        c = blocks - 1 - back
        r0 = pl.multiple_of(c * SPAN, SPAN)
        rows = pl.ds(r0, SPAN)
        cur = xr_ref[rows, :].astype(F32)
        v = v_ref[rows, :]
        sv = jax.nn.sigmoid(v)
        xc = (v * sv).astype(BF16).astype(F32)
        cp = colp_ref[0, rows, :]
        dtx = spread(cp[:, 4:8])
        px = spread(cp[:, 8:12])
        qx = spread(cp[:, 12:16])
        xd = (dtx * xc).astype(BF16)
        xdf = xd.astype(F32)
        gate = gate_ref[rows, :]
        y = y_ref[rows, :]
        dh = dh_ref[rows, :].astype(F32)
        ir = twice(ir_ref[rows, :])
        cf = twice(cf_ref[rows, :])
        sg = jax.nn.sigmoid(gate)
        sl = gate * sg
        gated = y * sl
        dgd = ir * (dh * chan_ref[6:7, :]) - gated * cf
        dy = dgd * sl
        dgate = dgd * y * (sg * (1.0 + gate * (1.0 - sg)))
        dgate_ref[rows, :] = dgate.astype(BF16)
        dyb = dy.astype(BF16)
        gt = gt_ref[rows, :]
        lefts, rights = [], []
        acc = dgt[rows, :]
        for h in range(PER):
            gap = cumt_ref[0, h : h + 1, rows] - cp[:, h : h + 1]
            et = jnp.exp(jnp.minimum(gap, 0.0))
            lefts.append((gt * et).astype(BF16))
            dym = dyb * head_mask(h)
            rights.append(dym)
            acc = acc + dot_nt(xd, dym) * et
        dgt[rows, :] = acc
        u = dot_nn(jnp.concatenate(lefts, axis=1), jnp.concatenate(rights, axis=0))
        ds = dst[...]
        dsb = ds.astype(BF16)
        bb = bc_ref[rows, 0:STATE]
        cc = bc_ref[rows, STATE : 2 * STATE]
        ui = qx * dot_nn(bb, dsb)
        u = u + ui
        dxc = chan_ref[5:6, :] * dy + dtx * u
        yscan = y - chan_ref[5:6, :] * xc
        acc_a[rows, :] += per_head(dyb.astype(F32) * yscan - xdf * u)
        acc_d[rows, :] += per_head(xc * u)
        stb = st_ref[c]
        kx = kexp_ref[pl.ds(c, 1), :]
        end_ref[pl.ds(c, 1), :] = total(xdf * ui) + kx * total(ds * stb.astype(F32))
        pdy = (px * dyb.astype(F32)).astype(BF16)
        dbc_ref[rows, 0:STATE] += dot_nt((qx * xdf).astype(BF16), dsb)
        dbc_ref[rows, STATE : 2 * STATE] += dot_nt(pdy, stb)
        dst[...] = kx * ds + dot_nn(bct_ref[STATE : 2 * STATE, rows], pdy)
        dv = dxc * (sv * (1.0 + v * (1.0 - sv)))
        after = pl.ds(pl.multiple_of(r0 + SPAN, 8), 8)
        wide = jnp.concatenate([dv, head[...]], axis=0)
        lagw = jnp.concatenate([twice(lag_ref[rows, :]), twice(lag_ref[after, :])], axis=0)
        head[...] = dv[0:8]
        dxr = chan_ref[3:4, :] * dv
        chg_ref[3:4, :] += total(cur * dv)
        chg_ref[4:5, :] += total(dv)
        chg_ref[5:6, :] += total(dy * xc)
        for j in range(1, KW):
            later = pltpu.roll(jnp.where(lagw >= j, wide, 0.0), SPAN + 8 - j, 0)[0:SPAN]
            dxr = dxr + chan_ref[3 - j : 4 - j, :] * later
            chg_ref[3 - j : 4 - j, :] += total(cur * later)
        dxr_ref[rows, :] = dxr.astype(BF16)
        return carry

    lax.fori_loop(0, blocks, body, 0)

    acc_e[...] += dot_exact(end_ref[...], pick32)

    @pl.when(step == pl.num_programs(0) - 1)
    def _():
        tri_r = lax.broadcasted_iota(jnp.int32, (SPAN, SPAN), 0)
        tri_c = lax.broadcasted_iota(jnp.int32, (SPAN, SPAN), 1)
        upper = (tri_r <= tri_c).astype(F32)
        rate = jnp.exp(hp_ref[1:2, :])
        pg_ref[...] = jnp.zeros_like(pg_ref)
        for c in range(blocks):
            rows = slice(c * SPAN, (c + 1) * SPAN)
            same = across(segc_ref[rows, :]) == segr_ref[0:1, rows]
            full = jnp.where(same & (tri_r <= tri_c), dgt[rows, :], 0.0)
            turn = jnp.transpose(full)
            for value, here, there in ((full, 0, STATE), (turn, STATE, 0)):
                high = value.astype(BF16)
                low = (value - high.astype(F32)).astype(BF16)
                right = bc_ref[rows, there : there + STATE]
                dbc_ref[rows, here : here + STATE] += dot_nn(high, right) + dot_nn(low, right)
            da = dot_exact(upper, acc_a[rows, :]) + acc_e[c : c + 1, :]
            raw = small_ref[rows, 2 * STATE :]
            z = raw + hp_ref[0:1, :]
            dt = jnp.maximum(z, 0.0) + jnp.log1p(jnp.exp(-jnp.abs(z)))
            ddt = (acc_d[rows, :] - rate * da) * jax.nn.sigmoid(z)
            pg_ref[5:6, 0:128] += total(ddt)
            pg_ref[6:7, 0:128] += -rate * total(da * dt)
            ds_ref[rows, 2 * STATE :] = ddt.astype(BF16)
        raw = small_ref[:, 0 : 2 * STATE]
        lag = twice(lag_ref[0:length, :])
        v = bcp_ref[4:5, :] + bcp_ref[3:4, :] * raw
        for j in range(1, KW):
            v = v + bcp_ref[3 - j : 4 - j, :] * jnp.where(lag >= j, pltpu.roll(raw, j, 0), 0.0)
        sv = jax.nn.sigmoid(v)
        dv = dbc_ref[...] * (sv * (1.0 + v * (1.0 - sv)))
        dr = bcp_ref[3:4, :] * dv
        pg_ref[3:4, :] = total(raw * dv)
        pg_ref[4:5, :] = total(dv)
        for j in range(1, KW):
            later = pltpu.roll(jnp.where(lag >= j, dv, 0.0), length - j, 0)
            dr = dr + bcp_ref[3 - j : 4 - j, :] * later
            pg_ref[3 - j : 4 - j, :] = total(raw * later)
        ds_ref[:, 0 : 2 * STATE] = dr.astype(BF16)


def whole(shape):
    return pl.BlockSpec(shape, lambda g: (0,) * len(shape))


def once(shape):
    return pl.BlockSpec(shape, lambda g: (0,) * len(shape), pipeline_mode=pl.Buffered(1))


def tile(rows):
    return pl.BlockSpec((rows, GROUP), lambda g: (0, g))


def prep_shapes(length, groups):
    return (
        jax.ShapeDtypeStruct((length, 2 * STATE), BF16),
        jax.ShapeDtypeStruct((2 * STATE, length), BF16),
        jax.ShapeDtypeStruct((length, SPAN), F32),
        jax.ShapeDtypeStruct((length, SPAN), F32),
        jax.ShapeDtypeStruct((groups, length, 16), F32),
        jax.ShapeDtypeStruct((groups, 8, length), F32),
        jax.ShapeDtypeStruct((8, 128), F32),
        jax.ShapeDtypeStruct((length + 8, 128), F32),
    )


def prep(small, segc, segr, bcp, hp, groups):
    return pl.pallas_call(
        prep_kernel,
        out_shape=prep_shapes(small.shape[0], groups),
        compiler_params=pltpu.CompilerParams(vmem_limit_bytes=VMEM_LIMIT),
        name="prep",
    )(small, segc, segr, bcp, hp)


def scan_specs(length, width, gb):
    last = 2 * gb - 1

    def at(g):
        return jnp.minimum(g, last)

    def strip(rows):
        return pl.BlockSpec((rows, GROUP), lambda g: (0, at(g)))

    weight = pl.BlockSpec((None, width, GROUP), lambda g: (at(g) // gb, 0, at(g) % gb))
    return [
        once((length, width)),
        weight,
        weight,
        strip(8),
        once((length + 8, 128)),
        once((length, 2 * STATE)),
        once((2 * STATE, length)),
        once((length, SPAN)),
        pl.BlockSpec((1, length, 16), lambda g: (at(g), 0, 0)),
        pl.BlockSpec((1, 8, length), lambda g: (at(g), 0, 0)),
        strip(8),
    ], [
        strip(length),
        strip(length),
        strip(length),
        strip(length),
        strip(length),
        whole((length, 128)),
        pl.BlockSpec((length // SPAN, STATE, GROUP), lambda g: (0, 0, at(g))),
    ]


def scan_shapes(length, channels):
    return (
        jax.ShapeDtypeStruct((length, channels), F32),
        jax.ShapeDtypeStruct((length, channels), BF16),
        jax.ShapeDtypeStruct((length, channels), F32),
        jax.ShapeDtypeStruct((length, channels), F32),
        jax.ShapeDtypeStruct((length, channels), BF16),
        jax.ShapeDtypeStruct((length, 128), F32),
        jax.ShapeDtypeStruct((length // SPAN, STATE, channels), BF16),
    )


def scan(nb, wg, wx, chan, *rest):
    length, width = nb.shape
    channels = chan.shape[1]
    in_specs, out_specs = scan_specs(length, width, channels // GROUP // 2)
    return pl.pallas_call(
        scan_kernel,
        grid=(channels // GROUP,),
        in_specs=in_specs,
        out_specs=out_specs,
        out_shape=scan_shapes(length, channels),
        scratch_shapes=[pltpu.VMEM((length, GROUP), F32), pltpu.VMEM((STATE, GROUP), F32)],
        compiler_params=pltpu.CompilerParams(vmem_limit_bytes=VMEM_LIMIT),
        name="scan",
    )(nb, wg, wx, chan, *rest)


def scan_grad_specs(length, channels, shift=0):
    blocks = length // SPAN
    groups = channels // GROUP

    def at(g):
        return lax.rem(g + shift, groups)

    def tile(rows):
        return pl.BlockSpec((rows, GROUP), lambda g: (0, at(g)))

    ins = [
        tile(length),
        tile(length),
        tile(length),
        tile(length),
        tile(length),
        tile(8),
        once((length + 8, 128)),
        once((length, 128)),
        once((length, 128)),
        once((length, 2 * STATE)),
        once((2 * STATE, length)),
        once((length, SPAN)),
        pl.BlockSpec((1, length, 16), lambda g: (at(g), 0, 0)),
        pl.BlockSpec((1, 8, length), lambda g: (at(g), 0, 0)),
        tile(8),
        pl.BlockSpec((blocks, STATE, GROUP), lambda g: (0, 0, at(g))),
        once((length, 128)),
        once((8, length)),
        once((length, 2 * STATE + 128)),
        once((8, 128)),
        once((8, 2 * STATE)),
    ]
    outs = [
        tile(length),
        tile(length),
        tile(8),
        once((length, 2 * STATE + 128)),
        once((8, 2 * STATE)),
    ]
    shapes = (
        jax.ShapeDtypeStruct((length, channels), BF16),
        jax.ShapeDtypeStruct((length, channels), BF16),
        jax.ShapeDtypeStruct((8, channels), F32),
        jax.ShapeDtypeStruct((length, 2 * STATE + 128), BF16),
        jax.ShapeDtypeStruct((8, 2 * STATE), F32),
    )
    scratch = [
        pltpu.VMEM((STATE, GROUP), F32),
        pltpu.VMEM((8, GROUP), F32),
        pltpu.VMEM((length, SPAN), F32),
        pltpu.VMEM((length, 2 * STATE), F32),
        pltpu.VMEM((8, GROUP), F32),
        pltpu.VMEM((length, 128), F32),
        pltpu.VMEM((length, 128), F32),
        pltpu.VMEM((8, 128), F32),
    ]
    return ins, outs, shapes, scratch


def scan_grad(*args):
    length, channels = args[0].shape
    ins, outs, shapes, scratch = scan_grad_specs(length, channels)
    return pl.pallas_call(
        lambda *refs: scan_grad_kernel(pl.program_id(0), *refs),
        grid=(channels // GROUP,),
        in_specs=ins,
        out_specs=outs,
        out_shape=shapes,
        scratch_shapes=scratch,
        compiler_params=pltpu.CompilerParams(vmem_limit_bytes=VMEM_LIMIT),
        name="scan_grad",
    )(*args)


def back_kernel(a0, a1, a2, w0, w1, w2, nb_ref, dn_ref, gg_ref):
    cb = w0.shape[2]
    total = dot_nt(a2[...], w2[...])
    for a, w in ((a0, w0), (a1, w1)):
        for b in range(2):
            total = total + dot_nt(a[:, b * cb : (b + 1) * cb], w[b])
    dn_ref[0] = total.astype(BF16)
    gg = jnp.sum(total * nb_ref[...].astype(F32), axis=0, keepdims=True)
    gg_ref[...] = jnp.broadcast_to(gg, gg_ref.shape)


def back(dgate, dxr, d_small, wg, wx, w_small, nb):
    length, width = nb.shape
    cb = wg.shape[2]
    feat = max(width // 4, 256)
    per = feat // 256
    wide = pl.BlockSpec((2, 256, cb), lambda n: (0, n, 0))
    return pl.pallas_call(
        back_kernel,
        grid=(width // 256,),
        in_specs=[once(a.shape) for a in (dgate, dxr, d_small)]
        + [wide, wide]
        + [pl.BlockSpec((256, d_small.shape[1]), lambda n: (n, 0))]
        + [pl.BlockSpec((length, 256), lambda n: (0, n))],
        out_specs=[
            pl.BlockSpec((1, length, 256), lambda n: (n // per, 0, n % per)),
            pl.BlockSpec((8, 256), lambda n: (0, n)),
        ],
        out_shape=(
            jax.ShapeDtypeStruct((width // feat, length, feat), BF16),
            jax.ShapeDtypeStruct((8, width), F32),
        ),
        compiler_params=pltpu.CompilerParams(vmem_limit_bytes=VMEM_LIMIT),
        name="back",
    )(dgate, dxr, d_small, wg, wx, w_small, nb)


MESH_ID = pl.DeviceIdType.MESH


class Copies:
    def __init__(self, send, recv):
        self.send, self.recv, self.count, self.open = send, recv, 0, []

    def start(self, src, dst, to):
        copy = pltpu.make_async_remote_copy(
            src_ref=src, dst_ref=dst, send_sem=self.send.at[self.count],
            recv_sem=self.recv.at[self.count], device_id=to, device_id_type=MESH_ID,
        )
        self.count += 1
        copy.start()
        self.open.append(copy)
        return copy

    def finish(self):
        for copy in self.open:
            copy.wait_send()


def places():
    h, l, r = lax.axis_index("zh"), lax.axis_index("zl"), lax.axis_index("row")
    c, x, y = lax.rem(r, 2), lax.rem(r // 2, 2), r // 4
    rx, ry = r + 2 - 4 * x, r + 4 - 8 * y
    rc = r + 1 - 2 * c
    return h, l, r, c, x, y, rx, ry, rc


def meet(peers):
    barrier = pltpu.get_barrier_semaphore()
    for to in peers:
        pl.semaphore_signal(barrier, inc=1, device_id=to, device_id_type=MESH_ID)
    pl.semaphore_wait(barrier, len(peers))


GATHER_COPIES = 96
PIECES = 4
FINE = 8


def gather_kernel(
    x_ref, wg_ref, wx_ref, thin_ref, par_ref, segc_ref, segr_ref,
    nb_ref, nt_ref, ir_ref, par_out, ws_ref, small_ref, hp_ref, bcp_ref,
    bc_ref, bct_ref, g_ref, gt_ref, colp_ref, cumt_ref, kexp_ref, lag_ref, wg_out, wx_out,
    xv, parv, thin_v, stage, send, recv, local,
):
    h, l, r, c, x, y, rx, ry, rc = places()
    rd = rx + ry - r
    me, zhp = h * 2 + l, (1 - h) * 2 + l
    zh, zl, zd = {"zh": 1 - h}, {"zl": 1 - l}, {"zh": 1 - h, "zl": 1 - l}
    to_x, to_y, to_c = {"row": rx}, {"row": ry}, {"row": rc}
    length, feat = x_ref.shape[1], x_ref.shape[2]
    step = length // FINE
    shard = wg_ref.shape[0]
    meet((zh, zl, zd, to_x, to_y, to_c))
    copies = Copies(send, recv)
    start = copies.start

    def cols(block):
        return pl.ds(pl.multiple_of(block * feat, feat), feat)

    def toks(p):
        return pl.ds(p * step, step)

    def rows(row):
        return pl.ds(pl.multiple_of(row * shard, shard), shard)

    src = (wg_ref, wx_ref)
    dst = ((wg_out.at[0], wx_out.at[0]), (wg_out.at[1], wx_out.at[1]))
    keeps = [
        pltpu.make_async_copy(par_ref, parv.at[me], local.at[0]),
        pltpu.make_async_copy(thin_ref, thin_v.at[r, me], local.at[1]),
        pltpu.make_async_copy(x_ref.at[h], xv.at[:, cols(me)], local.at[2]),
        pltpu.make_async_copy(wg_ref, stage.at[0], local.at[3]),
        pltpu.make_async_copy(wx_ref, stage.at[1], local.at[4]),
    ]
    for keep in keeps:
        keep.start()
    laid = [pltpu.make_async_copy(stage.at[k], dst[0][k].at[rows(r)], local.at[5 + k]) for k in range(2)]
    pars = [start(par_ref, parv.at[me], to) for to in (zh, zl, zd)]
    thins = [start(thin_ref, thin_v.at[r, me], to) for to in (zh, zl, zd)]
    sib, sib_thin, x1, x3, wz, got, far = [], [], [], [], [], {}, {}
    bcn, hb = 2 * STATE // 4, colp_ref.shape[0] * PER // 2
    part = shard // 2

    def chunk(b, q, row):
        if b == 0:
            return dst[0][q].at[rows(row)]
        return dst[1][q // 2].at[pl.ds(pl.multiple_of(row * shard + q % 2 * part, part), part)]

    def send_w(q):
        wz.append(start(src[q // 2].at[pl.ds(q % 2 * part, part)], chunk(1, q, r), zh))

    def deal(b, q):
        if b == 0:
            got[b, q] = [start(src[q], chunk(b, q, r), to) for to in (to_x, to_y, to_c)]
        else:
            wz[q].wait_recv()
            got[b, q] = [start(chunk(b, q, r), chunk(b, q, r), to) for to in (to_x, to_y, to_c)]
        sib.append(got[b, q][2])

    def pass_on(b, q, n):
        piece = chunk(b, q, (rx, ry)[n])
        got[b, q][n].wait_recv()
        if n == q % 2:
            far[b, q] = start(piece, piece, (to_y, to_x)[n])
        sib.append(start(piece, piece, to_c))

    def corner(b, q):
        far[b, q].wait_recv()
        sib.append(start(chunk(b, q, rd), chunk(b, q, rd), to_c))

    def send_x():
        if len(x1) < FINE:
            p = len(x1)
            x1.append(start(x_ref.at[1 - h, toks(p)], xv.at[toks(p), cols(me)], zh))

    def pass_x(p):
        x1[p].wait_recv()
        x3.append(start(xv.at[toks(p), cols(zhp)], xv.at[toks(p), cols(zhp)], zl))

    x2 = {}

    def send_own(k):
        rows_k = pl.ds(k * 2 * step, 2 * step)
        x2[k] = start(x_ref.at[h, rows_k], xv.at[rows_k, cols(me)], zl)

    def thin_on(n):
        row = (rx, ry, rd)[n]
        thin_go[n].wait_recv()
        if n == 0:
            thin_go.append(start(thin_v.at[row], thin_v.at[row], to_y))
        sib_thin.append(start(thin_v.at[row], thin_v.at[row], to_c))

    def norm(p):
        if p % 2 == 0:
            x2[p // 2].wait_recv()
        x3[p].wait_recv()
        total = jnp.zeros((step, 1), F32)
        for b in range(4):
            value = xv[toks(p), b * feat : (b + 1) * feat].astype(F32)
            total = total + jnp.sum(value * value, axis=1, keepdims=True)
        root = lax.rsqrt(total / (4 * feat) + EPS)
        ir_ref[toks(p), :] = jnp.broadcast_to(root, (step, 128))
        for b in range(8):
            value = xv[toks(p), b * shard : (b + 1) * shard].astype(F32)
            gain = parv[b // 2, 8:9, b % 2 * shard : (b % 2 + 1) * shard]
            value = (value * root * gain).astype(BF16)
            nb_ref[toks(p), b * shard : (b + 1) * shard] = value
            nt_ref[b % 2, b // 2 * shard : (b // 2 + 1) * shard, toks(p)] = turned(value)

    prep_refs = (
        small_ref, segc_ref, segr_ref, bcp_ref, hp_ref,
        bc_ref, bct_ref, g_ref, gt_ref, colp_ref, cumt_ref, kexp_ref, lag_ref,
    )

    def narrow(p):
        lo, hi = p * (length // 2), (p + 1) * (length // 2)
        small_ref[lo:hi, :] = dot_nn(nb_ref[lo:hi, :], ws_ref[...])
        prep_rows(lo, hi, *prep_refs)

    def parameters():
        for copy in pars:
            copy.wait_recv()
        for n in range(3):
            if n != 1:
                keeps[n].wait()
        par_out[...] = parv[...]
        bcp_ref[...] = jnp.zeros_like(bcp_ref)
        bcp_ref[0:5, :] = sum(parv[b, 9:14, 0 : 2 * STATE] for b in range(4))
        hp_ref[...] = jnp.zeros_like(hp_ref)
        hp_ref[0:2, :] = parv[me, 14:16, 0:128] + pltpu.roll(parv[zhp, 14:16, 0:128], hb, 1)
        prep_lags(segc_ref, kexp_ref, lag_ref)

    def narrow_weights():
        for copy in sib_thin:
            copy.wait_recv()
        ws_ref[...] = jnp.zeros_like(ws_ref)
        for row in range(8):
            at = slice(row * shard, (row + 1) * shard)
            for b in range(4):
                ws_ref[at, b * bcn : (b + 1) * bcn] = thin_v[row, b, :, 0:bcn]
            ws_ref[at, 2 * STATE : 2 * STATE + hb] = thin_v[row, me, :, bcn : bcn + hb]
            ws_ref[at, 2 * STATE + hb : 2 * STATE + 2 * hb] = thin_v[row, zhp, :, bcn : bcn + hb]

    send_w(0)
    send_own(2)
    send_x()
    deal(0, 0)
    send_own(3)
    deal(0, 1)
    send_x()
    send_x()
    for k in range(2):
        keeps[3 + k].wait()
        laid[k].start()
    pass_on(0, 1, 1)
    keeps[1].wait()
    for copy in thins:
        copy.wait_recv()
    thin_go = [start(thin_v.at[r], thin_v.at[r], to) for to in (to_x, to_y, to_c)]
    sib_thin.append(thin_go.pop())
    parameters()
    send_w(1)
    send_own(1)
    thin_on(0)
    pass_on(0, 0, 0)
    pass_x(0)
    send_own(0)
    send_w(2)
    thin_on(1)
    send_x()
    thin_on(2)
    pass_x(1)
    pass_on(0, 0, 1)
    send_w(3)
    deal(1, 0)
    pass_on(1, 0, 0)
    corner(0, 1)
    pass_x(2)
    send_x()
    deal(1, 1)
    norm(0)
    pass_x(3)
    pass_on(1, 1, 1)
    deal(1, 2)
    pass_x(4)
    send_x()
    corner(0, 0)
    narrow_weights()
    deal(1, 3)
    corner(1, 0)
    norm(1)
    norm(2)
    send_x()
    norm(3)
    pass_x(5)
    pass_on(1, 3, 1)
    send_x()
    norm(4)
    corner(1, 1)
    narrow(0)
    pass_x(6)
    pass_on(1, 2, 1)
    pass_on(1, 3, 0)
    pass_on(1, 1, 0)
    pass_on(1, 2, 0)
    norm(5)
    pass_on(0, 1, 0)
    pass_on(1, 0, 1)
    pass_x(7)
    corner(1, 2)
    norm(6)
    corner(1, 3)
    norm(7)
    narrow(1)
    for copy in sib:
        copy.wait_recv()
    for move in laid:
        move.wait()
    copies.finish()


def gather_all(x, wg, wx, thin, par, segc, segr, groups):
    _, length, feat = x.shape
    shard, cb = wg.shape
    anywhere = pl.BlockSpec(memory_space=pl.ANY)
    inside = pl.BlockSpec(memory_space=pltpu.VMEM)
    weight = jax.ShapeDtypeStruct((2, 8 * shard, cb), BF16)
    return pl.pallas_call(
        gather_kernel,
        in_specs=[anywhere] * 5 + [inside] * 2,
        out_specs=[inside] * 16 + [anywhere] * 2,
        out_shape=(
            jax.ShapeDtypeStruct((length, 4 * feat), BF16),
            jax.ShapeDtypeStruct((2, 4 * shard, length), BF16),
            jax.ShapeDtypeStruct((length, 128), F32),
            jax.ShapeDtypeStruct((4,) + par.shape, F32),
            jax.ShapeDtypeStruct((8 * shard, 2 * STATE + 128), BF16),
            jax.ShapeDtypeStruct((length, 2 * STATE + 128), F32),
            jax.ShapeDtypeStruct((8, 128), F32),
            jax.ShapeDtypeStruct((8, 2 * STATE), F32),
        )
        + prep_shapes(length, groups)
        + (weight, weight),
        scratch_shapes=[
            pltpu.VMEM((length, 4 * feat), BF16),
            pltpu.VMEM((4,) + par.shape, F32),
            pltpu.VMEM((8, 4) + thin.shape, BF16),
            pltpu.VMEM((2, shard, cb), BF16),
            pltpu.SemaphoreType.DMA((GATHER_COPIES,)),
            pltpu.SemaphoreType.DMA((GATHER_COPIES,)),
            pltpu.SemaphoreType.DMA((8,)),
        ],
        compiler_params=pltpu.CompilerParams(
            collective_id=0, has_side_effects=True, vmem_limit_bytes=VMEM_LIMIT
        ),
        name="gather_all",
    )(x, wg, wx, thin, par, segc, segr)


GRAD_COPIES = 96
HALVES = 2


def grad_kernel(
    raw_ref, wg_ref, wx_ref, ws_ref, nb_ref, gate_ref, nt_ref, dg_ref, dx_ref, ds_ref, small_ref, ir_ref,
    gz_ref, thin_out, small_out, own_out, away_out, row_out,
    raw_v, dn_v, wt, wst, nbt, ggv, ndv, tile_sem, pr, rowv, rowr, local, cs, cr, ts, tr, fs, fr, ss, sr, zs, zr, tfs, tfr, tss, tsr, tz, tzr,
    sbuf, srecv, szr, send, recv,
):
    h, l, r, c, x, y, rx, ry, rc = places()
    me = h * 2 + l
    zh, zl, zd = {"zh": 1 - h}, {"zl": 1 - l}, {"zh": 1 - h, "zl": 1 - l}
    to_x, to_y, to_c = {"row": rx}, {"row": ry}, {"row": rc}
    shard = gz_ref.shape[1]
    ncol = gz_ref.shape[2]
    meet((zh, zl, zd, to_x, to_y, to_c))
    copies = Copies(send, recv)
    start = copies.start

    def product(side, d_ref, at):
        return dot_nn(nt_ref[side], d_ref[:, at])

    def tiles(d_ref, body):
        width = d_ref.shape[1]
        wide = 256 if width % 256 == 0 else 128

        def one(n, carry):
            body(pl.ds(pl.multiple_of(n * wide, wide), wide))
            return carry

        lax.fori_loop(0, width // wide, one, 0)

    _, length, feat = dn_v.shape
    piece = length // HALVES
    strips = 4 * feat // 256

    def toks(p):
        return pl.ds(p * piece, piece)

    raw_copy = pltpu.make_async_copy(raw_ref.at[1], raw_v, local.at[0])
    raw_copy.start()

    def loads(k, slot):
        strip = pl.ds(pl.multiple_of(lax.rem(k, strips) * 256, 256), 256)
        rows = pl.ds(pl.multiple_of(k // strips * piece, piece), piece)
        return [
            pltpu.make_async_copy(wg_ref.at[:, strip], wt.at[slot, 0], tile_sem.at[slot, 0]),
            pltpu.make_async_copy(wx_ref.at[:, strip], wt.at[slot, 1], tile_sem.at[slot, 1]),
            pltpu.make_async_copy(ws_ref.at[strip], wst.at[slot], tile_sem.at[slot, 2]),
            pltpu.make_async_copy(nb_ref.at[rows, strip], nbt.at[slot], tile_sem.at[slot, 3]),
        ]

    for move in loads(0, 0):
        move.start()
    ggv[...] = jnp.zeros_like(ggv)
    ndv[...] = jnp.zeros_like(ndv)
    pair, far, kept = [], [], []

    def back(p):
        def strip(n, carry):
            k = p * strips + n
            slot = lax.rem(k, 2)
            for move in loads(k, slot):
                move.wait()

            @pl.when(k + 1 < HALVES * strips)
            def _():
                for move in loads(k + 1, 1 - slot):
                    move.start()

            value = dot_nt(ds_ref[toks(p), :], wst[slot])
            for m, d_ref in enumerate((dg_ref, dx_ref)):
                for b in range(2):
                    value = value + dot_nt(d_ref[toks(p), b * ncol : (b + 1) * ncol], wt[slot, m, b])
            lanes = pl.ds(pl.multiple_of(lax.rem(n, feat // 256) * 256, 256), 256)
            dn_v[n // (feat // 256), toks(p), lanes] = value.astype(BF16)
            value = value * nbt[slot].astype(F32)
            ggv[pl.ds(n, 1), :] += jnp.sum(value, axis=0, keepdims=True)
            ndv[toks(p), :] += value[:, 0:128] + value[:, 128:256]
            return carry

        lax.fori_loop(0, strips, strip, 0)
        pair.append([start(dn_v.at[2 * k + 1 - l, toks(p)], pr.at[k, toks(p)], zl) for k in range(2)])

    def pair_done(p):
        for move in pair[p]:
            move.wait_recv()
        away, own = 2 * (1 - h) + l, 2 * h + l
        value = dn_v[away, toks(p)].astype(F32) + pr[1 - h, toks(p)].astype(F32)
        dn_v[away, toks(p)] = value.astype(BF16)
        far.append(start(dn_v.at[away, toks(p)], away_out.at[toks(p)], zh))
        value = dn_v[own, toks(p)].astype(F32) + pr[h, toks(p)].astype(F32)
        dn_v[own, toks(p)] = value.astype(BF16)
        kept.append(pltpu.make_async_copy(dn_v.at[own, toks(p)], own_out.at[toks(p)], local.at[1 + p]))
        kept[p].start()

    z_copy = [start(gate_ref, zr.at[0], zh), None]

    def begin_small():
        sbuf[0] = small_ref[...]
        for n in range(strips):
            row, lanes = n // 4, slice(n % 4 * 256, n % 4 * 256 + 256)
            sbuf[0, 16 + row : 17 + row, lanes] = ggv[n : n + 1, :] / small_ref[20 + row : 21 + row, lanes]
        return start(sbuf.at[0], srecv.at[0], to_c)

    dx0, dx1 = dx_ref.at[:, 0:ncol], dx_ref.at[:, ncol : 2 * ncol]
    quarters = [
        dict(d=dx1, first=to_x, second=to_y, mine=x, along=y, swap=False),
        dict(d=dx0, first=to_y, second=to_x, mine=y, along=x, swap=True),
        dict(first=to_y, second=to_x, mine=y, along=x, swap=True),
    ]

    def spot(q, first, second):
        return 2 * first + second if q["swap"] else 2 * second + first

    def refs(i):
        if i == 4:
            return ts, tr, tfs, tfr, tss, tsr
        return cs, cr.at[i], fs.at[i // 2], fr.at[i], ss.at[i], sr.at[i]

    thin_q = dict(d=ds_ref, first=to_y, second=to_x, mine=y, along=x, swap=True)

    def gone(i, name):
        if i == 1:
            earlier = quarters[0][name]
            earlier.wait_send()
            copies.open = [move for move in copies.open if move is not earlier]

    def first_done(q):
        if "seen" not in q:
            q["f"].wait_recv()
            q["seen"] = True

    def to_core(i, q):
        out, back = refs(i)[0:2]
        if i == 2:
            q["core"] = start(raw_ref.at[0], back, to_c)
            return
        gone(i, "core")

        def body(at):
            value = product(1 - c, q["d"], at).astype(BF16)
            for j in range(4):
                out[j, :, at] = value[j * shard : (j + 1) * shard]

        tiles(q["d"], body)
        q["core"] = start(out, back, to_c)

    def to_first(i, q, after=None):
        _, back, fsend, frecv, _, _ = refs(i)
        q["core"].wait_recv()
        if i == 2:
            raw_copy.wait()
            for j in range(4):
                back[j] = (raw_v[j].astype(F32) + back[j].astype(F32)).astype(BF16)
        else:

            def body(at):
                value = product(c, q["d"], at)
                for j in range(4):
                    part = value[j * shard : (j + 1) * shard] + back[j, :, at].astype(F32)
                    back[j, :, at] = part.astype(BF16)

            tiles(q["d"], body)
        gone(i, "f")
        for n in range(2):
            fsend[n] = back[spot(q, 1 - q["mine"], n)]
        if after is not None:
            first_done(after)
        q["f"] = start(fsend, frecv, q["first"])

    def to_second(i, q):
        _, back, _, frecv, ssend, srcv = refs(i)
        first_done(q)
        far = 1 - q["along"]
        kept = back[spot(q, q["mine"], far)].astype(F32)
        ssend[...] = (kept + frecv[far].astype(F32)).astype(BF16)
        q["s"] = start(ssend, srcv, q["second"])

    def settle(i, q):
        _, back, _, frecv, _, srcv = refs(i)
        q["s"].wait_recv()
        near = q["along"]
        kept = back[spot(q, q["mine"], near)].astype(F32)
        return kept + frecv[near].astype(F32) + srcv[...].astype(F32)

    def hop_small(n, to):
        small_copy[0].wait_recv()
        sbuf[n] = sbuf[n - 1] + srecv[n - 1]
        if to is not None:
            small_copy[0] = start(sbuf.at[n], srecv.at[n], to)

    to_core(2, quarters[2])
    back(0)
    to_core(0, quarters[0])
    to_first(2, quarters[2])
    to_first(0, quarters[0])
    back(1)
    pair_done(0)
    rowv[...] = jnp.zeros_like(rowv)
    rowv[0:1, :] = jnp.sum(jnp.transpose(ndv[...]), axis=0, keepdims=True)
    rowv[1:2, :] = jnp.transpose(ir_ref[...])[0:1, :]
    row_copies = [start(rowv, rowr.at[n], to) for n, to in enumerate((zh, zl, zd))]
    to_core(1, quarters[1])
    to_second(0, quarters[0])
    to_core(4, thin_q)
    small_copy = [begin_small()]
    zs[...] = settle(0, quarters[0]).astype(BF16)
    z_copy[1] = start(zs, zr.at[1], zh)
    to_first(4, thin_q)
    hop_small(1, to_x)
    to_second(2, quarters[2])
    to_first(1, quarters[1])
    to_second(4, thin_q)
    tz[...] = settle(4, thin_q).astype(BF16)
    thin_z = []
    for n, (to, block) in enumerate(((zh, 2 * (1 - h) + l), (zl, 2 * h + 1 - l), (zd, 2 * (1 - h) + 1 - l))):
        lanes = pl.ds(pl.multiple_of(block // 2 * 128, 128), 128)
        thin_z.append(start(tz.at[:, lanes], tzr.at[n], to))
    thin_z.append(start(tz.at[:, 2 * STATE :], tzr.at[3], zh))
    hop_small(2, to_y)
    pair_done(1)
    hop_small(3, None)
    small_z = [
        start(sbuf.at[3, lo:], szr.at[n, lo:], to) for n, (to, lo) in enumerate(((zh, 8), (zl, 16), (zd, 16)))
    ]
    to_second(1, quarters[1])
    gz_ref[0] = settle(2, quarters[2])
    gz_ref[1] = settle(1, quarters[1])
    row_out[0] = rowv[...]
    for n in range(3):
        row_copies[n].wait_recv()
        row_out[n + 1] = rowr[n]
    for copy in thin_z:
        copy.wait_recv()
    for copy in small_z:
        copy.wait_recv()
    total = tz[:, pl.ds(pl.multiple_of(h * 128, 128), 128)].astype(F32)
    for n in range(3):
        total = total + tzr[n].astype(F32)
    thin_out[:, 0:128] = total
    thin_out[:, 128:256] = tz[:, 2 * STATE :].astype(F32)
    thin_out[:, 256:384] = tzr[3].astype(F32)
    small_out[...] = jnp.zeros_like(small_out)
    small_out[0] = sbuf[3]
    for n, lo in enumerate((8, 16, 16)):
        small_out[n + 1, lo:] = szr[n, lo:]
    for move in far:
        move.wait_recv()
    for move in kept:
        move.wait()
    for k in range(2):
        z_copy[k].wait_recv()
        gz_ref[k] += zr[k].astype(F32)
    copies.finish()


def grad_all(raw, wg, wx, ws, nb, gate_got, nt, dgate, dxr, d_small, small, ir):
    _, half, length = nt.shape
    feat = half // 2
    shard, cb = half // 4, dxr.shape[1] // 2
    ns = d_small.shape[1]
    inside = pl.BlockSpec(memory_space=pltpu.VMEM)
    anywhere = pl.BlockSpec(memory_space=pl.ANY)
    V = pltpu.VMEM
    return pl.pallas_call(
        grad_kernel,
        in_specs=[anywhere] * 6 + [inside] * 6,
        out_specs=[inside] * 3 + [anywhere, anywhere, inside],
        out_shape=(
            jax.ShapeDtypeStruct((2, shard, cb), F32),
            jax.ShapeDtypeStruct((shard, 384), F32),
            jax.ShapeDtypeStruct((4,) + small.shape, F32),
            jax.ShapeDtypeStruct((length, feat), BF16),
            jax.ShapeDtypeStruct((length, feat), BF16),
            jax.ShapeDtypeStruct((4, 8, length), F32),
        ),
        scratch_shapes=[
            V((4, shard, cb), BF16),
            V((4, length, feat), BF16),
            V((2, 2, 2, 256, cb), BF16),
            V((2, 256, ns), BF16),
            V((2, length // HALVES, 256), BF16),
            V((4 * feat // 256, 256), F32),
            V((length, 128), F32),
            pltpu.SemaphoreType.DMA((2, 4)),
            V((2, length, feat), BF16),
            V((8, length), F32),
            V((3, 8, length), F32),
            pltpu.SemaphoreType.DMA((1 + HALVES,)),
            V((4, shard, cb), BF16),
            V((3, 4, shard, cb), BF16),
            V((4, shard, ns), BF16),
            V((4, shard, ns), BF16),
            V((2, 2, shard, cb), BF16),
            V((3, 2, shard, cb), BF16),
            V((3, shard, cb), BF16),
            V((3, shard, cb), BF16),
            V((shard, cb), BF16),
            V((2, shard, cb), BF16),
            V((2, shard, ns), BF16),
            V((2, shard, ns), BF16),
            V((shard, ns), BF16),
            V((shard, ns), BF16),
            V((shard, ns), BF16),
            V((4, shard, 128), BF16),
            V((4,) + small.shape, F32),
            V((3,) + small.shape, F32),
            V((3,) + small.shape, F32),
            pltpu.SemaphoreType.DMA((GRAD_COPIES,)),
            pltpu.SemaphoreType.DMA((GRAD_COPIES,)),
        ],
        compiler_params=pltpu.CompilerParams(
            collective_id=1, has_side_effects=True, vmem_limit_bytes=VMEM_LIMIT
        ),
        name="grad_all",
    )(raw, wg, wx, ws, nb, gate_got, nt, dgate, dxr, d_small, small, ir)


def table(send, recv):
    def copy(n, src, dst, to):
        return pltpu.make_async_remote_copy(
            src_ref=src, dst_ref=dst, send_sem=send.at[n], recv_sem=recv.at[n],
            device_id=to, device_id_type=MESH_ID,
        )

    return copy


SCAN_COPIES = 32


def scan_all_kernel(*refs):
    (cot_ref, out_ref, gains_ref), refs = refs[0:3], refs[3:]
    ins, refs = refs[0:11], refs[11:]
    gate_ref, xr_ref, v_ref, y_ref, hid_ref, sq_ref, st_ref, po_ref, ir_ref, cf_ref, wo_ref = refs[0:11]
    xs, state, cot_v, out_v, rows_v, sums, other, send, recv, local, row_sem = refs[11:]
    h, l, r, c, x, y, rx, ry, rc = places()
    rd = rx + ry - r
    me, zhp = h * 2 + l, (1 - h) * 2 + l
    zh, zl = {"zh": 1 - h}, {"zl": 1 - l}
    to_x, to_y, to_c = {"row": rx}, {"row": ry}, {"row": rc}
    length, feat = cot_ref.shape[1], cot_ref.shape[2]
    piece = length // PIECES
    shard = out_ref.shape[0]
    copy = table(send, recv)
    step = pl.program_id(0)
    channels = hid_ref.shape[1]
    groups = channels // GROUP

    def toks(p):
        return pl.ds(p * piece, piece)

    def cols(block):
        return pl.ds(pl.multiple_of(block * feat, feat), feat)

    def rows(row, half=None):
        if half is None:
            return pl.ds(pl.multiple_of(row * shard, shard), shard)
        return pl.ds(pl.multiple_of(row * shard + half * (shard // 2), shard // 2), shard // 2)

    def g1(p):
        return copy(p, cot_ref.at[1 - h, toks(p)], cf_ref.at[toks(p), cols(me)], zh)

    def g2():
        return copy(4, cot_ref.at[h], cf_ref.at[:, cols(me)], zl)

    def g3(p):
        part = cf_ref.at[toks(p), cols(zhp)]
        return copy(8 + p, part, part, zl)

    def wz():
        return copy(12, out_ref, wo_ref.at[1, rows(r)], zh)

    def own(n):
        return copy(13 + n, out_ref, wo_ref.at[0, rows(r)], (to_x, to_y, to_c)[n])

    def got(n):
        part = wo_ref.at[1, rows(r)]
        return copy(16 + n, part, part, (to_x, to_y, to_c)[n])

    def diag(b, n):
        part = wo_ref.at[b, rows((rx, ry)[n], n)]
        return copy(19 + 5 * b + n, part, part, (to_y, to_x)[n])

    def sib(b, n):
        part = wo_ref.at[b, rows((rx, ry, rd)[n])]
        return copy(21 + 5 * b + n, part, part, to_c)

    def load(n):
        return pltpu.make_async_copy((cot_ref.at[h], out_ref)[n], (cot_v, out_v)[n], local.at[n])

    def keep(n):
        to = (cf_ref.at[:, cols(me)], wo_ref.at[0, rows(r)])[n]
        return pltpu.make_async_copy((cot_v, out_v)[n], to, local.at[2 + n])

    def load_rows(n, slot):
        part = pl.ds(pl.multiple_of(n * 256, 256), 256)
        return pltpu.make_async_copy(wo_ref.at[:, part], rows_v.at[slot], row_sem.at[slot])

    def onward(p):
        g1(p).wait_recv()
        g3(p).start()

    def step0():
        meet((zh, zl, to_x, to_y, to_c))
        wz().start()
        for n in range(2):
            load(n).start()
        for n in range(3):
            own(n).start()
        g2().start()

    def step1():
        for n in range(2):
            load(n).wait()
            keep(n).start()

    def step2():
        g1(0).start()
        for n in range(2):
            own(n).wait_recv()
        for n in range(2):
            diag(0, n).start()
            sib(0, n).start()

    def step3():
        g1(1).start()
        wz().wait_recv()
        for n in range(3):
            got(n).start()

    def step4():
        g1(2).start()
        g1(3).start()
        for n in range(2):
            diag(0, n).wait_recv()
        sib(0, 2).start()

    def step5():
        for n in range(2):
            got(n).wait_recv()
        for n in range(2):
            diag(1, n).start()
            sib(1, n).start()

    def step6():
        for n in range(2):
            diag(1, n).wait_recv()
        sib(1, 2).start()
        onward(0)

    def step8():
        onward(1)

    def step9():
        onward(2)

    def step10():
        onward(3)

    acts = {
        0: step0, 1: step1, 2: step2, 3: step3, 4: step4, 5: step5, 6: step6, 8: step8, 9: step9, 10: step10,
    }
    for at, act in acts.items():
        pl.when(step == at)(act)

    @pl.when(step < groups)
    def _():
        part = hid_ref.at[:, pl.ds(pl.multiple_of(step * GROUP, GROUP), GROUP)]
        scan_kernel(*ins, gate_ref, xr_ref, v_ref, y_ref, part, sq_ref, st_ref, xs, state)

    def swap_sums():
        return copy(29, sums, other, zl)

    @pl.when(step == groups)
    def _():
        sums[...] = jnp.zeros_like(sums)
        sums[0:1, :] = jnp.sum(jnp.transpose(sq_ref[...]), axis=0, keepdims=True)
        swap_sums().start()
        keep(1).wait()
        for move in [own(2), got(2)] + [sib(b, n) for b in range(2) for n in range(3)]:
            move.wait_recv()
        load_rows(0, 0).start()
        swap_sums().wait()
        root = lax.rsqrt((sums[0:1, :] + other[0:1, :]) / (2 * channels) + EPS)
        ir_ref[...] = jnp.transpose(jnp.broadcast_to(root, (128, length)))
        for n in range(groups):
            part = slice(n * GROUP, (n + 1) * GROUP)
            value = hid_ref[:, part].astype(F32) * twice(ir_ref[...]) * gains_ref[6:7, part]
            hid_ref[:, part] = value.astype(BF16)

    @pl.when(step >= groups)
    def _():
        n = step - groups
        slot = lax.rem(n, 2)
        load_rows(n, slot).wait()

        @pl.when(step < 2 * groups - 1)
        def _():
            load_rows(n + 1, 1 - slot).start()

        half = channels // 2
        out = dot_nt(hid_ref[:, 0:half], rows_v[slot, 0]) + dot_nt(hid_ref[:, half:], rows_v[slot, 1])
        po_ref[0] = out.astype(BF16)

    @pl.when(step == 2 * groups - 1)
    def _():
        late = [g2()] + [g3(p) for p in range(PIECES)]
        for move in late:
            move.wait_recv()
        keep(0).wait()
        sent = [g1(p) for p in range(PIECES)] + late + [wz()]
        sent += [own(n) for n in range(3)] + [got(n) for n in range(3)]
        sent += [diag(b, n) for b in range(2) for n in range(2)]
        sent += [sib(b, n) for b in range(2) for n in range(3)]
        for move in sent:
            move.wait_send()


def scan_all(cot, out_proj, nb, wg, wx, chan, *rest):
    length, width = nb.shape
    channels = chan.shape[1]
    cb = channels // 2
    feat, shard = width // 4, out_proj.shape[0]
    groups = channels // GROUP
    per = feat // 256
    assert groups == 8 and width // 256 == groups
    in_specs, out_specs = scan_specs(length, width, cb // GROUP)
    out_specs[4] = once((length, channels))
    anywhere = pl.BlockSpec(memory_space=pl.ANY)
    shapes = scan_shapes(length, channels)

    def strip(g):
        n = jnp.maximum(g - groups, 0)
        return n // per, 0, n % per

    return pl.pallas_call(
        scan_all_kernel,
        grid=(2 * groups,),
        in_specs=[anywhere] * 2 + [once((8, channels))] + in_specs,
        out_specs=out_specs
        + [pl.BlockSpec((1, length, 256), strip), once((length, 128)), anywhere, anywhere],
        out_shape=shapes
        + (
            jax.ShapeDtypeStruct((4, length, feat), BF16),
            jax.ShapeDtypeStruct((length, 128), F32),
            jax.ShapeDtypeStruct((length, width), BF16),
            jax.ShapeDtypeStruct((2, width, cb), BF16),
        ),
        scratch_shapes=[
            pltpu.VMEM((length, GROUP), F32),
            pltpu.VMEM((STATE, GROUP), F32),
            pltpu.VMEM((length, feat), BF16),
            pltpu.VMEM((shard, cb), BF16),
            pltpu.VMEM((2, 2, 256, cb), BF16),
            pltpu.VMEM((8, length), F32),
            pltpu.VMEM((8, length), F32),
            pltpu.SemaphoreType.DMA((SCAN_COPIES,)),
            pltpu.SemaphoreType.DMA((SCAN_COPIES,)),
            pltpu.SemaphoreType.DMA((4,)),
            pltpu.SemaphoreType.DMA((2,)),
        ],
        compiler_params=pltpu.CompilerParams(
            collective_id=2, has_side_effects=True, vmem_limit_bytes=VMEM_LIMIT
        ),
        name="scan_all",
    )(cot, out_proj, chan, nb, wg, wx, chan, *rest)


EARLY = 640


def mid_kernel(
    cf_ref, wc_ref, hid_ref, ir_ref, po_ref,
    dh_ref, go_ref, coef_ref, ig_ref, sum_out,
    ct, dots, sums, other, send, recv,
):
    phase, g = pl.program_id(0), pl.program_id(1)
    last = pl.num_programs(1) - 1
    length, channels = hid_ref.shape
    shard = go_ref.shape[1]
    h, l = lax.axis_index("zh"), lax.axis_index("zl")
    to, zd = {"zl": 1 - l}, {"zh": 1 - h, "zl": 1 - l}
    copy = table(send, recv)
    at = pl.ds(pl.multiple_of(g * GROUP, GROUP), GROUP)

    def part():
        return copy(1, po_ref.at[2 * (1 - h) + 1 - l, pl.ds(0, EARLY)], sum_out, zd)

    @pl.when((phase == 0) & (g == 0))
    def _():
        meet((to, zd))
        part().start()
        dots[...] = jnp.zeros_like(dots)

    @pl.when(phase == 0)
    def _():
        dh = dot_nn(cf_ref[...], wc_ref[...])
        dh_ref[...] = dh.astype(BF16)
        term = dh * hid_ref[:, at].astype(F32)
        dots[...] += term[:, 0:128] + term[:, 128:256]
        ig_ref[...] = jnp.broadcast_to(jnp.sum(term, axis=0, keepdims=True), ig_ref.shape)
        ct[at, :] = turned(cf_ref[:, at])

    @pl.when((phase == 0) & (g == last))
    def _():
        sums[...] = jnp.zeros_like(sums)
        sums[0:1, :] = jnp.sum(jnp.transpose(dots[...]), axis=0, keepdims=True)
        move = copy(0, sums, other, to)
        move.start()
        move.wait()
        both = jnp.broadcast_to(sums[0:1, :] + other[0:1, :], (128, length))
        coef_ref[...] = jnp.transpose(both) * ir_ref[...] * ir_ref[...] / (2 * channels)

    @pl.when(phase == 1)
    def _():
        right = hid_ref[:, at]
        for n in range(go_ref.shape[0] // 4):
            value = dot_nn(ct[4 * n * shard : 4 * (n + 1) * shard, :], right).astype(BF16)
            for m in range(4):
                go_ref[4 * n + m] = value[m * shard : (m + 1) * shard]

    @pl.when((phase == 1) & (g == last))
    def _():
        part().wait()


def middle(cf, wo, hid, ir, po):
    length, width = cf.shape
    channels = hid.shape[1]
    gb = channels // 2 // GROUP
    n = channels // GROUP
    shard = width // 8
    assert n == width // 256

    def const(shape):
        return pl.BlockSpec(shape, lambda p, g: (0,) * len(shape), pipeline_mode=pl.Buffered(1))

    def first(p, g):
        return jnp.where(p == 0, g, n - 1)

    return pl.pallas_call(
        mid_kernel,
        grid=(2, n),
        in_specs=[
            const((length, width)),
            pl.BlockSpec((None, width, GROUP), lambda p, g: (first(p, g) // gb, 0, first(p, g) % gb)),
            const((length, channels)),
            const((length, 128)),
            pl.BlockSpec(memory_space=pl.ANY),
        ],
        out_specs=[
            pl.BlockSpec((length, GROUP), lambda p, g: (0, first(p, g))),
            pl.BlockSpec((8, shard, GROUP), lambda p, g: (0, 0, g * p)),
            const((length, 128)),
            pl.BlockSpec((8, GROUP), lambda p, g: (0, first(p, g))),
            pl.BlockSpec(memory_space=pl.ANY),
        ],
        out_shape=(
            jax.ShapeDtypeStruct((length, channels), BF16),
            jax.ShapeDtypeStruct((8, shard, channels), BF16),
            jax.ShapeDtypeStruct((length, 128), F32),
            jax.ShapeDtypeStruct((8, channels), F32),
            jax.ShapeDtypeStruct((EARLY, po.shape[2]), BF16),
        ),
        scratch_shapes=[
            pltpu.VMEM((width, length), BF16),
            pltpu.VMEM((length, 128), F32),
            pltpu.VMEM((8, length), F32),
            pltpu.VMEM((8, length), F32),
            pltpu.SemaphoreType.DMA((2,)),
            pltpu.SemaphoreType.DMA((2,)),
        ],
        compiler_params=pltpu.CompilerParams(
            collective_id=3, has_side_effects=True, vmem_limit_bytes=VMEM_LIMIT
        ),
        name="middle",
    )(cf, wo, hid, ir, po)


SHIP_COPIES = 24


def scan_grad_all_kernel(*refs):
    (go_ref, po_ref, nt_ref), refs = refs[0:3], refs[3:]
    ins, refs = refs[0:21], refs[21:]
    outs, refs = refs[0:5], refs[5:]
    own_out, raw_out, gate_out, sum0, sum1, sum2 = refs[0:6]
    scratch, refs = refs[6:14], refs[14:]
    gm, gr, gf, gfr, gs, gsr, gz, gzr, tm, ts, tr, tf, tfr, tg, tgr, send, recv, local = refs
    h, l, _, c, x, y, rx, ry, rc = places()
    zh, zl, zd = {"zh": 1 - h}, {"zl": 1 - l}, {"zh": 1 - h, "zl": 1 - l}
    to_x, to_y, to_c = {"row": rx}, {"row": ry}, {"row": rc}
    shard, cb = own_out.shape
    copy = table(send, recv)
    step = pl.program_id(0)
    groups = pl.num_programs(0)
    first, second = (to_x, to_y), (to_y, to_x)
    mine, along = (x, y), (y, x)
    dgate_ref = outs[0]

    def near(b, j):
        lanes = slice(b * cb, (b + 1) * cb)
        return pltpu.make_async_copy(go_ref.at[2 * j + c, :, lanes], gm.at[b, j], local.at[4 * b + j])

    def core(b, j):
        lanes = slice(b * cb, (b + 1) * cb)
        return copy(4 * b + j, go_ref.at[2 * j + 1 - c, :, lanes], gr.at[b, j], to_c)

    def hop1(b):
        return copy(8 + b, gf.at[b], gfr.at[b], first[b])

    def hop2(b):
        return copy(10 + b, gs.at[b], gsr.at[b], second[b])

    def hop3():
        return copy(18, gz, gzr, zh)

    def settle(b):
        hop2(b).wait_recv()
        own = along[b]
        return add(gm[b, spot(b, mine[b], own)], gfr[b, own]) + gsr[b].astype(F32)

    def out_sums():
        late = pl.ds(EARLY, po_ref.shape[1] - EARLY)
        return [
            copy(12, po_ref.at[2 * h + 1 - l], sum0, zl),
            copy(13, po_ref.at[2 * (1 - h) + l], sum1, zh),
            copy(14, po_ref.at[2 * (1 - h) + 1 - l, late], sum2, zd),
        ]

    def gate_core():
        return copy(15, ts, tr, to_c)

    def gate_hop1():
        return copy(16, tf, tfr, to_y)

    def gate_hop2():
        return copy(17, tg, tgr, to_x)

    def spot(b, at_first, at_second):
        return 2 * at_first + at_second if b else 2 * at_second + at_first

    def add(a, b):
        return a.astype(F32) + b.astype(F32)

    @pl.when(step == 0)
    def _():
        meet((zh, zl, zd, to_x, to_y, to_c))
        for b in range(2):
            for j in range(4):
                core(b, j).start()
                near(b, j).start()
        for move in out_sums():
            move.start()

    @pl.when(step == 1)
    def _():
        for b in range(2):
            for j in range(4):
                near(b, j).wait()
                core(b, j).wait_recv()
            for s in range(2):
                j = spot(b, 1 - mine[b], s)
                gf[b, s] = add(gm[b, j], gr[b, j]).astype(BF16)
            hop1(b).start()
            for s in range(2):
                j = spot(b, mine[b], s)
                gm[b, j] = add(gm[b, j], gr[b, j]).astype(BF16)

    @pl.when(step == 4)
    def _():
        for b in range(2):
            hop1(b).wait_recv()
            far = 1 - along[b]
            gs[b] = add(gm[b, spot(b, mine[b], far)], gfr[b, far]).astype(BF16)
            hop2(b).start()

    @pl.when(step == 5)
    def _():
        gate_core().wait_recv()
        for n in range(2):
            tf[n] = add(tm[spot(1, 1 - y, n)], tr[spot(1, 1 - y, n)]).astype(BF16)
        gate_hop1().start()
        for n in range(2):
            tm[spot(1, y, n)] = add(tm[spot(1, y, n)], tr[spot(1, y, n)]).astype(BF16)

    @pl.when(step == 6)
    def _():
        gz[...] = settle(1).astype(BF16)
        hop3().start()

    @pl.when(step == groups - 1)
    def _():
        gate_hop1().wait_recv()
        tg[...] = add(tm[spot(1, y, 1 - x)], tfr[1 - x]).astype(BF16)
        gate_hop2().start()

    scan_grad_kernel(lax.rem(step + groups // 2, groups), *ins, *outs, *scratch)

    def products(other, own):
        for side, ref in ((1 - c, other), (c, own)):
            value = dot_nn(nt_ref[side], dgate_ref[...]).astype(BF16)
            for j in range(4):
                ref[j] = value[j * shard : (j + 1) * shard]

    @pl.when(step < groups // 2)
    def _():
        lanes = pl.ds(pl.multiple_of(step * GROUP, GROUP), GROUP)
        products(ts.at[:, :, lanes], tm.at[:, :, lanes])

    @pl.when(step == groups // 2 - 1)
    def _():
        gate_core().start()

    @pl.when(step >= groups // 2)
    def _():
        products(raw_out.at[0], raw_out.at[1])

    @pl.when(step == groups - 1)
    def _():
        own_out[...] = settle(0)
        hop3().wait_recv()
        own_out[...] += gzr[...].astype(F32)
        gate_hop2().wait_recv()
        total = add(tm[spot(1, y, x)], tfr[x]) + tgr[...].astype(F32)
        gate_out[...] = total.astype(BF16)
        for b in range(2):
            for j in range(4):
                core(b, j).wait_send()
            hop1(b).wait_send()
            hop2(b).wait_send()
        for move in (gate_core(), gate_hop1(), gate_hop2(), hop3()):
            move.wait_send()
        for move in out_sums():
            move.wait()


def scan_grad_all(go, po, nt, *args):
    length, channels = args[0].shape
    groups = channels // GROUP
    ins, outs, shapes, scratch = scan_grad_specs(length, channels, groups // 2)
    _, shard, _ = go.shape
    feat = po.shape[2]
    cb = channels // 2
    anywhere = pl.BlockSpec(memory_space=pl.ANY)
    V = pltpu.VMEM
    return pl.pallas_call(
        scan_grad_all_kernel,
        grid=(groups,),
        in_specs=[anywhere, anywhere, once(nt.shape)] + ins,
        out_specs=outs
        + [
            once((shard, cb)),
            pl.BlockSpec((2, 4, shard, GROUP), lambda g: (0, 0, 0, jnp.maximum(g - groups // 2, 0))),
            once((shard, cb)),
            anywhere,
            anywhere,
            anywhere,
        ],
        out_shape=shapes
        + (
            jax.ShapeDtypeStruct((shard, cb), F32),
            jax.ShapeDtypeStruct((2, 4, shard, cb), BF16),
            jax.ShapeDtypeStruct((shard, cb), BF16),
            jax.ShapeDtypeStruct((length, feat), BF16),
            jax.ShapeDtypeStruct((length, feat), BF16),
            jax.ShapeDtypeStruct((length - EARLY, feat), BF16),
        ),
        scratch_shapes=scratch
        + [
            V((2, 4, shard, cb), BF16),
            V((2, 4, shard, cb), BF16),
            V((2, 2, shard, cb), BF16),
            V((2, 2, shard, cb), BF16),
            V((2, shard, cb), BF16),
            V((2, shard, cb), BF16),
            V((shard, cb), BF16),
            V((shard, cb), BF16),
            V((4, shard, cb), BF16),
            V((4, shard, cb), BF16),
            V((4, shard, cb), BF16),
            V((2, shard, cb), BF16),
            V((2, shard, cb), BF16),
            V((shard, cb), BF16),
            V((shard, cb), BF16),
            pltpu.SemaphoreType.DMA((SHIP_COPIES,)),
            pltpu.SemaphoreType.DMA((SHIP_COPIES,)),
            pltpu.SemaphoreType.DMA((8,)),
        ],
        compiler_params=pltpu.CompilerParams(
            collective_id=4, has_side_effects=True, vmem_limit_bytes=VMEM_LIMIT
        ),
        name="scan_grad_all",
    )(go, po, nt, *args)


def finish_kernel(
    at_ref, tok_ref, cot_ref, s0_ref, s1_ref, s2_ref, s3_ref, own_ref, away_ref, rowv_ref, small_ref,
    thin_ref, gain_ref, po_ref,
    out_ref, grad_ref, gg_ref, cx_ref, cb_ref, ig_ref, heads_ref, bct_ref, bcb_ref, tb_ref, td_ref,
    po_v, root_v, tail_v, sem,
):
    h, l = at_ref[0], at_ref[1]
    _, length, feat = tok_ref.shape
    hb = td_ref.shape[1]
    block = pltpu.make_async_copy(po_ref.at[2 * h + l], po_v, sem.at[0])
    block.start()

    def pick(v):
        n = v.shape[1] // 2
        v = jnp.where(h == 0, v[:, 0:n], v[:, n:])
        return half(v)

    def half(v):
        n = v.shape[1] // 2
        return jnp.where(l == 0, v[:, 0:n], v[:, n:])

    chg = small_ref[0, 0:8] + small_ref[1, 8:16]
    cx_ref[...] = chg[0:KW]
    cb_ref[...] = chg[4:5]
    ig_ref[...] = chg[6:7]
    wide = chg.shape[1]
    pick_r = lax.broadcasted_iota(jnp.int32, (wide, 128), 0)
    pick_c = lax.broadcasted_iota(jnp.int32, (wide, 128), 1)
    heads_ref[...] = dot_exact(chg, (pick_r // HEADDIM == pick_c).astype(F32))
    heads_ref[0:1, :] = chg[7:8, 0:128]
    last = small_ref[0, 16:24] + small_ref[1, 16:24] + small_ref[2, 16:24] + small_ref[3, 16:24]
    gg_ref[...] = half(jnp.where(h == 0, last[0:1], last[1:2]))
    for n in range(KW):
        bct_ref[n : n + 1, :] = pick(last[2:3, n * 256 : n * 256 + 256])
    bcb_ref[...] = pick(last[3:4, 0:256])
    tb_ref[...] = half(thin_ref[:, 0:128])
    td_ref[...] = thin_ref[:, 128 : 128 + hb] + thin_ref[:, 256 + hb : 256 + 2 * hb]

    def column(v):
        return jnp.transpose(jnp.broadcast_to(v, (128, length)))

    for n in range(2):
        root = rowv_ref[n, 1:2]
        dots = rowv_ref[n, 0:1] + rowv_ref[n + 2, 0:1]
        root_v[n] = column(root)
        tail_v[n] = column(root * root / (4 * feat) * dots)
    block.wait()

    def piece(p, carry):
        rows = pl.ds(pl.multiple_of(p * 128, 128), 128)
        for n, seq, d_ref in ((0, h, own_ref), (1, 1 - h, away_ref)):
            x = tok_ref[seq, rows].astype(F32)
            root = jnp.concatenate([root_v[n, rows, :]] * (feat // 128), axis=1)
            tail = jnp.concatenate([tail_v[n, rows, :]] * (feat // 128), axis=1)
            grad = cot_ref[seq, rows].astype(F32) + root * gain_ref[...] * d_ref[rows].astype(F32)
            grad_ref[seq, rows] = (grad - x * tail).astype(BF16)
        total = tok_ref[h, rows].astype(F32) + po_v[rows].astype(F32) + s0_ref[rows].astype(F32)
        out_ref[h, rows] = total.astype(BF16)
        return carry

    lax.fori_loop(0, length // 128, piece, 0)
    for lo, hi, part in ((0, EARLY, s3_ref), (EARLY, length, s2_ref)):
        total = tok_ref[1 - h, lo:hi].astype(F32) + s1_ref[lo:hi].astype(F32) + part[...].astype(F32)
        out_ref[1 - h, lo:hi] = total.astype(BF16)


def finish(at, tok, cot, s0, s1, s2, s3, own, away, rowv, small, thin, gain, po, hb):
    _, length, feat = tok.shape
    shard, cb = thin.shape[0], small.shape[2]
    inside = pl.BlockSpec(memory_space=pltpu.VMEM)
    rows = jax.ShapeDtypeStruct((2, length, feat), BF16)

    def f32(*shape):
        return jax.ShapeDtypeStruct(shape, F32)

    return pl.pallas_call(
        finish_kernel,
        in_specs=[pl.BlockSpec(memory_space=pltpu.SMEM)] + [inside] * 12 + [pl.BlockSpec(memory_space=pl.ANY)],
        out_specs=[inside] * 11,
        out_shape=(
            rows, rows, f32(1, feat), f32(KW, cb), f32(1, cb), f32(1, cb), f32(8, 128), f32(KW, STATE // 2),
            f32(1, STATE // 2), f32(shard, STATE // 2), f32(shard, hb),
        ),
        scratch_shapes=[
            pltpu.VMEM((length, feat), BF16),
            pltpu.VMEM((2, length, 128), F32),
            pltpu.VMEM((2, length, 128), F32),
            pltpu.SemaphoreType.DMA((1,)),
        ],
        compiler_params=pltpu.CompilerParams(vmem_limit_bytes=VMEM_LIMIT),
        name="finish",
    )(at, tok, cot, s0, s1, s2, s3, own, away, rowv, small, thin, gain, po)


def build(nrow, nl):
    direct = nrow == 8 and nl == 2
    col = ("zh", "zl")

    def swap(v):
        return lax.ppermute(v, "zh", [(0, 1), (1, 0)])

    def pair_sum(v):
        return lax.psum(v, "zl")

    def row_gather(v):
        return lax.all_gather(v, "row", axis=0, tiled=True)

    def row_scatter(v):
        return lax.psum_scatter(v, "row", scatter_dimension=0, tiled=True)

    def per_device(
        tokens, segment_ids, norm_gain, in_zx, in_dt, in_bc, conv_x, conv_x_bias, conv_bc,
        conv_bc_bias, dt_bias, a_log, d_skip, inner_gain, out_proj, cotangent,
    ):
        seq_count, length = segment_ids.shape
        assert seq_count == 2
        feat = tokens.shape[1]
        width = feat * 2 * nl
        cb = inner_gain.shape[0]
        hb = dt_bias.shape[0]
        inner = cb * 2 * nl
        blocks = length // SPAN
        gb = cb // GROUP
        mh = lax.axis_index("zh")
        ml = lax.axis_index("zl")
        first_h = mh == 0
        here = mh * nl + ml
        bcn = conv_bc.shape[1]

        def mine(v, axis=0):
            return lax.dynamic_index_in_dim(v, mh, axis, keepdims=False)

        def other(v, axis=0):
            return lax.dynamic_index_in_dim(v, 1 - mh, axis, keepdims=False)

        def seqs(v):
            return v.reshape(2, length, feat)

        def by_seq(own, away):
            return jnp.where(first_h, jnp.stack([own, away]), jnp.stack([away, own]))

        def place(own, away):
            both = jnp.zeros((2,) + own.shape, own.dtype)
            both = lax.dynamic_update_slice(both, own[None], (mh, 0, 0))
            return lax.dynamic_update_slice(both, away[None], (1 - mh, 0, 0)).reshape(-1, own.shape[1])

        def gather_features(v):
            own, away = mine(seqs(v)), other(seqs(v))
            both = by_seq(own, swap(away))
            every = jnp.moveaxis(lax.all_gather(both, "zl"), 0, 1)
            return jnp.transpose(every, (2, 0, 1, 3)).reshape(length, width)

        def scatter_features(v):
            parts = v.reshape(length, 2, nl, feat)
            both = lax.psum_scatter(parts, "zl", scatter_dimension=2, tiled=False)
            return by_seq(mine(both, 1), swap(other(both, 1))).astype(F32)

        chan = jnp.concatenate(
            [
                conv_x,
                conv_x_bias[None],
                jnp.repeat(d_skip, HEADDIM)[None],
                inner_gain[None],
                jnp.pad(jnp.concatenate([dt_bias, a_log]), (0, cb - 2 * hb))[None],
            ],
            axis=0,
        )
        thin = jnp.concatenate([in_bc, in_dt], axis=1)
        bc_rows = jnp.concatenate([conv_bc, conv_bc_bias[None]], axis=0)
        seg = mine(segment_ids)
        segc = jnp.broadcast_to(seg[:, None], (length, 128))
        segr = jnp.broadcast_to(seg[None, :], (8, length))
        if direct:
            extra = jnp.zeros((8, cb), F32)
            extra = lax.dynamic_update_slice(extra, norm_gain[None], (0, 0))
            extra = lax.dynamic_update_slice(extra, bc_rows, (1, here * bcn))
            extra = lax.dynamic_update_slice(extra, jnp.stack([dt_bias, a_log]), (6, 0))
            thin = jnp.pad(thin, ((0, 0), (0, 128 - thin.shape[1])))
            (
                normed, normed_t, inv_root, par, w_small, small, hp, bcp,
                bc, bct, gmat, gtmat, colp, cumt, kexp, lag, w_gate, w_x,
            ) = gather_all(
                seqs(tokens), in_zx[:, 0], in_zx[:, 1], thin, jnp.concatenate([chan, extra], axis=0),
                segc, segr, 2 * gb,
            )
            chan_got = lax.dynamic_index_in_dim(par, (1 - mh) * nl + ml, 0, keepdims=False)[0:8]
            gain = par[:, 8, :feat].reshape(width)
        else:
            chan_got = swap(chan)
            packed = jnp.concatenate([norm_gain, bc_rows.reshape(-1)])
            packs = lax.all_gather(packed, col)
            gain = packs[:, :feat].reshape(width)
            bc_all = jnp.moveaxis(packs[:, feat:].reshape(-1, KW + 1, bcn), 0, 1)
            bcp = jnp.pad(bc_all.reshape(KW + 1, 2 * STATE), ((0, 7 - KW), (0, 0)))
            hp = jnp.concatenate([c[7, : 2 * hb].reshape(2, hb) for c in (chan, chan_got)], axis=1)
            hp = jnp.pad(hp, ((0, 6), (0, 128 - 2 * hb)))
            thin = lax.all_gather(thin, ("row", "zh", "zl")).reshape(nrow, 2, nl, -1, bcn + hb)
            thin = jnp.moveaxis(thin, 3, 1).reshape(width, 2, nl, bcn + hb)
            w_gate = jnp.stack([row_gather(w) for w in (in_zx[:, 0], swap(in_zx[:, 0]))])
            w_x = jnp.stack([row_gather(w) for w in (in_zx[:, 1], swap(in_zx[:, 1]))])
            w_bc = thin[..., :bcn].reshape(width, 2 * STATE)
            w_dt = lax.dynamic_index_in_dim(thin[..., bcn:], ml, 2, keepdims=False)
            w_small = jnp.concatenate([w_bc, mine(w_dt, 1), other(w_dt, 1)], axis=1)
            w_small = jnp.pad(w_small, ((0, 0), (0, 384 - w_small.shape[1])))
            x32 = gather_features(tokens).astype(F32)
            inv_root = lax.rsqrt(jnp.mean(x32 * x32, axis=1, keepdims=True) + EPS)
            normed = (x32 * inv_root * gain).astype(BF16)
            small = dot_nn(normed, w_small)
            bc, bct, gmat, gtmat, colp, cumt, kexp, lag = prep(small, segc, segr, bcp, hp, 2 * gb)
        chans = jnp.concatenate([chan, chan_got], axis=1)
        kexp = jnp.repeat(kexp[:, : 2 * hb], HEADDIM, axis=1)

        seq_args = (lag, bc, bct, gmat, colp, cumt, kexp)
        gain_in = chans[6]
        if direct:
            gates, xrs, vs, ys, hidden, _, sts, partial_out, ir, c_full, w_out = scan_all(
                seqs(cotangent), out_proj, normed, w_gate, w_x, chans, *seq_args
            )
            dh, g_out, cf, g_ig, sum3 = middle(c_full, w_out, hidden, ir, partial_out)
        else:
            w_out = [row_gather(w) for w in (out_proj, swap(out_proj))]
            c_full = gather_features(cotangent)
            gates, xrs, vs, ys, gateds, sq, sts = scan(normed, w_gate, w_x, chans, *seq_args)
            dh = jnp.concatenate([dot_nn(c_full, w).astype(BF16) for w in w_out], axis=1)
            gate_sq = pair_sum(jnp.sum(sq, axis=1))
            inner_root = lax.rsqrt(gate_sq / inner + EPS)[:, None]
            gate_dot = jnp.sum(dh.astype(F32) * gateds.astype(F32) * gain_in, axis=1)
            gate_dot = pair_sum(gate_dot)[:, None]
            hidden = (gateds.astype(F32) * inner_root * gain_in).astype(BF16)
            partial_out = dot_nt(hidden[:, :cb], w_out[0]) + dot_nt(hidden[:, cb:], w_out[1])
            partial_out = partial_out.astype(BF16)
            ir = jnp.broadcast_to(inner_root, (length, 128))
            cf = jnp.broadcast_to(inner_root**3 / inner * gate_dot, (length, 128))
            g_out = [dot_tn(c_full, hidden[:, :cb]), dot_tn(c_full, hidden[:, cb:])]
            g_out = [row_scatter(g.astype(BF16)) for g in g_out]
            g_wout = g_out[0].astype(F32) + swap(g_out[1]).astype(F32)
            out_here = scatter_features(partial_out)
            g_ig = jnp.sum(dh.astype(F32) * hidden.astype(F32), axis=0, keepdims=True)

        grad_args = (
            gates, xrs, vs, ys, dh, chans, lag, ir, cf, bc, bct, gtmat, colp, cumt, kexp, sts, segc, segr,
            small, hp, bcp,
        )
        if direct:
            (
                dgates, dxrs, chg, d_small, pg, g_wout, gate_own, gate_got, sum0, sum1, sum2,
            ) = scan_grad_all(g_out, partial_out, normed_t, *grad_args)
        else:
            dgates, dxrs, chg, d_small, pg = scan_grad(*grad_args)
            output = (out_here + seqs(tokens)).astype(BF16).reshape(tokens.shape)
        chg = jnp.concatenate([chg[0:6], g_ig[0:1] / gain_in, chg[7:8]], axis=0)
        g_dtb, g_alog = pg[5, : 2 * hb], pg[6, : 2 * hb]
        g_bcs = pg[: KW + 1]

        def token_grad(pick, d, root, dot):
            root, dot = root[:, None], dot[:, None]
            grad = pick(seqs(cotangent)).astype(F32) + root * norm_gain * d
            return (grad - pick(seqs(tokens)).astype(F32) * (root * root / width * dot)).astype(BF16)

        if direct:
            rows = []
            for b in range(2):
                hs = slice(b * hb, (b + 1) * hb)
                heads = jnp.concatenate([g_dtb[hs], g_alog[hs]])
                rows += [chg[0:7, b * cb : (b + 1) * cb], jnp.pad(heads, (0, cb - 2 * hb))[None]]
            last = jnp.pad(g_bcs.reshape(-1), (0, width - g_bcs.size))
            last = jnp.concatenate([jnp.zeros_like(gain), last, gain, jnp.zeros_like(gain)]).reshape(8, cb)
            gz, thins, smalls, d_own, d_away, rowv = grad_all(
                gate_own, w_gate, w_x, w_small, normed, gate_got, normed_t, dgates, dxrs, d_small,
                jnp.concatenate(rows + [last], axis=0), inv_root,
            )
            (
                output, tokens_grad, g_gain, g_cx, g_cxb, g_igain, heads, g_cb, g_cbb, g_bc, g_dt,
            ) = finish(
                jnp.stack([mh, ml]).astype(jnp.int32), seqs(tokens), seqs(cotangent), sum0, sum1, sum2, sum3,
                d_own, d_away, rowv, smalls, thins, norm_gain[None], partial_out, hb,
            )
            return (
                output.reshape(tokens.shape), tokens_grad.reshape(tokens.shape), g_gain.reshape(feat),
                jnp.transpose(gz, (1, 0, 2)), g_dt, g_bc, g_cx, g_cxb.reshape(cb), g_cb, g_cbb.reshape(bcn),
                heads[0, :hb], heads[0, hb : 2 * hb], heads[5, :hb], g_igain.reshape(cb), g_wout,
            )
        else:
            dn, gg = back(dgates, dxrs, d_small, w_gate, w_x, w_small, normed)
            g_gain = gg[0] / gain
            dn = jnp.moveaxis(dn, 0, 1).reshape(length, width)
            d_here = scatter_features(dn)
            dots = pair_sum(jnp.sum(dn.astype(F32) * normed.astype(F32), axis=1))
            own = token_grad(mine, mine(d_here), inv_root[:, 0], dots)
            away = token_grad(other, other(d_here), swap(inv_root[:, 0]), swap(dots))
            tokens_grad = place(own, away)

            def join(own, away):
                return own.astype(F32) + swap(away).astype(F32)

            halves = (slice(0, cb), slice(cb, 2 * cb))
            g_gate = [row_scatter(dot_tn(normed, dgates[:, n]).astype(BF16)) for n in halves]
            g_x = [row_scatter(dot_tn(normed, dxrs[:, n]).astype(BF16)) for n in halves]
            g_zx = jnp.stack([join(*g_gate), join(*g_x)], axis=1)
            thins = row_scatter(dot_tn(normed, d_small))
            g_bc = lax.psum(thins[:, : 2 * STATE], col).reshape(-1, 2 * nl, bcn)
            g_bc = lax.dynamic_index_in_dim(g_bc, here, 1, keepdims=False)
            g_dts = thins[:, 2 * STATE : 2 * STATE + 2 * hb].reshape(-1, 2, hb)
            g_dt = g_dts[:, 0] + swap(g_dts[:, 1])
            every = ("row", "zh", "zl")
            g_gain, g_bcs = lax.psum((g_gain, g_bcs), every)
            g_gain = lax.dynamic_slice(g_gain, (here * feat,), (feat,))
            g_bcs = g_bcs.reshape(KW + 1, 2 * nl, bcn)
            g_bcs = lax.dynamic_index_in_dim(g_bcs, here, 1, keepdims=False)
            chg = chg[:, :cb] + swap(chg[:, cb:])
            g_dtb = g_dtb[:hb] + swap(g_dtb[hb:])
            g_alog = g_alog[:hb] + swap(g_alog[hb:])
            chg, g_dtb, g_alog = lax.psum((chg, g_dtb, g_alog), "row")
        return (
            output,
            tokens_grad,
            g_gain,
            g_zx,
            g_dt,
            g_bc,
            chg[0:KW],
            chg[4],
            g_bcs[0:KW],
            g_bcs[KW],
            g_dtb,
            g_alog,
            chg[5].reshape(hb, HEADDIM).sum(1),
            chg[6],
            g_wout,
        )

    return per_device


def solution(mesh):
    nrow, ncol = mesh.shape["row"], mesh.shape["col"]
    nl = ncol // 2
    split = Mesh(mesh.devices.reshape(nrow, 2, nl), ("row", "zh", "zl"))
    col = ("zh", "zl")
    in_specs = (
        P("row", col), P("row", None), P(col), P("row", None, col), P("row", col), P("row", col),
        P(None, col), P(col), P(None, col), P(col), P(col), P(col), P(col), P(col),
        P("row", col), P("row", col),
    )
    out_specs = (
        P("row", col), P("row", col), P(col), P("row", None, col), P("row", col), P("row", col),
        P(None, col), P(col), P(None, col), P(col), P(col), P(col), P(col), P(col), P("row", col),
    )
    return jax.shard_map(
        build(nrow, nl), mesh=split, in_specs=in_specs, out_specs=out_specs, check_vma=False
    )
```

```python
import functools

import jax
import jax.numpy as jnp
from jax import lax
from jax.experimental import pallas as pl
from jax.experimental.pallas import tpu as pltpu
from jax.sharding import Mesh, PartitionSpec as P

HEADDIM = 64
STATE = 128
KW = 4
EPS = 1e-05
SPAN = 256
GROUP = 256
PER = GROUP // HEADDIM
F32 = jnp.float32
BF16 = jnp.bfloat16
VMEM_LIMIT = 60 * 1024 * 1024


def dot_nn(a, b):
    return lax.dot_general(a, b, (((1,), (0,)), ((), ())), preferred_element_type=F32)


def dot_nt(a, b):
    return lax.dot_general(a, b, (((1,), (1,)), ((), ())), preferred_element_type=F32)


def dot_tn(a, b):
    return lax.dot_general(a, b, (((0,), (0,)), ((), ())), preferred_element_type=F32)


def dot_exact(a, b):
    return lax.dot_general(
        a, b, (((1,), (0,)), ((), ())), preferred_element_type=F32, precision=lax.Precision.HIGHEST
    )


def twice(v):
    return jnp.concatenate([v, v], axis=1)


def across(v):
    return v if SPAN == 128 else twice(v)


def turned(v):
    n = v.shape[1]
    row = lax.broadcasted_iota(jnp.int32, (n, n), 0)
    col = lax.broadcasted_iota(jnp.int32, (n, n), 1)
    return dot_nt((row == col).astype(F32).astype(BF16), v).astype(BF16)


def spread(cols):
    rows = cols.shape[0]
    lane = lax.broadcasted_iota(jnp.int32, (rows, 128), 1)
    low = lane < HEADDIM
    first = jnp.where(low, cols[:, 0:1], cols[:, 1:2])
    second = jnp.where(low, cols[:, 2:3], cols[:, 3:4])
    return jnp.concatenate([first, second], axis=1)


def head_mask(h):
    lane = lax.broadcasted_iota(jnp.int32, (1, GROUP), 1)
    return ((lane >= h * HEADDIM) & (lane < (h + 1) * HEADDIM)).astype(F32).astype(BF16)


def prep_lags(segc_ref, kexp_ref, lag_ref):
    seg = segc_ref[...]
    length = seg.shape[0]
    pos = lax.broadcasted_iota(jnp.int32, (length, 128), 0)
    lag = jnp.zeros((length, 128), F32)
    for j in range(1, KW):
        lag = lag + ((pltpu.roll(seg, j, 0) == seg) & (pos >= j)).astype(F32)
    lag_ref[0:length, :] = lag
    lag_ref[length:, :] = jnp.zeros((8, 128), F32)
    kexp_ref[...] = jnp.zeros_like(kexp_ref)


def prep_rows(
    lo, hi, small_ref, segc_ref, segr_ref, bcp_ref, hp_ref,
    bc_ref, bct_ref, g_ref, gt_ref, colp_ref, cumt_ref, kexp_ref, lag_ref,
):
    groups = colp_ref.shape[0]
    some = slice(lo, hi)
    lag2 = twice(lag_ref[some, :])
    raw = small_ref[some, 0:256]
    wide = raw if lo == 0 else small_ref[lo - 8 : hi, 0:256]
    v = bcp_ref[4:5, :] + bcp_ref[3:4, :] * raw
    for j in range(1, KW):
        earlier = pltpu.roll(wide, j, 0)[wide.shape[0] - (hi - lo) :]
        v = v + bcp_ref[3 - j : 4 - j, :] * jnp.where(lag2 >= j, earlier, 0.0)
    act = (v * jax.nn.sigmoid(v)).astype(BF16)
    bc_ref[some, :] = act
    bct_ref[:, some] = turned(act)
    z = small_ref[some, 256:384] + hp_ref[0:1, :]
    dt = jnp.maximum(z, 0.0) + jnp.log1p(jnp.exp(-jnp.abs(z)))
    a = -dt * jnp.exp(hp_ref[1:2, :])
    tri_r = lax.broadcasted_iota(jnp.int32, (SPAN, SPAN), 0)
    tri_c = lax.broadcasted_iota(jnp.int32, (SPAN, SPAN), 1)
    lower = (tri_r >= tri_c).astype(F32)
    seg_row = segr_ref[0:1, :]
    for c in range(lo // SPAN, hi // SPAN):
        r0 = c * SPAN
        rows = slice(r0, r0 + SPAN)
        here = slice(r0 - lo, r0 - lo + SPAN)
        cum = dot_exact(lower, a[here])
        segb = segc_ref[rows, :]
        last = segc_ref[r0 + SPAN - 1 : r0 + SPAN, :]
        tail = (segb == last).astype(F32)
        end = cum[SPAN - 1 : SPAN]
        q = jnp.exp(end - cum) * tail
        if c > 0:
            prev = segc_ref[r0 - 1 : r0, :]
            p = jnp.exp(cum) * (segb == prev).astype(F32)
            kexp_ref[c : c + 1, :] = jnp.exp(end) * (last == prev).astype(F32)
        else:
            p = jnp.zeros_like(cum)
        cumt = jnp.transpose(cum)
        dtb = dt[here]
        for g in range(groups):
            hs = slice(PER * g, PER * g + PER)
            colp_ref[g, rows, 0:4] = cum[:, hs]
            colp_ref[g, rows, 4:8] = dtb[:, hs]
            colp_ref[g, rows, 8:12] = p[:, hs]
            colp_ref[g, rows, 12:16] = q[:, hs]
            cumt_ref[g, 0:4, rows] = cumt[hs, :]
        bb = bc_ref[rows, 0:STATE]
        cc = bc_ref[rows, STATE : 2 * STATE]
        same = across(segb) == seg_row[:, rows]
        g_ref[rows, :] = jnp.where(same & (tri_r >= tri_c), dot_nt(cc, bb), 0.0)
        gt_ref[rows, :] = jnp.where(same & (tri_r <= tri_c), dot_nt(bb, cc), 0.0)


def prep_kernel(*refs):
    prep_lags(refs[1], refs[-2], refs[-1])
    prep_rows(0, refs[0].shape[0], *refs)


def conv_rows(xr_ref, lag_ref, chan_ref, r0):
    cur = xr_ref[pl.ds(r0, SPAN), :]
    before = xr_ref[pl.ds(pl.multiple_of(jnp.maximum(r0 - 8, 0), 8), 8), :]
    both = jnp.concatenate([before, cur], axis=0)
    lag = twice(lag_ref[pl.ds(r0, SPAN), :])
    v = chan_ref[4:5, :] + chan_ref[3:4, :] * cur
    for j in range(1, KW):
        earlier = pltpu.roll(both, j, 0)[8:]
        v = v + chan_ref[3 - j : 4 - j, :] * jnp.where(lag >= j, earlier, 0.0)
    return cur, v


def scan_kernel(
    nb_ref, wg_ref, wx_ref, chan_ref, lag_ref, bc_ref, bct_ref, g_ref, colp_ref, cumt_ref, kexp_ref,
    gate_ref, xr_ref, v_ref, y_ref, gated_ref, sq_ref, st_ref, xs, state,
):
    length = gate_ref.shape[0]
    blocks = length // SPAN
    state[...] = jnp.zeros_like(state)

    @pl.when(pl.program_id(0) == 0)
    def _():
        sq_ref[...] = jnp.zeros_like(sq_ref)

    def project(c, carry):
        rows = pl.ds(pl.multiple_of(c * 512, 512), 512)
        gate_ref[rows, :] = dot_nn(nb_ref[rows, :], wg_ref[...])
        xs[rows, :] = dot_nn(nb_ref[rows, :], wx_ref[...])
        return carry

    lax.fori_loop(0, length // 512, project, 0)

    def body(c, carry):
        r0 = pl.multiple_of(c * SPAN, SPAN)
        rows = pl.ds(r0, SPAN)
        cur, v = conv_rows(xs, lag_ref, chan_ref, r0)
        xr_ref[rows, :] = cur.astype(BF16)
        v_ref[rows, :] = v
        xc = (v * jax.nn.sigmoid(v)).astype(BF16).astype(F32)
        cp = colp_ref[0, rows, :]
        xd = (spread(cp[:, 4:8]) * xc).astype(BF16)
        px = spread(cp[:, 8:12])
        qx = spread(cp[:, 12:16])
        gb = g_ref[rows, :]
        lefts, rights = [], []
        for h in range(PER):
            gap = cp[:, h : h + 1] - cumt_ref[0, h : h + 1, rows]
            lefts.append((gb * jnp.exp(jnp.minimum(gap, 0.0))).astype(BF16))
            rights.append(xd * head_mask(h))
        y = dot_nn(jnp.concatenate(lefts, axis=1), jnp.concatenate(rights, axis=0))
        st = state[...]
        stb = st.astype(BF16)
        st_ref[c] = stb
        y = y + px * dot_nn(bc_ref[rows, STATE : 2 * STATE], stb)
        kx = kexp_ref[pl.ds(c, 1), :]
        state[...] = kx * st + dot_nn(bct_ref[0:STATE, rows], (qx * xd.astype(F32)).astype(BF16))
        y = y + chan_ref[5:6, :] * xc
        y_ref[rows, :] = y
        gate = gate_ref[rows, :]
        gated = y * (gate * jax.nn.sigmoid(gate))
        gated_ref[rows, :] = gated.astype(BF16)
        sq = gated * gated
        sq_ref[rows, :] += sq[:, 0:128] + sq[:, 128:256]
        return carry

    lax.fori_loop(0, blocks, body, 0)


def scan_grad_kernel(
    place, gate_ref, xr_ref, v_ref, y_ref, dh_ref, chan_ref, lag_ref, ir_ref, cf_ref, bc_ref, bct_ref, gt_ref,
    colp_ref, cumt_ref, kexp_ref, st_ref, segc_ref, segr_ref,
    small_ref, hp_ref, bcp_ref,
    dgate_ref, dxr_ref, chg_ref, ds_ref, pg_ref,
    dst, head, dgt, dbc_ref, end_ref, acc_a, acc_d, acc_e,
):
    length = gate_ref.shape[0]
    blocks = length // SPAN
    step = pl.program_id(0)
    dst[...] = jnp.zeros_like(dst)
    head[...] = jnp.zeros_like(head)
    end_ref[...] = jnp.zeros_like(end_ref)
    chg_ref[...] = jnp.zeros_like(chg_ref)

    @pl.when(step == 0)
    def _():
        dgt[...] = jnp.zeros_like(dgt)
        dbc_ref[...] = jnp.zeros_like(dbc_ref)
        acc_a[...] = jnp.zeros_like(acc_a)
        acc_d[...] = jnp.zeros_like(acc_d)
        acc_e[...] = jnp.zeros_like(acc_e)

    pick_r = lax.broadcasted_iota(jnp.int32, (GROUP, 128), 0)
    pick_c = lax.broadcasted_iota(jnp.int32, (GROUP, 128), 1)
    pick32 = (pick_r // HEADDIM + PER * place == pick_c).astype(F32)
    pick = pick32.astype(BF16)

    def per_head(v):
        hi = v.astype(BF16)
        lo = (v - hi.astype(F32)).astype(BF16)
        return dot_nn(hi, pick) + dot_nn(lo, pick)

    def total(v):
        return jnp.sum(v, axis=0, keepdims=True)

    def body(back, carry):
        c = blocks - 1 - back
        r0 = pl.multiple_of(c * SPAN, SPAN)
        rows = pl.ds(r0, SPAN)
        cur = xr_ref[rows, :].astype(F32)
        v = v_ref[rows, :]
        sv = jax.nn.sigmoid(v)
        xc = (v * sv).astype(BF16).astype(F32)
        cp = colp_ref[0, rows, :]
        dtx = spread(cp[:, 4:8])
        px = spread(cp[:, 8:12])
        qx = spread(cp[:, 12:16])
        xd = (dtx * xc).astype(BF16)
        xdf = xd.astype(F32)
        gate = gate_ref[rows, :]
        y = y_ref[rows, :]
        dh = dh_ref[rows, :].astype(F32)
        ir = twice(ir_ref[rows, :])
        cf = twice(cf_ref[rows, :])
        sg = jax.nn.sigmoid(gate)
        sl = gate * sg
        gated = y * sl
        dgd = ir * (dh * chan_ref[6:7, :]) - gated * cf
        dy = dgd * sl
        dgate = dgd * y * (sg * (1.0 + gate * (1.0 - sg)))
        dgate_ref[rows, :] = dgate.astype(BF16)
        dyb = dy.astype(BF16)
        gt = gt_ref[rows, :]
        lefts, rights = [], []
        acc = dgt[rows, :]
        for h in range(PER):
            gap = cumt_ref[0, h : h + 1, rows] - cp[:, h : h + 1]
            et = jnp.exp(jnp.minimum(gap, 0.0))
            lefts.append((gt * et).astype(BF16))
            dym = dyb * head_mask(h)
            rights.append(dym)
            acc = acc + dot_nt(xd, dym) * et
        dgt[rows, :] = acc
        u = dot_nn(jnp.concatenate(lefts, axis=1), jnp.concatenate(rights, axis=0))
        ds = dst[...]
        dsb = ds.astype(BF16)
        bb = bc_ref[rows, 0:STATE]
        cc = bc_ref[rows, STATE : 2 * STATE]
        ui = qx * dot_nn(bb, dsb)
        u = u + ui
        dxc = chan_ref[5:6, :] * dy + dtx * u
        yscan = y - chan_ref[5:6, :] * xc
        acc_a[rows, :] += per_head(dyb.astype(F32) * yscan - xdf * u)
        acc_d[rows, :] += per_head(xc * u)
        stb = st_ref[c]
        kx = kexp_ref[pl.ds(c, 1), :]
        end_ref[pl.ds(c, 1), :] = total(xdf * ui) + kx * total(ds * stb.astype(F32))
        pdy = (px * dyb.astype(F32)).astype(BF16)
        dbc_ref[rows, 0:STATE] += dot_nt((qx * xdf).astype(BF16), dsb)
        dbc_ref[rows, STATE : 2 * STATE] += dot_nt(pdy, stb)
        dst[...] = kx * ds + dot_nn(bct_ref[STATE : 2 * STATE, rows], pdy)
        dv = dxc * (sv * (1.0 + v * (1.0 - sv)))
        after = pl.ds(pl.multiple_of(r0 + SPAN, 8), 8)
        wide = jnp.concatenate([dv, head[...]], axis=0)
        lagw = jnp.concatenate([twice(lag_ref[rows, :]), twice(lag_ref[after, :])], axis=0)
        head[...] = dv[0:8]
        dxr = chan_ref[3:4, :] * dv
        chg_ref[3:4, :] += total(cur * dv)
        chg_ref[4:5, :] += total(dv)
        chg_ref[5:6, :] += total(dy * xc)
        for j in range(1, KW):
            later = pltpu.roll(jnp.where(lagw >= j, wide, 0.0), SPAN + 8 - j, 0)[0:SPAN]
            dxr = dxr + chan_ref[3 - j : 4 - j, :] * later
            chg_ref[3 - j : 4 - j, :] += total(cur * later)
        dxr_ref[rows, :] = dxr.astype(BF16)
        return carry

    lax.fori_loop(0, blocks, body, 0)

    acc_e[...] += dot_exact(end_ref[...], pick32)

    @pl.when(step == pl.num_programs(0) - 1)
    def _():
        tri_r = lax.broadcasted_iota(jnp.int32, (SPAN, SPAN), 0)
        tri_c = lax.broadcasted_iota(jnp.int32, (SPAN, SPAN), 1)
        upper = (tri_r <= tri_c).astype(F32)
        rate = jnp.exp(hp_ref[1:2, :])
        pg_ref[...] = jnp.zeros_like(pg_ref)
        for c in range(blocks):
            rows = slice(c * SPAN, (c + 1) * SPAN)
            same = across(segc_ref[rows, :]) == segr_ref[0:1, rows]
            full = jnp.where(same & (tri_r <= tri_c), dgt[rows, :], 0.0)
            turn = jnp.transpose(full)
            for value, here, there in ((full, 0, STATE), (turn, STATE, 0)):
                high = value.astype(BF16)
                low = (value - high.astype(F32)).astype(BF16)
                right = bc_ref[rows, there : there + STATE]
                dbc_ref[rows, here : here + STATE] += dot_nn(high, right) + dot_nn(low, right)
            da = dot_exact(upper, acc_a[rows, :]) + acc_e[c : c + 1, :]
            raw = small_ref[rows, 2 * STATE :]
            z = raw + hp_ref[0:1, :]
            dt = jnp.maximum(z, 0.0) + jnp.log1p(jnp.exp(-jnp.abs(z)))
            ddt = (acc_d[rows, :] - rate * da) * jax.nn.sigmoid(z)
            pg_ref[5:6, 0:128] += total(ddt)
            pg_ref[6:7, 0:128] += -rate * total(da * dt)
            ds_ref[rows, 2 * STATE :] = ddt.astype(BF16)
        raw = small_ref[:, 0 : 2 * STATE]
        lag = twice(lag_ref[0:length, :])
        v = bcp_ref[4:5, :] + bcp_ref[3:4, :] * raw
        for j in range(1, KW):
            v = v + bcp_ref[3 - j : 4 - j, :] * jnp.where(lag >= j, pltpu.roll(raw, j, 0), 0.0)
        sv = jax.nn.sigmoid(v)
        dv = dbc_ref[...] * (sv * (1.0 + v * (1.0 - sv)))
        dr = bcp_ref[3:4, :] * dv
        pg_ref[3:4, :] = total(raw * dv)
        pg_ref[4:5, :] = total(dv)
        for j in range(1, KW):
            later = pltpu.roll(jnp.where(lag >= j, dv, 0.0), length - j, 0)
            dr = dr + bcp_ref[3 - j : 4 - j, :] * later
            pg_ref[3 - j : 4 - j, :] = total(raw * later)
        ds_ref[:, 0 : 2 * STATE] = dr.astype(BF16)


def whole(shape):
    return pl.BlockSpec(shape, lambda g: (0,) * len(shape))


def once(shape):
    return pl.BlockSpec(shape, lambda g: (0,) * len(shape), pipeline_mode=pl.Buffered(1))


def tile(rows):
    return pl.BlockSpec((rows, GROUP), lambda g: (0, g))


def prep_shapes(length, groups):
    return (
        jax.ShapeDtypeStruct((length, 2 * STATE), BF16),
        jax.ShapeDtypeStruct((2 * STATE, length), BF16),
        jax.ShapeDtypeStruct((length, SPAN), F32),
        jax.ShapeDtypeStruct((length, SPAN), F32),
        jax.ShapeDtypeStruct((groups, length, 16), F32),
        jax.ShapeDtypeStruct((groups, 8, length), F32),
        jax.ShapeDtypeStruct((8, 128), F32),
        jax.ShapeDtypeStruct((length + 8, 128), F32),
    )


def prep(small, segc, segr, bcp, hp, groups):
    return pl.pallas_call(
        prep_kernel,
        out_shape=prep_shapes(small.shape[0], groups),
        compiler_params=pltpu.CompilerParams(vmem_limit_bytes=VMEM_LIMIT),
        name="prep",
    )(small, segc, segr, bcp, hp)


def scan_specs(length, width, gb):
    last = 2 * gb - 1

    def at(g):
        return jnp.minimum(g, last)

    def strip(rows):
        return pl.BlockSpec((rows, GROUP), lambda g: (0, at(g)))

    weight = pl.BlockSpec((None, width, GROUP), lambda g: (at(g) // gb, 0, at(g) % gb))
    return [
        once((length, width)),
        weight,
        weight,
        strip(8),
        once((length + 8, 128)),
        once((length, 2 * STATE)),
        once((2 * STATE, length)),
        once((length, SPAN)),
        pl.BlockSpec((1, length, 16), lambda g: (at(g), 0, 0)),
        pl.BlockSpec((1, 8, length), lambda g: (at(g), 0, 0)),
        strip(8),
    ], [
        strip(length),
        strip(length),
        strip(length),
        strip(length),
        strip(length),
        whole((length, 128)),
        pl.BlockSpec((length // SPAN, STATE, GROUP), lambda g: (0, 0, at(g))),
    ]


def scan_shapes(length, channels):
    return (
        jax.ShapeDtypeStruct((length, channels), F32),
        jax.ShapeDtypeStruct((length, channels), BF16),
        jax.ShapeDtypeStruct((length, channels), F32),
        jax.ShapeDtypeStruct((length, channels), F32),
        jax.ShapeDtypeStruct((length, channels), BF16),
        jax.ShapeDtypeStruct((length, 128), F32),
        jax.ShapeDtypeStruct((length // SPAN, STATE, channels), BF16),
    )


def scan(nb, wg, wx, chan, *rest):
    length, width = nb.shape
    channels = chan.shape[1]
    in_specs, out_specs = scan_specs(length, width, channels // GROUP // 2)
    return pl.pallas_call(
        scan_kernel,
        grid=(channels // GROUP,),
        in_specs=in_specs,
        out_specs=out_specs,
        out_shape=scan_shapes(length, channels),
        scratch_shapes=[pltpu.VMEM((length, GROUP), F32), pltpu.VMEM((STATE, GROUP), F32)],
        compiler_params=pltpu.CompilerParams(vmem_limit_bytes=VMEM_LIMIT),
        name="scan",
    )(nb, wg, wx, chan, *rest)


def scan_grad_specs(length, channels, shift=0):
    blocks = length // SPAN
    groups = channels // GROUP

    def at(g):
        return lax.rem(g + shift, groups)

    def tile(rows):
        return pl.BlockSpec((rows, GROUP), lambda g: (0, at(g)))

    ins = [
        tile(length),
        tile(length),
        tile(length),
        tile(length),
        tile(length),
        tile(8),
        once((length + 8, 128)),
        once((length, 128)),
        once((length, 128)),
        once((length, 2 * STATE)),
        once((2 * STATE, length)),
        once((length, SPAN)),
        pl.BlockSpec((1, length, 16), lambda g: (at(g), 0, 0)),
        pl.BlockSpec((1, 8, length), lambda g: (at(g), 0, 0)),
        tile(8),
        pl.BlockSpec((blocks, STATE, GROUP), lambda g: (0, 0, at(g))),
        once((length, 128)),
        once((8, length)),
        once((length, 2 * STATE + 128)),
        once((8, 128)),
        once((8, 2 * STATE)),
    ]
    outs = [
        tile(length),
        tile(length),
        tile(8),
        once((length, 2 * STATE + 128)),
        once((8, 2 * STATE)),
    ]
    shapes = (
        jax.ShapeDtypeStruct((length, channels), BF16),
        jax.ShapeDtypeStruct((length, channels), BF16),
        jax.ShapeDtypeStruct((8, channels), F32),
        jax.ShapeDtypeStruct((length, 2 * STATE + 128), BF16),
        jax.ShapeDtypeStruct((8, 2 * STATE), F32),
    )
    scratch = [
        pltpu.VMEM((STATE, GROUP), F32),
        pltpu.VMEM((8, GROUP), F32),
        pltpu.VMEM((length, SPAN), F32),
        pltpu.VMEM((length, 2 * STATE), F32),
        pltpu.VMEM((8, GROUP), F32),
        pltpu.VMEM((length, 128), F32),
        pltpu.VMEM((length, 128), F32),
        pltpu.VMEM((8, 128), F32),
    ]
    return ins, outs, shapes, scratch


def scan_grad(*args):
    length, channels = args[0].shape
    ins, outs, shapes, scratch = scan_grad_specs(length, channels)
    return pl.pallas_call(
        lambda *refs: scan_grad_kernel(pl.program_id(0), *refs),
        grid=(channels // GROUP,),
        in_specs=ins,
        out_specs=outs,
        out_shape=shapes,
        scratch_shapes=scratch,
        compiler_params=pltpu.CompilerParams(vmem_limit_bytes=VMEM_LIMIT),
        name="scan_grad",
    )(*args)


def back_kernel(a0, a1, a2, w0, w1, w2, nb_ref, dn_ref, gg_ref):
    cb = w0.shape[2]
    total = dot_nt(a2[...], w2[...])
    for a, w in ((a0, w0), (a1, w1)):
        for b in range(2):
            total = total + dot_nt(a[:, b * cb : (b + 1) * cb], w[b])
    dn_ref[0] = total.astype(BF16)
    gg = jnp.sum(total * nb_ref[...].astype(F32), axis=0, keepdims=True)
    gg_ref[...] = jnp.broadcast_to(gg, gg_ref.shape)


def back(dgate, dxr, d_small, wg, wx, w_small, nb):
    length, width = nb.shape
    cb = wg.shape[2]
    feat = max(width // 4, 256)
    per = feat // 256
    wide = pl.BlockSpec((2, 256, cb), lambda n: (0, n, 0))
    return pl.pallas_call(
        back_kernel,
        grid=(width // 256,),
        in_specs=[once(a.shape) for a in (dgate, dxr, d_small)]
        + [wide, wide]
        + [pl.BlockSpec((256, d_small.shape[1]), lambda n: (n, 0))]
        + [pl.BlockSpec((length, 256), lambda n: (0, n))],
        out_specs=[
            pl.BlockSpec((1, length, 256), lambda n: (n // per, 0, n % per)),
            pl.BlockSpec((8, 256), lambda n: (0, n)),
        ],
        out_shape=(
            jax.ShapeDtypeStruct((width // feat, length, feat), BF16),
            jax.ShapeDtypeStruct((8, width), F32),
        ),
        compiler_params=pltpu.CompilerParams(vmem_limit_bytes=VMEM_LIMIT),
        name="back",
    )(dgate, dxr, d_small, wg, wx, w_small, nb)


MESH_ID = pl.DeviceIdType.MESH


class Copies:
    def __init__(self, send, recv):
        self.send, self.recv, self.count, self.open = send, recv, 0, []

    def start(self, src, dst, to):
        copy = pltpu.make_async_remote_copy(
            src_ref=src, dst_ref=dst, send_sem=self.send.at[self.count],
            recv_sem=self.recv.at[self.count], device_id=to, device_id_type=MESH_ID,
        )
        self.count += 1
        copy.start()
        self.open.append(copy)
        return copy

    def finish(self):
        for copy in self.open:
            copy.wait_send()


def places():
    h, l, r = lax.axis_index("zh"), lax.axis_index("zl"), lax.axis_index("row")
    c, x, y = lax.rem(r, 2), lax.rem(r // 2, 2), r // 4
    rx, ry = r + 2 - 4 * x, r + 4 - 8 * y
    rc = r + 1 - 2 * c
    return h, l, r, c, x, y, rx, ry, rc


def meet(peers):
    barrier = pltpu.get_barrier_semaphore()
    for to in peers:
        pl.semaphore_signal(barrier, inc=1, device_id=to, device_id_type=MESH_ID)
    pl.semaphore_wait(barrier, len(peers))


GATHER_COPIES = 96
PIECES = 4
FINE = 8


def gather_kernel(
    x_ref, wg_ref, wx_ref, thin_ref, par_ref, segc_ref, segr_ref,
    nb_ref, nt_ref, ir_ref, par_out, ws_ref, small_ref, hp_ref, bcp_ref,
    bc_ref, bct_ref, g_ref, gt_ref, colp_ref, cumt_ref, kexp_ref, lag_ref, wg_out, wx_out,
    xv, parv, thin_v, stage, send, recv, local,
):
    h, l, r, c, x, y, rx, ry, rc = places()
    rd = rx + ry - r
    me, zhp = h * 2 + l, (1 - h) * 2 + l
    zh, zl, zd = {"zh": 1 - h}, {"zl": 1 - l}, {"zh": 1 - h, "zl": 1 - l}
    to_x, to_y, to_c = {"row": rx}, {"row": ry}, {"row": rc}
    length, feat = x_ref.shape[1], x_ref.shape[2]
    step = length // FINE
    shard = wg_ref.shape[0]
    meet((zh, zl, zd, to_x, to_y, to_c))
    copies = Copies(send, recv)
    start = copies.start

    def cols(block):
        return pl.ds(pl.multiple_of(block * feat, feat), feat)

    def toks(p):
        return pl.ds(p * step, step)

    def rows(row):
        return pl.ds(pl.multiple_of(row * shard, shard), shard)

    src = (wg_ref, wx_ref)
    dst = ((wg_out.at[0], wx_out.at[0]), (wg_out.at[1], wx_out.at[1]))
    keeps = [
        pltpu.make_async_copy(par_ref, parv.at[me], local.at[0]),
        pltpu.make_async_copy(thin_ref, thin_v.at[r, me], local.at[1]),
        pltpu.make_async_copy(x_ref.at[h], xv.at[:, cols(me)], local.at[2]),
        pltpu.make_async_copy(wg_ref, stage.at[0], local.at[3]),
        pltpu.make_async_copy(wx_ref, stage.at[1], local.at[4]),
    ]
    for keep in keeps:
        keep.start()
    laid = [pltpu.make_async_copy(stage.at[k], dst[0][k].at[rows(r)], local.at[5 + k]) for k in range(2)]
    pars = [start(par_ref, parv.at[me], to) for to in (zh, zl, zd)]
    thins = [start(thin_ref, thin_v.at[r, me], to) for to in (zh, zl, zd)]
    sib, sib_thin, x1, x3, wz, got, far = [], [], [], [], [], {}, {}
    bcn, hb = 2 * STATE // 4, colp_ref.shape[0] * PER // 2
    part = shard // 2

    def chunk(b, q, row):
        if b == 0:
            return dst[0][q].at[rows(row)]
        return dst[1][q // 2].at[pl.ds(pl.multiple_of(row * shard + q % 2 * part, part), part)]

    def send_w(q):
        wz.append(start(src[q // 2].at[pl.ds(q % 2 * part, part)], chunk(1, q, r), zh))

    def deal(b, q):
        if b == 0:
            got[b, q] = [start(src[q], chunk(b, q, r), to) for to in (to_x, to_y, to_c)]
        else:
            wz[q].wait_recv()
            got[b, q] = [start(chunk(b, q, r), chunk(b, q, r), to) for to in (to_x, to_y, to_c)]
        sib.append(got[b, q][2])

    def pass_on(b, q, n):
        piece = chunk(b, q, (rx, ry)[n])
        got[b, q][n].wait_recv()
        if n == q % 2:
            far[b, q] = start(piece, piece, (to_y, to_x)[n])
        sib.append(start(piece, piece, to_c))

    def corner(b, q):
        far[b, q].wait_recv()
        sib.append(start(chunk(b, q, rd), chunk(b, q, rd), to_c))

    def send_x():
        if len(x1) < FINE:
            p = len(x1)
            x1.append(start(x_ref.at[1 - h, toks(p)], xv.at[toks(p), cols(me)], zh))

    def pass_x(p):
        x1[p].wait_recv()
        x3.append(start(xv.at[toks(p), cols(zhp)], xv.at[toks(p), cols(zhp)], zl))

    x2 = {}

    def send_own(k):
        rows_k = pl.ds(k * 2 * step, 2 * step)
        x2[k] = start(x_ref.at[h, rows_k], xv.at[rows_k, cols(me)], zl)

    def thin_on(n):
        row = (rx, ry, rd)[n]
        thin_go[n].wait_recv()
        if n == 0:
            thin_go.append(start(thin_v.at[row], thin_v.at[row], to_y))
        sib_thin.append(start(thin_v.at[row], thin_v.at[row], to_c))

    def norm(p):
        if p % 2 == 0:
            x2[p // 2].wait_recv()
        x3[p].wait_recv()
        total = jnp.zeros((step, 1), F32)
        for b in range(4):
            value = xv[toks(p), b * feat : (b + 1) * feat].astype(F32)
            total = total + jnp.sum(value * value, axis=1, keepdims=True)
        root = lax.rsqrt(total / (4 * feat) + EPS)
        ir_ref[toks(p), :] = jnp.broadcast_to(root, (step, 128))
        for b in range(8):
            value = xv[toks(p), b * shard : (b + 1) * shard].astype(F32)
            gain = parv[b // 2, 8:9, b % 2 * shard : (b % 2 + 1) * shard]
            value = (value * root * gain).astype(BF16)
            nb_ref[toks(p), b * shard : (b + 1) * shard] = value
            nt_ref[b % 2, b // 2 * shard : (b // 2 + 1) * shard, toks(p)] = turned(value)

    prep_refs = (
        small_ref, segc_ref, segr_ref, bcp_ref, hp_ref,
        bc_ref, bct_ref, g_ref, gt_ref, colp_ref, cumt_ref, kexp_ref, lag_ref,
    )

    def narrow(p):
        lo, hi = p * (length // 2), (p + 1) * (length // 2)
        small_ref[lo:hi, :] = dot_nn(nb_ref[lo:hi, :], ws_ref[...])
        prep_rows(lo, hi, *prep_refs)

    def parameters():
        for copy in pars:
            copy.wait_recv()
        for n in range(3):
            if n != 1:
                keeps[n].wait()
        par_out[...] = parv[...]
        bcp_ref[...] = jnp.zeros_like(bcp_ref)
        bcp_ref[0:5, :] = sum(parv[b, 9:14, 0 : 2 * STATE] for b in range(4))
        hp_ref[...] = jnp.zeros_like(hp_ref)
        hp_ref[0:2, :] = parv[me, 14:16, 0:128] + pltpu.roll(parv[zhp, 14:16, 0:128], hb, 1)
        prep_lags(segc_ref, kexp_ref, lag_ref)

    def narrow_weights():
        for copy in sib_thin:
            copy.wait_recv()
        ws_ref[...] = jnp.zeros_like(ws_ref)
        for row in range(8):
            at = slice(row * shard, (row + 1) * shard)
            for b in range(4):
                ws_ref[at, b * bcn : (b + 1) * bcn] = thin_v[row, b, :, 0:bcn]
            ws_ref[at, 2 * STATE : 2 * STATE + hb] = thin_v[row, me, :, bcn : bcn + hb]
            ws_ref[at, 2 * STATE + hb : 2 * STATE + 2 * hb] = thin_v[row, zhp, :, bcn : bcn + hb]

    send_w(0)
    send_own(2)
    send_x()
    deal(0, 0)
    send_own(3)
    deal(0, 1)
    send_x()
    send_x()
    for k in range(2):
        keeps[3 + k].wait()
        laid[k].start()
    pass_on(0, 1, 1)
    keeps[1].wait()
    for copy in thins:
        copy.wait_recv()
    thin_go = [start(thin_v.at[r], thin_v.at[r], to) for to in (to_x, to_y, to_c)]
    sib_thin.append(thin_go.pop())
    parameters()
    send_w(1)
    send_own(1)
    thin_on(0)
    pass_on(0, 0, 0)
    pass_x(0)
    send_own(0)
    send_w(2)
    thin_on(1)
    send_x()
    thin_on(2)
    pass_x(1)
    pass_on(0, 0, 1)
    send_w(3)
    deal(1, 0)
    pass_on(1, 0, 0)
    corner(0, 1)
    pass_x(2)
    send_x()
    deal(1, 1)
    norm(0)
    pass_x(3)
    pass_on(1, 1, 1)
    deal(1, 2)
    pass_x(4)
    send_x()
    corner(0, 0)
    narrow_weights()
    deal(1, 3)
    corner(1, 0)
    norm(1)
    norm(2)
    send_x()
    norm(3)
    pass_x(5)
    pass_on(1, 3, 1)
    send_x()
    norm(4)
    corner(1, 1)
    narrow(0)
    pass_x(6)
    pass_on(1, 2, 1)
    pass_on(1, 3, 0)
    pass_on(1, 1, 0)
    pass_on(1, 2, 0)
    norm(5)
    pass_on(0, 1, 0)
    pass_on(1, 0, 1)
    pass_x(7)
    corner(1, 2)
    norm(6)
    corner(1, 3)
    norm(7)
    narrow(1)
    for copy in sib:
        copy.wait_recv()
    for move in laid:
        move.wait()
    copies.finish()


def gather_all(x, wg, wx, thin, par, segc, segr, groups):
    _, length, feat = x.shape
    shard, cb = wg.shape
    anywhere = pl.BlockSpec(memory_space=pl.ANY)
    inside = pl.BlockSpec(memory_space=pltpu.VMEM)
    weight = jax.ShapeDtypeStruct((2, 8 * shard, cb), BF16)
    return pl.pallas_call(
        gather_kernel,
        in_specs=[anywhere] * 5 + [inside] * 2,
        out_specs=[inside] * 16 + [anywhere] * 2,
        out_shape=(
            jax.ShapeDtypeStruct((length, 4 * feat), BF16),
            jax.ShapeDtypeStruct((2, 4 * shard, length), BF16),
            jax.ShapeDtypeStruct((length, 128), F32),
            jax.ShapeDtypeStruct((4,) + par.shape, F32),
            jax.ShapeDtypeStruct((8 * shard, 2 * STATE + 128), BF16),
            jax.ShapeDtypeStruct((length, 2 * STATE + 128), F32),
            jax.ShapeDtypeStruct((8, 128), F32),
            jax.ShapeDtypeStruct((8, 2 * STATE), F32),
        )
        + prep_shapes(length, groups)
        + (weight, weight),
        scratch_shapes=[
            pltpu.VMEM((length, 4 * feat), BF16),
            pltpu.VMEM((4,) + par.shape, F32),
            pltpu.VMEM((8, 4) + thin.shape, BF16),
            pltpu.VMEM((2, shard, cb), BF16),
            pltpu.SemaphoreType.DMA((GATHER_COPIES,)),
            pltpu.SemaphoreType.DMA((GATHER_COPIES,)),
            pltpu.SemaphoreType.DMA((8,)),
        ],
        compiler_params=pltpu.CompilerParams(
            collective_id=0, has_side_effects=True, vmem_limit_bytes=VMEM_LIMIT
        ),
        name="gather_all",
    )(x, wg, wx, thin, par, segc, segr)


GRAD_COPIES = 96
HALVES = 2


def grad_kernel(
    raw_ref, wg_ref, wx_ref, ws_ref, nb_ref, gate_ref, nt_ref, dg_ref, dx_ref, ds_ref, small_ref, ir_ref,
    gz_ref, thin_out, small_out, own_out, away_out, row_out,
    raw_v, dn_v, wt, wst, nbt, ggv, ndv, tile_sem, pr, rowv, rowr, local, cs, cr, ts, tr, fs, fr, ss, sr, zs, zr, tfs, tfr, tss, tsr, tz, tzr,
    sbuf, srecv, szr, send, recv,
):
    h, l, r, c, x, y, rx, ry, rc = places()
    me = h * 2 + l
    zh, zl, zd = {"zh": 1 - h}, {"zl": 1 - l}, {"zh": 1 - h, "zl": 1 - l}
    to_x, to_y, to_c = {"row": rx}, {"row": ry}, {"row": rc}
    shard = gz_ref.shape[1]
    ncol = gz_ref.shape[2]
    meet((zh, zl, zd, to_x, to_y, to_c))
    copies = Copies(send, recv)
    start = copies.start

    def product(side, d_ref, at):
        return dot_nn(nt_ref[side], d_ref[:, at])

    def tiles(d_ref, body):
        width = d_ref.shape[1]
        wide = 256 if width % 256 == 0 else 128

        def one(n, carry):
            body(pl.ds(pl.multiple_of(n * wide, wide), wide))
            return carry

        lax.fori_loop(0, width // wide, one, 0)

    _, length, feat = dn_v.shape
    piece = length // HALVES
    strips = 4 * feat // 256

    def toks(p):
        return pl.ds(p * piece, piece)

    raw_copy = pltpu.make_async_copy(raw_ref.at[1], raw_v, local.at[0])
    raw_copy.start()

    def loads(k, slot):
        strip = pl.ds(pl.multiple_of(lax.rem(k, strips) * 256, 256), 256)
        rows = pl.ds(pl.multiple_of(k // strips * piece, piece), piece)
        return [
            pltpu.make_async_copy(wg_ref.at[:, strip], wt.at[slot, 0], tile_sem.at[slot, 0]),
            pltpu.make_async_copy(wx_ref.at[:, strip], wt.at[slot, 1], tile_sem.at[slot, 1]),
            pltpu.make_async_copy(ws_ref.at[strip], wst.at[slot], tile_sem.at[slot, 2]),
            pltpu.make_async_copy(nb_ref.at[rows, strip], nbt.at[slot], tile_sem.at[slot, 3]),
        ]

    for move in loads(0, 0):
        move.start()
    ggv[...] = jnp.zeros_like(ggv)
    ndv[...] = jnp.zeros_like(ndv)
    pair, far, kept = [], [], []

    def back(p):
        def strip(n, carry):
            k = p * strips + n
            slot = lax.rem(k, 2)
            for move in loads(k, slot):
                move.wait()

            @pl.when(k + 1 < HALVES * strips)
            def _():
                for move in loads(k + 1, 1 - slot):
                    move.start()

            value = dot_nt(ds_ref[toks(p), :], wst[slot])
            for m, d_ref in enumerate((dg_ref, dx_ref)):
                for b in range(2):
                    value = value + dot_nt(d_ref[toks(p), b * ncol : (b + 1) * ncol], wt[slot, m, b])
            lanes = pl.ds(pl.multiple_of(lax.rem(n, feat // 256) * 256, 256), 256)
            dn_v[n // (feat // 256), toks(p), lanes] = value.astype(BF16)
            value = value * nbt[slot].astype(F32)
            ggv[pl.ds(n, 1), :] += jnp.sum(value, axis=0, keepdims=True)
            ndv[toks(p), :] += value[:, 0:128] + value[:, 128:256]
            return carry

        lax.fori_loop(0, strips, strip, 0)
        pair.append([start(dn_v.at[2 * k + 1 - l, toks(p)], pr.at[k, toks(p)], zl) for k in range(2)])

    def pair_done(p):
        for move in pair[p]:
            move.wait_recv()
        away, own = 2 * (1 - h) + l, 2 * h + l
        value = dn_v[away, toks(p)].astype(F32) + pr[1 - h, toks(p)].astype(F32)
        dn_v[away, toks(p)] = value.astype(BF16)
        far.append(start(dn_v.at[away, toks(p)], away_out.at[toks(p)], zh))
        value = dn_v[own, toks(p)].astype(F32) + pr[h, toks(p)].astype(F32)
        dn_v[own, toks(p)] = value.astype(BF16)
        kept.append(pltpu.make_async_copy(dn_v.at[own, toks(p)], own_out.at[toks(p)], local.at[1 + p]))
        kept[p].start()

    z_copy = [start(gate_ref, zr.at[0], zh), None]

    def begin_small():
        sbuf[0] = small_ref[...]
        for n in range(strips):
            row, lanes = n // 4, slice(n % 4 * 256, n % 4 * 256 + 256)
            sbuf[0, 16 + row : 17 + row, lanes] = ggv[n : n + 1, :] / small_ref[20 + row : 21 + row, lanes]
        return start(sbuf.at[0], srecv.at[0], to_c)

    dx0, dx1 = dx_ref.at[:, 0:ncol], dx_ref.at[:, ncol : 2 * ncol]
    quarters = [
        dict(d=dx1, first=to_x, second=to_y, mine=x, along=y, swap=False),
        dict(d=dx0, first=to_y, second=to_x, mine=y, along=x, swap=True),
        dict(first=to_y, second=to_x, mine=y, along=x, swap=True),
    ]

    def spot(q, first, second):
        return 2 * first + second if q["swap"] else 2 * second + first

    def refs(i):
        if i == 4:
            return ts, tr, tfs, tfr, tss, tsr
        return cs, cr.at[i], fs.at[i // 2], fr.at[i], ss.at[i], sr.at[i]

    thin_q = dict(d=ds_ref, first=to_y, second=to_x, mine=y, along=x, swap=True)

    def gone(i, name):
        if i == 1:
            earlier = quarters[0][name]
            earlier.wait_send()
            copies.open = [move for move in copies.open if move is not earlier]

    def first_done(q):
        if "seen" not in q:
            q["f"].wait_recv()
            q["seen"] = True

    def to_core(i, q):
        out, back = refs(i)[0:2]
        if i == 2:
            q["core"] = start(raw_ref.at[0], back, to_c)
            return
        gone(i, "core")

        def body(at):
            value = product(1 - c, q["d"], at).astype(BF16)
            for j in range(4):
                out[j, :, at] = value[j * shard : (j + 1) * shard]

        tiles(q["d"], body)
        q["core"] = start(out, back, to_c)

    def to_first(i, q, after=None):
        _, back, fsend, frecv, _, _ = refs(i)
        q["core"].wait_recv()
        if i == 2:
            raw_copy.wait()
            for j in range(4):
                back[j] = (raw_v[j].astype(F32) + back[j].astype(F32)).astype(BF16)
        else:

            def body(at):
                value = product(c, q["d"], at)
                for j in range(4):
                    part = value[j * shard : (j + 1) * shard] + back[j, :, at].astype(F32)
                    back[j, :, at] = part.astype(BF16)

            tiles(q["d"], body)
        gone(i, "f")
        for n in range(2):
            fsend[n] = back[spot(q, 1 - q["mine"], n)]
        if after is not None:
            first_done(after)
        q["f"] = start(fsend, frecv, q["first"])

    def to_second(i, q):
        _, back, _, frecv, ssend, srcv = refs(i)
        first_done(q)
        far = 1 - q["along"]
        kept = back[spot(q, q["mine"], far)].astype(F32)
        ssend[...] = (kept + frecv[far].astype(F32)).astype(BF16)
        q["s"] = start(ssend, srcv, q["second"])

    def settle(i, q):
        _, back, _, frecv, _, srcv = refs(i)
        q["s"].wait_recv()
        near = q["along"]
        kept = back[spot(q, q["mine"], near)].astype(F32)
        return kept + frecv[near].astype(F32) + srcv[...].astype(F32)

    def hop_small(n, to):
        small_copy[0].wait_recv()
        sbuf[n] = sbuf[n - 1] + srecv[n - 1]
        if to is not None:
            small_copy[0] = start(sbuf.at[n], srecv.at[n], to)

    to_core(2, quarters[2])
    back(0)
    to_core(0, quarters[0])
    to_first(2, quarters[2])
    to_first(0, quarters[0])
    back(1)
    pair_done(0)
    rowv[...] = jnp.zeros_like(rowv)
    rowv[0:1, :] = jnp.sum(jnp.transpose(ndv[...]), axis=0, keepdims=True)
    rowv[1:2, :] = jnp.transpose(ir_ref[...])[0:1, :]
    row_copies = [start(rowv, rowr.at[n], to) for n, to in enumerate((zh, zl, zd))]
    to_core(1, quarters[1])
    to_second(0, quarters[0])
    to_core(4, thin_q)
    small_copy = [begin_small()]
    zs[...] = settle(0, quarters[0]).astype(BF16)
    z_copy[1] = start(zs, zr.at[1], zh)
    to_first(4, thin_q)
    hop_small(1, to_x)
    to_second(2, quarters[2])
    to_first(1, quarters[1])
    to_second(4, thin_q)
    tz[...] = settle(4, thin_q).astype(BF16)
    thin_z = []
    for n, (to, block) in enumerate(((zh, 2 * (1 - h) + l), (zl, 2 * h + 1 - l), (zd, 2 * (1 - h) + 1 - l))):
        lanes = pl.ds(pl.multiple_of(block // 2 * 128, 128), 128)
        thin_z.append(start(tz.at[:, lanes], tzr.at[n], to))
    thin_z.append(start(tz.at[:, 2 * STATE :], tzr.at[3], zh))
    hop_small(2, to_y)
    pair_done(1)
    hop_small(3, None)
    small_z = [
        start(sbuf.at[3, lo:], szr.at[n, lo:], to) for n, (to, lo) in enumerate(((zh, 8), (zl, 16), (zd, 16)))
    ]
    to_second(1, quarters[1])
    gz_ref[0] = settle(2, quarters[2])
    gz_ref[1] = settle(1, quarters[1])
    row_out[0] = rowv[...]
    for n in range(3):
        row_copies[n].wait_recv()
        row_out[n + 1] = rowr[n]
    for copy in thin_z:
        copy.wait_recv()
    for copy in small_z:
        copy.wait_recv()
    total = tz[:, pl.ds(pl.multiple_of(h * 128, 128), 128)].astype(F32)
    for n in range(3):
        total = total + tzr[n].astype(F32)
    thin_out[:, 0:128] = total
    thin_out[:, 128:256] = tz[:, 2 * STATE :].astype(F32)
    thin_out[:, 256:384] = tzr[3].astype(F32)
    small_out[...] = jnp.zeros_like(small_out)
    small_out[0] = sbuf[3]
    for n, lo in enumerate((8, 16, 16)):
        small_out[n + 1, lo:] = szr[n, lo:]
    for move in far:
        move.wait_recv()
    for move in kept:
        move.wait()
    for k in range(2):
        z_copy[k].wait_recv()
        gz_ref[k] += zr[k].astype(F32)
    copies.finish()


def grad_all(raw, wg, wx, ws, nb, gate_got, nt, dgate, dxr, d_small, small, ir):
    _, half, length = nt.shape
    feat = half // 2
    shard, cb = half // 4, dxr.shape[1] // 2
    ns = d_small.shape[1]
    inside = pl.BlockSpec(memory_space=pltpu.VMEM)
    anywhere = pl.BlockSpec(memory_space=pl.ANY)
    V = pltpu.VMEM
    return pl.pallas_call(
        grad_kernel,
        in_specs=[anywhere] * 6 + [inside] * 6,
        out_specs=[inside] * 3 + [anywhere, anywhere, inside],
        out_shape=(
            jax.ShapeDtypeStruct((2, shard, cb), F32),
            jax.ShapeDtypeStruct((shard, 384), F32),
            jax.ShapeDtypeStruct((4,) + small.shape, F32),
            jax.ShapeDtypeStruct((length, feat), BF16),
            jax.ShapeDtypeStruct((length, feat), BF16),
            jax.ShapeDtypeStruct((4, 8, length), F32),
        ),
        scratch_shapes=[
            V((4, shard, cb), BF16),
            V((4, length, feat), BF16),
            V((2, 2, 2, 256, cb), BF16),
            V((2, 256, ns), BF16),
            V((2, length // HALVES, 256), BF16),
            V((4 * feat // 256, 256), F32),
            V((length, 128), F32),
            pltpu.SemaphoreType.DMA((2, 4)),
            V((2, length, feat), BF16),
            V((8, length), F32),
            V((3, 8, length), F32),
            pltpu.SemaphoreType.DMA((1 + HALVES,)),
            V((4, shard, cb), BF16),
            V((3, 4, shard, cb), BF16),
            V((4, shard, ns), BF16),
            V((4, shard, ns), BF16),
            V((2, 2, shard, cb), BF16),
            V((3, 2, shard, cb), BF16),
            V((3, shard, cb), BF16),
            V((3, shard, cb), BF16),
            V((shard, cb), BF16),
            V((2, shard, cb), BF16),
            V((2, shard, ns), BF16),
            V((2, shard, ns), BF16),
            V((shard, ns), BF16),
            V((shard, ns), BF16),
            V((shard, ns), BF16),
            V((4, shard, 128), BF16),
            V((4,) + small.shape, F32),
            V((3,) + small.shape, F32),
            V((3,) + small.shape, F32),
            pltpu.SemaphoreType.DMA((GRAD_COPIES,)),
            pltpu.SemaphoreType.DMA((GRAD_COPIES,)),
        ],
        compiler_params=pltpu.CompilerParams(
            collective_id=1, has_side_effects=True, vmem_limit_bytes=VMEM_LIMIT
        ),
        name="grad_all",
    )(raw, wg, wx, ws, nb, gate_got, nt, dgate, dxr, d_small, small, ir)


def table(send, recv):
    def copy(n, src, dst, to):
        return pltpu.make_async_remote_copy(
            src_ref=src, dst_ref=dst, send_sem=send.at[n], recv_sem=recv.at[n],
            device_id=to, device_id_type=MESH_ID,
        )

    return copy


SCAN_COPIES = 32


def scan_all_kernel(*refs):
    (cot_ref, out_ref, gains_ref), refs = refs[0:3], refs[3:]
    ins, refs = refs[0:11], refs[11:]
    gate_ref, xr_ref, v_ref, y_ref, hid_ref, sq_ref, st_ref, po_ref, ir_ref, cf_ref, wo_ref = refs[0:11]
    xs, state, cot_v, out_v, rows_v, sums, other, send, recv, local, row_sem = refs[11:]
    h, l, r, c, x, y, rx, ry, rc = places()
    rd = rx + ry - r
    me, zhp = h * 2 + l, (1 - h) * 2 + l
    zh, zl = {"zh": 1 - h}, {"zl": 1 - l}
    to_x, to_y, to_c = {"row": rx}, {"row": ry}, {"row": rc}
    length, feat = cot_ref.shape[1], cot_ref.shape[2]
    piece = length // PIECES
    shard = out_ref.shape[0]
    copy = table(send, recv)
    step = pl.program_id(0)
    channels = hid_ref.shape[1]
    groups = channels // GROUP

    def toks(p):
        return pl.ds(p * piece, piece)

    def cols(block):
        return pl.ds(pl.multiple_of(block * feat, feat), feat)

    def rows(row, half=None):
        if half is None:
            return pl.ds(pl.multiple_of(row * shard, shard), shard)
        return pl.ds(pl.multiple_of(row * shard + half * (shard // 2), shard // 2), shard // 2)

    def g1(p):
        return copy(p, cot_ref.at[1 - h, toks(p)], cf_ref.at[toks(p), cols(me)], zh)

    def g2():
        return copy(4, cot_ref.at[h], cf_ref.at[:, cols(me)], zl)

    def g3(p):
        part = cf_ref.at[toks(p), cols(zhp)]
        return copy(8 + p, part, part, zl)

    def wz():
        return copy(12, out_ref, wo_ref.at[1, rows(r)], zh)

    def own(n):
        return copy(13 + n, out_ref, wo_ref.at[0, rows(r)], (to_x, to_y, to_c)[n])

    def got(n):
        part = wo_ref.at[1, rows(r)]
        return copy(16 + n, part, part, (to_x, to_y, to_c)[n])

    def diag(b, n):
        part = wo_ref.at[b, rows((rx, ry)[n], n)]
        return copy(19 + 5 * b + n, part, part, (to_y, to_x)[n])

    def sib(b, n):
        part = wo_ref.at[b, rows((rx, ry, rd)[n])]
        return copy(21 + 5 * b + n, part, part, to_c)

    def load(n):
        return pltpu.make_async_copy((cot_ref.at[h], out_ref)[n], (cot_v, out_v)[n], local.at[n])

    def keep(n):
        to = (cf_ref.at[:, cols(me)], wo_ref.at[0, rows(r)])[n]
        return pltpu.make_async_copy((cot_v, out_v)[n], to, local.at[2 + n])

    def load_rows(n, slot):
        part = pl.ds(pl.multiple_of(n * 256, 256), 256)
        return pltpu.make_async_copy(wo_ref.at[:, part], rows_v.at[slot], row_sem.at[slot])

    def onward(p):
        g1(p).wait_recv()
        g3(p).start()

    def step0():
        meet((zh, zl, to_x, to_y, to_c))
        wz().start()
        for n in range(2):
            load(n).start()
        for n in range(3):
            own(n).start()
        g2().start()

    def step1():
        for n in range(2):
            load(n).wait()
            keep(n).start()

    def step2():
        g1(0).start()
        for n in range(2):
            own(n).wait_recv()
        for n in range(2):
            diag(0, n).start()
            sib(0, n).start()

    def step3():
        g1(1).start()
        wz().wait_recv()
        for n in range(3):
            got(n).start()

    def step4():
        g1(2).start()
        g1(3).start()
        for n in range(2):
            diag(0, n).wait_recv()
        sib(0, 2).start()

    def step5():
        for n in range(2):
            got(n).wait_recv()
        for n in range(2):
            diag(1, n).start()
            sib(1, n).start()

    def step6():
        for n in range(2):
            diag(1, n).wait_recv()
        sib(1, 2).start()
        onward(0)

    def step8():
        onward(1)

    def step9():
        onward(2)

    def step10():
        onward(3)

    acts = {
        0: step0, 1: step1, 2: step2, 3: step3, 4: step4, 5: step5, 6: step6, 8: step8, 9: step9, 10: step10,
    }
    for at, act in acts.items():
        pl.when(step == at)(act)

    @pl.when(step < groups)
    def _():
        part = hid_ref.at[:, pl.ds(pl.multiple_of(step * GROUP, GROUP), GROUP)]
        scan_kernel(*ins, gate_ref, xr_ref, v_ref, y_ref, part, sq_ref, st_ref, xs, state)

    def swap_sums():
        return copy(29, sums, other, zl)

    @pl.when(step == groups)
    def _():
        sums[...] = jnp.zeros_like(sums)
        sums[0:1, :] = jnp.sum(jnp.transpose(sq_ref[...]), axis=0, keepdims=True)
        swap_sums().start()
        keep(1).wait()
        for move in [own(2), got(2)] + [sib(b, n) for b in range(2) for n in range(3)]:
            move.wait_recv()
        load_rows(0, 0).start()
        swap_sums().wait()
        root = lax.rsqrt((sums[0:1, :] + other[0:1, :]) / (2 * channels) + EPS)
        ir_ref[...] = jnp.transpose(jnp.broadcast_to(root, (128, length)))
        for n in range(groups):
            part = slice(n * GROUP, (n + 1) * GROUP)
            value = hid_ref[:, part].astype(F32) * twice(ir_ref[...]) * gains_ref[6:7, part]
            hid_ref[:, part] = value.astype(BF16)

    @pl.when(step >= groups)
    def _():
        n = step - groups
        slot = lax.rem(n, 2)
        load_rows(n, slot).wait()

        @pl.when(step < 2 * groups - 1)
        def _():
            load_rows(n + 1, 1 - slot).start()

        half = channels // 2
        out = dot_nt(hid_ref[:, 0:half], rows_v[slot, 0]) + dot_nt(hid_ref[:, half:], rows_v[slot, 1])
        po_ref[0] = out.astype(BF16)

    @pl.when(step == 2 * groups - 1)
    def _():
        late = [g2()] + [g3(p) for p in range(PIECES)]
        for move in late:
            move.wait_recv()
        keep(0).wait()
        sent = [g1(p) for p in range(PIECES)] + late + [wz()]
        sent += [own(n) for n in range(3)] + [got(n) for n in range(3)]
        sent += [diag(b, n) for b in range(2) for n in range(2)]
        sent += [sib(b, n) for b in range(2) for n in range(3)]
        for move in sent:
            move.wait_send()


def scan_all(cot, out_proj, nb, wg, wx, chan, *rest):
    length, width = nb.shape
    channels = chan.shape[1]
    cb = channels // 2
    feat, shard = width // 4, out_proj.shape[0]
    groups = channels // GROUP
    per = feat // 256
    assert groups == 8 and width // 256 == groups
    in_specs, out_specs = scan_specs(length, width, cb // GROUP)
    out_specs[4] = once((length, channels))
    anywhere = pl.BlockSpec(memory_space=pl.ANY)
    shapes = scan_shapes(length, channels)

    def strip(g):
        n = jnp.maximum(g - groups, 0)
        return n // per, 0, n % per

    return pl.pallas_call(
        scan_all_kernel,
        grid=(2 * groups,),
        in_specs=[anywhere] * 2 + [once((8, channels))] + in_specs,
        out_specs=out_specs
        + [pl.BlockSpec((1, length, 256), strip), once((length, 128)), anywhere, anywhere],
        out_shape=shapes
        + (
            jax.ShapeDtypeStruct((4, length, feat), BF16),
            jax.ShapeDtypeStruct((length, 128), F32),
            jax.ShapeDtypeStruct((length, width), BF16),
            jax.ShapeDtypeStruct((2, width, cb), BF16),
        ),
        scratch_shapes=[
            pltpu.VMEM((length, GROUP), F32),
            pltpu.VMEM((STATE, GROUP), F32),
            pltpu.VMEM((length, feat), BF16),
            pltpu.VMEM((shard, cb), BF16),
            pltpu.VMEM((2, 2, 256, cb), BF16),
            pltpu.VMEM((8, length), F32),
            pltpu.VMEM((8, length), F32),
            pltpu.SemaphoreType.DMA((SCAN_COPIES,)),
            pltpu.SemaphoreType.DMA((SCAN_COPIES,)),
            pltpu.SemaphoreType.DMA((4,)),
            pltpu.SemaphoreType.DMA((2,)),
        ],
        compiler_params=pltpu.CompilerParams(
            collective_id=2, has_side_effects=True, vmem_limit_bytes=VMEM_LIMIT
        ),
        name="scan_all",
    )(cot, out_proj, chan, nb, wg, wx, chan, *rest)


EARLY = 640


def mid_kernel(
    cf_ref, wc_ref, hid_ref, ir_ref, po_ref,
    dh_ref, go_ref, coef_ref, ig_ref, sum_out,
    ct, dots, sums, other, send, recv,
):
    phase, g = pl.program_id(0), pl.program_id(1)
    last = pl.num_programs(1) - 1
    length, channels = hid_ref.shape
    shard = go_ref.shape[1]
    h, l = lax.axis_index("zh"), lax.axis_index("zl")
    to, zd = {"zl": 1 - l}, {"zh": 1 - h, "zl": 1 - l}
    copy = table(send, recv)
    at = pl.ds(pl.multiple_of(g * GROUP, GROUP), GROUP)

    def part():
        return copy(1, po_ref.at[2 * (1 - h) + 1 - l, pl.ds(0, EARLY)], sum_out, zd)

    @pl.when((phase == 0) & (g == 0))
    def _():
        meet((to, zd))
        part().start()
        dots[...] = jnp.zeros_like(dots)

    @pl.when(phase == 0)
    def _():
        dh = dot_nn(cf_ref[...], wc_ref[...])
        dh_ref[...] = dh.astype(BF16)
        term = dh * hid_ref[:, at].astype(F32)
        dots[...] += term[:, 0:128] + term[:, 128:256]
        ig_ref[...] = jnp.broadcast_to(jnp.sum(term, axis=0, keepdims=True), ig_ref.shape)
        ct[at, :] = turned(cf_ref[:, at])

    @pl.when((phase == 0) & (g == last))
    def _():
        sums[...] = jnp.zeros_like(sums)
        sums[0:1, :] = jnp.sum(jnp.transpose(dots[...]), axis=0, keepdims=True)
        move = copy(0, sums, other, to)
        move.start()
        move.wait()
        both = jnp.broadcast_to(sums[0:1, :] + other[0:1, :], (128, length))
        coef_ref[...] = jnp.transpose(both) * ir_ref[...] * ir_ref[...] / (2 * channels)

    @pl.when(phase == 1)
    def _():
        right = hid_ref[:, at]
        for n in range(go_ref.shape[0] // 4):
            value = dot_nn(ct[4 * n * shard : 4 * (n + 1) * shard, :], right).astype(BF16)
            for m in range(4):
                go_ref[4 * n + m] = value[m * shard : (m + 1) * shard]

    @pl.when((phase == 1) & (g == last))
    def _():
        part().wait()


def middle(cf, wo, hid, ir, po):
    length, width = cf.shape
    channels = hid.shape[1]
    gb = channels // 2 // GROUP
    n = channels // GROUP
    shard = width // 8
    assert n == width // 256

    def const(shape):
        return pl.BlockSpec(shape, lambda p, g: (0,) * len(shape), pipeline_mode=pl.Buffered(1))

    def first(p, g):
        return jnp.where(p == 0, g, n - 1)

    return pl.pallas_call(
        mid_kernel,
        grid=(2, n),
        in_specs=[
            const((length, width)),
            pl.BlockSpec((None, width, GROUP), lambda p, g: (first(p, g) // gb, 0, first(p, g) % gb)),
            const((length, channels)),
            const((length, 128)),
            pl.BlockSpec(memory_space=pl.ANY),
        ],
        out_specs=[
            pl.BlockSpec((length, GROUP), lambda p, g: (0, first(p, g))),
            pl.BlockSpec((8, shard, GROUP), lambda p, g: (0, 0, g * p)),
            const((length, 128)),
            pl.BlockSpec((8, GROUP), lambda p, g: (0, first(p, g))),
            pl.BlockSpec(memory_space=pl.ANY),
        ],
        out_shape=(
            jax.ShapeDtypeStruct((length, channels), BF16),
            jax.ShapeDtypeStruct((8, shard, channels), BF16),
            jax.ShapeDtypeStruct((length, 128), F32),
            jax.ShapeDtypeStruct((8, channels), F32),
            jax.ShapeDtypeStruct((EARLY, po.shape[2]), BF16),
        ),
        scratch_shapes=[
            pltpu.VMEM((width, length), BF16),
            pltpu.VMEM((length, 128), F32),
            pltpu.VMEM((8, length), F32),
            pltpu.VMEM((8, length), F32),
            pltpu.SemaphoreType.DMA((2,)),
            pltpu.SemaphoreType.DMA((2,)),
        ],
        compiler_params=pltpu.CompilerParams(
            collective_id=3, has_side_effects=True, vmem_limit_bytes=VMEM_LIMIT
        ),
        name="middle",
    )(cf, wo, hid, ir, po)


SHIP_COPIES = 24


def scan_grad_all_kernel(*refs):
    (go_ref, po_ref, nt_ref), refs = refs[0:3], refs[3:]
    ins, refs = refs[0:21], refs[21:]
    outs, refs = refs[0:5], refs[5:]
    own_out, raw_out, gate_out, sum0, sum1, sum2 = refs[0:6]
    scratch, refs = refs[6:14], refs[14:]
    gm, gr, gf, gfr, gs, gsr, gz, gzr, tm, ts, tr, tf, tfr, tg, tgr, send, recv, local = refs
    h, l, _, c, x, y, rx, ry, rc = places()
    zh, zl, zd = {"zh": 1 - h}, {"zl": 1 - l}, {"zh": 1 - h, "zl": 1 - l}
    to_x, to_y, to_c = {"row": rx}, {"row": ry}, {"row": rc}
    shard, cb = own_out.shape
    copy = table(send, recv)
    step = pl.program_id(0)
    groups = pl.num_programs(0)
    first, second = (to_x, to_y), (to_y, to_x)
    mine, along = (x, y), (y, x)
    dgate_ref = outs[0]

    def near(b, j):
        lanes = slice(b * cb, (b + 1) * cb)
        return pltpu.make_async_copy(go_ref.at[2 * j + c, :, lanes], gm.at[b, j], local.at[4 * b + j])

    def core(b, j):
        lanes = slice(b * cb, (b + 1) * cb)
        return copy(4 * b + j, go_ref.at[2 * j + 1 - c, :, lanes], gr.at[b, j], to_c)

    def hop1(b):
        return copy(8 + b, gf.at[b], gfr.at[b], first[b])

    def hop2(b):
        return copy(10 + b, gs.at[b], gsr.at[b], second[b])

    def hop3():
        return copy(18, gz, gzr, zh)

    def settle(b):
        hop2(b).wait_recv()
        own = along[b]
        return add(gm[b, spot(b, mine[b], own)], gfr[b, own]) + gsr[b].astype(F32)

    def out_sums():
        late = pl.ds(EARLY, po_ref.shape[1] - EARLY)
        return [
            copy(12, po_ref.at[2 * h + 1 - l], sum0, zl),
            copy(13, po_ref.at[2 * (1 - h) + l], sum1, zh),
            copy(14, po_ref.at[2 * (1 - h) + 1 - l, late], sum2, zd),
        ]

    def gate_core():
        return copy(15, ts, tr, to_c)

    def gate_hop1():
        return copy(16, tf, tfr, to_y)

    def gate_hop2():
        return copy(17, tg, tgr, to_x)

    def spot(b, at_first, at_second):
        return 2 * at_first + at_second if b else 2 * at_second + at_first

    def add(a, b):
        return a.astype(F32) + b.astype(F32)

    @pl.when(step == 0)
    def _():
        meet((zh, zl, zd, to_x, to_y, to_c))
        for b in range(2):
            for j in range(4):
                core(b, j).start()
                near(b, j).start()
        for move in out_sums():
            move.start()

    @pl.when(step == 1)
    def _():
        for b in range(2):
            for j in range(4):
                near(b, j).wait()
                core(b, j).wait_recv()
            for s in range(2):
                j = spot(b, 1 - mine[b], s)
                gf[b, s] = add(gm[b, j], gr[b, j]).astype(BF16)
            hop1(b).start()
            for s in range(2):
                j = spot(b, mine[b], s)
                gm[b, j] = add(gm[b, j], gr[b, j]).astype(BF16)

    @pl.when(step == 4)
    def _():
        for b in range(2):
            hop1(b).wait_recv()
            far = 1 - along[b]
            gs[b] = add(gm[b, spot(b, mine[b], far)], gfr[b, far]).astype(BF16)
            hop2(b).start()

    @pl.when(step == 5)
    def _():
        gate_core().wait_recv()
        for n in range(2):
            tf[n] = add(tm[spot(1, 1 - y, n)], tr[spot(1, 1 - y, n)]).astype(BF16)
        gate_hop1().start()
        for n in range(2):
            tm[spot(1, y, n)] = add(tm[spot(1, y, n)], tr[spot(1, y, n)]).astype(BF16)

    @pl.when(step == 6)
    def _():
        gz[...] = settle(1).astype(BF16)
        hop3().start()

    @pl.when(step == groups - 1)
    def _():
        gate_hop1().wait_recv()
        tg[...] = add(tm[spot(1, y, 1 - x)], tfr[1 - x]).astype(BF16)
        gate_hop2().start()

    scan_grad_kernel(lax.rem(step + groups // 2, groups), *ins, *outs, *scratch)

    def products(other, own):
        for side, ref in ((1 - c, other), (c, own)):
            value = dot_nn(nt_ref[side], dgate_ref[...]).astype(BF16)
            for j in range(4):
                ref[j] = value[j * shard : (j + 1) * shard]

    @pl.when(step < groups // 2)
    def _():
        lanes = pl.ds(pl.multiple_of(step * GROUP, GROUP), GROUP)
        products(ts.at[:, :, lanes], tm.at[:, :, lanes])

    @pl.when(step == groups // 2 - 1)
    def _():
        gate_core().start()

    @pl.when(step >= groups // 2)
    def _():
        products(raw_out.at[0], raw_out.at[1])

    @pl.when(step == groups - 1)
    def _():
        own_out[...] = settle(0)
        hop3().wait_recv()
        own_out[...] += gzr[...].astype(F32)
        gate_hop2().wait_recv()
        total = add(tm[spot(1, y, x)], tfr[x]) + tgr[...].astype(F32)
        gate_out[...] = total.astype(BF16)
        for b in range(2):
            for j in range(4):
                core(b, j).wait_send()
            hop1(b).wait_send()
            hop2(b).wait_send()
        for move in (gate_core(), gate_hop1(), gate_hop2(), hop3()):
            move.wait_send()
        for move in out_sums():
            move.wait()


def scan_grad_all(go, po, nt, *args):
    length, channels = args[0].shape
    groups = channels // GROUP
    ins, outs, shapes, scratch = scan_grad_specs(length, channels, groups // 2)
    _, shard, _ = go.shape
    feat = po.shape[2]
    cb = channels // 2
    anywhere = pl.BlockSpec(memory_space=pl.ANY)
    V = pltpu.VMEM
    return pl.pallas_call(
        scan_grad_all_kernel,
        grid=(groups,),
        in_specs=[anywhere, anywhere, once(nt.shape)] + ins,
        out_specs=outs
        + [
            once((shard, cb)),
            pl.BlockSpec((2, 4, shard, GROUP), lambda g: (0, 0, 0, jnp.maximum(g - groups // 2, 0))),
            once((shard, cb)),
            anywhere,
            anywhere,
            anywhere,
        ],
        out_shape=shapes
        + (
            jax.ShapeDtypeStruct((shard, cb), F32),
            jax.ShapeDtypeStruct((2, 4, shard, cb), BF16),
            jax.ShapeDtypeStruct((shard, cb), BF16),
            jax.ShapeDtypeStruct((length, feat), BF16),
            jax.ShapeDtypeStruct((length, feat), BF16),
            jax.ShapeDtypeStruct((length - EARLY, feat), BF16),
        ),
        scratch_shapes=scratch
        + [
            V((2, 4, shard, cb), BF16),
            V((2, 4, shard, cb), BF16),
            V((2, 2, shard, cb), BF16),
            V((2, 2, shard, cb), BF16),
            V((2, shard, cb), BF16),
            V((2, shard, cb), BF16),
            V((shard, cb), BF16),
            V((shard, cb), BF16),
            V((4, shard, cb), BF16),
            V((4, shard, cb), BF16),
            V((4, shard, cb), BF16),
            V((2, shard, cb), BF16),
            V((2, shard, cb), BF16),
            V((shard, cb), BF16),
            V((shard, cb), BF16),
            pltpu.SemaphoreType.DMA((SHIP_COPIES,)),
            pltpu.SemaphoreType.DMA((SHIP_COPIES,)),
            pltpu.SemaphoreType.DMA((8,)),
        ],
        compiler_params=pltpu.CompilerParams(
            collective_id=4, has_side_effects=True, vmem_limit_bytes=VMEM_LIMIT
        ),
        name="scan_grad_all",
    )(go, po, nt, *args)


def finish_kernel(
    at_ref, tok_ref, cot_ref, s0_ref, s1_ref, s2_ref, s3_ref, own_ref, away_ref, rowv_ref, small_ref,
    thin_ref, gain_ref, po_ref,
    out_ref, grad_ref, gg_ref, cx_ref, cb_ref, ig_ref, heads_ref, bct_ref, bcb_ref, tb_ref, td_ref,
    po_v, root_v, tail_v, sem,
):
    h, l = at_ref[0], at_ref[1]
    _, length, feat = tok_ref.shape
    hb = td_ref.shape[1]
    block = pltpu.make_async_copy(po_ref.at[2 * h + l], po_v, sem.at[0])
    block.start()

    def pick(v):
        n = v.shape[1] // 2
        v = jnp.where(h == 0, v[:, 0:n], v[:, n:])
        return half(v)

    def half(v):
        n = v.shape[1] // 2
        return jnp.where(l == 0, v[:, 0:n], v[:, n:])

    chg = small_ref[0, 0:8] + small_ref[1, 8:16]
    cx_ref[...] = chg[0:KW]
    cb_ref[...] = chg[4:5]
    ig_ref[...] = chg[6:7]
    wide = chg.shape[1]
    pick_r = lax.broadcasted_iota(jnp.int32, (wide, 128), 0)
    pick_c = lax.broadcasted_iota(jnp.int32, (wide, 128), 1)
    heads_ref[...] = dot_exact(chg, (pick_r // HEADDIM == pick_c).astype(F32))
    heads_ref[0:1, :] = chg[7:8, 0:128]
    last = small_ref[0, 16:24] + small_ref[1, 16:24] + small_ref[2, 16:24] + small_ref[3, 16:24]
    gg_ref[...] = half(jnp.where(h == 0, last[0:1], last[1:2]))
    for n in range(KW):
        bct_ref[n : n + 1, :] = pick(last[2:3, n * 256 : n * 256 + 256])
    bcb_ref[...] = pick(last[3:4, 0:256])
    tb_ref[...] = half(thin_ref[:, 0:128])
    td_ref[...] = thin_ref[:, 128 : 128 + hb] + thin_ref[:, 256 + hb : 256 + 2 * hb]

    def column(v):
        return jnp.transpose(jnp.broadcast_to(v, (128, length)))

    for n in range(2):
        root = rowv_ref[n, 1:2]
        dots = rowv_ref[n, 0:1] + rowv_ref[n + 2, 0:1]
        root_v[n] = column(root)
        tail_v[n] = column(root * root / (4 * feat) * dots)
    block.wait()

    def piece(p, carry):
        rows = pl.ds(pl.multiple_of(p * 128, 128), 128)
        for n, seq, d_ref in ((0, h, own_ref), (1, 1 - h, away_ref)):
            x = tok_ref[seq, rows].astype(F32)
            root = jnp.concatenate([root_v[n, rows, :]] * (feat // 128), axis=1)
            tail = jnp.concatenate([tail_v[n, rows, :]] * (feat // 128), axis=1)
            grad = cot_ref[seq, rows].astype(F32) + root * gain_ref[...] * d_ref[rows].astype(F32)
            grad_ref[seq, rows] = (grad - x * tail).astype(BF16)
        total = tok_ref[h, rows].astype(F32) + po_v[rows].astype(F32) + s0_ref[rows].astype(F32)
        out_ref[h, rows] = total.astype(BF16)
        return carry

    lax.fori_loop(0, length // 128, piece, 0)
    for lo, hi, part in ((0, EARLY, s3_ref), (EARLY, length, s2_ref)):
        total = tok_ref[1 - h, lo:hi].astype(F32) + s1_ref[lo:hi].astype(F32) + part[...].astype(F32)
        out_ref[1 - h, lo:hi] = total.astype(BF16)


def finish(at, tok, cot, s0, s1, s2, s3, own, away, rowv, small, thin, gain, po, hb):
    _, length, feat = tok.shape
    shard, cb = thin.shape[0], small.shape[2]
    inside = pl.BlockSpec(memory_space=pltpu.VMEM)
    rows = jax.ShapeDtypeStruct((2, length, feat), BF16)

    def f32(*shape):
        return jax.ShapeDtypeStruct(shape, F32)

    return pl.pallas_call(
        finish_kernel,
        in_specs=[pl.BlockSpec(memory_space=pltpu.SMEM)] + [inside] * 12 + [pl.BlockSpec(memory_space=pl.ANY)],
        out_specs=[inside] * 11,
        out_shape=(
            rows, rows, f32(1, feat), f32(KW, cb), f32(1, cb), f32(1, cb), f32(8, 128), f32(KW, STATE // 2),
            f32(1, STATE // 2), f32(shard, STATE // 2), f32(shard, hb),
        ),
        scratch_shapes=[
            pltpu.VMEM((length, feat), BF16),
            pltpu.VMEM((2, length, 128), F32),
            pltpu.VMEM((2, length, 128), F32),
            pltpu.SemaphoreType.DMA((1,)),
        ],
        compiler_params=pltpu.CompilerParams(vmem_limit_bytes=VMEM_LIMIT),
        name="finish",
    )(at, tok, cot, s0, s1, s2, s3, own, away, rowv, small, thin, gain, po)


def pack_kernel(
    at_ref, cx_ref, cb_ref, ds_ref, ig_ref, dtb_ref, alog_ref, ng_ref, bct_ref, bcb_ref, seg_ref,
    par_ref, segc_ref, segr_ref,
):
    h, l = at_ref[0], at_ref[1]
    here = 2 * h + l
    wide, hb = par_ref.shape[1], ds_ref.shape[1]
    bcn = bct_ref.shape[1]
    par_ref[...] = jnp.zeros_like(par_ref)
    par_ref[0:KW, :] = cx_ref[...]
    par_ref[4:5, :] = cb_ref[...]
    head = lax.broadcasted_iota(jnp.int32, (hb, wide), 0)
    lane = lax.broadcasted_iota(jnp.int32, (hb, wide), 1)
    skip = dot_exact(jnp.broadcast_to(ds_ref[...], (8, hb)), (lane // HEADDIM == head).astype(F32))
    par_ref[5:6, :] = skip[0:1]
    par_ref[6:7, :] = ig_ref[...]
    par_ref[8:9, 0 : ng_ref.shape[1]] = ng_ref[...]
    for n in range(4):
        lanes = slice(n * bcn, (n + 1) * bcn)
        par_ref[9 : 9 + KW, lanes] = jnp.where(here == n, bct_ref[...], 0.0)
        par_ref[9 + KW : 10 + KW, lanes] = jnp.where(here == n, bcb_ref[...], 0.0)
    par_ref[14:15, 0:hb] = dtb_ref[...]
    par_ref[15:16, 0:hb] = alog_ref[...]
    row = jnp.where(h == 0, seg_ref[0:1, :], seg_ref[1:2, :])
    segr_ref[...] = jnp.broadcast_to(row, segr_ref.shape)
    cols = jnp.transpose(jnp.broadcast_to(row.astype(F32), (128, row.shape[1])))
    segc_ref[...] = cols.astype(jnp.int32)


def pack(at, cx, cxb, ds, ig, dtb, alog, ng, bct, bcb, seg):
    length, cb = seg.shape[1], cx.shape[1]
    return pl.pallas_call(
        pack_kernel,
        in_specs=[pl.BlockSpec(memory_space=pltpu.SMEM)] + [pl.BlockSpec(memory_space=pltpu.VMEM)] * 10,
        out_shape=(
            jax.ShapeDtypeStruct((16, cb), F32),
            jax.ShapeDtypeStruct((length, 128), jnp.int32),
            jax.ShapeDtypeStruct((8, length), jnp.int32),
        ),
        compiler_params=pltpu.CompilerParams(vmem_limit_bytes=VMEM_LIMIT),
        name="pack",
    )(at, cx, cxb[None], ds[None], ig[None], dtb[None], alog[None], ng[None], bct, bcb[None], seg)


def build(nrow, nl):
    direct = nrow == 8 and nl == 2
    col = ("zh", "zl")

    def swap(v):
        return lax.ppermute(v, "zh", [(0, 1), (1, 0)])

    def pair_sum(v):
        return lax.psum(v, "zl")

    def row_gather(v):
        return lax.all_gather(v, "row", axis=0, tiled=True)

    def row_scatter(v):
        return lax.psum_scatter(v, "row", scatter_dimension=0, tiled=True)

    def per_device(
        tokens, segment_ids, norm_gain, in_zx, in_dt, in_bc, conv_x, conv_x_bias, conv_bc,
        conv_bc_bias, dt_bias, a_log, d_skip, inner_gain, out_proj, cotangent,
    ):
        seq_count, length = segment_ids.shape
        assert seq_count == 2
        feat = tokens.shape[1]
        width = feat * 2 * nl
        cb = inner_gain.shape[0]
        hb = dt_bias.shape[0]
        inner = cb * 2 * nl
        blocks = length // SPAN
        gb = cb // GROUP
        mh = lax.axis_index("zh")
        ml = lax.axis_index("zl")
        first_h = mh == 0
        here = mh * nl + ml
        bcn = conv_bc.shape[1]

        def mine(v, axis=0):
            return lax.dynamic_index_in_dim(v, mh, axis, keepdims=False)

        def other(v, axis=0):
            return lax.dynamic_index_in_dim(v, 1 - mh, axis, keepdims=False)

        def seqs(v):
            return v.reshape(2, length, feat)

        def by_seq(own, away):
            return jnp.where(first_h, jnp.stack([own, away]), jnp.stack([away, own]))

        def place(own, away):
            both = jnp.zeros((2,) + own.shape, own.dtype)
            both = lax.dynamic_update_slice(both, own[None], (mh, 0, 0))
            return lax.dynamic_update_slice(both, away[None], (1 - mh, 0, 0)).reshape(-1, own.shape[1])

        def gather_features(v):
            own, away = mine(seqs(v)), other(seqs(v))
            both = by_seq(own, swap(away))
            every = jnp.moveaxis(lax.all_gather(both, "zl"), 0, 1)
            return jnp.transpose(every, (2, 0, 1, 3)).reshape(length, width)

        def scatter_features(v):
            parts = v.reshape(length, 2, nl, feat)
            both = lax.psum_scatter(parts, "zl", scatter_dimension=2, tiled=False)
            return by_seq(mine(both, 1), swap(other(both, 1))).astype(F32)

        chan = jnp.concatenate(
            [
                conv_x,
                conv_x_bias[None],
                jnp.repeat(d_skip, HEADDIM)[None],
                inner_gain[None],
                jnp.pad(jnp.concatenate([dt_bias, a_log]), (0, cb - 2 * hb))[None],
            ],
            axis=0,
        )
        thin = jnp.concatenate([in_bc, in_dt], axis=1)
        bc_rows = jnp.concatenate([conv_bc, conv_bc_bias[None]], axis=0)
        seg = mine(segment_ids)
        segc = jnp.broadcast_to(seg[:, None], (length, 128))
        segr = jnp.broadcast_to(seg[None, :], (8, length))
        if direct:
            at = jnp.stack([mh, ml]).astype(jnp.int32)
            par, segc, segr = pack(
                at, conv_x, conv_x_bias, d_skip, inner_gain, dt_bias, a_log, norm_gain, conv_bc, conv_bc_bias,
                segment_ids,
            )
            chan = par[0:8]
            thin = jnp.pad(thin, ((0, 0), (0, 128 - thin.shape[1])))
            (
                normed, normed_t, inv_root, par, w_small, small, hp, bcp,
                bc, bct, gmat, gtmat, colp, cumt, kexp, lag, w_gate, w_x,
            ) = gather_all(
                seqs(tokens), in_zx[:, 0], in_zx[:, 1], thin, par, segc, segr, 2 * gb,
            )
            chan_got = lax.dynamic_index_in_dim(par, (1 - mh) * nl + ml, 0, keepdims=False)[0:8]
            gain = par[:, 8, :feat].reshape(width)
        else:
            chan_got = swap(chan)
            packed = jnp.concatenate([norm_gain, bc_rows.reshape(-1)])
            packs = lax.all_gather(packed, col)
            gain = packs[:, :feat].reshape(width)
            bc_all = jnp.moveaxis(packs[:, feat:].reshape(-1, KW + 1, bcn), 0, 1)
            bcp = jnp.pad(bc_all.reshape(KW + 1, 2 * STATE), ((0, 7 - KW), (0, 0)))
            hp = jnp.concatenate([c[7, : 2 * hb].reshape(2, hb) for c in (chan, chan_got)], axis=1)
            hp = jnp.pad(hp, ((0, 6), (0, 128 - 2 * hb)))
            thin = lax.all_gather(thin, ("row", "zh", "zl")).reshape(nrow, 2, nl, -1, bcn + hb)
            thin = jnp.moveaxis(thin, 3, 1).reshape(width, 2, nl, bcn + hb)
            w_gate = jnp.stack([row_gather(w) for w in (in_zx[:, 0], swap(in_zx[:, 0]))])
            w_x = jnp.stack([row_gather(w) for w in (in_zx[:, 1], swap(in_zx[:, 1]))])
            w_bc = thin[..., :bcn].reshape(width, 2 * STATE)
            w_dt = lax.dynamic_index_in_dim(thin[..., bcn:], ml, 2, keepdims=False)
            w_small = jnp.concatenate([w_bc, mine(w_dt, 1), other(w_dt, 1)], axis=1)
            w_small = jnp.pad(w_small, ((0, 0), (0, 384 - w_small.shape[1])))
            x32 = gather_features(tokens).astype(F32)
            inv_root = lax.rsqrt(jnp.mean(x32 * x32, axis=1, keepdims=True) + EPS)
            normed = (x32 * inv_root * gain).astype(BF16)
            small = dot_nn(normed, w_small)
            bc, bct, gmat, gtmat, colp, cumt, kexp, lag = prep(small, segc, segr, bcp, hp, 2 * gb)
        chans = jnp.concatenate([chan, chan_got], axis=1)
        kexp = jnp.repeat(kexp[:, : 2 * hb], HEADDIM, axis=1)

        seq_args = (lag, bc, bct, gmat, colp, cumt, kexp)
        gain_in = chans[6]
        if direct:
            gates, xrs, vs, ys, hidden, _, sts, partial_out, ir, c_full, w_out = scan_all(
                seqs(cotangent), out_proj, normed, w_gate, w_x, chans, *seq_args
            )
            dh, g_out, cf, g_ig, sum3 = middle(c_full, w_out, hidden, ir, partial_out)
        else:
            w_out = [row_gather(w) for w in (out_proj, swap(out_proj))]
            c_full = gather_features(cotangent)
            gates, xrs, vs, ys, gateds, sq, sts = scan(normed, w_gate, w_x, chans, *seq_args)
            dh = jnp.concatenate([dot_nn(c_full, w).astype(BF16) for w in w_out], axis=1)
            gate_sq = pair_sum(jnp.sum(sq, axis=1))
            inner_root = lax.rsqrt(gate_sq / inner + EPS)[:, None]
            gate_dot = jnp.sum(dh.astype(F32) * gateds.astype(F32) * gain_in, axis=1)
            gate_dot = pair_sum(gate_dot)[:, None]
            hidden = (gateds.astype(F32) * inner_root * gain_in).astype(BF16)
            partial_out = dot_nt(hidden[:, :cb], w_out[0]) + dot_nt(hidden[:, cb:], w_out[1])
            partial_out = partial_out.astype(BF16)
            ir = jnp.broadcast_to(inner_root, (length, 128))
            cf = jnp.broadcast_to(inner_root**3 / inner * gate_dot, (length, 128))
            g_out = [dot_tn(c_full, hidden[:, :cb]), dot_tn(c_full, hidden[:, cb:])]
            g_out = [row_scatter(g.astype(BF16)) for g in g_out]
            g_wout = g_out[0].astype(F32) + swap(g_out[1]).astype(F32)
            out_here = scatter_features(partial_out)
            g_ig = jnp.sum(dh.astype(F32) * hidden.astype(F32), axis=0, keepdims=True)

        grad_args = (
            gates, xrs, vs, ys, dh, chans, lag, ir, cf, bc, bct, gtmat, colp, cumt, kexp, sts, segc, segr,
            small, hp, bcp,
        )
        if direct:
            (
                dgates, dxrs, chg, d_small, pg, g_wout, gate_own, gate_got, sum0, sum1, sum2,
            ) = scan_grad_all(g_out, partial_out, normed_t, *grad_args)
        else:
            dgates, dxrs, chg, d_small, pg = scan_grad(*grad_args)
            output = (out_here + seqs(tokens)).astype(BF16).reshape(tokens.shape)
        chg = jnp.concatenate([chg[0:6], g_ig[0:1] / gain_in, chg[7:8]], axis=0)
        g_dtb, g_alog = pg[5, : 2 * hb], pg[6, : 2 * hb]
        g_bcs = pg[: KW + 1]

        def token_grad(pick, d, root, dot):
            root, dot = root[:, None], dot[:, None]
            grad = pick(seqs(cotangent)).astype(F32) + root * norm_gain * d
            return (grad - pick(seqs(tokens)).astype(F32) * (root * root / width * dot)).astype(BF16)

        if direct:
            rows = []
            for b in range(2):
                hs = slice(b * hb, (b + 1) * hb)
                heads = jnp.concatenate([g_dtb[hs], g_alog[hs]])
                rows += [chg[0:7, b * cb : (b + 1) * cb], jnp.pad(heads, (0, cb - 2 * hb))[None]]
            last = jnp.pad(g_bcs.reshape(-1), (0, width - g_bcs.size))
            last = jnp.concatenate([jnp.zeros_like(gain), last, gain, jnp.zeros_like(gain)]).reshape(8, cb)
            gz, thins, smalls, d_own, d_away, rowv = grad_all(
                gate_own, w_gate, w_x, w_small, normed, gate_got, normed_t, dgates, dxrs, d_small,
                jnp.concatenate(rows + [last], axis=0), inv_root,
            )
            (
                output, tokens_grad, g_gain, g_cx, g_cxb, g_igain, heads, g_cb, g_cbb, g_bc, g_dt,
            ) = finish(
                at, seqs(tokens), seqs(cotangent), sum0, sum1, sum2, sum3,
                d_own, d_away, rowv, smalls, thins, norm_gain[None], partial_out, hb,
            )
            return (
                output.reshape(tokens.shape), tokens_grad.reshape(tokens.shape), g_gain.reshape(feat),
                jnp.transpose(gz, (1, 0, 2)), g_dt, g_bc, g_cx, g_cxb.reshape(cb), g_cb, g_cbb.reshape(bcn),
                heads[0, :hb], heads[0, hb : 2 * hb], heads[5, :hb], g_igain.reshape(cb), g_wout,
            )
        else:
            dn, gg = back(dgates, dxrs, d_small, w_gate, w_x, w_small, normed)
            g_gain = gg[0] / gain
            dn = jnp.moveaxis(dn, 0, 1).reshape(length, width)
            d_here = scatter_features(dn)
            dots = pair_sum(jnp.sum(dn.astype(F32) * normed.astype(F32), axis=1))
            own = token_grad(mine, mine(d_here), inv_root[:, 0], dots)
            away = token_grad(other, other(d_here), swap(inv_root[:, 0]), swap(dots))
            tokens_grad = place(own, away)

            def join(own, away):
                return own.astype(F32) + swap(away).astype(F32)

            halves = (slice(0, cb), slice(cb, 2 * cb))
            g_gate = [row_scatter(dot_tn(normed, dgates[:, n]).astype(BF16)) for n in halves]
            g_x = [row_scatter(dot_tn(normed, dxrs[:, n]).astype(BF16)) for n in halves]
            g_zx = jnp.stack([join(*g_gate), join(*g_x)], axis=1)
            thins = row_scatter(dot_tn(normed, d_small))
            g_bc = lax.psum(thins[:, : 2 * STATE], col).reshape(-1, 2 * nl, bcn)
            g_bc = lax.dynamic_index_in_dim(g_bc, here, 1, keepdims=False)
            g_dts = thins[:, 2 * STATE : 2 * STATE + 2 * hb].reshape(-1, 2, hb)
            g_dt = g_dts[:, 0] + swap(g_dts[:, 1])
            every = ("row", "zh", "zl")
            g_gain, g_bcs = lax.psum((g_gain, g_bcs), every)
            g_gain = lax.dynamic_slice(g_gain, (here * feat,), (feat,))
            g_bcs = g_bcs.reshape(KW + 1, 2 * nl, bcn)
            g_bcs = lax.dynamic_index_in_dim(g_bcs, here, 1, keepdims=False)
            chg = chg[:, :cb] + swap(chg[:, cb:])
            g_dtb = g_dtb[:hb] + swap(g_dtb[hb:])
            g_alog = g_alog[:hb] + swap(g_alog[hb:])
            chg, g_dtb, g_alog = lax.psum((chg, g_dtb, g_alog), "row")
        return (
            output,
            tokens_grad,
            g_gain,
            g_zx,
            g_dt,
            g_bc,
            chg[0:KW],
            chg[4],
            g_bcs[0:KW],
            g_bcs[KW],
            g_dtb,
            g_alog,
            chg[5].reshape(hb, HEADDIM).sum(1),
            chg[6],
            g_wout,
        )

    return per_device


def solution(mesh):
    nrow, ncol = mesh.shape["row"], mesh.shape["col"]
    nl = ncol // 2
    split = Mesh(mesh.devices.reshape(nrow, 2, nl), ("row", "zh", "zl"))
    col = ("zh", "zl")
    in_specs = (
        P("row", col), P("row", None), P(col), P("row", None, col), P("row", col), P("row", col),
        P(None, col), P(col), P(None, col), P(col), P(col), P(col), P(col), P(col),
        P("row", col), P("row", col),
    )
    out_specs = (
        P("row", col), P("row", col), P(col), P("row", None, col), P("row", col), P("row", col),
        P(None, col), P(col), P(None, col), P(col), P(col), P(col), P(col), P(col), P("row", col),
    )
    return jax.shard_map(
        build(nrow, nl), mesh=split, in_specs=in_specs, out_specs=out_specs, check_vma=False
    )
```
